32 devices in a mesh: section: 4 (over x, core), seq: 8 (over z, y).
Axes of the slice: x: 2, y: 2, z: 4, core: 2. Of those that a mesh axis runs over, the one named last changes fastest.
Arguments:
- inputs: bfloat16 [4, 2048, 1536], P('section', 'seq'), may hold values from -6 to 6
- lengths: int32 [4], replicated, may hold values from 256 to 2048, as said below
- cotangent: bfloat16 [4, 2048, 1536], P('section', 'seq'), may hold values from -6 to 6
- attn_gain: float32 [4, 1536], P('section', 'seq'), may hold values from 0.5 to 1.5
- w_query: float32 [4, 1536, 1536], P('section', 'seq'), may hold values from -0.15625 to 0.15625
- key_projection: float32 [4, 1536, 768], P('section', 'seq'), may hold values from -0.15625 to 0.15625
- value_projection: float32 [4, 1536, 768], P('section', 'seq'), may hold values from -0.15625 to 0.15625
- w_out: float32 [4, 1536, 1536], P('section', None, 'seq'), may hold values from -3.5 to 3.5
- mlp_gain: float32 [4, 1536], P('section', 'seq'), may hold values from 0.5 to 1.5
- w_gate: float32 [4, 1536, 4096], P('section', 'seq'), may hold values from -0.15625 to 0.15625
- w_up: float32 [4, 1536, 4096], P('section', 'seq'), may hold values from -0.15625 to 0.15625
- w_down: float32 [4, 4096, 1536], P('section', None, 'seq'), may hold values from -0.09375 to 0.09375
Outputs:
- output: bfloat16 [4, 2048, 1536], P('section', 'seq')
- input_grad: bfloat16 [4, 2048, 1536], P('section', 'seq')
- attn_gain_grad: float32 [4, 1536], P('section', 'seq')
- query_weight_grad: float32 [4, 1536, 1536], P('section', 'seq')
- key_weight_grad: float32 [4, 1536, 768], P('section', 'seq')
- value_weight_grad: float32 [4, 1536, 768], P('section', 'seq')
- out_weight_grad: float32 [4, 1536, 1536], P('section', None, 'seq')
- mlp_gain_grad: float32 [4, 1536], P('section', 'seq')
- gate_weight_grad: float32 [4, 1536, 4096], P('section', 'seq')
- up_weight_grad: float32 [4, 1536, 4096], P('section', 'seq')
- down_weight_grad: float32 [4, 4096, 1536], P('section', None, 'seq')
The draws below stay inside these ranges and needn't reach their ends.
Inputs may be any that keep to these rules, and one draw needn't show every extreme that they name: Every micro-batch's sequence holds its first lengths[m] positions; one has 2048 and one 2048 // 8.
All inputs are finite; a program needn't handle non-finite values.
Results may differ from the reference program's by a relative error of at most 0.035.
Values may be sent and summed in bfloat16 or wider, within the bound.
A program may use at most 704 MiB of HBM per device.

```python
import math
import jax
import jax.numpy as jnp
from jax import lax

MODEL_WIDTH = 1536
QUERY_HEADS = 16
KEY_VALUE_HEADS = 8
HEAD_SIZE = 96
FF = 4096
PADDED_LENGTH = 2048
MICRO = 4
DECODER_LAYERS = 4


def draw_lengths(key, part):
    key = jax.random.fold_in(key, 7)
    first_key, second_key = jax.random.split(key)
    shortest = PADDED_LENGTH // 8
    value_rows = jax.random.randint(first_key, (MICRO,), shortest, PADDED_LENGTH + 1)
    order = jax.random.permutation(second_key, MICRO)
    value_rows = jnp.where(order == 0, PADDED_LENGTH, value_rows)
    value_rows = jnp.where(order == 1, shortest, value_rows)
    return value_rows.astype(jnp.int32)


def steps_of(stream_key, dims, cuts, smallest, high):
    gain, own = 1.0, jax.random.fold_in(stream_key, 6)
    for position, parts in cuts:
        draws = jnp.exp(jax.random.uniform(jax.random.fold_in(own, position), (parts,), jnp.float32, smallest / len(cuts), high / len(cuts)))
        gain = gain * jnp.repeat(draws, dims[position] // parts).reshape([-1 if axis == position else 1 for axis in range(len(dims))])
    return gain


def bell_draw(key, shape, width, bound, cuts=(), kind=jnp.bfloat16):
    values = jax.random.normal(key, shape, jnp.float32) * width
    if len(cuts) > 0:
        values = steps_of(key, shape, cuts, -0.22, 0.18) * values
    return jnp.clip(values, min=-bound, max=bound).astype(kind)


def setup_inputs(seed: int = 0) -> dict:
    keys = jax.random.split(jax.random.key(seed), 13)
    inputs = bell_draw(keys[0], (MICRO, PADDED_LENGTH, MODEL_WIDTH), 1.0, 6.0, ((0, 4), (1, 8)))
    lengths = draw_lengths(jax.random.fold_in(keys[12], 71), 0)
    cotangent = bell_draw(keys[2], (MICRO, PADDED_LENGTH, MODEL_WIDTH), 1.0, 6.0, ((0, 4), (1, 8)))
    attn_gain = jnp.clip(1.0 + 0.1 * jax.random.normal(keys[3], (DECODER_LAYERS, MODEL_WIDTH), jnp.float32), 0.5, 1.5)
    w_query = bell_draw(keys[4], (DECODER_LAYERS, MODEL_WIDTH, QUERY_HEADS * HEAD_SIZE), MODEL_WIDTH ** -0.5, 0.15625, ((0, 4), (1, 8)), jnp.float32)
    key_projection = bell_draw(keys[5], (DECODER_LAYERS, MODEL_WIDTH, KEY_VALUE_HEADS * HEAD_SIZE), MODEL_WIDTH ** -0.5, 0.15625, ((0, 4), (1, 8)), jnp.float32)
    value_projection = bell_draw(keys[6], (DECODER_LAYERS, MODEL_WIDTH, KEY_VALUE_HEADS * HEAD_SIZE), MODEL_WIDTH ** -0.5, 0.15625, ((0, 4), (1, 8)), jnp.float32)
    w_out = bell_draw(keys[7], (DECODER_LAYERS, QUERY_HEADS * HEAD_SIZE, MODEL_WIDTH), (max(1, 4 * QUERY_HEADS * HEAD_SIZE // PADDED_LENGTH)) ** -0.5, 3.5, ((0, 4), (2, 8)), jnp.float32)
    mlp_gain = jnp.clip(1.0 + 0.1 * jax.random.normal(keys[8], (DECODER_LAYERS, MODEL_WIDTH), jnp.float32), 0.5, 1.5)
    w_gate = bell_draw(keys[9], (DECODER_LAYERS, MODEL_WIDTH, FF), MODEL_WIDTH ** -0.5, 0.15625, ((0, 4), (1, 8)), jnp.float32)
    w_up = bell_draw(keys[10], (DECODER_LAYERS, MODEL_WIDTH, FF), MODEL_WIDTH ** -0.5, 0.15625, ((0, 4), (1, 8)), jnp.float32)
    w_down = bell_draw(keys[11], (DECODER_LAYERS, FF, MODEL_WIDTH), FF ** -0.5, 0.09375, ((0, 4), (2, 8)), jnp.float32)
    return {"inputs": inputs, "lengths": lengths, "cotangent": cotangent, "attn_gain": attn_gain, "w_query": w_query, "key_projection": key_projection, "value_projection": value_projection, "w_out": w_out, "mlp_gain": mlp_gain, "w_gate": w_gate, "w_up": w_up, "w_down": w_down}


EPS = 1e-05
THETA = 100000.0
LOWER_LIMIT = -1e+30
UPPER_LIMIT = lax.Precision.HIGHEST

@jax.custom_vjp
def lower_precision(v):
    return lax.optimization_barrier(v.astype(jnp.bfloat16)).astype(jnp.float32)

@jax.custom_vjp
def lower_backward(v):
    return v

def low_keep(v):
    return (lower_precision(v), None)

def low_pass(kept, grad):
    return (grad,)

def back_keep(v):
    return (v, None)

def back_low(kept, grad):
    return (lower_precision(grad),)
lower_precision.defvjp(low_keep, low_pass)
lower_backward.defvjp(back_keep, back_low)

def rms_inverse(tensor):
    return lax.rsqrt(lax.optimization_barrier(jnp.mean(tensor * tensor, axis=-1, keepdims=True)) + EPS)

def rotate_halves(tensor, cosine_table, sine_values):
    half_width = tensor.shape[-1] // 2
    first_half = tensor[..., :half_width]
    second_half = tensor[..., half_width:]
    return jnp.concatenate([first_half * cosine_table - second_half * sine_values, second_half * cosine_table + first_half * sine_values], axis=-1)

def rope_tables(count_of_rows):
    positions = jnp.arange(count_of_rows).astype(jnp.float32)
    exponents = 2.0 * jnp.arange(HEAD_SIZE // 2).astype(jnp.float32) / HEAD_SIZE
    angles = positions[:, None] * (THETA ** (-exponents))[None, :]
    return (jnp.cos(angles)[:, None, :], jnp.sin(angles)[:, None, :])

def attend(query_matrix, key_rows, value_rows, length):
    block_rows = math.gcd(PADDED_LENGTH, 512)
    positions = jnp.arange(PADDED_LENGTH, dtype=jnp.int32)
    score_scale = 1.0 / math.sqrt(HEAD_SIZE)

    def one_block(index):
        start_row = (index * block_rows).astype(jnp.int32)
        rows = lax.dynamic_slice_in_dim(query_matrix, start_row, block_rows, 0)
        scores = lower_backward(jnp.einsum('tkgd,nkd->tkgn', rows, key_rows, precision=UPPER_LIMIT) * score_scale)
        row_pos = start_row + jnp.arange(block_rows, dtype=jnp.int32)
        allowed = (positions[None, :] <= row_pos[:, None]) & (positions[None, :] < length)
        scores = jnp.where(allowed[:, None, None, :], scores, LOWER_LIMIT)
        probs = lower_precision(jax.nn.softmax(scores, axis=-1))
        return jnp.einsum('tkgn,nkd->tkgd', probs, value_rows, precision=UPPER_LIMIT)
    blocks = lax.map(jax.checkpoint(one_block), jnp.arange(PADDED_LENGTH // block_rows, dtype=jnp.int32))
    return blocks.reshape(PADDED_LENGTH, QUERY_HEADS * HEAD_SIZE)

def layer(hidden_in, length, weights, cosine_table, sine_values):
    gain_one, w_q, key_weight, value_weight, w_o, gain_two, w_g, w_u, w_d = weights
    first_input = lower_precision(hidden_in * rms_inverse(hidden_in) * lower_precision(gain_one))
    query_matrix = lower_backward(jnp.dot(first_input, lower_precision(w_q), precision=UPPER_LIMIT)).reshape(PADDED_LENGTH, QUERY_HEADS, HEAD_SIZE)
    key_rows = lower_backward(jnp.dot(first_input, lower_precision(key_weight), precision=UPPER_LIMIT)).reshape(PADDED_LENGTH, KEY_VALUE_HEADS, HEAD_SIZE)
    value_rows = lower_precision(lower_backward(jnp.dot(first_input, lower_precision(value_weight), precision=UPPER_LIMIT))).reshape(PADDED_LENGTH, KEY_VALUE_HEADS, HEAD_SIZE)
    query_matrix = lower_precision(rotate_halves(query_matrix, cosine_table, sine_values)).reshape(PADDED_LENGTH, KEY_VALUE_HEADS, QUERY_HEADS // KEY_VALUE_HEADS, HEAD_SIZE)
    key_rows = lower_precision(rotate_halves(key_rows, cosine_table, sine_values))
    attended_output = lower_precision(lower_backward(attend(query_matrix, key_rows, value_rows, length)))
    middle = hidden_in + lower_backward(jnp.dot(attended_output, lower_precision(w_o), precision=UPPER_LIMIT))
    second_in = lower_precision(middle * rms_inverse(middle) * lower_precision(gain_two))
    gate_pre = lower_backward(jnp.dot(second_in, lower_precision(w_g), precision=UPPER_LIMIT))
    up_pre = lower_backward(jnp.dot(second_in, lower_precision(w_u), precision=UPPER_LIMIT))
    hidden = lower_precision(jax.nn.silu(gate_pre) * up_pre)
    return middle + lower_backward(jnp.dot(hidden, lower_precision(w_d), precision=UPPER_LIMIT))

def reference(inputs, lengths, cotangent, attn_gain, w_query, key_projection, value_projection, w_out, mlp_gain, w_gate, w_up, w_down):
    cosine_table, sine_values = rope_tables(PADDED_LENGTH)

    def forward(source, *weights):

        def one_sequence(operand):
            tokens, length = operand
            for depth in range(DECODER_LAYERS):
                tokens = layer(tokens, length, tuple((matrix[depth] for matrix in weights)), cosine_table, sine_values)
                if depth + 1 < DECODER_LAYERS:
                    tokens = lower_backward(lower_precision(tokens))
            return tokens
        return lax.map(one_sequence, (source, lengths))
    weights = tuple((matrix.astype(jnp.float32) for matrix in (attn_gain, w_query, key_projection, value_projection, w_out, mlp_gain, w_gate, w_up, w_down)))
    positions = jnp.arange(PADDED_LENGTH, dtype=jnp.int32)
    keep = (positions[None, :] < lengths[:, None]).astype(jnp.float32)
    start_grad = cotangent.astype(jnp.float32) * keep[:, :, None]
    result, pullback = jax.vjp(forward, inputs.astype(jnp.float32), *weights)
    grads = pullback(start_grad)
    return (result.astype(jnp.bfloat16), grads[0].astype(jnp.bfloat16), grads[1], grads[2], grads[3], grads[4], grads[5], grads[6], grads[7], grads[8], grads[9])
```

```python
import math

import jax
import jax.numpy as jnp
from jax import lax
from jax.sharding import Mesh
from jax.sharding import PartitionSpec as P

QUERY_HEADS = 16
KEY_VALUE_HEADS = 8
HEAD_SIZE = 96
FF = 4096

EPS = 1e-05
THETA = 100000.0
LOWER_LIMIT = -1e30

BF = jnp.bfloat16
F32 = jnp.float32

PLANE = ("x", "c", "y")


def dot(a, b, dims):
    return lax.dot_general(a, b, (dims, ((), ())), preferred_element_type=F32)


def dot_nn(a, b):
    return dot(a, b, ((1,), (0,)))


def dot_nt(a, b):
    return dot(a, b, ((1,), (1,)))


def dot_tn(a, b):
    return dot(a, b, ((0,), (0,)))


def rotate_halves(tensor, cosine, sine):
    half = tensor.shape[-1] // 2
    first = tensor[..., :half]
    second = tensor[..., half:]
    return jnp.concatenate(
        [first * cosine - second * sine, second * cosine + first * sine], axis=-1
    )


def norm_back(upstream, normed, inverse, gain_row):
    scaled = upstream * gain_row
    return inverse * (scaled - normed * jnp.mean(scaled * normed, axis=-1, keepdims=True))


def body(
    inputs,
    lengths,
    cotangent,
    attn_gain,
    w_query,
    key_projection,
    value_projection,
    w_out,
    mlp_gain,
    w_gate,
    w_up,
    w_down,
):
    sections = lax.axis_size("x") * lax.axis_size("c")
    planes = lax.axis_size("z")
    halves = lax.axis_size("y")
    extra = lax.axis_size("e")
    ranks = sections * halves
    layers = sections
    block = inputs.shape[1]
    width = inputs.shape[2]
    rows = w_query.shape[1]
    tokens = block * ranks
    all_tokens = tokens * extra
    head_group = QUERY_HEADS // KEY_VALUE_HEADS
    q_cols = head_group * HEAD_SIZE
    kv_cols = HEAD_SIZE
    ff_cols = FF // ranks
    score_scale = 1.0 / math.sqrt(HEAD_SIZE)

    def swap(array):
        names = ("x", "c", "z")
        pairs = [
            (s * planes + z, z * planes + s) for s in range(sections) for z in range(planes)
        ]
        return lax.ppermute(array, names, pairs)

    def gather_tokens(shard):
        return lax.all_gather(shard, PLANE, axis=0, tiled=True)

    def scatter_tokens(partial):
        return lax.psum_scatter(partial.astype(BF), PLANE, scatter_dimension=0, tiled=True).astype(F32)

    def by_rank(matrix):
        return matrix.reshape(rows, ranks, -1)

    attn_pack = jnp.concatenate(
        [
            by_rank(w_query[0]),
            by_rank(key_projection[0]),
            by_rank(value_projection[0]),
            by_rank(w_out[0].T),
        ],
        axis=2,
    )
    mlp_pack = jnp.concatenate(
        [by_rank(w_gate[0]), by_rank(w_up[0]), by_rank(w_down[0].T)], axis=2
    )

    def exchange(pack):
        moved = lax.all_to_all(
            jnp.swapaxes(pack.astype(BF), 0, 1), PLANE, split_axis=0, concat_axis=0, tiled=True
        )
        return moved.reshape(layers, halves, rows, pack.shape[2])

    def whole(part):
        if extra > 1:
            part = lax.all_gather(part, "e", axis=1, tiled=False)
        return lax.all_gather(part.reshape(-1, part.shape[-1]), "z", axis=0, tiled=True)

    def reduce_rows(grad):
        mine = lax.psum_scatter(grad.astype(BF), "z", scatter_dimension=0, tiled=True)
        mine = mine.reshape(halves, extra, rows, -1)
        if extra > 1:
            return lax.psum_scatter(mine, "e", scatter_dimension=1, tiled=False)
        return mine[:, 0]

    attn_parts = exchange(attn_pack)
    mlp_parts = exchange(mlp_pack)
    gains = jnp.stack([attn_gain[0], mlp_gain[0]]).astype(BF)
    gains = lax.all_gather(gains, ("x", "c", "z", "y", "e"), axis=0, tiled=False)
    gains = gains.reshape(layers, -1, 2, rows).transpose(0, 2, 1, 3).reshape(layers, 2, 1, width)
    gains = gains.astype(F32)

    rank = (lax.axis_index("x") * lax.axis_size("c") + lax.axis_index("c")) * halves + lax.axis_index("y")
    spot = lax.axis_index("e")
    length = lengths[lax.axis_index("z")]

    block_start = (jnp.arange(ranks) * extra + spot) * block
    positions = (block_start[:, None] + jnp.arange(block)[None, :]).reshape(tokens)
    exponents = 2.0 * jnp.arange(HEAD_SIZE // 2).astype(F32) / HEAD_SIZE
    angles = positions.astype(F32)[:, None] * (THETA ** (-exponents))[None, :]
    cosine = jnp.cos(angles)[:, None, :]
    sine = jnp.sin(angles)[:, None, :]
    key_positions = jnp.arange(all_tokens)
    allowed = (key_positions[None, :] <= positions[:, None]) & (key_positions[None, :] < length)
    allowed = allowed[:, None, :]

    def rotated(columns, heads, sign):
        turned = rotate_halves(columns.reshape(tokens, heads, HEAD_SIZE), cosine, sign * sine)
        return turned.reshape(tokens, heads * HEAD_SIZE).astype(BF)

    def all_keys(array):
        if extra == 1:
            return array
        stacked = lax.all_gather(array.reshape(ranks, block, -1), "e", axis=1, tiled=False)
        return stacked.reshape(all_tokens, -1)

    def own_keys(array):
        if extra == 1:
            return array
        stacked = array.astype(BF).reshape(ranks, extra, block, -1)
        return lax.psum_scatter(stacked, "e", scatter_dimension=1, tiled=False).reshape(tokens, -1).astype(F32)

    def attend(q, keys, values):
        scores = jnp.einsum(
            "tgd,nd->tgn", q.reshape(tokens, head_group, HEAD_SIZE), keys, preferred_element_type=F32
        ) * score_scale
        scores = jnp.where(allowed, scores, LOWER_LIMIT)
        top = jnp.max(scores, axis=-1, keepdims=True)
        weights = jnp.where(allowed, jnp.exp(scores - top), 0.0)
        total = jnp.sum(weights, axis=-1, keepdims=True)
        summed = jnp.einsum("tgn,nd->tgd", weights.astype(BF), values, preferred_element_type=F32)
        out = (summed / total).reshape(tokens, q_cols).astype(BF)
        return out, top + jnp.log(total)

    def attend_back(q, keys, values, out, log_total, grad_out):
        q3 = q.reshape(tokens, head_group, HEAD_SIZE)
        g3 = grad_out.reshape(tokens, head_group, HEAD_SIZE)
        scores = jnp.einsum("tgd,nd->tgn", q3, keys, preferred_element_type=F32) * score_scale
        weights = jnp.where(allowed, jnp.exp(jnp.where(allowed, scores, LOWER_LIMIT) - log_total), 0.0)
        delta = jnp.sum(
            g3.astype(F32) * out.reshape(tokens, head_group, HEAD_SIZE).astype(F32), axis=-1, keepdims=True
        )
        weight_grad = jnp.einsum("tgd,nd->tgn", g3, values, preferred_element_type=F32)
        score_grad = (weights * (weight_grad - delta)).astype(BF)
        dq = jnp.einsum("tgn,nd->tgd", score_grad, keys, preferred_element_type=F32) * score_scale
        dk = jnp.einsum("tgn,tgd->nd", score_grad, q3, preferred_element_type=F32) * score_scale
        dv = jnp.einsum("tgn,tgd->nd", weights.astype(BF), g3, preferred_element_type=F32)
        return dq.reshape(tokens, q_cols), dk, dv

    def inverse_of(x):
        return lax.rsqrt(jnp.mean(x * x, axis=-1, keepdims=True) + EPS)

    hidden_state = swap(inputs[0])
    saved = []
    for layer in range(layers):
        attn_w = whole(attn_parts[layer])
        mlp_w = whole(mlp_parts[layer])
        w_qkv, w_o = attn_w[:, : q_cols + 2 * kv_cols], attn_w[:, q_cols + 2 * kv_cols :]
        w_gu, w_d = mlp_w[:, : 2 * ff_cols], mlp_w[:, 2 * ff_cols :]
        h = hidden_state.astype(F32)
        r1 = inverse_of(h)
        a1 = gather_tokens((h * r1 * gains[layer, 0]).astype(BF))
        qkv = dot_nn(a1, w_qkv)
        q = rotated(qkv[:, :q_cols], head_group, 1.0)
        k = all_keys(rotated(qkv[:, q_cols : q_cols + kv_cols], 1, 1.0))
        v = all_keys(qkv[:, q_cols + kv_cols :].astype(BF))
        o, log_total = attend(q, k, v)
        mid = h + scatter_tokens(dot_nt(o, w_o))
        r2 = inverse_of(mid)
        a2 = gather_tokens((mid * r2 * gains[layer, 1]).astype(BF))
        gu = dot_nn(a2, w_gu)
        g, u = gu[:, :ff_cols], gu[:, ff_cols:]
        hid = (jax.nn.silu(g) * u).astype(BF)
        after = mid + scatter_tokens(dot_nt(hid, w_d))
        saved.append(
            (hidden_state, r1, a1, q, k, v, o, log_total, mid, r2, a2, gu.astype(BF), hid, w_qkv, w_o, w_gu, w_d)
        )
        hidden_state = after.astype(BF)
    output = swap(hidden_state)[None]

    my_positions = (rank * extra + spot) * block + jnp.arange(block)
    e = swap(cotangent[0])
    e = jnp.where((my_positions < length)[:, None], e, jnp.zeros_like(e))
    attn_grads = [None] * layers
    mlp_grads = [None] * layers
    gain_grads = [None] * layers
    for layer in reversed(range(layers)):
        (h_low, r1, a1, q, k, v, o, log_total, mid, r2, a2, gu, hid, w_qkv, w_o, w_gu, w_d) = saved[layer]
        e_all = gather_tokens(e)
        dhid = dot_nn(e_all, w_d)
        g, u = gu[:, :ff_cols].astype(F32), gu[:, ff_cols:].astype(F32)
        sig = jax.nn.sigmoid(g)
        dgu = jnp.concatenate([dhid * u * sig * (1.0 + g * (1.0 - sig)), dhid * g * sig], axis=1).astype(BF)
        da2 = scatter_tokens(dot_nt(dgu, w_gu))
        mlp_grads[layer] = reduce_rows(jnp.concatenate([dot_tn(a2, dgu), dot_tn(e_all, hid)], axis=1))
        n2 = mid * r2
        gain2 = jnp.sum(da2 * n2, axis=0)
        dmid = e.astype(F32) + norm_back(da2, n2, r2, gains[layer, 1])
        dat = gather_tokens(dmid.astype(BF))
        dob = dot_nn(dat, w_o).astype(BF)
        dq, dk, dv = attend_back(q, k, v, o, log_total, dob)
        dqkv = jnp.concatenate(
            [rotated(dq, head_group, -1.0), rotated(own_keys(dk), 1, -1.0), own_keys(dv).astype(BF)], axis=1
        )
        da1 = scatter_tokens(dot_nt(dqkv, w_qkv))
        attn_grads[layer] = reduce_rows(jnp.concatenate([dot_tn(a1, dqkv), dot_tn(dat, o)], axis=1))
        n1 = h_low.astype(F32) * r1
        gain1 = jnp.sum(da1 * n1, axis=0)
        gain_grads[layer] = jnp.stack([gain1, gain2])
        e = (dmid + norm_back(da1, n1, r1, gains[layer, 0])).astype(BF)
    input_grad = swap(e)[None]

    def send_home(grads):
        stacked = jnp.stack(grads).reshape(ranks, rows, -1)
        back = lax.all_to_all(stacked, PLANE, split_axis=0, concat_axis=0, tiled=True)
        return back.astype(F32)

    def columns(back, start, count):
        return jnp.swapaxes(back[:, :, start : start + count], 0, 1).reshape(rows, ranks * count)

    attn_back = send_home(attn_grads)
    mlp_back = send_home(mlp_grads)
    gain_all = jnp.stack(gain_grads).reshape(layers, 2, -1, rows).transpose(0, 2, 1, 3).reshape(-1, 2, rows)
    gain_all = lax.psum_scatter(gain_all, ("x", "c", "z", "y", "e"), scatter_dimension=0, tiled=False)
    at = q_cols + 2 * kv_cols
    return (
        output,
        input_grad,
        gain_all[0:1],
        columns(attn_back, 0, q_cols)[None],
        columns(attn_back, q_cols, kv_cols)[None],
        columns(attn_back, q_cols + kv_cols, kv_cols)[None],
        columns(attn_back, at, q_cols).T[None],
        gain_all[1:2],
        columns(mlp_back, 0, ff_cols)[None],
        columns(mlp_back, ff_cols, ff_cols)[None],
        columns(mlp_back, 2 * ff_cols, ff_cols).T[None],
    )


def solution(mesh):
    section, seq = mesh.devices.shape
    halves = KEY_VALUE_HEADS // section
    extra = seq // (section * halves)
    fine = Mesh(
        mesh.devices.reshape(section // 2, 2, section, halves, extra), ("x", "c", "z", "y", "e")
    )
    sec, sq = ("x", "c"), ("z", "y", "e")
    rows3 = P(sec, sq, None)
    cols3 = P(sec, None, sq)
    in_specs = (rows3, P(), rows3, P(sec, sq), rows3, rows3, rows3, cols3, P(sec, sq), rows3, rows3, cols3)
    out_specs = (rows3, rows3, P(sec, sq), rows3, rows3, rows3, cols3, P(sec, sq), rows3, rows3, cols3)
    return jax.shard_map(body, mesh=fine, in_specs=in_specs, out_specs=out_specs, check_vma=False)
```

```python
import functools
import math

import jax
import jax.numpy as jnp
from jax import lax
from jax.experimental import pallas as pl
from jax.experimental.pallas import tpu as pltpu
from jax.sharding import Mesh
from jax.sharding import PartitionSpec as P

QUERY_HEADS = 16
KEY_VALUE_HEADS = 8
HEAD_SIZE = 96
FF = 4096

EPS = 1e-05
THETA = 100000.0
LOWER_LIMIT = -1e30

BF = jnp.bfloat16
F32 = jnp.float32

LANES = 128
HALF = HEAD_SIZE // 2
VMEM_LIMIT = 56 * 1024 * 1024
MESH = pl.DeviceIdType.MESH

OWN, X, Y, D = (0, 0), (1, 0), (0, 1), (1, 1)

def place():
    return lax.axis_index("x"), lax.axis_index("c"), lax.axis_index("y")

def flip(index, by):
    return 1 - index if by else index

def rank_of(here, dx, dc, dy):
    x, c, y = here
    return (flip(x, dx) * 2 + flip(c, dc)) * 2 + flip(y, dy)

def greet(here):
    x, c, y = here
    barrier = pltpu.get_barrier_semaphore()
    for peer in ({"x": 1 - x}, {"c": 1 - c}, {"y": 1 - y}):
        pl.semaphore_signal(barrier, inc=1, device_id=peer, device_id_type=MESH)
    pl.semaphore_wait(barrier, 3)

def ag_kernel(shard, full, send_sem, recv_sem, local_sem):
    here = place()
    x, c, y = here
    block = shard.shape[0]
    piece = block // 4
    to_x, to_y, to_c = {"x": 1 - x}, {"y": 1 - y}, {"c": 1 - c}
    sent = []

    def slot(role, chunk, count=1):
        start = rank_of(here, *role) * block + chunk * piece
        return full.at[pl.ds(pl.multiple_of(start, piece), piece * count)]

    def send(src, dst, peer, role, chunk):
        copy = pltpu.make_async_remote_copy(
            src_ref=src, dst_ref=dst, send_sem=send_sem.at[len(sent)],
            recv_sem=recv_sem.at[role[0] * 4 + role[1] * 2 + role[2], chunk],
            device_id=peer, device_id_type=MESH)
        copy.start()
        sent.append(copy)

    def arrived(role, chunk, count=1):
        where = slot(role, chunk, count)
        pltpu.make_async_remote_copy(
            src_ref=where, dst_ref=where, send_sem=send_sem.at[0],
            recv_sem=recv_sem.at[role[0] * 4 + role[1] * 2 + role[2], chunk],
            device_id=to_c, device_id_type=MESH).wait_recv()

    mine = pltpu.make_async_copy(shard, slot((0, 0, 0), 0, 4), local_sem)
    mine.start()
    greet(here)
    own = (0, 0, 0)
    for cx, cy in ((2, 0), (3, 1), (0, 2), (1, 3)):
        send(shard.at[pl.ds(cx * piece, piece)], slot(own, cx), to_x, (1, 0, 0), cx)
        send(shard.at[pl.ds(cy * piece, piece)], slot(own, cy), to_y, (0, 0, 1), cy)
    send(shard, slot(own, 0, 4), to_c, (0, 1, 0), 0)
    for cx, cy in ((2, 0), (3, 1), (0, 2), (1, 3)):
        arrived((1, 0, 0), cx)
        if cx >= 2:
            send(slot((1, 0, 0), cx), slot((1, 0, 0), cx), to_y, (1, 0, 1), cx)
        send(slot((1, 0, 0), cx), slot((1, 0, 0), cx), to_c, (1, 1, 0), cx)
        arrived((0, 0, 1), cy)
        if cy < 2:
            send(slot((0, 0, 1), cy), slot((0, 0, 1), cy), to_x, (1, 0, 1), cy)
        send(slot((0, 0, 1), cy), slot((0, 0, 1), cy), to_c, (0, 1, 1), cy)
    for chunk in (0, 2, 1, 3):
        arrived((1, 0, 1), chunk)
        send(slot((1, 0, 1), chunk), slot((1, 0, 1), chunk), to_c, (1, 1, 1), chunk)
    arrived((0, 1, 0), 0, 4)
    for role in ((1, 1, 0), (0, 1, 1), (1, 1, 1)):
        for chunk in range(4):
            arrived(role, chunk)
    mine.wait()
    for copy in sent:
        copy.wait_send()

def gather_tokens(shard):
    block, width = shard.shape
    return pl.pallas_call(
        ag_kernel,
        out_shape=jax.ShapeDtypeStruct((8 * block, width), shard.dtype),
        in_specs=[pl.BlockSpec(memory_space=pl.ANY)],
        out_specs=pl.BlockSpec(memory_space=pl.ANY),
        scratch_shapes=[pltpu.SemaphoreType.DMA((32,)), pltpu.SemaphoreType.DMA((8, 4)), pltpu.SemaphoreType.DMA],
        compiler_params=pltpu.CompilerParams(collective_id=0, has_side_effects=True),
        name="plane_gather",
        cost_estimate=pl.CostEstimate(flops=0, bytes_accessed=90000000, transcendentals=0),
    )(shard)

def rs_kernel(partial, out, from_c, acc, via_x, via_y, from_x, from_y, send_sem, recv_sem, local_sem):
    here = place()
    x, c, y = here
    block = out.shape[0]
    half = block // 2
    to_x, to_y, to_c = {"x": 1 - x}, {"y": 1 - y}, {"c": 1 - c}
    order = (D, X, Y, OWN)
    lower, upper = pl.ds(0, half), pl.ds(half, half)
    sent = []

    def rows(pos, dc):
        return partial.at[pl.ds(pl.multiple_of(rank_of(here, pos[0], dc, pos[1]) * block, block), block)]

    def send(src, dst, peer, sem):
        copy = pltpu.make_async_remote_copy(
            src_ref=src, dst_ref=dst, send_sem=send_sem.at[len(sent)], recv_sem=recv_sem.at[sem],
            device_id=peer, device_id_type=MESH)
        copy.start()
        sent.append(copy)

    def arrived(where, sem):
        pltpu.make_async_remote_copy(
            src_ref=where, dst_ref=where, send_sem=send_sem.at[0], recv_sem=recv_sem.at[sem],
            device_id=to_c, device_id_type=MESH).wait_recv()

    def add(slot, where, more):
        acc[slot, where] = (acc[slot, where].astype(F32) + more.astype(F32)).astype(BF)

    loads = []
    for slot, pos in enumerate(order):
        load = pltpu.make_async_copy(rows(pos, 0), acc.at[slot], local_sem.at[slot])
        load.start()
        loads.append(load)
    greet(here)
    for slot, pos in enumerate(order):
        send(rows(pos, 1), from_c.at[slot], to_c, slot)
    whole = pl.ds(0, block)
    for slot in range(3):
        loads[slot].wait()
        arrived(from_c.at[slot], slot)
        add(slot, whole, from_c[slot])
        if slot == 0:
            send(acc.at[0, upper], via_x, to_x, 4)
            send(acc.at[0, lower], via_y, to_y, 5)
        elif slot == 1:
            send(acc.at[1, upper], from_x.at[upper], to_x, 6)
        else:
            send(acc.at[2, lower], from_y.at[lower], to_y, 7)
    arrived(via_y, 5)
    add(1, lower, via_y[...])
    send(acc.at[1, lower], from_x.at[lower], to_x, 8)
    arrived(via_x, 4)
    add(2, upper, via_x[...])
    send(acc.at[2, upper], from_y.at[upper], to_y, 9)
    loads[3].wait()
    arrived(from_c.at[3], 3)
    out[...] = acc[3].astype(F32) + from_c[3].astype(F32)
    arrived(from_x.at[upper], 6)
    arrived(from_y.at[lower], 7)
    out[upper] = out[upper] + from_x[upper].astype(F32)
    out[lower] = out[lower] + from_y[lower].astype(F32)
    arrived(from_x.at[lower], 8)
    arrived(from_y.at[upper], 9)
    out[lower] = out[lower] + from_x[lower].astype(F32)
    out[upper] = out[upper] + from_y[upper].astype(F32)
    for copy in sent:
        copy.wait_send()

def scatter_tokens(partial):
    block, width = partial.shape[0] // 8, partial.shape[1]
    half = block // 2
    return pl.pallas_call(
        rs_kernel,
        out_shape=jax.ShapeDtypeStruct((block, width), F32),
        in_specs=[pl.BlockSpec(memory_space=pl.ANY)],
        out_specs=pl.BlockSpec(memory_space=pltpu.VMEM),
        scratch_shapes=[
            pltpu.VMEM((4, block, width), BF), pltpu.VMEM((4, block, width), BF),
            pltpu.VMEM((half, width), BF), pltpu.VMEM((half, width), BF),
            pltpu.VMEM((block, width), BF), pltpu.VMEM((block, width), BF),
            pltpu.SemaphoreType.DMA((10,)), pltpu.SemaphoreType.DMA((10,)), pltpu.SemaphoreType.DMA((4,)),
        ],
        compiler_params=pltpu.CompilerParams(collective_id=1, has_side_effects=True, vmem_limit_bytes=VMEM_LIMIT),
        name="plane_scatter",
        cost_estimate=pl.CostEstimate(flops=0, bytes_accessed=90000000, transcendentals=0),
    )(partial)


LOWER=-1e30
def dot(a, b, dims):
    return lax.dot_general(a, b, (dims, ((), ())), preferred_element_type=F32)

def attend_kernel(scale2, bq, bk, bounds, length, q, k, v, qpos, out, lse):
    groups = q.shape[0]
    i = pl.program_id(0)
    rows = groups * bq
    qs = q[...].reshape(rows, LANES)
    pos = qpos[0]
    pos2 = jnp.concatenate([pos] * groups, axis=1)
    def step(masked, j, state):
        top, total, acc = state
        at = pl.ds(pl.multiple_of(j * bk, bk), bk)
        s = dot(k[at, :], qs, ((1,), (1,)))
        if masked:
            kp = j * bk + lax.broadcasted_iota(jnp.int32, (bk, 1), 0)
            ok = (kp <= pos2) & (kp < length[0])
            s = jnp.where(ok, s, LOWER)
        new = jnp.maximum(top, jnp.max(s, axis=0, keepdims=True) * scale2)
        p = jnp.exp2(s * scale2 - new)
        alpha = jnp.exp2(top - new)
        total = total * alpha + jnp.sum(p, axis=0, keepdims=True)
        acc = acc * alpha + dot(v[at, :], p.astype(BF), ((0,), (0,)))
        return new, total, acc
    state = (jnp.full((1, rows), LOWER, F32), jnp.zeros((1, rows), F32), jnp.zeros((LANES, rows), F32))
    full, end = bounds[0, i], bounds[1, i]
    state = lax.fori_loop(0, full, functools.partial(step, False), state)
    top, total, acc = lax.fori_loop(full, end, functools.partial(step, True), state)
    o = (acc / total).T.astype(BF)
    for g in range(groups):
        out[:, g * LANES:(g + 1) * LANES] = o[g * bq:(g + 1) * bq]
    lse[...] = (top + jnp.log2(total))[None]

def attend(q, k, v, qpos, bounds, length, bq, bk, scale2):
    groups, tokens, _ = q.shape
    n = tokens // bq
    out, lse = pl.pallas_call(
        functools.partial(attend_kernel, scale2, bq, bk),
        grid_spec=pltpu.PrefetchScalarGridSpec(
            num_scalar_prefetch=2, grid=(n,),
            in_specs=[
                pl.BlockSpec((groups, bq, LANES), lambda i, *_: (0, i, 0)),
                pl.BlockSpec(k.shape, lambda i, *_: (0, 0)),
                pl.BlockSpec(v.shape, lambda i, *_: (0, 0)),
                pl.BlockSpec((1, 1, bq), lambda i, *_: (i, 0, 0)),
            ],
            out_specs=[
                pl.BlockSpec((bq, groups * LANES), lambda i, *_: (i, 0)),
                pl.BlockSpec((1, 1, groups * bq), lambda i, *_: (i, 0, 0)),
            ]),
        out_shape=[jax.ShapeDtypeStruct((tokens, groups * LANES), BF), jax.ShapeDtypeStruct((n, 1, groups * bq), F32)],
        compiler_params=pltpu.CompilerParams(vmem_limit_bytes=VMEM_LIMIT),
        name="attend",
        cost_estimate=pl.CostEstimate(flops=0, bytes_accessed=45000000, transcendentals=0),
    )(bounds, length, q, k, v, qpos)
    return out, lse

def back_kernel(scale, scale2, bq, bk, bounds, length, q, k, v, qpos, o, do, lse, dq, dk, dv):
    groups = q.shape[0]
    i = pl.program_id(0)
    @pl.when(i == 0)
    def _():
        dk[...] = jnp.zeros_like(dk)
        dv[...] = jnp.zeros_like(dv)
    qs = q[...].reshape(groups * bq, LANES)
    dos = jnp.concatenate([do[:, g * LANES:(g + 1) * LANES] for g in range(groups)], axis=0)
    os_ = jnp.concatenate([o[:, g * LANES:(g + 1) * LANES] for g in range(groups)], axis=0)
    delta = jnp.sum(dos.astype(F32) * os_.astype(F32), axis=1, keepdims=True).reshape(1, groups * bq)
    lse_row = lse[0]
    pos = qpos[0]
    pos2 = jnp.concatenate([pos] * groups, axis=1)
    def step(masked, j, acc):
        at = pl.ds(pl.multiple_of(j * bk, bk), bk)
        kb, vb = k[at, :], v[at, :]
        s = dot(kb, qs, ((1,), (1,)))
        p = jnp.exp2(s * scale2 - lse_row)
        if masked:
            kp = j * bk + lax.broadcasted_iota(jnp.int32, (bk, 1), 0)
            ok = (kp <= pos2) & (kp < length[0])
            p = jnp.where(ok, p, 0.0)
        dp = dot(vb, dos, ((1,), (1,)))
        ds = (p * (dp - delta)).astype(BF)
        dv[at, :] += dot(p.astype(BF), dos, ((1,), (0,)))
        dk[at, :] += dot(ds, qs, ((1,), (0,))) * scale
        return acc + dot(ds, kb, ((0,), (0,)))
    full, end = bounds[0, i], bounds[1, i]
    acc = jnp.zeros((groups * bq, LANES), F32)
    acc = lax.fori_loop(0, full, functools.partial(step, False), acc)
    acc = lax.fori_loop(full, end, functools.partial(step, True), acc) * scale
    for g in range(groups):
        dq[:, g * LANES:(g + 1) * LANES] = acc[g * bq:(g + 1) * bq]

def attend_back(q, k, v, qpos_row, o, do, lse, bounds, length, bq, bk, scale, scale2):
    groups, tokens, _ = q.shape
    n = tokens // bq
    wide = pl.BlockSpec((bq, groups * LANES), lambda i, *_: (i, 0))
    return pl.pallas_call(
        functools.partial(back_kernel, scale, scale2, bq, bk),
        grid_spec=pltpu.PrefetchScalarGridSpec(
            num_scalar_prefetch=2, grid=(n,),
            in_specs=[
                pl.BlockSpec((groups, bq, LANES), lambda i, *_: (0, i, 0)),
                pl.BlockSpec(k.shape, lambda i, *_: (0, 0)),
                pl.BlockSpec(v.shape, lambda i, *_: (0, 0)),
                pl.BlockSpec((1, 1, bq), lambda i, *_: (i, 0, 0)),
                wide, wide,
                pl.BlockSpec((1, 1, groups * bq), lambda i, *_: (i, 0, 0)),
            ],
            out_specs=[wide, pl.BlockSpec(k.shape, lambda i, *_: (0, 0)), pl.BlockSpec(k.shape, lambda i, *_: (0, 0))]),
        out_shape=[jax.ShapeDtypeStruct((tokens, groups * LANES), F32), jax.ShapeDtypeStruct(k.shape, F32), jax.ShapeDtypeStruct(k.shape, F32)],
        compiler_params=pltpu.CompilerParams(vmem_limit_bytes=VMEM_LIMIT),
        name="attend_back",
        cost_estimate=pl.CostEstimate(flops=0, bytes_accessed=65000000, transcendentals=0),
    )(bounds, length, q, k, v, qpos_row, o, do, lse)

def bounds_of(positions, length, bq, bk):
    p = positions.reshape(-1, bq)
    lo = jnp.minimum(jnp.min(p, axis=1) + 1, length) // bk
    hi = -(-jnp.minimum(jnp.max(p, axis=1) + 1, length) // bk)
    return jnp.stack([lo, hi]).astype(jnp.int32)


PLANE = ("x", "c", "y")

def dot_nn(a, b):
    return dot(a, b, ((1,), (0,)))


def dot_nt(a, b):
    return dot(a, b, ((1,), (1,)))


def dot_tn(a, b):
    return dot(a, b, ((0,), (0,)))


def spread(matrix, heads):
    split = matrix.reshape(matrix.shape[0], heads, 2, HALF)
    return jnp.pad(split, ((0, 0), (0, 0), (0, 0), (0, LANES // 2 - HALF))).reshape(-1, heads * LANES)


def unspread(matrix, heads):
    return matrix.reshape(-1, heads, 2, LANES // 2)[..., :HALF].reshape(-1, heads * HEAD_SIZE)


def widen(matrix, heads):
    split = matrix.reshape(matrix.shape[0], heads, HEAD_SIZE)
    return jnp.pad(split, ((0, 0), (0, 0), (0, LANES - HEAD_SIZE))).reshape(-1, heads * LANES)


def narrow(matrix, heads):
    return matrix.reshape(-1, heads, LANES)[..., :HEAD_SIZE].reshape(-1, heads * HEAD_SIZE)


def norm_back(upstream, normed, inverse, gain_row):
    scaled = upstream * gain_row
    return inverse * (scaled - normed * jnp.mean(scaled * normed, axis=-1, keepdims=True))


def body(
    inputs,
    lengths,
    cotangent,
    attn_gain,
    w_query,
    key_projection,
    value_projection,
    w_out,
    mlp_gain,
    w_gate,
    w_up,
    w_down,
):
    sections = lax.axis_size("x") * lax.axis_size("c")
    planes = lax.axis_size("z")
    halves = lax.axis_size("y")
    extra = lax.axis_size("e")
    ranks = sections * halves
    layers = sections
    block = inputs.shape[1]
    width = inputs.shape[2]
    rows = w_query.shape[1]
    tokens = block * ranks
    all_tokens = tokens * extra
    head_group = QUERY_HEADS // KEY_VALUE_HEADS
    q_cols = head_group * HEAD_SIZE
    kv_cols = HEAD_SIZE
    ff_cols = FF // ranks
    scale = 1.0 / math.sqrt(HEAD_SIZE)
    scale2 = scale * math.log2(math.e)

    def swap(array):
        names = ("x", "c", "z")
        pairs = [
            (s * planes + z, z * planes + s) for s in range(sections) for z in range(planes)
        ]
        return lax.ppermute(array, names, pairs)

    def by_rank(matrix):
        return matrix.reshape(rows, ranks, -1)

    attn_pack = jnp.concatenate(
        [
            by_rank(w_query[0]),
            by_rank(key_projection[0]),
            by_rank(value_projection[0]),
            by_rank(w_out[0].T),
        ],
        axis=2,
    )
    mlp_pack = jnp.concatenate(
        [by_rank(w_gate[0]), by_rank(w_up[0]), by_rank(w_down[0].T)], axis=2
    )

    def exchange(pack):
        moved = lax.all_to_all(
            jnp.swapaxes(pack.astype(BF), 0, 1), PLANE, split_axis=0, concat_axis=0, tiled=True
        )
        return moved.reshape(layers, halves, rows, pack.shape[2])

    def whole(part):
        if extra > 1:
            part = lax.all_gather(part, "e", axis=1, tiled=False)
        return lax.all_gather(part.reshape(-1, part.shape[-1]), "z", axis=0, tiled=True)

    def reduce_rows(grad):
        mine = lax.psum_scatter(grad.astype(BF), "z", scatter_dimension=0, tiled=True)
        mine = mine.reshape(halves, extra, rows, -1)
        if extra > 1:
            return lax.psum_scatter(mine, "e", scatter_dimension=1, tiled=False)
        return mine[:, 0]

    attn_parts = exchange(attn_pack)
    mlp_parts = exchange(mlp_pack)
    gains = jnp.stack([attn_gain[0], mlp_gain[0]]).astype(BF)
    gains = lax.all_gather(gains, ("x", "c", "z", "y", "e"), axis=0, tiled=False)
    gains = gains.reshape(layers, -1, 2, rows).transpose(0, 2, 1, 3).reshape(layers, 2, 1, width)
    gains = gains.astype(F32)

    rank = (lax.axis_index("x") * lax.axis_size("c") + lax.axis_index("c")) * halves + lax.axis_index("y")
    spot = lax.axis_index("e")
    length = lengths[lax.axis_index("z")]

    block_start = (jnp.arange(ranks) * extra + spot) * block
    positions = (block_start[:, None] + jnp.arange(block)[None, :]).reshape(tokens)
    exponents = 2.0 * jnp.arange(HEAD_SIZE // 2).astype(F32) / HEAD_SIZE
    angles = positions.astype(F32)[:, None] * (THETA ** (-exponents))[None, :]
    table = lambda values: jnp.pad(values, ((0, 0), (0, LANES // 2 - HALF)))
    cosine = jnp.concatenate([table(jnp.cos(angles))] * 2, axis=1)
    sine = jnp.concatenate([table(-jnp.sin(angles)), table(jnp.sin(angles))], axis=1)
    bq = math.gcd(tokens, 512)
    bk = math.gcd(all_tokens, 512)
    bounds = bounds_of(positions, length, bq, bk)
    length1 = length.reshape(1)
    query_rows = positions.astype(jnp.int32).reshape(-1, 1, bq)

    def rotated(head, sign):
        turned = jnp.concatenate([head[:, LANES // 2 :], head[:, : LANES // 2]], axis=1)
        return (head * cosine + turned * (sign * sine)).astype(BF)

    def all_keys(array):
        if extra == 1:
            return array
        stacked = lax.all_gather(array.reshape(ranks, block, -1), "e", axis=1, tiled=False)
        return stacked.reshape(all_tokens, -1)

    def own_keys(array):
        if extra == 1:
            return array
        stacked = array.astype(BF).reshape(ranks, extra, block, -1)
        return lax.psum_scatter(stacked, "e", scatter_dimension=1, tiled=False).reshape(tokens, -1).astype(F32)

    def inverse_of(x):
        return lax.rsqrt(jnp.mean(x * x, axis=-1, keepdims=True) + EPS)

    hidden_state = swap(inputs[0])
    saved = []
    for layer in range(layers):
        attn_w = whole(attn_parts[layer])
        mlp_w = whole(mlp_parts[layer])
        qk_cols = q_cols + kv_cols
        w_qkv = jnp.concatenate(
            [spread(attn_w[:, :qk_cols], head_group + 1), widen(attn_w[:, qk_cols : qk_cols + kv_cols], 1)], axis=1
        )
        w_o = widen(attn_w[:, qk_cols + kv_cols :], head_group)
        w_gu, w_d = mlp_w[:, : 2 * ff_cols], mlp_w[:, 2 * ff_cols :]
        h = hidden_state.astype(F32)
        r1 = inverse_of(h)
        a1 = gather_tokens((h * r1 * gains[layer, 0]).astype(BF))
        qkv = dot_nn(a1, w_qkv)
        heads = [qkv[:, n * LANES : (n + 1) * LANES] for n in range(head_group + 2)]
        q = jnp.stack([rotated(head, 1.0) for head in heads[:head_group]])
        k = all_keys(rotated(heads[head_group], 1.0))
        v = all_keys(heads[head_group + 1].astype(BF))
        o, log_total = attend(q, k, v, query_rows, bounds, length1, bq, bk, scale2)
        mid = h + scatter_tokens(dot_nt(o, w_o).astype(BF))
        r2 = inverse_of(mid)
        a2 = gather_tokens((mid * r2 * gains[layer, 1]).astype(BF))
        gu = dot_nn(a2, w_gu)
        g, u = gu[:, :ff_cols], gu[:, ff_cols:]
        hid = (jax.nn.silu(g) * u).astype(BF)
        after = mid + scatter_tokens(dot_nt(hid, w_d).astype(BF))
        saved.append(
            (hidden_state, r1, a1, q, k, v, o, log_total, mid, r2, a2, gu.astype(BF), hid, w_qkv, w_o, w_gu, w_d)
        )
        hidden_state = after.astype(BF)
    output = swap(hidden_state)[None]

    my_positions = (rank * extra + spot) * block + jnp.arange(block)
    e = swap(cotangent[0])
    e = jnp.where((my_positions < length)[:, None], e, jnp.zeros_like(e))
    attn_grads = [None] * layers
    mlp_grads = [None] * layers
    gain_grads = [None] * layers
    for layer in reversed(range(layers)):
        (h_low, r1, a1, q, k, v, o, log_total, mid, r2, a2, gu, hid, w_qkv, w_o, w_gu, w_d) = saved[layer]
        e_all = gather_tokens(e)
        dhid = dot_nn(e_all, w_d)
        g, u = gu[:, :ff_cols].astype(F32), gu[:, ff_cols:].astype(F32)
        sig = jax.nn.sigmoid(g)
        dgu = jnp.concatenate([dhid * u * sig * (1.0 + g * (1.0 - sig)), dhid * g * sig], axis=1).astype(BF)
        da2 = scatter_tokens(dot_nt(dgu, w_gu).astype(BF))
        mlp_grads[layer] = reduce_rows(jnp.concatenate([dot_tn(a2, dgu), dot_tn(e_all, hid)], axis=1))
        n2 = mid * r2
        gain2 = jnp.sum(da2 * n2, axis=0)
        dmid = e.astype(F32) + norm_back(da2, n2, r2, gains[layer, 1])
        dat = gather_tokens(dmid.astype(BF))
        dob = dot_nn(dat, w_o).astype(BF)
        dq, dk, dv = attend_back(q, k, v, query_rows, o, dob, log_total, bounds, length1, bq, bk, scale, scale2)
        dqkv = jnp.concatenate(
            [rotated(dq[:, n * LANES : (n + 1) * LANES], -1.0) for n in range(head_group)]
            + [rotated(own_keys(dk), -1.0), own_keys(dv).astype(BF)],
            axis=1,
        )
        da1 = scatter_tokens(dot_nt(dqkv, w_qkv).astype(BF))
        dqkv_w = dot_tn(a1, dqkv).astype(BF)
        qk_wide = (head_group + 1) * LANES
        attn_grads[layer] = reduce_rows(
            jnp.concatenate(
                [
                    unspread(dqkv_w[:, :qk_wide], head_group + 1),
                    narrow(dqkv_w[:, qk_wide:], 1),
                    narrow(dot_tn(dat, o).astype(BF), head_group),
                ],
                axis=1,
            )
        )
        n1 = h_low.astype(F32) * r1
        gain1 = jnp.sum(da1 * n1, axis=0)
        gain_grads[layer] = jnp.stack([gain1, gain2])
        e = (dmid + norm_back(da1, n1, r1, gains[layer, 0])).astype(BF)
    input_grad = swap(e)[None]

    def send_home(grads):
        stacked = jnp.stack(grads).reshape(ranks, rows, -1)
        back = lax.all_to_all(stacked, PLANE, split_axis=0, concat_axis=0, tiled=True)
        return back.astype(F32)

    def columns(back, start, count):
        return jnp.swapaxes(back[:, :, start : start + count], 0, 1).reshape(rows, ranks * count)

    attn_back = send_home(attn_grads)
    mlp_back = send_home(mlp_grads)
    gain_all = jnp.stack(gain_grads).reshape(layers, 2, -1, rows).transpose(0, 2, 1, 3).reshape(-1, 2, rows)
    gain_all = lax.psum_scatter(gain_all, ("x", "c", "z", "y", "e"), scatter_dimension=0, tiled=False)
    at = q_cols + 2 * kv_cols
    return (
        output,
        input_grad,
        gain_all[0:1],
        columns(attn_back, 0, q_cols)[None],
        columns(attn_back, q_cols, kv_cols)[None],
        columns(attn_back, q_cols + kv_cols, kv_cols)[None],
        columns(attn_back, at, q_cols).T[None],
        gain_all[1:2],
        columns(mlp_back, 0, ff_cols)[None],
        columns(mlp_back, ff_cols, ff_cols)[None],
        columns(mlp_back, 2 * ff_cols, ff_cols).T[None],
    )


def solution(mesh):
    section, seq = mesh.devices.shape
    halves = KEY_VALUE_HEADS // section
    extra = seq // (section * halves)
    fine = Mesh(
        mesh.devices.reshape(section // 2, 2, section, halves, extra), ("x", "c", "z", "y", "e")
    )
    sec, sq = ("x", "c"), ("z", "y", "e")
    rows3 = P(sec, sq, None)
    cols3 = P(sec, None, sq)
    in_specs = (rows3, P(), rows3, P(sec, sq), rows3, rows3, rows3, cols3, P(sec, sq), rows3, rows3, cols3)
    out_specs = (rows3, rows3, P(sec, sq), rows3, rows3, rows3, cols3, P(sec, sq), rows3, rows3, cols3)
    return jax.shard_map(body, mesh=fine, in_specs=in_specs, out_specs=out_specs, check_vma=False)
```

```python
import functools
import math

import jax
import jax.numpy as jnp
from jax import lax
from jax.experimental import pallas as pl
from jax.experimental.pallas import tpu as pltpu
from jax.sharding import Mesh
from jax.sharding import PartitionSpec as P

QUERY_HEADS = 16
KEY_VALUE_HEADS = 8
HEAD_SIZE = 96
FF = 4096

EPS = 1e-05
THETA = 100000.0
LOWER_LIMIT = -1e30

BF = jnp.bfloat16
F32 = jnp.float32

LANES = 128
HALF = HEAD_SIZE // 2
VMEM_LIMIT = 56 * 1024 * 1024


def dot(a, b, dims):
    return lax.dot_general(a, b, (dims, ((), ())), preferred_element_type=F32)


def dot_nn(a, b):
    return dot(a, b, ((1,), (0,)))


def dot_nt(a, b):
    return dot(a, b, ((1,), (1,)))


def dot_tn(a, b):
    return dot(a, b, ((0,), (0,)))


MESH = pl.DeviceIdType.MESH

OWN, X, Y, D = (0, 0), (1, 0), (0, 1), (1, 1)


def place():
    return lax.axis_index("x"), lax.axis_index("c"), lax.axis_index("y")


def flip(index, by):
    return 1 - index if by else index


def rank_of(here, dx, dc, dy):
    x, c, y = here
    return (flip(x, dx) * 2 + flip(c, dc)) * 2 + flip(y, dy)


def greet(here):
    x, c, y = here
    barrier = pltpu.get_barrier_semaphore()
    for peer in ({"x": 1 - x}, {"c": 1 - c}, {"y": 1 - y}):
        pl.semaphore_signal(barrier, inc=1, device_id=peer, device_id_type=MESH)
    pl.semaphore_wait(barrier, 3)


class Sender:
    def __init__(self, here, send_sem, recv_sem):
        x, c, y = here
        self.peers = {"x": {"x": 1 - x}, "c": {"c": 1 - c}, "y": {"y": 1 - y}}
        self.send_sem, self.recv_sem = send_sem, recv_sem
        self.sent = []

    def copy(self, src, dst, index, to, number):
        return pltpu.make_async_remote_copy(
            src_ref=src,
            dst_ref=dst,
            send_sem=self.send_sem.at[number],
            recv_sem=self.recv_sem.at[index],
            device_id=self.peers[to],
            device_id_type=MESH,
        )

    def send(self, src, dst, index, to):
        started = self.copy(src, dst, index, to, len(self.sent))
        started.start()
        self.sent.append(started)

    def arrived(self, where, index):
        self.copy(where, where, index, "c", 0).wait_recv()

    def drain(self):
        for started in self.sent:
            started.wait_send()


def run_gather(here, full, sems, on_block):
    block = full.shape[1]
    piece = block // 4
    net = Sender(here, *sems)

    def index(role, chunk):
        return (role[0] * 4 + role[1] * 2 + role[2]) * 4 + chunk

    def slot(role, chunk, count=1):
        return full.at[rank_of(here, *role), pl.ds(chunk * piece, piece * count)]

    def send(role, chunk, to, as_role, count=1):
        where = slot(role, chunk, count)
        net.send(where, where, index(as_role, chunk), to)

    def arrived(role, chunk, count=1):
        net.arrived(slot(role, chunk, count), index(role, chunk))

    def whole(role):
        for chunk in range(4):
            arrived(role, chunk)

    def done(role):
        on_block(rank_of(here, *role))

    own, at_x, at_y, at_d, at_c = (0, 0, 0), (1, 0, 0), (0, 0, 1), (1, 0, 1), (0, 1, 0)
    xc, yc, dc = (1, 1, 0), (0, 1, 1), (1, 1, 1)
    for cx, cy in ((2, 0), (3, 1), (0, 2), (1, 3)):
        send(own, cx, "x", at_x)
        send(own, cy, "y", at_y)
    send(own, 0, "c", at_c, 4)

    def pass_on(cx, cy):
        arrived(at_x, cx)
        if cx >= 2:
            send(at_x, cx, "y", at_d)
        send(at_x, cx, "c", xc)
        arrived(at_y, cy)
        if cy < 2:
            send(at_y, cy, "x", at_d)
        send(at_y, cy, "c", yc)

    def pass_last(chunks):
        for chunk in chunks:
            arrived(at_d, chunk)
            send(at_d, chunk, "c", dc)

    done(own)
    pass_on(2, 0)
    arrived(at_c, 0, 4)
    done(at_c)
    pass_on(3, 1)
    pass_on(0, 2)
    pass_on(1, 3)
    done(at_x)
    done(at_y)
    pass_last((0, 2))
    whole(xc)
    done(xc)
    whole(yc)
    done(yc)
    pass_last((1, 3))
    done(at_d)
    whole(dc)
    done(dc)
    return net


def run_scatter(here, parts, total, bufs, sems, fill=None, beside=None):
    from_c, via_x, via_y, from_x, from_y = bufs
    block = parts.shape[1]
    half = block // 2
    net = Sender(here, *sems)
    order = (D, X, Y, OWN)
    lower, upper = pl.ds(0, half), pl.ds(half, half)

    def rank(n, dc):
        return rank_of(here, order[n][0], dc, order[n][1])

    def make(r):
        if fill is not None:
            fill(r)

    def sibling(n):
        r = rank(n, 1)
        make(r)
        net.send(parts.at[r], from_c.at[n], n, "c")

    def add(n, where, more):
        r = rank(n, 0)
        parts[r, where] = (parts[r, where].astype(F32) + more.astype(F32)).astype(BF)

    def mine(n, where):
        return parts.at[rank(n, 0), where]

    def combine(n):
        net.arrived(from_c.at[n], n)
        if n < 3:
            add(n, pl.ds(0, block), from_c[n])

    sibling(0)
    make(rank(0, 0))
    sibling(1)
    sibling(2)
    combine(0)
    net.send(mine(0, upper), via_x, 4, "x")
    net.send(mine(0, lower), via_y, 5, "y")
    make(rank(1, 0))
    combine(1)
    net.send(mine(1, upper), from_x.at[upper], 6, "x")
    make(rank(2, 0))
    combine(2)
    net.send(mine(2, lower), from_y.at[lower], 7, "y")
    sibling(3)
    make(rank(3, 0))
    combine(3)
    total[...] = parts[rank(3, 0)].astype(F32) + from_c[3].astype(F32)
    if beside is not None:
        beside(0)
    net.arrived(via_y, 5)
    add(1, lower, via_y[...])
    net.send(mine(1, lower), from_x.at[lower], 8, "x")
    net.arrived(via_x, 4)
    add(2, upper, via_x[...])
    net.send(mine(2, upper), from_y.at[upper], 9, "y")
    if beside is not None:
        beside(1)
    net.arrived(from_x.at[upper], 6)
    net.arrived(from_y.at[lower], 7)
    total[upper] += from_x[upper].astype(F32)
    total[lower] += from_y[lower].astype(F32)
    net.arrived(from_x.at[lower], 8)
    net.arrived(from_y.at[upper], 9)
    total[lower] += from_x[lower].astype(F32)
    total[upper] += from_y[upper].astype(F32)
    return net


def gather_sems():
    return [pltpu.SemaphoreType.DMA((32,)), pltpu.SemaphoreType.DMA((32,))]


def scatter_scratch(block, width):
    half = block // 2
    return [
        pltpu.VMEM((4, block, width), BF),
        pltpu.VMEM((half, width), BF),
        pltpu.VMEM((half, width), BF),
        pltpu.VMEM((block, width), BF),
        pltpu.VMEM((block, width), BF),
        pltpu.SemaphoreType.DMA((10,)),
        pltpu.SemaphoreType.DMA((10,)),
    ]


class Loads:
    def __init__(self, sem):
        self.sem = sem
        self.count = 0

    def start(self, src, dst):
        copy = pltpu.make_async_copy(src, dst, self.sem.at[self.count])
        self.count += 1
        copy.start()
        return copy


def inverse_of(x):
    return lax.rsqrt(jnp.mean(x * x, axis=-1, keepdims=True) + EPS)


def turn(head, cosine, sine):
    return head * cosine + pltpu.roll(head, LANES // 2, 1) * sine


def plane_call(kernel, name, number, out_shape, out_specs, in_specs, scratch, time_us, *operands):
    return pl.pallas_call(
        kernel,
        out_shape=out_shape,
        in_specs=in_specs,
        out_specs=out_specs,
        scratch_shapes=scratch,
        compiler_params=pltpu.CompilerParams(
            collective_id=number, has_side_effects=True, vmem_limit_bytes=VMEM_LIMIT
        ),
        cost_estimate=pl.CostEstimate(flops=0, bytes_accessed=time_us * 3000000, transcendentals=0),
        name=name,
    )(*operands)


ANYWHERE = pl.BlockSpec(memory_space=pl.ANY)
IN_VMEM = pl.BlockSpec(memory_space=pltpu.VMEM)


def attn_in_kernel(heads, h, gain, w_hbm, cosine, sine, a1_out, q_out, k_out, v_out, full, w, send, recv, local):
    here = place()
    loads = Loads(local)
    w_load = loads.start(w_hbm, w)
    x = h[...].astype(F32)
    full[rank_of(here, 0, 0, 0)] = (x * inverse_of(x) * gain[...]).astype(BF)
    greet(here)
    saves = []

    def on_block(r):
        if not saves:
            w_load.wait()
        saves.append(loads.start(full.at[r], a1_out.at[r]))
        qkv = dot_nn(full[r], w[...])
        cos, sin = cosine[r], sine[r]
        part = lambda n: qkv[:, n * LANES : (n + 1) * LANES]
        for n in range(heads):
            q_out[n, r] = turn(part(n), cos, sin).astype(BF)
        k_out[r] = turn(part(heads), cos, sin).astype(BF)
        v_out[r] = part(heads + 1).astype(BF)

    net = run_gather(here, full, (send, recv), on_block)
    net.drain()
    for save in saves:
        save.wait()


def attn_in(h, gain, w, cosine, sine, heads):
    block, width = h.shape
    cols = w.shape[1]
    return plane_call(
        functools.partial(attn_in_kernel, heads),
        "attn_in",
        0,
        [
            jax.ShapeDtypeStruct((8, block, width), BF),
            jax.ShapeDtypeStruct((heads, 8, block, LANES), BF),
            jax.ShapeDtypeStruct((8, block, LANES), BF),
            jax.ShapeDtypeStruct((8, block, LANES), BF),
        ],
        [ANYWHERE, IN_VMEM, IN_VMEM, IN_VMEM],
        [IN_VMEM, IN_VMEM, ANYWHERE, IN_VMEM, IN_VMEM],
        [pltpu.VMEM((8, block, width), BF), pltpu.VMEM((width, cols), BF)]
        + gather_sems()
        + [pltpu.SemaphoreType.DMA((9,))],
        34,
        h, gain, w, cosine, sine,
    )


def mlp_kernel(
    ff, h, o, gain, wo_hbm, wgu_hbm, wd_hbm, mid_out, a2_out, gu_out, hid_out, next_out,
    full, parts, gu, hid, wo, wgu, wd, total,
    from_c, via_x, via_y, from_x, from_y, send1, recv1, send2, recv2,
    from_c3, via_x3, via_y3, from_x3, from_y3, send3, recv3, local,
):
    here = place()
    loads = Loads(local)
    wo_load = loads.start(wo_hbm, wo)
    wgu_load = loads.start(wgu_hbm, wgu)
    wd_load = loads.start(wd_hbm, wd)
    greet(here)
    wo_load.wait()

    def fill(r):
        parts[r] = dot_nt(o[r], wo[...]).astype(BF)

    bufs = (from_c, via_x, via_y, from_x, from_y)
    net1 = run_scatter(here, parts, total, bufs, (send1, recv1), fill)
    mid = h[...].astype(F32) + total[...]
    mid_out[...] = mid
    full[rank_of(here, 0, 0, 0)] = (mid * inverse_of(mid) * gain[...]).astype(BF)
    net1.drain()
    saves = []

    def on_block(r):
        if not saves:
            wgu_load.wait()
            wd_load.wait()
        saves.append(loads.start(full.at[r], a2_out.at[r]))
        a2 = full[r]
        g = dot_nn(a2, wgu[:, :ff])
        u = dot_nn(a2, wgu[:, ff:])
        gu[r, :, :ff] = g.astype(BF)
        gu[r, :, ff:] = u.astype(BF)
        low = (g * (1.0 / (1.0 + jnp.exp(-g))) * u).astype(BF)
        hid[r] = low
        saves.append(loads.start(gu.at[r], gu_out.at[r]))
        saves.append(loads.start(hid.at[r], hid_out.at[r]))
        parts[r] = dot_nt(low, wd[...]).astype(BF)

    net2 = run_gather(here, full, (send2, recv2), on_block)
    bufs3 = (from_c3, via_x3, via_y3, from_x3, from_y3)
    net3 = run_scatter(here, parts, total, bufs3, (send3, recv3))
    next_out[...] = (mid_out[...] + total[...]).astype(BF)
    net2.drain()
    net3.drain()
    for save in saves:
        save.wait()


def mlp(h, o, gain, wo, wgu, wd):
    block, width = h.shape
    ff = wd.shape[1]
    return plane_call(
        functools.partial(mlp_kernel, ff),
        "mlp",
        1,
        [
            jax.ShapeDtypeStruct((block, width), F32),
            jax.ShapeDtypeStruct((8, block, width), BF),
            jax.ShapeDtypeStruct((8, block, 2 * ff), BF),
            jax.ShapeDtypeStruct((8, block, ff), BF),
            jax.ShapeDtypeStruct((block, width), BF),
        ],
        [IN_VMEM, ANYWHERE, ANYWHERE, ANYWHERE, IN_VMEM],
        [IN_VMEM, IN_VMEM, IN_VMEM, ANYWHERE, ANYWHERE, ANYWHERE],
        [
            pltpu.VMEM((8, block, width), BF),
            pltpu.VMEM((8, block, width), BF),
            pltpu.VMEM((8, block, 2 * ff), BF),
            pltpu.VMEM((8, block, ff), BF),
            pltpu.VMEM(wo.shape, BF),
            pltpu.VMEM(wgu.shape, BF),
            pltpu.VMEM(wd.shape, BF),
            pltpu.VMEM((block, width), F32),
        ]
        + scatter_scratch(block, width)
        + gather_sems()
        + scatter_scratch(block, width)
        + [pltpu.SemaphoreType.DMA((27,))],
        96,
        h, o, gain, wo, wgu, wd,
    )


def norm_back(upstream, normed, inverse, gain_row):
    scaled = upstream * gain_row
    return inverse * (scaled - normed * jnp.mean(scaled * normed, axis=-1, keepdims=True))


def mlp_back_kernel(
    ff, e, mid, gain, gu_hbm, wd_hbm, wgu_hbm, wo_hbm, e_out, dgu_out, dmid_out, gain_out, dat_out, dob_out,
    full, full2, parts, gu, wd, wgu, wo, total, send1, recv1,
    from_c, via_x, via_y, from_x, from_y, send2, recv2, send3, recv3, local,
):
    here = place()
    loads = Loads(local)
    wd_load = loads.start(wd_hbm, wd)
    gu_load = loads.start(gu_hbm, gu)
    wgu_load = loads.start(wgu_hbm, wgu)
    wo_load = loads.start(wo_hbm, wo)
    own = rank_of(here, 0, 0, 0)
    full[own] = e[...]
    greet(here)
    saves = []

    def on_block(r):
        first = not saves
        if first:
            wd_load.wait()
            gu_load.wait()
        saves.append(loads.start(full.at[r], e_out.at[r]))
        dhid = dot_nn(full[r], wd[...])
        g = gu[r, :, :ff].astype(F32)
        u = gu[r, :, ff:].astype(F32)
        sig = 1.0 / (1.0 + jnp.exp(-g))
        du = dhid * g * sig
        dg = dhid * u * sig * (1.0 + g * (1.0 - sig))
        gu[r, :, :ff] = dg.astype(BF)
        gu[r, :, ff:] = du.astype(BF)
        saves.append(loads.start(gu.at[r], dgu_out.at[r]))
        if first:
            wgu_load.wait()
        parts[r] = dot_nt(gu[r], wgu[...]).astype(BF)

    net1 = run_gather(here, full, (send1, recv1), on_block)
    net2 = run_scatter(here, parts, total, (from_c, via_x, via_y, from_x, from_y), (send2, recv2))
    da2 = total[...]
    m = mid[...]
    r2 = inverse_of(m)
    n2 = m * r2
    gain_out[...] = jnp.sum(da2 * n2, axis=0, keepdims=True)
    dmid = e[...].astype(F32) + norm_back(da2, n2, r2, gain[...])
    dmid_out[...] = dmid
    full2[own] = dmid.astype(BF)
    wo_load.wait()

    def on_second(r):
        saves.append(loads.start(full2.at[r], dat_out.at[r]))
        dob_out[r] = dot_nn(full2[r], wo[...]).astype(BF)

    net3 = run_gather(here, full2, (send3, recv3), on_second)
    for net in (net1, net2, net3):
        net.drain()
    for save in saves:
        save.wait()


def mlp_back(e, mid, gain, gu, wd, wgu, wo):
    block, width = e.shape
    ff = wd.shape[1]
    cols = wo.shape[1]
    return plane_call(
        functools.partial(mlp_back_kernel, ff),
        "mlp_back",
        2,
        [
            jax.ShapeDtypeStruct((8, block, width), BF),
            jax.ShapeDtypeStruct((8, block, 2 * ff), BF),
            jax.ShapeDtypeStruct((block, width), F32),
            jax.ShapeDtypeStruct((1, width), F32),
            jax.ShapeDtypeStruct((8, block, width), BF),
            jax.ShapeDtypeStruct((8, block, cols), BF),
        ],
        [ANYWHERE, ANYWHERE, IN_VMEM, IN_VMEM, ANYWHERE, IN_VMEM],
        [IN_VMEM, IN_VMEM, IN_VMEM, ANYWHERE, ANYWHERE, ANYWHERE, ANYWHERE],
        [
            pltpu.VMEM((8, block, width), BF),
            pltpu.VMEM((8, block, width), BF),
            pltpu.VMEM((8, block, width), BF),
            pltpu.VMEM((8, block, 2 * ff), BF),
            pltpu.VMEM(wd.shape, BF),
            pltpu.VMEM(wgu.shape, BF),
            pltpu.VMEM(wo.shape, BF),
            pltpu.VMEM((block, width), F32),
        ]
        + gather_sems()
        + scatter_scratch(block, width)
        + gather_sems()
        + [pltpu.SemaphoreType.DMA((28,))],
        100,
        e, mid, gain, gu, wd, wgu, wo,
    )


def attn_back_kernel(
    h, dmid, gain, dq, dk, dv, cosine, sine, w_hbm, dqkv_out, e_out, gain_out,
    parts, w, total, from_c, via_x, via_y, from_x, from_y, send, recv, local,
):
    here = place()
    w_load = Loads(local).start(w_hbm, w)
    greet(here)
    w_load.wait()
    q_cols = dq.shape[2]

    def fill(r):
        dqkv_out[r, :, :q_cols] = dq[r]
        dqkv_out[r, :, q_cols : q_cols + LANES] = turn(dk[r], cosine[r], -sine[r]).astype(BF)
        dqkv_out[r, :, q_cols + LANES :] = dv[r].astype(BF)
        parts[r] = dot_nt(dqkv_out[r], w[...]).astype(BF)

    net = run_scatter(here, parts, total, (from_c, via_x, via_y, from_x, from_y), (send, recv), fill)
    da1 = total[...]
    x = h[...].astype(F32)
    r1 = inverse_of(x)
    n1 = x * r1
    gain_out[...] = jnp.sum(da1 * n1, axis=0, keepdims=True)
    e_out[...] = (dmid[...] + norm_back(da1, n1, r1, gain[...])).astype(BF)
    net.drain()


def attn_back(h, dmid, gain, dq, dk, dv, cosine, sine, w):
    block, width = h.shape
    cols = w.shape[1]
    return plane_call(
        attn_back_kernel,
        "attn_back",
        3,
        [
            jax.ShapeDtypeStruct((8, block, cols), BF),
            jax.ShapeDtypeStruct((block, width), BF),
            jax.ShapeDtypeStruct((1, width), F32),
        ],
        [IN_VMEM, IN_VMEM, IN_VMEM],
        [IN_VMEM] * 8 + [ANYWHERE],
        [pltpu.VMEM((8, block, width), BF), pltpu.VMEM(w.shape, BF), pltpu.VMEM((block, width), F32)]
        + scatter_scratch(block, width)
        + [pltpu.SemaphoreType.DMA((1,))],
        36,
        h, dmid, gain, dq, dk, dv, cosine, sine, w,
    )


LOWER=-1e30
def dot(a, b, dims):
    return lax.dot_general(a, b, (dims, ((), ())), preferred_element_type=F32)

def attend_kernel(scale2, bq, bk, bounds, length, q, k, v, qpos, out, lse):
    groups = q.shape[0]
    i = pl.program_id(0)
    rows = groups * bq
    qs = q[...].reshape(rows, LANES)
    pos = qpos[0]
    pos2 = jnp.concatenate([pos] * groups, axis=1)
    def step(masked, j, state):
        top, total, acc = state
        at = pl.ds(pl.multiple_of(j * bk, bk), bk)
        s = dot(k[at, :], qs, ((1,), (1,)))
        if masked:
            kp = j * bk + lax.broadcasted_iota(jnp.int32, (bk, 1), 0)
            ok = (kp <= pos2) & (kp < length[0])
            s = jnp.where(ok, s, LOWER)
        new = jnp.maximum(top, jnp.max(s, axis=0, keepdims=True) * scale2)
        p = jnp.exp2(s * scale2 - new)
        alpha = jnp.exp2(top - new)
        total = total * alpha + jnp.sum(p, axis=0, keepdims=True)
        acc = acc * alpha + dot(v[at, :], p.astype(BF), ((0,), (0,)))
        return new, total, acc
    state = (jnp.full((1, rows), LOWER, F32), jnp.zeros((1, rows), F32), jnp.zeros((LANES, rows), F32))
    full, end = bounds[0, i], bounds[1, i]
    state = lax.fori_loop(0, full, functools.partial(step, False), state)
    top, total, acc = lax.fori_loop(full, end, functools.partial(step, True), state)
    o = (acc / total).T.astype(BF)
    for g in range(groups):
        out[:, g * LANES:(g + 1) * LANES] = o[g * bq:(g + 1) * bq]
    lse[...] = (top + jnp.log2(total))[None]

def attend(q, k, v, qpos, bounds, length, bq, bk, scale2):
    groups, tokens, _ = q.shape
    n = tokens // bq
    out, lse = pl.pallas_call(
        functools.partial(attend_kernel, scale2, bq, bk),
        grid_spec=pltpu.PrefetchScalarGridSpec(
            num_scalar_prefetch=2, grid=(n,),
            in_specs=[
                pl.BlockSpec((groups, bq, LANES), lambda i, *_: (0, i, 0)),
                pl.BlockSpec(k.shape, lambda i, *_: (0, 0)),
                pl.BlockSpec(v.shape, lambda i, *_: (0, 0)),
                pl.BlockSpec((1, 1, bq), lambda i, *_: (i, 0, 0)),
            ],
            out_specs=[
                pl.BlockSpec((bq, groups * LANES), lambda i, *_: (i, 0)),
                pl.BlockSpec((1, 1, groups * bq), lambda i, *_: (i, 0, 0)),
            ]),
        out_shape=[jax.ShapeDtypeStruct((tokens, groups * LANES), BF), jax.ShapeDtypeStruct((n, 1, groups * bq), F32)],
        compiler_params=pltpu.CompilerParams(vmem_limit_bytes=VMEM_LIMIT),
        name="attend",
        cost_estimate=pl.CostEstimate(flops=0, bytes_accessed=45000000, transcendentals=0),
    )(bounds, length, q, k, v, qpos)
    return out, lse

def back_kernel(scale, scale2, bq, bk, bounds, length, q, k, v, qpos, o, do, lse, cosine, sine, dq, dk, dv):
    groups = q.shape[0]
    i = pl.program_id(0)
    @pl.when(i == 0)
    def _():
        dk[...] = jnp.zeros_like(dk)
        dv[...] = jnp.zeros_like(dv)
    qs = q[...].reshape(groups * bq, LANES)
    dos = jnp.concatenate([do[:, g * LANES:(g + 1) * LANES] for g in range(groups)], axis=0)
    os_ = jnp.concatenate([o[:, g * LANES:(g + 1) * LANES] for g in range(groups)], axis=0)
    delta = jnp.sum(dos.astype(F32) * os_.astype(F32), axis=1, keepdims=True).reshape(1, groups * bq)
    lse_row = lse[0]
    pos = qpos[0]
    pos2 = jnp.concatenate([pos] * groups, axis=1)
    def step(masked, j, acc):
        at = pl.ds(pl.multiple_of(j * bk, bk), bk)
        kb, vb = k[at, :], v[at, :]
        s = dot(kb, qs, ((1,), (1,)))
        p = jnp.exp2(s * scale2 - lse_row)
        if masked:
            kp = j * bk + lax.broadcasted_iota(jnp.int32, (bk, 1), 0)
            ok = (kp <= pos2) & (kp < length[0])
            p = jnp.where(ok, p, 0.0)
        dp = dot(vb, dos, ((1,), (1,)))
        ds = (p * (dp - delta)).astype(BF)
        dv[at, :] += dot(p.astype(BF), dos, ((1,), (0,)))
        dk[at, :] += dot(ds, qs, ((1,), (0,))) * scale
        return acc + dot(ds, kb, ((0,), (0,)))
    full, end = bounds[0, i], bounds[1, i]
    acc = jnp.zeros((groups * bq, LANES), F32)
    acc = lax.fori_loop(0, full, functools.partial(step, False), acc)
    acc = lax.fori_loop(full, end, functools.partial(step, True), acc) * scale
    for g in range(groups):
        dq[:, g * LANES:(g + 1) * LANES] = turn(acc[g * bq:(g + 1) * bq], cosine[...], -sine[...]).astype(BF)

def attend_back(q, k, v, qpos_row, o, do, lse, cosine, sine, bounds, length, bq, bk, scale, scale2):
    groups, tokens, _ = q.shape
    n = tokens // bq
    wide = pl.BlockSpec((bq, groups * LANES), lambda i, *_: (i, 0))
    return pl.pallas_call(
        functools.partial(back_kernel, scale, scale2, bq, bk),
        grid_spec=pltpu.PrefetchScalarGridSpec(
            num_scalar_prefetch=2, grid=(n,),
            in_specs=[
                pl.BlockSpec((groups, bq, LANES), lambda i, *_: (0, i, 0)),
                pl.BlockSpec(k.shape, lambda i, *_: (0, 0)),
                pl.BlockSpec(v.shape, lambda i, *_: (0, 0)),
                pl.BlockSpec((1, 1, bq), lambda i, *_: (i, 0, 0)),
                wide, wide,
                pl.BlockSpec((1, 1, groups * bq), lambda i, *_: (i, 0, 0)),
                pl.BlockSpec((bq, LANES), lambda i, *_: (i, 0)),
                pl.BlockSpec((bq, LANES), lambda i, *_: (i, 0)),
            ],
            out_specs=[wide, pl.BlockSpec(k.shape, lambda i, *_: (0, 0)), pl.BlockSpec(k.shape, lambda i, *_: (0, 0))]),
        out_shape=[jax.ShapeDtypeStruct((tokens, groups * LANES), BF), jax.ShapeDtypeStruct(k.shape, F32), jax.ShapeDtypeStruct(k.shape, F32)],
        compiler_params=pltpu.CompilerParams(vmem_limit_bytes=VMEM_LIMIT),
        name="attend_back",
        cost_estimate=pl.CostEstimate(flops=0, bytes_accessed=65000000, transcendentals=0),
    )(bounds, length, q, k, v, qpos_row, o, do, lse, cosine, sine)

def bounds_of(positions, length, bq, bk):
    p = positions.reshape(-1, bq)
    lo = jnp.minimum(jnp.min(p, axis=1) + 1, length) // bk
    hi = -(-jnp.minimum(jnp.max(p, axis=1) + 1, length) // bk)
    return jnp.stack([lo, hi]).astype(jnp.int32)


PLANE = ("x", "c", "y")

def spread(matrix, heads):
    split = matrix.reshape(matrix.shape[0], heads, 2, HALF)
    return jnp.pad(split, ((0, 0), (0, 0), (0, 0), (0, LANES // 2 - HALF))).reshape(-1, heads * LANES)


def unspread(matrix, heads):
    return matrix.reshape(-1, heads, 2, LANES // 2)[..., :HALF].reshape(-1, heads * HEAD_SIZE)


def widen(matrix, heads):
    split = matrix.reshape(matrix.shape[0], heads, HEAD_SIZE)
    return jnp.pad(split, ((0, 0), (0, 0), (0, LANES - HEAD_SIZE))).reshape(-1, heads * LANES)


def narrow(matrix, heads):
    return matrix.reshape(-1, heads, LANES)[..., :HEAD_SIZE].reshape(-1, heads * HEAD_SIZE)


def together(*arrays):
    return lax.optimization_barrier(arrays)


def body(
    inputs,
    lengths,
    cotangent,
    attn_gain,
    w_query,
    key_projection,
    value_projection,
    w_out,
    mlp_gain,
    w_gate,
    w_up,
    w_down,
):
    sections = lax.axis_size("x") * lax.axis_size("c")
    planes = lax.axis_size("z")
    halves = lax.axis_size("y")
    extra = lax.axis_size("e")
    ranks = sections * halves
    layers = sections
    block = inputs.shape[1]
    width = inputs.shape[2]
    rows = w_query.shape[1]
    tokens = block * ranks
    all_tokens = tokens * extra
    head_group = QUERY_HEADS // KEY_VALUE_HEADS
    q_cols = head_group * HEAD_SIZE
    kv_cols = HEAD_SIZE
    ff_cols = FF // ranks
    scale = 1.0 / math.sqrt(HEAD_SIZE)
    scale2 = scale * math.log2(math.e)

    def swap(array):
        names = ("x", "c", "z")
        pairs = [
            (s * planes + z, z * planes + s) for s in range(sections) for z in range(planes)
        ]
        return lax.ppermute(array, names, pairs)

    def by_rank(matrix):
        return matrix.reshape(rows, ranks, -1)

    attn_pack = jnp.concatenate(
        [
            by_rank(w_query[0]),
            by_rank(key_projection[0]),
            by_rank(value_projection[0]),
            by_rank(w_out[0].T),
            jnp.broadcast_to(jnp.stack([attn_gain[0], mlp_gain[0]], axis=1)[:, None, :], (rows, ranks, 2)),
        ],
        axis=2,
    )
    mlp_pack = jnp.concatenate(
        [by_rank(w_gate[0]), by_rank(w_up[0]), by_rank(w_down[0].T)], axis=2
    )

    def exchange(pack):
        moved = lax.all_to_all(
            jnp.swapaxes(pack.astype(BF), 0, 1), PLANE, split_axis=0, concat_axis=0, tiled=True
        )
        return moved.reshape(layers, halves, rows, pack.shape[2])

    def whole(part):
        if extra > 1:
            part = lax.all_gather(part, "e", axis=1, tiled=False)
        return lax.all_gather(part.reshape(-1, part.shape[-1]), "z", axis=0, tiled=True)

    def reduce_rows(grad):
        mine = lax.psum_scatter(grad.astype(BF), "z", scatter_dimension=0, tiled=True)
        mine = mine.reshape(halves, extra, rows, -1)
        if extra > 1:
            return lax.psum_scatter(mine, "e", scatter_dimension=1, tiled=False)
        return mine[:, 0]

    attn_parts = exchange(attn_pack)
    mlp_parts = exchange(mlp_pack)

    rank = (lax.axis_index("x") * lax.axis_size("c") + lax.axis_index("c")) * halves + lax.axis_index("y")
    spot = lax.axis_index("e")
    length = lengths[lax.axis_index("z")]

    block_start = (jnp.arange(ranks) * extra + spot) * block
    positions = (block_start[:, None] + jnp.arange(block)[None, :]).reshape(tokens)
    exponents = 2.0 * jnp.arange(HEAD_SIZE // 2).astype(F32) / HEAD_SIZE
    angles = positions.astype(F32)[:, None] * (THETA ** (-exponents))[None, :]
    table = lambda values: jnp.pad(values, ((0, 0), (0, LANES // 2 - HALF)))
    cosine = jnp.concatenate([table(jnp.cos(angles))] * 2, axis=1)
    sine = jnp.concatenate([table(-jnp.sin(angles)), table(jnp.sin(angles))], axis=1)
    bq = math.gcd(tokens, 512)
    bk = math.gcd(all_tokens, 512)
    bounds = bounds_of(positions, length, bq, bk)
    length1 = length.reshape(1)
    query_rows = positions.astype(jnp.int32).reshape(-1, 1, bq)

    def all_keys(array):
        if extra == 1:
            return array
        stacked = lax.all_gather(array.reshape(ranks, block, -1), "e", axis=1, tiled=False)
        return stacked.reshape(all_tokens, -1)

    def own_keys(array):
        if extra == 1:
            return array
        stacked = array.astype(BF).reshape(ranks, extra, block, -1)
        return lax.psum_scatter(stacked, "e", scatter_dimension=1, tiled=False).reshape(tokens, -1).astype(F32)

    cosine3 = cosine.reshape(ranks, block, LANES)
    sine3 = sine.reshape(ranks, block, LANES)

    def flat(array):
        return array.reshape(tokens, array.shape[-1])

    hidden_state = swap(inputs[0])
    qk_cols = q_cols + kv_cols
    qkv_cols = qk_cols + kv_cols
    saved = []
    gu_parts = [part[..., : 2 * ff_cols] for part in mlp_parts]
    d_parts = [part[..., 2 * ff_cols :] for part in mlp_parts]
    attn_w, gu_part, d_part = together(whole(attn_parts[0]), gu_parts[0], d_parts[0])
    w_gu, w_d = whole(gu_part), whole(d_part)
    for layer in range(layers):
        w_qkv = jnp.concatenate(
            [spread(attn_w[:, :qk_cols], head_group + 1), widen(attn_w[:, qk_cols:qkv_cols], 1)], axis=1
        )
        w_o = widen(attn_w[:, qkv_cols : qkv_cols + q_cols], head_group)
        gains = attn_w[:, qkv_cols + q_cols :].astype(F32).T
        gain1, gain2 = gains[0:1], gains[1:2]
        a1, q, k, v = attn_in(hidden_state, gain1, w_qkv, cosine3, sine3, head_group)
        q, k, v = q.reshape(head_group, tokens, LANES), all_keys(flat(k)), all_keys(flat(v))
        o, log_total = attend(q, k, v, query_rows, bounds, length1, bq, bk, scale2)
        if layer + 1 < layers:
            o, attn_part, gu_part = together(o, attn_parts[layer + 1], gu_parts[layer + 1])
            attn_w, next_gu = whole(attn_part), whole(gu_part)
        mid, a2, gu, hid, after_mlp = mlp(
            hidden_state, o.reshape(ranks, block, -1), gain2, w_o, w_gu, w_d
        )
        saved.append(
            (hidden_state, a1, q, k, v, o, log_total, mid, a2, gu, hid, w_qkv, w_o, w_gu, w_d, gain1, gain2)
        )
        hidden_state = after_mlp
        if layer + 1 < layers:
            hidden_state, attn_w, w_gu, d_part = together(hidden_state, attn_w, next_gu, d_parts[layer + 1])
            w_d = whole(d_part)
    output = swap(hidden_state)[None]

    my_positions = (rank * extra + spot) * block + jnp.arange(block)
    e = swap(cotangent[0])
    e = jnp.where((my_positions < length)[:, None], e, jnp.zeros_like(e))
    attn_grads = [None] * layers
    gu_grads = [None] * layers
    d_grads = [None] * layers
    for layer in reversed(range(layers)):
        (h, a1, q, k, v, o, log_total, mid, a2, gu, hid, w_qkv, w_o, w_gu, w_d, gain1, gain2) = saved[layer]
        e_all, dgu, dmid, gain2_grad, dat, dob = mlp_back(e, mid, gain2, gu, w_d, w_gu, w_o)
        gu_sums = dot_tn(flat(a2), flat(dgu)).astype(BF)
        d_sums = dot_tn(flat(e_all), flat(hid)).astype(BF)
        dob, gu_sums, d_sums = together(dob, gu_sums, d_sums)
        if layer + 1 < layers:
            dob, attn_grads[layer + 1], d_grads[layer + 1] = together(
                dob, attn_grads[layer + 1], d_grads[layer + 1]
            )
        gu_grads[layer] = reduce_rows(gu_sums)
        if layer == 0:
            d_grads[layer] = reduce_rows(d_sums)
        dq, dk, dv = attend_back(
            q, k, v, query_rows, o, flat(dob), log_total, cosine, sine, bounds, length1, bq, bk, scale, scale2
        )
        dk, dv = own_keys(dk), own_keys(dv)
        dqkv, e, gain1_grad = attn_back(
            h, dmid, gain1, *(array.reshape(ranks, block, -1) for array in (dq, dk, dv)), cosine3, sine3, w_qkv
        )
        dqkv_w = dot_tn(flat(a1), flat(dqkv)).astype(BF)
        qk_wide = (head_group + 1) * LANES
        attn_sums = jnp.concatenate(
            [
                unspread(dqkv_w[:, :qk_wide], head_group + 1),
                narrow(dqkv_w[:, qk_wide:], 1),
                narrow(dot_tn(flat(dat), o).astype(BF), head_group),
                jnp.concatenate([gain1_grad, gain2_grad], axis=0).T.astype(BF),
            ],
            axis=1,
        )
        if layer > 0:
            e, attn_sums, d_sums, gu_grads[layer] = together(e, attn_sums, d_sums, gu_grads[layer])
            d_grads[layer] = reduce_rows(d_sums)
        else:
            e, attn_sums, gu_grads[layer], d_grads[layer] = together(e, attn_sums, gu_grads[layer], d_grads[layer])
        attn_grads[layer] = reduce_rows(attn_sums)
    input_grad = swap(e)[None]

    def send_home(grads):
        stacked = jnp.stack(grads).reshape(ranks, rows, -1)
        back = lax.all_to_all(stacked, PLANE, split_axis=0, concat_axis=0, tiled=True)
        return back.astype(F32)

    def columns(back, start, count):
        return jnp.swapaxes(back[:, :, start : start + count], 0, 1).reshape(rows, ranks * count)

    mlp_back_home = send_home([jnp.concatenate(pair, axis=2) for pair in zip(gu_grads, d_grads)])
    attn_back_home = send_home(attn_grads)
    at = q_cols + 2 * kv_cols
    gain_sums = jnp.sum(attn_back_home[:, :, at + q_cols :], axis=0)
    return (
        output,
        input_grad,
        gain_sums[:, 0][None],
        columns(attn_back_home, 0, q_cols)[None],
        columns(attn_back_home, q_cols, kv_cols)[None],
        columns(attn_back_home, q_cols + kv_cols, kv_cols)[None],
        columns(attn_back_home, at, q_cols).T[None],
        gain_sums[:, 1][None],
        columns(mlp_back_home, 0, ff_cols)[None],
        columns(mlp_back_home, ff_cols, ff_cols)[None],
        columns(mlp_back_home, 2 * ff_cols, ff_cols).T[None],
    )


def solution(mesh):
    section, seq = mesh.devices.shape
    halves = KEY_VALUE_HEADS // section
    extra = seq // (section * halves)
    fine = Mesh(
        mesh.devices.reshape(section // 2, 2, section, halves, extra), ("x", "c", "z", "y", "e")
    )
    sec, sq = ("x", "c"), ("z", "y", "e")
    rows3 = P(sec, sq, None)
    cols3 = P(sec, None, sq)
    in_specs = (rows3, P(), rows3, P(sec, sq), rows3, rows3, rows3, cols3, P(sec, sq), rows3, rows3, cols3)
    out_specs = (rows3, rows3, P(sec, sq), rows3, rows3, rows3, cols3, P(sec, sq), rows3, rows3, cols3)
    return jax.shard_map(body, mesh=fine, in_specs=in_specs, out_specs=out_specs, check_vma=False)
```

```python
import functools
import math

import jax
import jax.numpy as jnp
from jax import lax
from jax.experimental import pallas as pl
from jax.experimental.pallas import tpu as pltpu
from jax.sharding import Mesh
from jax.sharding import PartitionSpec as P

QUERY_HEADS = 16
KEY_VALUE_HEADS = 8
HEAD_SIZE = 96
FF = 4096

EPS = 1e-05
THETA = 100000.0
LOWER_LIMIT = -1e30

BF = jnp.bfloat16
F32 = jnp.float32

LANES = 128
HALF = HEAD_SIZE // 2
VMEM_LIMIT = 56 * 1024 * 1024


def dot(a, b, dims):
    return lax.dot_general(a, b, (dims, ((), ())), preferred_element_type=F32)


def dot_nn(a, b):
    return dot(a, b, ((1,), (0,)))


def dot_nt(a, b):
    return dot(a, b, ((1,), (1,)))


def dot_tn(a, b):
    return dot(a, b, ((0,), (0,)))


MESH = pl.DeviceIdType.MESH

OWN, X, Y, D = (0, 0), (1, 0), (0, 1), (1, 1)


def place():
    return lax.axis_index("x"), lax.axis_index("c"), lax.axis_index("y")


def flip(index, by):
    return 1 - index if by else index


def rank_of(here, dx, dc, dy):
    x, c, y = here
    return (flip(x, dx) * 2 + flip(c, dc)) * 2 + flip(y, dy)


class Swap:
    def __init__(self, here, moving, moved, sem):
        x, c, _ = here
        z = lax.axis_index("z")
        section = x * 2 + c
        self.away = section != z
        self.partner = {"x": z // 2, "c": lax.rem(z, 2), "z": section}
        self.remote = pltpu.make_async_remote_copy(
            src_ref=moving,
            dst_ref=moved,
            send_sem=sem.at[0],
            recv_sem=sem.at[1],
            device_id=self.partner,
            device_id_type=MESH,
        )
        self.local = pltpu.make_async_copy(moving, moved, sem.at[2])

    def greet(self, barrier):
        @pl.when(self.away)
        def _():
            pl.semaphore_signal(barrier, inc=1, device_id=self.partner, device_id_type=MESH)

    def either(self, remote, local):
        pl.when(self.away)(remote)
        pl.when(jnp.logical_not(self.away))(local)

    def start(self):
        self.either(lambda: self.remote.start(), lambda: self.local.start())

    def met(self, barrier, count):
        self.either(lambda: pl.semaphore_wait(barrier, count + 1), lambda: pl.semaphore_wait(barrier, count))

    def wait(self):
        self.either(lambda: self.remote.wait(), lambda: self.local.wait())


def with_swap(kernel, inputs, outputs):
    def wrapped(*refs):
        last = inputs + 1 + outputs
        kernel(
            *refs[:inputs],
            *refs[inputs + 1 : last],
            *refs[last + 1 : -1],
            swap=(refs[inputs], refs[last], refs[-1]),
        )

    return wrapped


def greet(here, swap=None):
    x, c, y = here
    barrier = pltpu.get_barrier_semaphore()
    for peer in ({"x": 1 - x}, {"c": 1 - c}, {"y": 1 - y}):
        pl.semaphore_signal(barrier, inc=1, device_id=peer, device_id_type=MESH)
    if swap is None:
        pl.semaphore_wait(barrier, 3)
    else:
        swap.greet(barrier)
        swap.met(barrier, 3)
        swap.start()


class Sender:
    def __init__(self, here, send_sem, recv_sem):
        x, c, y = here
        self.peers = {"x": {"x": 1 - x}, "c": {"c": 1 - c}, "y": {"y": 1 - y}}
        self.send_sem, self.recv_sem = send_sem, recv_sem
        self.sent = []

    def copy(self, src, dst, index, to, number):
        return pltpu.make_async_remote_copy(
            src_ref=src,
            dst_ref=dst,
            send_sem=self.send_sem.at[number],
            recv_sem=self.recv_sem.at[index],
            device_id=self.peers[to],
            device_id_type=MESH,
        )

    def send(self, src, dst, index, to):
        started = self.copy(src, dst, index, to, len(self.sent))
        started.start()
        self.sent.append(started)

    def arrived(self, where, index):
        self.copy(where, where, index, "c", 0).wait_recv()

    def drain(self):
        for started in self.sent:
            started.wait_send()


def run_gather(here, full, sems, on_block):
    block = full.shape[1]
    piece = block // 4
    net = Sender(here, *sems)

    def index(role, chunk):
        return (role[0] * 4 + role[1] * 2 + role[2]) * 4 + chunk

    def slot(role, chunk, count=1):
        return full.at[rank_of(here, *role), pl.ds(chunk * piece, piece * count)]

    def send(role, chunk, to, as_role, count=1):
        where = slot(role, chunk, count)
        net.send(where, where, index(as_role, chunk), to)

    def arrived(role, chunk, count=1):
        net.arrived(slot(role, chunk, count), index(role, chunk))

    def whole(role):
        for chunk in range(4):
            arrived(role, chunk)

    def done(role):
        on_block(rank_of(here, *role))

    own, at_x, at_y, at_d, at_c = (0, 0, 0), (1, 0, 0), (0, 0, 1), (1, 0, 1), (0, 1, 0)
    xc, yc, dc = (1, 1, 0), (0, 1, 1), (1, 1, 1)
    for cx, cy in ((2, 0), (3, 1), (0, 2), (1, 3)):
        send(own, cx, "x", at_x)
        send(own, cy, "y", at_y)
    send(own, 0, "c", at_c, 4)

    def pass_on(cx, cy):
        arrived(at_x, cx)
        if cx >= 2:
            send(at_x, cx, "y", at_d)
        send(at_x, cx, "c", xc)
        arrived(at_y, cy)
        if cy < 2:
            send(at_y, cy, "x", at_d)
        send(at_y, cy, "c", yc)

    def pass_last(chunks):
        for chunk in chunks:
            arrived(at_d, chunk)
            send(at_d, chunk, "c", dc)

    done(own)
    pass_on(2, 0)
    arrived(at_c, 0, 4)
    done(at_c)
    pass_on(3, 1)
    pass_on(0, 2)
    pass_on(1, 3)
    done(at_x)
    done(at_y)
    pass_last((0, 2))
    whole(xc)
    done(xc)
    whole(yc)
    done(yc)
    pass_last((1, 3))
    done(at_d)
    whole(dc)
    done(dc)
    return net


def run_scatter(here, parts, total, bufs, sems, fill=None, beside=None):
    from_c, via_x, via_y, from_x, from_y = bufs
    block = parts.shape[1]
    half = block // 2
    net = Sender(here, *sems)
    order = (D, X, Y, OWN)
    lower, upper = pl.ds(0, half), pl.ds(half, half)

    def rank(n, dc):
        return rank_of(here, order[n][0], dc, order[n][1])

    def make(r):
        if fill is not None:
            fill(r)

    def sibling(n):
        r = rank(n, 1)
        make(r)
        net.send(parts.at[r], from_c.at[n], n, "c")

    def add(n, where, more):
        r = rank(n, 0)
        parts[r, where] = (parts[r, where].astype(F32) + more.astype(F32)).astype(BF)

    def mine(n, where):
        return parts.at[rank(n, 0), where]

    def combine(n):
        net.arrived(from_c.at[n], n)
        if n < 3:
            add(n, pl.ds(0, block), from_c[n])

    sibling(0)
    make(rank(0, 0))
    sibling(1)
    sibling(2)
    combine(0)
    net.send(mine(0, upper), via_x, 4, "x")
    net.send(mine(0, lower), via_y, 5, "y")
    make(rank(1, 0))
    combine(1)
    net.send(mine(1, upper), from_x.at[upper], 6, "x")
    make(rank(2, 0))
    combine(2)
    net.send(mine(2, lower), from_y.at[lower], 7, "y")
    sibling(3)
    make(rank(3, 0))
    combine(3)
    total[...] = parts[rank(3, 0)].astype(F32) + from_c[3].astype(F32)
    if beside is not None:
        beside(0)
    net.arrived(via_y, 5)
    add(1, lower, via_y[...])
    net.send(mine(1, lower), from_x.at[lower], 8, "x")
    net.arrived(via_x, 4)
    add(2, upper, via_x[...])
    net.send(mine(2, upper), from_y.at[upper], 9, "y")
    if beside is not None:
        beside(1)
    net.arrived(from_x.at[upper], 6)
    net.arrived(from_y.at[lower], 7)
    total[upper] += from_x[upper].astype(F32)
    total[lower] += from_y[lower].astype(F32)
    net.arrived(from_x.at[lower], 8)
    net.arrived(from_y.at[upper], 9)
    total[lower] += from_x[lower].astype(F32)
    total[upper] += from_y[upper].astype(F32)
    return net


def gather_sems():
    return [pltpu.SemaphoreType.DMA((32,)), pltpu.SemaphoreType.DMA((32,))]


def scatter_scratch(block, width):
    half = block // 2
    return [
        pltpu.VMEM((4, block, width), BF),
        pltpu.VMEM((half, width), BF),
        pltpu.VMEM((half, width), BF),
        pltpu.VMEM((block, width), BF),
        pltpu.VMEM((block, width), BF),
        pltpu.SemaphoreType.DMA((10,)),
        pltpu.SemaphoreType.DMA((10,)),
    ]


class Loads:
    def __init__(self, sem):
        self.sem = sem
        self.count = 0

    def start(self, src, dst):
        copy = pltpu.make_async_copy(src, dst, self.sem.at[self.count])
        self.count += 1
        copy.start()
        return copy


def inverse_of(x):
    return lax.rsqrt(jnp.mean(x * x, axis=-1, keepdims=True) + EPS)


def lane(x):
    return lax.broadcasted_iota(jnp.int32, x.shape, 1)


def turn(head, cosine, sine):
    return head * cosine + pltpu.roll(head, LANES // 2, 1) * sine


def open_halves(head):
    return jnp.where(lane(head) < LANES // 2, head, pltpu.roll(head, LANES // 2 - HALF, 1))


def close_halves(head):
    low = lane(head) < LANES // 2
    return jnp.where(low, head, 0.0) + pltpu.roll(jnp.where(low, 0.0, head), LANES // 2 + HALF, 1)


def four_heads(a, b, c):
    at = lane(a)
    return (
        a,
        pltpu.roll(jnp.where(at >= 96, a, b), 32, 1),
        pltpu.roll(jnp.where(at >= 64, b, c), 64, 1),
        pltpu.roll(c, 96, 1),
    )


def three_lanes(heads):
    at = lane(heads[0])
    b, c, d = pltpu.roll(heads[1], 96, 1), pltpu.roll(heads[2], 64, 1), pltpu.roll(heads[3], 32, 1)
    return jnp.where(at < 96, heads[0], b), jnp.where(at < 64, b, c), jnp.where(at < 32, c, d)


def plane_call(kernel, name, number, out_shape, out_specs, in_specs, scratch, time_us, *operands, moving=None):
    if moving is not None:
        kernel = with_swap(kernel, len(in_specs), len(out_specs))
        out_shape = out_shape + [jax.ShapeDtypeStruct(moving.shape, moving.dtype)]
        in_specs, out_specs = in_specs + [ANYWHERE], out_specs + [ANYWHERE]
        scratch = scratch + [pltpu.SemaphoreType.DMA((3,))]
        operands = operands + (moving,)
    return pl.pallas_call(
        kernel,
        out_shape=out_shape,
        in_specs=in_specs,
        out_specs=out_specs,
        scratch_shapes=scratch,
        compiler_params=pltpu.CompilerParams(
            collective_id=number, has_side_effects=True, vmem_limit_bytes=VMEM_LIMIT
        ),
        cost_estimate=pl.CostEstimate(flops=0, bytes_accessed=time_us * 3000000, transcendentals=0),
        name=name,
    )(*operands)


ANYWHERE = pl.BlockSpec(memory_space=pl.ANY)
IN_VMEM = pl.BlockSpec(memory_space=pltpu.VMEM)
QKV = 4 * HEAD_SIZE
OUT = 2 * HEAD_SIZE
GAIN_AT = QKV + OUT
PACK = -(-(GAIN_AT + 2) // LANES) * LANES


def attn_in_kernel(h, w_hbm, cosine, sine, a1_out, q_out, k_out, v_out, gain_out, full, w, send, recv, local):
    here = place()
    loads = Loads(local)
    w_load = loads.start(w_hbm, w)
    x = h[...].astype(F32)
    n1 = x * inverse_of(x)
    w_load.wait()
    rows = w[:, PACK - LANES :].astype(F32).T
    gain_out[...] = rows[GAIN_AT - PACK + LANES : GAIN_AT - PACK + LANES + 2]
    full[rank_of(here, 0, 0, 0)] = (n1 * gain_out[0:1, :]).astype(BF)
    greet(here)
    saves = []

    def on_block(r):
        saves.append(loads.start(full.at[r], a1_out.at[r]))
        qkv = dot_nn(full[r], w[:, :QKV])
        heads = four_heads(*(qkv[:, n * LANES : (n + 1) * LANES] for n in range(3)))
        cos, sin = cosine[r], sine[r]
        for n in range(2):
            q_out[n, r] = turn(open_halves(heads[n]), cos, sin).astype(BF)
        k_out[r] = turn(open_halves(heads[2]), cos, sin).astype(BF)
        v_out[r] = jnp.where(lane(heads[3]) < HEAD_SIZE, heads[3], 0.0).astype(BF)

    net = run_gather(here, full, (send, recv), on_block)
    net.drain()
    for save in saves:
        save.wait()


def attn_in(h, w, cosine, sine):
    block, width = h.shape
    return plane_call(
        attn_in_kernel,
        "attn_in",
        0,
        [
            jax.ShapeDtypeStruct((8, block, width), BF),
            jax.ShapeDtypeStruct((2, 8, block, LANES), BF),
            jax.ShapeDtypeStruct((8, block, LANES), BF),
            jax.ShapeDtypeStruct((8, block, LANES), BF),
            jax.ShapeDtypeStruct((2, width), F32),
        ],
        [ANYWHERE, IN_VMEM, IN_VMEM, IN_VMEM, IN_VMEM],
        [IN_VMEM, ANYWHERE, IN_VMEM, IN_VMEM],
        [pltpu.VMEM((8, block, width), BF), pltpu.VMEM(w.shape, BF)]
        + gather_sems()
        + [pltpu.SemaphoreType.DMA((9,))],
        34,
        h, w, cosine, sine,
    )


def mlp_kernel(
    ff, h, o, gain, wa_hbm, w1_hbm, w2_hbm, mid_out, a2_out, gu_out, hid_out, next_out,
    full, parts, gu, hid, wa, wm, total,
    from_c, via_x, via_y, from_x, from_y, send1, recv1, send2, recv2,
    from_c3, via_x3, via_y3, from_x3, from_y3, send3, recv3, local, swap=None,
):
    here = place()
    swap = swap and Swap(here, *swap)
    loads = Loads(local)
    wa_load = loads.start(wa_hbm, wa)
    split = w1_hbm.shape[1]
    w1_load = loads.start(w1_hbm, wm.at[:, pl.ds(0, split)])
    w2_load = loads.start(w2_hbm, wm.at[:, pl.ds(split, 3 * ff - split)])
    greet(here, swap)
    wa_load.wait()

    def fill(r):
        parts[r] = dot_nt(o[r], wa[:, QKV:GAIN_AT]).astype(BF)

    bufs = (from_c, via_x, via_y, from_x, from_y)
    net1 = run_scatter(here, parts, total, bufs, (send1, recv1), fill)
    mid = h[...].astype(F32) + total[...]
    mid_out[...] = mid
    full[rank_of(here, 0, 0, 0)] = (mid * inverse_of(mid) * gain[1:2, :]).astype(BF)
    net1.drain()
    saves = []

    def on_block(r):
        if not saves:
            w1_load.wait()
            w2_load.wait()
        saves.append(loads.start(full.at[r], a2_out.at[r]))
        a2 = full[r]
        g = dot_nn(a2, wm[:, :ff])
        u = dot_nn(a2, wm[:, ff : 2 * ff])
        gu[r, :, :ff] = g.astype(BF)
        gu[r, :, ff:] = u.astype(BF)
        low = (g * (1.0 / (1.0 + jnp.exp(-g))) * u).astype(BF)
        hid[r] = low
        saves.append(loads.start(gu.at[r], gu_out.at[r]))
        saves.append(loads.start(hid.at[r], hid_out.at[r]))
        parts[r] = dot_nt(low, wm[:, 2 * ff :]).astype(BF)

    net2 = run_gather(here, full, (send2, recv2), on_block)
    bufs3 = (from_c3, via_x3, via_y3, from_x3, from_y3)
    net3 = run_scatter(here, parts, total, bufs3, (send3, recv3))
    next_out[...] = (mid_out[...] + total[...]).astype(BF)
    net2.drain()
    net3.drain()
    for save in saves:
        save.wait()
    if swap is not None:
        swap.wait()


def mlp(h, o, gain, wa, w1, w2, moving=None):
    block, width = h.shape
    ff = (w1.shape[1] + w2.shape[1]) // 3
    return plane_call(
        functools.partial(mlp_kernel, ff),
        "mlp",
        1 if moving is None else 8,
        [
            jax.ShapeDtypeStruct((block, width), F32),
            jax.ShapeDtypeStruct((8, block, width), BF),
            jax.ShapeDtypeStruct((8, block, 2 * ff), BF),
            jax.ShapeDtypeStruct((8, block, ff), BF),
            jax.ShapeDtypeStruct((block, width), BF),
        ],
        [IN_VMEM, ANYWHERE, ANYWHERE, ANYWHERE, IN_VMEM],
        [IN_VMEM, IN_VMEM, IN_VMEM, ANYWHERE, ANYWHERE, ANYWHERE],
        [
            pltpu.VMEM((8, block, width), BF),
            pltpu.VMEM((8, block, width), BF),
            pltpu.VMEM((8, block, 2 * ff), BF),
            pltpu.VMEM((8, block, ff), BF),
            pltpu.VMEM(wa.shape, BF),
            pltpu.VMEM((width, 3 * ff), BF),
            pltpu.VMEM((block, width), F32),
        ]
        + scatter_scratch(block, width)
        + gather_sems()
        + scatter_scratch(block, width)
        + [pltpu.SemaphoreType.DMA((27,))],
        96,
        h, o, gain, wa, w1, w2,
        moving=moving,
    )


def norm_back(upstream, normed, inverse, gain_row):
    scaled = upstream * gain_row
    return inverse * (scaled - normed * jnp.mean(scaled * normed, axis=-1, keepdims=True))


def flat_tn(a, cols, b):
    total = dot_tn(a[0, :, cols], b[0])
    for n in range(1, a.shape[0]):
        total = total + dot_tn(a[n, :, cols], b[n])
    return total


def mlp_back_kernel(
    ff, step, e, mid, gain, gu_hbm, hid_hbm, a2_hbm, w1_hbm, w2_hbm, wa_hbm, dmid_out, gain_out, dat_out, dob_out,
    gu_sums, d_sums, full, full2, parts, a2, gu, hid, wm, wa, total, stage, send1, recv1,
    from_c, via_x, via_y, from_x, from_y, send2, recv2, send3, recv3, local, swap=None,
):
    here = place()
    swap = swap and Swap(here, *swap)
    loads = Loads(local)
    split = w1_hbm.shape[1]
    w2_load = loads.start(w2_hbm, wm.at[:, pl.ds(split, 3 * ff - split)])
    gu_load = loads.start(gu_hbm, gu)
    w1_load = loads.start(w1_hbm, wm.at[:, pl.ds(0, split)])
    wa_load = loads.start(wa_hbm, wa)
    a2_load = loads.start(a2_hbm, a2)
    hid_load = loads.start(hid_hbm, hid)
    own = rank_of(here, 0, 0, 0)
    full[own] = e[...]
    greet(here, swap)
    w2_load.wait()
    gu_load.wait()
    w1_load.wait()

    def on_block(r):
        dhid = dot_nn(full[r], wm[:, 2 * ff :])
        g = gu[r, :, :ff].astype(F32)
        u = gu[r, :, ff:].astype(F32)
        sig = 1.0 / (1.0 + jnp.exp(-g))
        du = dhid * g * sig
        dg = dhid * u * sig * (1.0 + g * (1.0 - sig))
        gu[r, :, :ff] = dg.astype(BF)
        gu[r, :, ff:] = du.astype(BF)
        parts[r] = dot_nt(gu[r], wm[:, : 2 * ff]).astype(BF)

    net1 = run_gather(here, full, (send1, recv1), on_block)
    a2_load.wait()
    hid_load.wait()
    sums = []
    count = full.shape[2] // step

    def beside(turn_number):
        half = (count + 1) // 2
        for number in range(turn_number * half, min((turn_number + 1) * half, count)):
            if number >= 2:
                for save in sums[number - 2]:
                    save.wait()
            at = slice(number * step, (number + 1) * step)
            held = stage.at[number % 2]
            held[:, : 2 * ff] = flat_tn(a2, at, gu).astype(BF)
            held[:, 2 * ff :] = flat_tn(full, at, hid).astype(BF)
            rows = pl.ds(number * step, step)
            sums.append(
                [
                    loads.start(held.at[:, pl.ds(0, 2 * ff)], gu_sums.at[rows]),
                    loads.start(held.at[:, pl.ds(2 * ff, ff)], d_sums.at[rows]),
                ]
            )

    net2 = run_scatter(
        here, parts, total, (from_c, via_x, via_y, from_x, from_y), (send2, recv2), beside=beside
    )
    da2 = total[...]
    m = mid[...]
    r2 = inverse_of(m)
    n2 = m * r2
    gain_out[...] = jnp.sum(da2 * n2, axis=0, keepdims=True)
    dmid = e[...].astype(F32) + norm_back(da2, n2, r2, gain[1:2, :])
    dmid_out[...] = dmid
    full2[own] = dmid.astype(BF)
    wa_load.wait()
    saves = []

    def on_second(r):
        saves.append(loads.start(full2.at[r], dat_out.at[r]))
        dob_out[r] = dot_nn(full2[r], wa[:, QKV:PACK]).astype(BF)

    net3 = run_gather(here, full2, (send3, recv3), on_second)
    for net in (net1, net2, net3):
        net.drain()
    for save in saves + sums[-2] + sums[-1]:
        save.wait()
    if swap is not None:
        swap.wait()


def mlp_back(e, mid, gain, gu, hid, a2, w1, w2, wa, moving=None):
    block, width = e.shape
    ff = hid.shape[2]
    cols = PACK - QKV
    step = math.gcd(width, 256)
    return plane_call(
        functools.partial(mlp_back_kernel, ff, step),
        "mlp_back",
        2 if moving is None else 9,
        [
            jax.ShapeDtypeStruct((block, width), F32),
            jax.ShapeDtypeStruct((1, width), F32),
            jax.ShapeDtypeStruct((8, block, width), BF),
            jax.ShapeDtypeStruct((8, block, cols), BF),
            jax.ShapeDtypeStruct((width, 2 * ff), BF),
            jax.ShapeDtypeStruct((width, ff), BF),
        ],
        [IN_VMEM, IN_VMEM, ANYWHERE, IN_VMEM, ANYWHERE, ANYWHERE],
        [IN_VMEM, IN_VMEM, IN_VMEM] + [ANYWHERE] * 6,
        [
            pltpu.VMEM((8, block, width), BF),
            pltpu.VMEM((8, block, width), BF),
            pltpu.VMEM((8, block, width), BF),
            pltpu.VMEM((8, block, width), BF),
            pltpu.VMEM((8, block, 2 * ff), BF),
            pltpu.VMEM((8, block, ff), BF),
            pltpu.VMEM((width, 3 * ff), BF),
            pltpu.VMEM(wa.shape, BF),
            pltpu.VMEM((block, width), F32),
            pltpu.VMEM((2, step, 3 * ff), BF),
        ]
        + gather_sems()
        + scatter_scratch(block, width)
        + gather_sems()
        + [pltpu.SemaphoreType.DMA((14 + 2 * (width // step),))],
        100,
        e, mid, gain, gu, hid, a2, w1, w2, wa,
        moving=moving,
    )


def attn_back_kernel(
    step, h, dmid, gain, gain2_grad, dq, dk, dv, cosine, sine, o, a1_hbm, dat_hbm, w_hbm, e_out, sums,
    parts, a1, dat, w, dqkv, gain_rows, total, from_c, via_x, via_y, from_x, from_y, send, recv, local,
):
    here = place()
    loads = Loads(local)
    w_load = loads.start(w_hbm, w)
    a1_load = loads.start(a1_hbm, a1)
    dat_load = loads.start(dat_hbm, dat)
    greet(here)
    w_load.wait()

    def fill(r):
        heads = [dq[r, :, n * LANES : (n + 1) * LANES].astype(F32) for n in range(2)]
        heads.append(turn(dk[r], cosine[r], -sine[r]))
        lanes = three_lanes([close_halves(head) for head in heads] + [dv[r]])
        for n in range(3):
            dqkv[r, :, n * LANES : (n + 1) * LANES] = lanes[n].astype(BF)
        parts[r] = dot_nt(dqkv[r], w[:, :QKV]).astype(BF)

    count = a1.shape[2] // step

    def beside(turn_number):
        if turn_number == 0:
            a1_load.wait()
            dat_load.wait()
        half = (count + 1) // 2
        for number in range(turn_number * half, min((turn_number + 1) * half, count)):
            at = slice(number * step, (number + 1) * step)
            sums[at, :QKV] = flat_tn(a1, at, dqkv).astype(BF)
            sums[at, QKV:GAIN_AT] = flat_tn(dat, at, o).astype(BF)

    net = run_scatter(
        here, parts, total, (from_c, via_x, via_y, from_x, from_y), (send, recv), fill, beside
    )
    da1 = total[...]
    x = h[...].astype(F32)
    r1 = inverse_of(x)
    n1 = x * r1
    e_out[...] = (dmid[...] + norm_back(da1, n1, r1, gain[0:1, :])).astype(BF)
    gain_rows[...] = jnp.zeros_like(gain_rows)
    first = GAIN_AT - PACK + LANES
    gain_rows[first : first + 1, :] = jnp.sum(da1 * n1, axis=0, keepdims=True)
    gain_rows[first + 1 : first + 2, :] = gain2_grad[...]
    columns = gain_rows[...].T
    last = sums[:, PACK - LANES :].astype(F32)
    sums[:, PACK - LANES :] = jnp.where(lane(last) < first, last, columns).astype(BF)
    net.drain()


def attn_back(h, dmid, gain, gain2_grad, dq, dk, dv, cosine, sine, o, a1, dat, w):
    block, width = h.shape
    step = math.gcd(width, 256)
    return plane_call(
        functools.partial(attn_back_kernel, step),
        "attn_back",
        3,
        [
            jax.ShapeDtypeStruct((block, width), BF),
            jax.ShapeDtypeStruct((width, PACK), BF),
        ],
        [IN_VMEM, IN_VMEM],
        [IN_VMEM] * 10 + [ANYWHERE] * 3,
        [
            pltpu.VMEM((8, block, width), BF),
            pltpu.VMEM((8, block, width), BF),
            pltpu.VMEM((8, block, width), BF),
            pltpu.VMEM(w.shape, BF),
            pltpu.VMEM((8, block, QKV), BF),
            pltpu.VMEM((LANES, width), F32),
            pltpu.VMEM((block, width), F32),
        ]
        + scatter_scratch(block, width)
        + [pltpu.SemaphoreType.DMA((3,))],
        36,
        h, dmid, gain, gain2_grad, dq, dk, dv, cosine, sine, o, a1, dat, w,
    )


def exchange_kernel(blocks, got, send_sem, recv_sem, local, swap=None):
    here = place()
    x, c, y = here
    swap = swap and Swap(here, *swap)
    masks = [(dx, dc, dy) for dx in range(2) for dc in range(2) for dy in range(2)][1:]
    peer = lambda mask: {"x": flip(x, mask[0]), "c": flip(c, mask[1]), "y": flip(y, mask[2])}
    own = rank_of(here, 0, 0, 0)
    mine = pltpu.make_async_copy(blocks.at[own], got.at[own], local)
    mine.start()
    barrier = pltpu.get_barrier_semaphore()
    for mask in masks:
        pl.semaphore_signal(barrier, inc=1, device_id=peer(mask), device_id_type=MESH)
    if swap is None:
        pl.semaphore_wait(barrier, 7)
    else:
        swap.greet(barrier)
        swap.met(barrier, 7)
        swap.start()

    def copy(n, src, dst):
        return pltpu.make_async_remote_copy(
            src_ref=src,
            dst_ref=dst,
            send_sem=send_sem.at[n],
            recv_sem=recv_sem.at[n],
            device_id=peer(masks[n]),
            device_id_type=MESH,
        )

    copies = [copy(n, blocks.at[rank_of(here, *mask)], got.at[own]) for n, mask in enumerate(masks)]
    for started in copies:
        started.start()
    mine.wait()
    for n, mask in enumerate(masks):
        where = got.at[rank_of(here, *mask)]
        copy(n, where, where).wait_recv()
    for started in copies:
        started.wait_send()
    if swap is not None:
        swap.wait()


def exchange(number, blocks, moving=None):
    return plane_call(
        exchange_kernel,
        "exchange",
        number,
        [jax.ShapeDtypeStruct(blocks.shape, BF)],
        [ANYWHERE],
        [ANYWHERE],
        [pltpu.SemaphoreType.DMA((7,)), pltpu.SemaphoreType.DMA((7,)), pltpu.SemaphoreType.DMA],
        blocks.size // 40000,
        blocks,
        moving=moving,
    )


def finish_kernel(ff, got, gate, up, down):
    gate[...] = got[0, :, :ff].astype(F32)
    up[...] = got[0, :, ff : 2 * ff].astype(F32)
    down[...] = got[0, :, 2 * ff :].astype(F32).T


def finish(got):
    ranks, rows, cols = got.shape
    ff = cols // 3
    return pl.pallas_call(
        functools.partial(finish_kernel, ff),
        grid=(ranks,),
        out_shape=[
            jax.ShapeDtypeStruct((rows, ranks * ff), F32),
            jax.ShapeDtypeStruct((rows, ranks * ff), F32),
            jax.ShapeDtypeStruct((ranks * ff, rows), F32),
        ],
        in_specs=[pl.BlockSpec((1, rows, cols), lambda i: (i, 0, 0))],
        out_specs=[
            pl.BlockSpec((rows, ff), lambda i: (0, i)),
            pl.BlockSpec((rows, ff), lambda i: (0, i)),
            pl.BlockSpec((ff, rows), lambda i: (i, 0)),
        ],
        compiler_params=pltpu.CompilerParams(vmem_limit_bytes=VMEM_LIMIT),
        name="finish",
    )(got)


LOWER=-1e30
def dot(a, b, dims):
    return lax.dot_general(a, b, (dims, ((), ())), preferred_element_type=F32)

def attend_kernel(scale2, bq, bk, bounds, length, q, k, v, qpos, out, lse):
    groups = q.shape[0]
    i = pl.program_id(0)
    rows = groups * bq
    qs = q[...].reshape(rows, LANES)
    pos = qpos[0]
    pos2 = jnp.concatenate([pos] * groups, axis=1)
    def step(masked, j, state):
        top, total, acc = state
        at = pl.ds(pl.multiple_of(j * bk, bk), bk)
        s = dot(k[at, :], qs, ((1,), (1,)))
        if masked:
            kp = j * bk + lax.broadcasted_iota(jnp.int32, (bk, 1), 0)
            ok = (kp <= pos2) & (kp < length[0])
            s = jnp.where(ok, s, LOWER)
        new = jnp.maximum(top, jnp.max(s, axis=0, keepdims=True) * scale2)
        p = jnp.exp2(s * scale2 - new)
        alpha = jnp.exp2(top - new)
        total = total * alpha + jnp.sum(p, axis=0, keepdims=True)
        acc = acc * alpha + dot(v[at, :], p.astype(BF), ((0,), (0,)))
        return new, total, acc
    state = (jnp.full((1, rows), LOWER, F32), jnp.zeros((1, rows), F32), jnp.zeros((LANES, rows), F32))
    full, end = bounds[0, i], bounds[1, i]
    state = lax.fori_loop(0, full, functools.partial(step, False), state)
    top, total, acc = lax.fori_loop(full, end, functools.partial(step, True), state)
    o = (acc / total).T
    first, second = o[:bq], pltpu.roll(o[bq:], HEAD_SIZE, 1)
    out[:, :LANES] = jnp.where(lane(first) < HEAD_SIZE, first, second).astype(BF)
    out[:, LANES:] = second[:, : OUT - LANES].astype(BF)
    lse[...] = (top + jnp.log2(total))[None]

def attend(q, k, v, qpos, bounds, length, bq, bk, scale2):
    groups, tokens, _ = q.shape
    n = tokens // bq
    out, lse = pl.pallas_call(
        functools.partial(attend_kernel, scale2, bq, bk),
        grid_spec=pltpu.PrefetchScalarGridSpec(
            num_scalar_prefetch=2, grid=(n,),
            in_specs=[
                pl.BlockSpec((groups, bq, LANES), lambda i, *_: (0, i, 0)),
                pl.BlockSpec(k.shape, lambda i, *_: (0, 0)),
                pl.BlockSpec(v.shape, lambda i, *_: (0, 0)),
                pl.BlockSpec((1, 1, bq), lambda i, *_: (i, 0, 0)),
            ],
            out_specs=[
                pl.BlockSpec((bq, OUT), lambda i, *_: (i, 0)),
                pl.BlockSpec((1, 1, groups * bq), lambda i, *_: (i, 0, 0)),
            ]),
        out_shape=[jax.ShapeDtypeStruct((tokens, OUT), BF), jax.ShapeDtypeStruct((n, 1, groups * bq), F32)],
        compiler_params=pltpu.CompilerParams(vmem_limit_bytes=VMEM_LIMIT),
        name="attend",
        cost_estimate=pl.CostEstimate(flops=0, bytes_accessed=45000000, transcendentals=0),
    )(bounds, length, q, k, v, qpos)
    return out, lse

def back_kernel(scale, scale2, bq, bk, bounds, length, q, k, v, qpos, o, do, lse, cosine, sine, dq, dk, dv):
    groups = q.shape[0]
    i = pl.program_id(0)
    @pl.when(i == 0)
    def _():
        dk[...] = jnp.zeros_like(dk)
        dv[...] = jnp.zeros_like(dv)
    qs = q[...].reshape(groups * bq, LANES)
    do0, do1 = do[:, :LANES].astype(F32), do[:, LANES : 2 * LANES].astype(F32)
    at = lane(do0)
    do1 = pltpu.roll(jnp.where(at >= HEAD_SIZE, do0, do1), LANES - HEAD_SIZE, 1)
    wide = jnp.concatenate([jnp.where(at < HEAD_SIZE, do0, 0.0), jnp.where(at < HEAD_SIZE, do1, 0.0)], axis=0)
    dos = wide.astype(BF)
    o0 = o[:, :LANES].astype(F32)
    o1 = jnp.concatenate([o[:, LANES:].astype(F32), jnp.zeros((bq, 2 * LANES - OUT), F32)], axis=1)
    o1 = pltpu.roll(jnp.where(at >= HEAD_SIZE, o0, o1), LANES - HEAD_SIZE, 1)
    delta = jnp.sum(wide * jnp.concatenate([o0, o1], axis=0), axis=1, keepdims=True).reshape(1, groups * bq)
    lse_row = lse[0]
    pos = qpos[0]
    pos2 = jnp.concatenate([pos] * groups, axis=1)
    def step(masked, j, acc):
        at = pl.ds(pl.multiple_of(j * bk, bk), bk)
        kb, vb = k[at, :], v[at, :]
        s = dot(kb, qs, ((1,), (1,)))
        p = jnp.exp2(s * scale2 - lse_row)
        if masked:
            kp = j * bk + lax.broadcasted_iota(jnp.int32, (bk, 1), 0)
            ok = (kp <= pos2) & (kp < length[0])
            p = jnp.where(ok, p, 0.0)
        dp = dot(vb, dos, ((1,), (1,)))
        ds = (p * (dp - delta)).astype(BF)
        dv[at, :] += dot(p.astype(BF), dos, ((1,), (0,)))
        dk[at, :] += dot(ds, qs, ((1,), (0,))) * scale
        return acc + dot(ds, kb, ((0,), (0,)))
    full, end = bounds[0, i], bounds[1, i]
    acc = jnp.zeros((groups * bq, LANES), F32)
    acc = lax.fori_loop(0, full, functools.partial(step, False), acc)
    acc = lax.fori_loop(full, end, functools.partial(step, True), acc) * scale
    for g in range(groups):
        dq[:, g * LANES:(g + 1) * LANES] = turn(acc[g * bq:(g + 1) * bq], cosine[...], -sine[...]).astype(BF)

def attend_back(q, k, v, qpos_row, o, do, lse, cosine, sine, bounds, length, bq, bk, scale, scale2):
    groups, tokens, _ = q.shape
    n = tokens // bq
    wide = pl.BlockSpec((bq, groups * LANES), lambda i, *_: (i, 0))
    narrow = pl.BlockSpec((bq, OUT), lambda i, *_: (i, 0))
    return pl.pallas_call(
        functools.partial(back_kernel, scale, scale2, bq, bk),
        grid_spec=pltpu.PrefetchScalarGridSpec(
            num_scalar_prefetch=2, grid=(n,),
            in_specs=[
                pl.BlockSpec((groups, bq, LANES), lambda i, *_: (0, i, 0)),
                pl.BlockSpec(k.shape, lambda i, *_: (0, 0)),
                pl.BlockSpec(v.shape, lambda i, *_: (0, 0)),
                pl.BlockSpec((1, 1, bq), lambda i, *_: (i, 0, 0)),
                narrow, wide,
                pl.BlockSpec((1, 1, groups * bq), lambda i, *_: (i, 0, 0)),
                pl.BlockSpec((bq, LANES), lambda i, *_: (i, 0)),
                pl.BlockSpec((bq, LANES), lambda i, *_: (i, 0)),
            ],
            out_specs=[wide, pl.BlockSpec(k.shape, lambda i, *_: (0, 0)), pl.BlockSpec(k.shape, lambda i, *_: (0, 0))]),
        out_shape=[jax.ShapeDtypeStruct((tokens, groups * LANES), BF), jax.ShapeDtypeStruct(k.shape, F32), jax.ShapeDtypeStruct(k.shape, F32)],
        compiler_params=pltpu.CompilerParams(vmem_limit_bytes=VMEM_LIMIT),
        name="attend_back",
        cost_estimate=pl.CostEstimate(flops=0, bytes_accessed=65000000, transcendentals=0),
    )(bounds, length, q, k, v, qpos_row, o, do, lse, cosine, sine)

def bounds_of(positions, length, bq, bk):
    p = positions.reshape(-1, bq)
    lo = jnp.minimum(jnp.min(p, axis=1) + 1, length) // bk
    hi = -(-jnp.minimum(jnp.max(p, axis=1) + 1, length) // bk)
    return jnp.stack([lo, hi]).astype(jnp.int32)


PLANE = ("x", "c", "y")

def together(*arrays):
    return lax.optimization_barrier(arrays)


def body(
    inputs,
    lengths,
    cotangent,
    attn_gain,
    w_query,
    key_projection,
    value_projection,
    w_out,
    mlp_gain,
    w_gate,
    w_up,
    w_down,
):
    sections = lax.axis_size("x") * lax.axis_size("c")
    planes = lax.axis_size("z")
    halves = lax.axis_size("y")
    extra = lax.axis_size("e")
    ranks = sections * halves
    layers = sections
    block = inputs.shape[1]
    width = inputs.shape[2]
    rows = w_query.shape[1]
    tokens = block * ranks
    all_tokens = tokens * extra
    head_group = QUERY_HEADS // KEY_VALUE_HEADS
    q_cols = head_group * HEAD_SIZE
    kv_cols = HEAD_SIZE
    ff_cols = FF // ranks
    scale = 1.0 / math.sqrt(HEAD_SIZE)
    scale2 = scale * math.log2(math.e)

    def by_rank(matrix):
        return matrix.reshape(rows, ranks, -1)

    attn_pack = jnp.concatenate(
        [
            by_rank(w_query[0]),
            by_rank(key_projection[0]),
            by_rank(value_projection[0]),
            by_rank(w_out[0].T),
            jnp.broadcast_to(jnp.stack([attn_gain[0], mlp_gain[0]], axis=1)[:, None, :], (rows, ranks, 2)),
            jnp.zeros((rows, ranks, PACK - GAIN_AT - 2), F32),
        ],
        axis=2,
    )
    mlp_pack = jnp.concatenate(
        [by_rank(w_gate[0]), by_rank(w_up[0]), by_rank(w_down[0].T)], axis=2
    )

    def by_layer(got):
        return got.reshape(layers, halves, rows, -1)

    def ready(pack):
        return jnp.swapaxes(pack.astype(BF), 0, 1)

    def whole(part):
        if extra > 1:
            part = lax.all_gather(part, "e", axis=1, tiled=False)
        return lax.all_gather(part.reshape(-1, part.shape[-1]), "z", axis=0, tiled=True)

    def reduce_rows(sums):
        mine = lax.psum_scatter(sums, "z", scatter_dimension=0, tiled=True)
        mine = mine.reshape(halves, extra, rows, -1)
        if extra > 1:
            return lax.psum_scatter(mine, "e", scatter_dimension=1, tiled=False)
        return mine[:, 0]

    cut = 3 * ff_cols * 7 // 12 // LANES * LANES
    mlp_blocks = ready(mlp_pack)
    (attn_got,) = exchange(4, ready(attn_pack))
    first_blocks, attn_got = together(mlp_blocks[..., :cut], attn_got)
    (first_got,) = exchange(5, first_blocks)
    second_blocks, first_got = together(mlp_blocks[..., cut:], first_got)
    second_got, hidden_state = exchange(6, second_blocks, inputs[0])
    attn_parts, first_parts, second_parts = by_layer(attn_got), by_layer(first_got), by_layer(second_got)

    rank = (lax.axis_index("x") * lax.axis_size("c") + lax.axis_index("c")) * halves + lax.axis_index("y")
    spot = lax.axis_index("e")
    length = lengths[lax.axis_index("z")]

    block_start = (jnp.arange(ranks) * extra + spot) * block
    positions = (block_start[:, None] + jnp.arange(block)[None, :]).reshape(tokens)
    exponents = 2.0 * jnp.arange(HEAD_SIZE // 2).astype(F32) / HEAD_SIZE
    angles = positions.astype(F32)[:, None] * (THETA ** (-exponents))[None, :]
    table = lambda values: jnp.pad(values, ((0, 0), (0, LANES // 2 - HALF)))
    cosine = jnp.concatenate([table(jnp.cos(angles))] * 2, axis=1)
    sine = jnp.concatenate([table(-jnp.sin(angles)), table(jnp.sin(angles))], axis=1)
    bq = math.gcd(tokens, 512)
    bk = math.gcd(all_tokens, 512)
    bounds = bounds_of(positions, length, bq, bk)
    length1 = length.reshape(1)
    query_rows = positions.astype(jnp.int32).reshape(-1, 1, bq)

    def all_keys(array):
        if extra == 1:
            return array
        stacked = lax.all_gather(array.reshape(ranks, block, -1), "e", axis=1, tiled=False)
        return stacked.reshape(all_tokens, -1)

    def own_keys(array):
        if extra == 1:
            return array
        stacked = array.astype(BF).reshape(ranks, extra, block, -1)
        return lax.psum_scatter(stacked, "e", scatter_dimension=1, tiled=False).reshape(tokens, -1).astype(F32)

    cosine3 = cosine.reshape(ranks, block, LANES)
    sine3 = sine.reshape(ranks, block, LANES)

    def flat(array):
        return array.reshape(tokens, array.shape[-1])

    saved = []
    attn_w, w_1 = whole(attn_parts[0]), whole(first_parts[0])
    w_2 = whole(second_parts[0])
    for layer in range(layers):
        a1, q, k, v, gain = attn_in(hidden_state, attn_w, cosine3, sine3)
        q, k, v = q.reshape(head_group, tokens, LANES), all_keys(flat(k)), all_keys(flat(v))
        o, log_total = attend(q, k, v, query_rows, bounds, length1, bq, bk, scale2)
        if layer + 1 < layers:
            o, attn_part, first_part = together(o, attn_parts[layer + 1], first_parts[layer + 1])
            next_attn, next_1 = whole(attn_part), whole(first_part)
        mid, a2, gu, hid, after_mlp, *moved = mlp(
            hidden_state, o.reshape(ranks, block, -1), gain, attn_w, w_1, w_2,
            cotangent[0] if layer + 1 == layers else None,
        )
        saved.append((hidden_state, a1, q, k, v, o, log_total, mid, a2, gu, hid, attn_w, w_1, w_2, gain))
        hidden_state = after_mlp
        if layer + 1 < layers:
            hidden_state, attn_w, w_1, second_part = together(hidden_state, next_attn, next_1, second_parts[layer + 1])
            w_2 = whole(second_part)
    output = hidden_state

    my_positions = (rank * extra + spot) * block + jnp.arange(block)
    (e,) = moved
    e = jnp.where((my_positions < length)[:, None], e, jnp.zeros_like(e))
    attn_grads = [None] * layers
    gu_grads = [None] * layers
    d_grads = [None] * layers
    for layer in reversed(range(layers)):
        (h, a1, q, k, v, o, log_total, mid, a2, gu, hid, attn_w, w_1, w_2, gain) = saved[layer]
        dmid, gain2, dat, dob, gu_sums, d_sums, *moved = mlp_back(
            e, mid, gain, gu, hid, a2, w_1, w_2, attn_w, output if layer + 1 == layers else None
        )
        if moved:
            (output,) = moved
        if layer + 1 < layers:
            dob, gu_sums, d_sums, attn_grads[layer + 1], d_grads[layer + 1] = together(
                dob, gu_sums, d_sums, attn_grads[layer + 1], d_grads[layer + 1]
            )
        gu_grads[layer] = reduce_rows(gu_sums)
        if layer == 0:
            d_grads[layer] = reduce_rows(d_sums)
        dq, dk, dv = attend_back(
            q, k, v, query_rows, o, flat(dob), log_total, cosine, sine, bounds, length1, bq, bk, scale, scale2
        )
        dk, dv = own_keys(dk), own_keys(dv)
        e, attn_sums = attn_back(
            h, dmid, gain, gain2, *(array.reshape(ranks, block, -1) for array in (dq, dk, dv)), cosine3, sine3,
            o.reshape(ranks, block, -1), a1, dat, attn_w,
        )
        if layer > 0:
            e, attn_sums, d_sums, gu_grads[layer] = together(e, attn_sums, d_sums, gu_grads[layer])
            d_grads[layer] = reduce_rows(d_sums)
        else:
            e, attn_sums, gu_grads[layer], d_grads[layer] = together(e, attn_sums, gu_grads[layer], d_grads[layer])
        attn_grads[layer] = reduce_rows(attn_sums)

    def by_place(grads):
        return jnp.stack(grads).reshape(ranks, rows, -1)

    mlp_blocks = by_place([jnp.concatenate(pair, axis=2) for pair in zip(gu_grads, d_grads)])
    mlp_home, input_grad = exchange(7, mlp_blocks, e)
    attn_blocks, mlp_home = together(by_place(attn_grads), mlp_home)
    (attn_home,) = exchange(10, attn_blocks)
    grad_gate, grad_up, grad_down = finish(mlp_home)
    attn_home = attn_home.astype(F32)
    gain_sums = jnp.sum(attn_home[:, :, GAIN_AT : GAIN_AT + 2], axis=0)

    def columns(start, count):
        return jnp.swapaxes(attn_home[:, :, start : start + count], 0, 1).reshape(rows, ranks * count)

    return (
        output[None],
        input_grad[None],
        gain_sums[:, 0][None],
        columns(0, q_cols)[None],
        columns(q_cols, kv_cols)[None],
        columns(q_cols + kv_cols, kv_cols)[None],
        jnp.swapaxes(attn_home[:, :, QKV:GAIN_AT], 1, 2).reshape(ranks * OUT, rows)[None],
        gain_sums[:, 1][None],
        grad_gate[None],
        grad_up[None],
        grad_down[None],
    )


def solution(mesh):
    section, seq = mesh.devices.shape
    halves = KEY_VALUE_HEADS // section
    extra = seq // (section * halves)
    fine = Mesh(
        mesh.devices.reshape(section // 2, 2, section, halves, extra), ("x", "c", "z", "y", "e")
    )
    sec, sq = ("x", "c"), ("z", "y", "e")
    rows3 = P(sec, sq, None)
    cols3 = P(sec, None, sq)
    in_specs = (rows3, P(), rows3, P(sec, sq), rows3, rows3, rows3, cols3, P(sec, sq), rows3, rows3, cols3)
    out_specs = (rows3, rows3, P(sec, sq), rows3, rows3, rows3, cols3, P(sec, sq), rows3, rows3, cols3)
    return jax.shard_map(body, mesh=fine, in_specs=in_specs, out_specs=out_specs, check_vma=False)
```

```python
import functools
import math

import jax
import jax.numpy as jnp
from jax import lax
from jax.experimental import pallas as pl
from jax.experimental.pallas import tpu as pltpu
from jax.sharding import Mesh
from jax.sharding import PartitionSpec as P

QUERY_HEADS = 16
KEY_VALUE_HEADS = 8
HEAD_SIZE = 96
FF = 4096

EPS = 1e-05
THETA = 100000.0
LOWER_LIMIT = -1e30

BF = jnp.bfloat16
F32 = jnp.float32

LANES = 128
HALF = HEAD_SIZE // 2
VMEM_LIMIT = 56 * 1024 * 1024


def dot(a, b, dims):
    return lax.dot_general(a, b, (dims, ((), ())), preferred_element_type=F32)


def dot_nn(a, b):
    return dot(a, b, ((1,), (0,)))


def dot_nt(a, b):
    return dot(a, b, ((1,), (1,)))


def dot_tn(a, b):
    return dot(a, b, ((0,), (0,)))


MESH = pl.DeviceIdType.MESH

OWN, X, Y, D = (0, 0), (1, 0), (0, 1), (1, 1)


def place():
    return lax.axis_index("x"), lax.axis_index("c"), lax.axis_index("y")


def xor(a, b):
    return a + b - 2 * a * b


def token_place():
    x, c, y = place()
    return xor(x, lax.rem(lax.axis_index("z"), 2)), c, y


def flip(index, by):
    return 1 - index if by else index


def rank_of(here, dx, dc, dy):
    x, c, y = here
    return (flip(x, dx) * 2 + flip(c, dc)) * 2 + flip(y, dy)


class Swap:
    def __init__(self, homeward, moving, moved, sem):
        x, c, _ = place()
        z = lax.axis_index("z")
        low = lax.rem(z, 2)
        out = {"x": xor(z // 2, c), "c": low, "z": x * 2 + c}
        back = {"x": z // 2, "c": low, "z": 2 * xor(x, low) + c}
        target, self.source = (back, out) if homeward else (out, back)
        self.away = (target["x"] != x) | (target["c"] != c) | (target["z"] != z)
        self.remote = pltpu.make_async_remote_copy(
            src_ref=moving,
            dst_ref=moved,
            send_sem=sem.at[0],
            recv_sem=sem.at[1],
            device_id=target,
            device_id_type=MESH,
        )
        self.local = pltpu.make_async_copy(moving, moved, sem.at[2])

    def greet(self, barrier):
        @pl.when(self.away)
        def _():
            pl.semaphore_signal(barrier, inc=1, device_id=self.source, device_id_type=MESH)

    def either(self, remote, local):
        pl.when(self.away)(remote)
        pl.when(jnp.logical_not(self.away))(local)

    def start(self):
        self.either(lambda: self.remote.start(), lambda: self.local.start())

    def met(self, barrier, count):
        self.either(lambda: pl.semaphore_wait(barrier, count + 1), lambda: pl.semaphore_wait(barrier, count))

    def wait(self):
        self.either(lambda: self.remote.wait(), lambda: self.local.wait())


def with_swap(kernel, inputs, outputs):
    def wrapped(*refs):
        last = inputs + 1 + outputs
        kernel(
            *refs[:inputs],
            *refs[inputs + 1 : last],
            *refs[last + 1 : -1],
            swap=(refs[inputs], refs[last], refs[-1]),
        )

    return wrapped


def greet(swap=None):
    x, c, y = place()
    barrier = pltpu.get_barrier_semaphore()
    for peer in ({"x": 1 - x}, {"c": 1 - c}, {"y": 1 - y}):
        pl.semaphore_signal(barrier, inc=1, device_id=peer, device_id_type=MESH)
    if swap is None:
        pl.semaphore_wait(barrier, 3)
    else:
        swap.greet(barrier)
        swap.met(barrier, 3)
        swap.start()


class Sender:
    def __init__(self, send_sem, recv_sem):
        x, c, y = place()
        self.peers = {"x": {"x": 1 - x}, "c": {"c": 1 - c}, "y": {"y": 1 - y}}
        self.send_sem, self.recv_sem = send_sem, recv_sem
        self.sent = []

    def copy(self, src, dst, index, to, number):
        return pltpu.make_async_remote_copy(
            src_ref=src,
            dst_ref=dst,
            send_sem=self.send_sem.at[number],
            recv_sem=self.recv_sem.at[index],
            device_id=self.peers[to],
            device_id_type=MESH,
        )

    def send(self, src, dst, index, to):
        started = self.copy(src, dst, index, to, len(self.sent))
        started.start()
        self.sent.append(started)

    def arrived(self, where, index):
        self.copy(where, where, index, "c", 0).wait_recv()

    def drain(self):
        for started in self.sent:
            started.wait_send()


def run_gather(here, full, sems, on_block, before_last=None):
    block = full.shape[1]
    piece = block // 4
    net = Sender(*sems)

    def index(role, chunk):
        return (role[0] * 4 + role[1] * 2 + role[2]) * 4 + chunk

    def slot(role, chunk, count=1):
        return full.at[rank_of(here, *role), pl.ds(chunk * piece, piece * count)]

    def send(role, chunk, to, as_role, count=1):
        where = slot(role, chunk, count)
        net.send(where, where, index(as_role, chunk), to)

    def arrived(role, chunk, count=1):
        net.arrived(slot(role, chunk, count), index(role, chunk))

    def whole(role):
        for chunk in range(4):
            arrived(role, chunk)

    def done(role):
        on_block(rank_of(here, *role))

    own, at_x, at_y, at_d, at_c = (0, 0, 0), (1, 0, 0), (0, 0, 1), (1, 0, 1), (0, 1, 0)
    xc, yc, dc = (1, 1, 0), (0, 1, 1), (1, 1, 1)
    for cx, cy in ((2, 0), (3, 1), (0, 2), (1, 3)):
        send(own, cx, "x", at_x)
        send(own, cy, "y", at_y)
    send(own, 0, "c", at_c, 4)

    def pass_on(cx, cy):
        arrived(at_x, cx)
        if cx >= 2:
            send(at_x, cx, "y", at_d)
        send(at_x, cx, "c", xc)
        arrived(at_y, cy)
        if cy < 2:
            send(at_y, cy, "x", at_d)
        send(at_y, cy, "c", yc)

    def pass_last(chunks):
        for chunk in chunks:
            arrived(at_d, chunk)
            send(at_d, chunk, "c", dc)

    done(own)
    pass_on(2, 0)
    arrived(at_c, 0, 4)
    done(at_c)
    pass_on(3, 1)
    pass_on(0, 2)
    pass_on(1, 3)
    done(at_x)
    done(at_y)
    pass_last((0, 2))
    whole(xc)
    done(xc)
    whole(yc)
    done(yc)
    if before_last is not None:
        before_last()
    pass_last((1, 3))
    done(at_d)
    whole(dc)
    done(dc)
    return net


class Scatter:
    order = (D, X, Y, OWN)

    def __init__(self, here, parts, total, bufs, sems, fill=None):
        self.here, self.parts, self.total, self.fill = here, parts, total, fill
        self.from_c, self.via_x, self.via_y, self.from_x, self.from_y = bufs
        half = parts.shape[1] // 2
        self.lower, self.upper = pl.ds(0, half), pl.ds(half, half)
        self.net = Sender(*sems)

    def rank(self, n, dc):
        return rank_of(self.here, self.order[n][0], dc, self.order[n][1])

    def make(self, r):
        if self.fill is not None:
            self.fill(r)

    def sibling(self, n):
        r = self.rank(n, 1)
        self.make(r)
        self.net.send(self.parts.at[r], self.from_c.at[n], n, "c")

    def add(self, n, where, more):
        r = self.rank(n, 0)
        self.parts[r, where] = (self.parts[r, where].astype(F32) + more.astype(F32)).astype(BF)

    def mine(self, n, where):
        return self.parts.at[self.rank(n, 0), where]

    def combine(self, n):
        self.make(self.rank(n, 0))
        self.net.arrived(self.from_c.at[n], n)
        if n < 3:
            self.add(n, pl.ds(0, self.parts.shape[1]), self.from_c[n])

    def to_diagonal(self):
        self.combine(0)
        self.net.send(self.mine(0, self.upper), self.via_x, 4, "x")
        self.net.send(self.mine(0, self.lower), self.via_y, 5, "y")

    def to_neighbours(self):
        self.combine(1)
        self.net.send(self.mine(1, self.upper), self.from_x.at[self.upper], 6, "x")
        self.combine(2)
        self.net.send(self.mine(2, self.lower), self.from_y.at[self.lower], 7, "y")

    def early(self):
        for n in (1, 2, 3):
            self.sibling(n)
        self.to_neighbours()

    def run(self, beside=None, early_done=False):
        net, total, lower, upper = self.net, self.total, self.lower, self.upper
        self.sibling(0)
        if early_done:
            self.to_diagonal()
        else:
            self.sibling(1)
            self.sibling(2)
            self.to_diagonal()
            self.to_neighbours()
            self.sibling(3)
        self.combine(3)
        total[...] = self.parts[self.rank(3, 0)].astype(F32) + self.from_c[3].astype(F32)
        if beside is not None:
            beside(0)
        net.arrived(self.via_y, 5)
        self.add(1, lower, self.via_y[...])
        net.send(self.mine(1, lower), self.from_x.at[lower], 8, "x")
        net.arrived(self.via_x, 4)
        self.add(2, upper, self.via_x[...])
        net.send(self.mine(2, upper), self.from_y.at[upper], 9, "y")
        if beside is not None:
            beside(1)
        net.arrived(self.from_x.at[upper], 6)
        net.arrived(self.from_y.at[lower], 7)
        total[upper] += self.from_x[upper].astype(F32)
        total[lower] += self.from_y[lower].astype(F32)
        net.arrived(self.from_x.at[lower], 8)
        net.arrived(self.from_y.at[upper], 9)
        total[lower] += self.from_x[lower].astype(F32)
        total[upper] += self.from_y[upper].astype(F32)
        return net


def gather_sems():
    return [pltpu.SemaphoreType.DMA((32,)), pltpu.SemaphoreType.DMA((32,))]


def scatter_scratch(block, width):
    half = block // 2
    return [
        pltpu.VMEM((4, block, width), BF),
        pltpu.VMEM((half, width), BF),
        pltpu.VMEM((half, width), BF),
        pltpu.VMEM((block, width), BF),
        pltpu.VMEM((block, width), BF),
        pltpu.SemaphoreType.DMA((10,)),
        pltpu.SemaphoreType.DMA((10,)),
    ]


class Loads:
    def __init__(self, sem):
        self.sem = sem
        self.count = 0

    def start(self, src, dst):
        copy = pltpu.make_async_copy(src, dst, self.sem.at[self.count])
        self.count += 1
        copy.start()
        return copy


def inverse_of(x):
    return lax.rsqrt(jnp.mean(x * x, axis=-1, keepdims=True) + EPS)


def lane(x):
    return lax.broadcasted_iota(jnp.int32, x.shape, 1)


def turn(head, cosine, sine):
    return head * cosine + pltpu.roll(head, LANES // 2, 1) * sine


def open_halves(head):
    return jnp.where(lane(head) < LANES // 2, head, pltpu.roll(head, LANES // 2 - HALF, 1))


def close_halves(head):
    low = lane(head) < LANES // 2
    return jnp.where(low, head, 0.0) + pltpu.roll(jnp.where(low, 0.0, head), LANES // 2 + HALF, 1)


def four_heads(a, b, c):
    at = lane(a)
    return (
        a,
        pltpu.roll(jnp.where(at >= 96, a, b), 32, 1),
        pltpu.roll(jnp.where(at >= 64, b, c), 64, 1),
        pltpu.roll(c, 96, 1),
    )


def three_lanes(heads):
    at = lane(heads[0])
    b, c, d = pltpu.roll(heads[1], 96, 1), pltpu.roll(heads[2], 64, 1), pltpu.roll(heads[3], 32, 1)
    return jnp.where(at < 96, heads[0], b), jnp.where(at < 64, b, c), jnp.where(at < 32, c, d)


def plane_call(kernel, name, number, out_shape, out_specs, in_specs, scratch, time_us, *operands, moving=None):
    if moving is not None:
        kernel = with_swap(kernel, len(in_specs), len(out_specs))
        out_shape = out_shape + [jax.ShapeDtypeStruct(moving.shape, moving.dtype)]
        in_specs, out_specs = in_specs + [ANYWHERE], out_specs + [ANYWHERE]
        scratch = scratch + [pltpu.SemaphoreType.DMA((3,))]
        operands = operands + (moving,)
    return pl.pallas_call(
        kernel,
        out_shape=out_shape,
        in_specs=in_specs,
        out_specs=out_specs,
        scratch_shapes=scratch,
        compiler_params=pltpu.CompilerParams(
            collective_id=number, has_side_effects=True, vmem_limit_bytes=VMEM_LIMIT
        ),
        cost_estimate=pl.CostEstimate(flops=0, bytes_accessed=time_us * 3000000, transcendentals=0),
        name=name,
    )(*operands)


ANYWHERE = pl.BlockSpec(memory_space=pl.ANY)
IN_VMEM = pl.BlockSpec(memory_space=pltpu.VMEM)
QKV = 4 * HEAD_SIZE
OUT = 2 * HEAD_SIZE
GAIN_AT = QKV + OUT
PACK = -(-(GAIN_AT + 2) // LANES) * LANES


def attn_in_kernel(h, w_hbm, cosine, sine, a1_out, q_out, k_out, v_out, gain_out, full, w, send, recv, local):
    here = token_place()
    loads = Loads(local)
    w_load = loads.start(w_hbm, w)
    x = h[...].astype(F32)
    n1 = x * inverse_of(x)
    w_load.wait()
    rows = w[:, PACK - LANES :].astype(F32).T
    gain_out[...] = rows[GAIN_AT - PACK + LANES : GAIN_AT - PACK + LANES + 2]
    full[rank_of(here, 0, 0, 0)] = (n1 * gain_out[0:1, :]).astype(BF)
    greet()
    saves = []

    def on_block(r):
        saves.append(loads.start(full.at[r], a1_out.at[r]))
        qkv = dot_nn(full[r], w[:, :QKV])
        heads = four_heads(*(qkv[:, n * LANES : (n + 1) * LANES] for n in range(3)))
        cos, sin = cosine[r], sine[r]
        for n in range(2):
            q_out[n, r] = turn(open_halves(heads[n]), cos, sin).astype(BF)
        k_out[r] = turn(open_halves(heads[2]), cos, sin).astype(BF)
        v_out[r] = jnp.where(lane(heads[3]) < HEAD_SIZE, heads[3], 0.0).astype(BF)

    net = run_gather(here, full, (send, recv), on_block)
    net.drain()
    for save in saves:
        save.wait()


def attn_in(h, w, cosine, sine):
    block, width = h.shape
    return plane_call(
        attn_in_kernel,
        "attn_in",
        0,
        [
            jax.ShapeDtypeStruct((8, block, width), BF),
            jax.ShapeDtypeStruct((2, 8, block, LANES), BF),
            jax.ShapeDtypeStruct((8, block, LANES), BF),
            jax.ShapeDtypeStruct((8, block, LANES), BF),
            jax.ShapeDtypeStruct((2, width), F32),
        ],
        [ANYWHERE, IN_VMEM, IN_VMEM, IN_VMEM, IN_VMEM],
        [IN_VMEM, ANYWHERE, IN_VMEM, IN_VMEM],
        [pltpu.VMEM((8, block, width), BF), pltpu.VMEM(w.shape, BF)]
        + gather_sems()
        + [pltpu.SemaphoreType.DMA((9,))],
        34,
        h, w, cosine, sine,
    )


def mlp_kernel(
    ff, homeward, h, o, gain, wa_hbm, w1_hbm, w2_hbm, mid_out, a2_out, gu_out, hid_out, next_out,
    full, parts, gu, hid, wa, wm, total,
    from_c, via_x, via_y, from_x, from_y, send1, recv1, send2, recv2,
    from_c3, via_x3, via_y3, from_x3, from_y3, send3, recv3, local, swap=None,
):
    here = token_place()
    swap = swap and Swap(homeward, *swap)
    loads = Loads(local)
    wa_load = loads.start(wa_hbm, wa)
    split = w1_hbm.shape[1]
    w1_load = loads.start(w1_hbm, wm.at[:, pl.ds(0, split)])
    w2_load = loads.start(w2_hbm, wm.at[:, pl.ds(split, 3 * ff - split)])
    greet(swap)
    wa_load.wait()

    def fill(r):
        parts[r] = dot_nt(o[r], wa[:, QKV:GAIN_AT]).astype(BF)

    bufs = (from_c, via_x, via_y, from_x, from_y)
    net1 = Scatter(here, parts, total, bufs, (send1, recv1), fill).run()
    mid = h[...].astype(F32) + total[...]
    mid_out[...] = mid
    full[rank_of(here, 0, 0, 0)] = (mid * inverse_of(mid) * gain[1:2, :]).astype(BF)
    net1.drain()
    saves = []

    def on_block(r):
        if not saves:
            w1_load.wait()
            w2_load.wait()
        saves.append(loads.start(full.at[r], a2_out.at[r]))
        a2 = full[r]
        g = dot_nn(a2, wm[:, :ff])
        u = dot_nn(a2, wm[:, ff : 2 * ff])
        gu[r, :, :ff] = g.astype(BF)
        gu[r, :, ff:] = u.astype(BF)
        low = (g * (1.0 / (1.0 + jnp.exp(-g))) * u).astype(BF)
        hid[r] = low
        saves.append(loads.start(gu.at[r], gu_out.at[r]))
        saves.append(loads.start(hid.at[r], hid_out.at[r]))
        parts[r] = dot_nt(low, wm[:, 2 * ff :]).astype(BF)

    bufs3 = (from_c3, via_x3, via_y3, from_x3, from_y3)
    scatter = Scatter(here, parts, total, bufs3, (send3, recv3))
    net2 = run_gather(here, full, (send2, recv2), on_block, scatter.early)
    net3 = scatter.run(early_done=True)
    next_out[...] = (mid_out[...] + total[...]).astype(BF)
    net2.drain()
    net3.drain()
    for save in saves:
        save.wait()
    if swap is not None:
        swap.wait()


def mlp(h, o, gain, wa, w1, w2, moving=None):
    block, width = h.shape
    ff = (w1.shape[1] + w2.shape[1]) // 3
    return plane_call(
        functools.partial(mlp_kernel, ff, False),
        "mlp",
        1 if moving is None else 8,
        [
            jax.ShapeDtypeStruct((block, width), F32),
            jax.ShapeDtypeStruct((8, block, width), BF),
            jax.ShapeDtypeStruct((8, block, 2 * ff), BF),
            jax.ShapeDtypeStruct((8, block, ff), BF),
            jax.ShapeDtypeStruct((block, width), BF),
        ],
        [IN_VMEM, ANYWHERE, ANYWHERE, ANYWHERE, IN_VMEM],
        [IN_VMEM, IN_VMEM, IN_VMEM, ANYWHERE, ANYWHERE, ANYWHERE],
        [
            pltpu.VMEM((8, block, width), BF),
            pltpu.VMEM((8, block, width), BF),
            pltpu.VMEM((8, block, 2 * ff), BF),
            pltpu.VMEM((8, block, ff), BF),
            pltpu.VMEM(wa.shape, BF),
            pltpu.VMEM((width, 3 * ff), BF),
            pltpu.VMEM((block, width), F32),
        ]
        + scatter_scratch(block, width)
        + gather_sems()
        + scatter_scratch(block, width)
        + [pltpu.SemaphoreType.DMA((27,))],
        96,
        h, o, gain, wa, w1, w2,
        moving=moving,
    )


def norm_back(upstream, normed, inverse, gain_row):
    scaled = upstream * gain_row
    return inverse * (scaled - normed * jnp.mean(scaled * normed, axis=-1, keepdims=True))


def flat_tn(a, cols, b):
    total = dot_tn(a[0, :, cols], b[0])
    for n in range(1, a.shape[0]):
        total = total + dot_tn(a[n, :, cols], b[n])
    return total


def mlp_back_kernel(
    ff, step, homeward, e, mid, gain, gu_hbm, hid_hbm, a2_hbm, w1_hbm, w2_hbm, wa_hbm, dmid_out, gain_out, dat_out, dob_out,
    gu_sums, d_sums, full, full2, parts, a2, gu, hid, wm, wa, total, stage, send1, recv1,
    from_c, via_x, via_y, from_x, from_y, send2, recv2, send3, recv3, local, swap=None, alone=False,
):
    here = token_place()
    swap = swap and Swap(homeward, *swap)
    loads = Loads(local)
    split = w1_hbm.shape[1]
    w2_load = loads.start(w2_hbm, wm.at[:, pl.ds(split, 3 * ff - split)])
    gu_load = loads.start(gu_hbm, gu)
    w1_load = loads.start(w1_hbm, wm.at[:, pl.ds(0, split)])
    wa_load = None if alone else loads.start(wa_hbm, wa)
    a2_load = loads.start(a2_hbm, a2)
    hid_load = loads.start(hid_hbm, hid)
    own = rank_of(here, 0, 0, 0)
    full[own] = e[...]
    greet(swap)
    w2_load.wait()
    gu_load.wait()
    w1_load.wait()

    def on_block(r):
        dhid = dot_nn(full[r], wm[:, 2 * ff :])
        g = gu[r, :, :ff].astype(F32)
        u = gu[r, :, ff:].astype(F32)
        sig = 1.0 / (1.0 + jnp.exp(-g))
        du = dhid * g * sig
        dg = dhid * u * sig * (1.0 + g * (1.0 - sig))
        gu[r, :, :ff] = dg.astype(BF)
        gu[r, :, ff:] = du.astype(BF)
        parts[r] = dot_nt(gu[r], wm[:, : 2 * ff]).astype(BF)

    scatter = Scatter(here, parts, total, (from_c, via_x, via_y, from_x, from_y), (send2, recv2))
    net1 = run_gather(here, full, (send1, recv1), on_block, scatter.early)
    a2_load.wait()
    hid_load.wait()
    sums = []
    count = full.shape[2] // step

    def beside(turn_number):
        half = (count + 1) // 2
        for number in range(turn_number * half, min((turn_number + 1) * half, count)):
            if number >= 2:
                for save in sums[number - 2]:
                    save.wait()
            at = slice(number * step, (number + 1) * step)
            held = stage.at[number % 2]
            held[:, : 2 * ff] = flat_tn(a2, at, gu).astype(BF)
            held[:, 2 * ff :] = flat_tn(full, at, hid).astype(BF)
            rows = pl.ds(number * step, step)
            sums.append(
                [
                    loads.start(held.at[:, pl.ds(0, 2 * ff)], gu_sums.at[rows]),
                    loads.start(held.at[:, pl.ds(2 * ff, ff)], d_sums.at[rows]),
                ]
            )

    net2 = scatter.run(beside, True)
    da2 = total[...]
    m = mid[...]
    r2 = inverse_of(m)
    n2 = m * r2
    gain_out[...] = jnp.sum(da2 * n2, axis=0, keepdims=True)
    dmid = e[...].astype(F32) + norm_back(da2, n2, r2, gain[1:2, :])
    dmid_out[...] = dmid
    saves = [save for pair in sums[-2:] for save in pair]
    nets = [net1, net2]
    if alone:
        dat_out[...] = dmid.astype(BF)
    else:
        full2[own] = dmid.astype(BF)
        wa_load.wait()

        def on_second(r):
            saves.append(loads.start(full2.at[r], dat_out.at[r]))
            dob_out[r] = dot_nn(full2[r], wa[:, QKV:PACK]).astype(BF)

        nets.append(run_gather(here, full2, (send3, recv3), on_second))
    for net in nets:
        net.drain()
    for save in saves:
        save.wait()
    if swap is not None:
        swap.wait()


def dat_kernel(dat, wa_hbm, dat_out, dob_out, full, wa, send, recv, local):
    here = token_place()
    loads = Loads(local)
    wa_load = loads.start(wa_hbm, wa)
    full[rank_of(here, 0, 0, 0)] = dat[...]
    greet()
    wa_load.wait()
    saves = []

    def on_block(r):
        saves.append(loads.start(full.at[r], dat_out.at[r]))
        dob_out[r] = dot_nn(full[r], wa[:, QKV:PACK]).astype(BF)

    run_gather(here, full, (send, recv), on_block).drain()
    for save in saves:
        save.wait()


def dat_gather(dat, wa):
    block, width = dat.shape
    return plane_call(
        dat_kernel,
        "dat_gather",
        12,
        [jax.ShapeDtypeStruct((8, block, width), BF), jax.ShapeDtypeStruct((8, block, PACK - QKV), BF)],
        [ANYWHERE, IN_VMEM],
        [IN_VMEM, ANYWHERE],
        [pltpu.VMEM((8, block, width), BF), pltpu.VMEM(wa.shape, BF)] + gather_sems() + [pltpu.SemaphoreType.DMA((9,))],
        32,
        dat, wa,
    )


def mlp_back_alone_kernel(
    ff, step, homeward, e, mid, gain, gu_hbm, hid_hbm, a2_hbm, w1_hbm, w2_hbm, dmid_out, gain_out, dat_out,
    gu_sums, d_sums, full, parts, a2, gu, hid, wm, total, stage, *rest
):
    mlp_back_kernel(
        ff, step, homeward, e, mid, gain, gu_hbm, hid_hbm, a2_hbm, w1_hbm, w2_hbm, None, dmid_out, gain_out,
        dat_out, None, gu_sums, d_sums, full, None, parts, a2, gu, hid, wm, None, total, stage,
        *rest[:-1], None, None, rest[-1], alone=True,
    )


def mlp_back_alone(e, mid, gain, gu, hid, a2, w1, w2):
    block, width = e.shape
    ff = hid.shape[2]
    step = math.gcd(width, 256)
    return plane_call(
        functools.partial(mlp_back_alone_kernel, ff, step, True),
        "mlp_back_alone",
        11,
        [
            jax.ShapeDtypeStruct((block, width), F32),
            jax.ShapeDtypeStruct((1, width), F32),
            jax.ShapeDtypeStruct((block, width), BF),
            jax.ShapeDtypeStruct((width, 2 * ff), BF),
            jax.ShapeDtypeStruct((width, ff), BF),
        ],
        [IN_VMEM, IN_VMEM, IN_VMEM, ANYWHERE, ANYWHERE],
        [IN_VMEM, IN_VMEM, IN_VMEM] + [ANYWHERE] * 5,
        [
            pltpu.VMEM((8, block, width), BF),
            pltpu.VMEM((8, block, width), BF),
            pltpu.VMEM((8, block, width), BF),
            pltpu.VMEM((8, block, 2 * ff), BF),
            pltpu.VMEM((8, block, ff), BF),
            pltpu.VMEM((width, 3 * ff), BF),
            pltpu.VMEM((block, width), F32),
            pltpu.VMEM((2, step, 3 * ff), BF),
        ]
        + gather_sems()
        + scatter_scratch(block, width)
        + [pltpu.SemaphoreType.DMA((5 + 2 * (width // step),))],
        68,
        e, mid, gain, gu, hid, a2, w1, w2,
    )


def mlp_back(e, mid, gain, gu, hid, a2, w1, w2, wa, moving=None):
    block, width = e.shape
    ff = hid.shape[2]
    cols = PACK - QKV
    step = math.gcd(width, 256)
    return plane_call(
        functools.partial(mlp_back_kernel, ff, step, True),
        "mlp_back",
        2 if moving is None else 9,
        [
            jax.ShapeDtypeStruct((block, width), F32),
            jax.ShapeDtypeStruct((1, width), F32),
            jax.ShapeDtypeStruct((8, block, width), BF),
            jax.ShapeDtypeStruct((8, block, cols), BF),
            jax.ShapeDtypeStruct((width, 2 * ff), BF),
            jax.ShapeDtypeStruct((width, ff), BF),
        ],
        [IN_VMEM, IN_VMEM, ANYWHERE, IN_VMEM, ANYWHERE, ANYWHERE],
        [IN_VMEM, IN_VMEM, IN_VMEM] + [ANYWHERE] * 6,
        [
            pltpu.VMEM((8, block, width), BF),
            pltpu.VMEM((8, block, width), BF),
            pltpu.VMEM((8, block, width), BF),
            pltpu.VMEM((8, block, width), BF),
            pltpu.VMEM((8, block, 2 * ff), BF),
            pltpu.VMEM((8, block, ff), BF),
            pltpu.VMEM((width, 3 * ff), BF),
            pltpu.VMEM(wa.shape, BF),
            pltpu.VMEM((block, width), F32),
            pltpu.VMEM((2, step, 3 * ff), BF),
        ]
        + gather_sems()
        + scatter_scratch(block, width)
        + gather_sems()
        + [pltpu.SemaphoreType.DMA((14 + 2 * (width // step),))],
        100,
        e, mid, gain, gu, hid, a2, w1, w2, wa,
        moving=moving,
    )


def attn_back_kernel(
    step, h, dmid, gain, gain2_grad, dq, dk, dv, cosine, sine, o, a1_hbm, dat_hbm, w_hbm, e_out, sums,
    parts, a1, dat, w, dqkv, gain_rows, total, from_c, via_x, via_y, from_x, from_y, send, recv, local,
):
    here = token_place()
    loads = Loads(local)
    w_load = loads.start(w_hbm, w)
    a1_load = loads.start(a1_hbm, a1)
    dat_load = loads.start(dat_hbm, dat)
    greet()
    w_load.wait()

    def fill(r):
        heads = [dq[r, :, n * LANES : (n + 1) * LANES].astype(F32) for n in range(2)]
        heads.append(turn(dk[r], cosine[r], -sine[r]))
        lanes = three_lanes([close_halves(head) for head in heads] + [dv[r]])
        for n in range(3):
            dqkv[r, :, n * LANES : (n + 1) * LANES] = lanes[n].astype(BF)
        parts[r] = dot_nt(dqkv[r], w[:, :QKV]).astype(BF)

    count = a1.shape[2] // step

    def beside(turn_number):
        if turn_number == 0:
            a1_load.wait()
            dat_load.wait()
        half = (count + 1) // 2
        for number in range(turn_number * half, min((turn_number + 1) * half, count)):
            at = slice(number * step, (number + 1) * step)
            sums[at, :QKV] = flat_tn(a1, at, dqkv).astype(BF)
            sums[at, QKV:GAIN_AT] = flat_tn(dat, at, o).astype(BF)

    net = Scatter(here, parts, total, (from_c, via_x, via_y, from_x, from_y), (send, recv), fill).run(beside)
    da1 = total[...]
    x = h[...].astype(F32)
    r1 = inverse_of(x)
    n1 = x * r1
    e_out[...] = (dmid[...] + norm_back(da1, n1, r1, gain[0:1, :])).astype(BF)
    gain_rows[...] = jnp.zeros_like(gain_rows)
    first = GAIN_AT - PACK + LANES
    gain_rows[first : first + 1, :] = jnp.sum(da1 * n1, axis=0, keepdims=True)
    gain_rows[first + 1 : first + 2, :] = gain2_grad[...]
    columns = gain_rows[...].T
    last = sums[:, PACK - LANES :].astype(F32)
    sums[:, PACK - LANES :] = jnp.where(lane(last) < first, last, columns).astype(BF)
    net.drain()


def attn_back(h, dmid, gain, gain2_grad, dq, dk, dv, cosine, sine, o, a1, dat, w):
    block, width = h.shape
    step = math.gcd(width, 256)
    return plane_call(
        functools.partial(attn_back_kernel, step),
        "attn_back",
        3,
        [
            jax.ShapeDtypeStruct((block, width), BF),
            jax.ShapeDtypeStruct((width, PACK), BF),
        ],
        [IN_VMEM, IN_VMEM],
        [IN_VMEM] * 10 + [ANYWHERE] * 3,
        [
            pltpu.VMEM((8, block, width), BF),
            pltpu.VMEM((8, block, width), BF),
            pltpu.VMEM((8, block, width), BF),
            pltpu.VMEM(w.shape, BF),
            pltpu.VMEM((8, block, QKV), BF),
            pltpu.VMEM((LANES, width), F32),
            pltpu.VMEM((block, width), F32),
        ]
        + scatter_scratch(block, width)
        + [pltpu.SemaphoreType.DMA((3,))],
        36,
        h, dmid, gain, gain2_grad, dq, dk, dv, cosine, sine, o, a1, dat, w,
    )


def exchange_kernel(homeward, blocks, got, send_sem, recv_sem, local, swap=None):
    here = place()
    x, c, y = here
    swap = swap and Swap(homeward, *swap)
    masks = [(dx, dc, dy) for dx in range(2) for dc in range(2) for dy in range(2)][1:]
    peer = lambda mask: {"x": flip(x, mask[0]), "c": flip(c, mask[1]), "y": flip(y, mask[2])}
    own = rank_of(here, 0, 0, 0)
    mine = pltpu.make_async_copy(blocks.at[own], got.at[own], local)
    mine.start()
    barrier = pltpu.get_barrier_semaphore()
    for mask in masks:
        pl.semaphore_signal(barrier, inc=1, device_id=peer(mask), device_id_type=MESH)
    if swap is None:
        pl.semaphore_wait(barrier, 7)
    else:
        swap.greet(barrier)
        swap.met(barrier, 7)
        swap.start()

    def copy(n, src, dst):
        return pltpu.make_async_remote_copy(
            src_ref=src,
            dst_ref=dst,
            send_sem=send_sem.at[n],
            recv_sem=recv_sem.at[n],
            device_id=peer(masks[n]),
            device_id_type=MESH,
        )

    copies = [copy(n, blocks.at[rank_of(here, *mask)], got.at[own]) for n, mask in enumerate(masks)]
    for started in copies:
        started.start()
    mine.wait()
    for n, mask in enumerate(masks):
        where = got.at[rank_of(here, *mask)]
        copy(n, where, where).wait_recv()
    for started in copies:
        started.wait_send()
    if swap is not None:
        swap.wait()


def exchange(number, blocks, moving=None, homeward=False):
    return plane_call(
        functools.partial(exchange_kernel, homeward),
        "exchange",
        number,
        [jax.ShapeDtypeStruct(blocks.shape, BF)],
        [ANYWHERE],
        [ANYWHERE],
        [pltpu.SemaphoreType.DMA((7,)), pltpu.SemaphoreType.DMA((7,)), pltpu.SemaphoreType.DMA],
        blocks.size // 40000,
        blocks,
        moving=moving,
    )


def finish_kernel(ff, got, gate, up, down):
    gate[...] = got[0, :, :ff].astype(F32)
    up[...] = got[0, :, ff : 2 * ff].astype(F32)
    down[...] = got[0, :, 2 * ff :].astype(F32)


def finish(got):
    ranks, rows, cols = got.shape
    ff = cols // 3
    return pl.pallas_call(
        functools.partial(finish_kernel, ff),
        grid=(ranks,),
        out_shape=[jax.ShapeDtypeStruct((rows, ranks * ff), F32)] * 3,
        in_specs=[pl.BlockSpec((1, rows, cols), lambda i: (i, 0, 0))],
        out_specs=[pl.BlockSpec((rows, ff), lambda i: (0, i))] * 3,
        compiler_params=pltpu.CompilerParams(vmem_limit_bytes=VMEM_LIMIT),
        name="finish",
    )(got)


LOWER=-1e30
def dot(a, b, dims):
    return lax.dot_general(a, b, (dims, ((), ())), preferred_element_type=F32)

def attend_kernel(scale2, bq, bk, bounds, length, q, k, v, qpos, out, lse):
    groups = q.shape[0]
    i = pl.program_id(0)
    rows = groups * bq
    qs = q[...].reshape(rows, LANES)
    pos = qpos[0]
    pos2 = jnp.concatenate([pos] * groups, axis=1)
    def step(masked, j, state):
        top, total, acc = state
        at = pl.ds(pl.multiple_of(j * bk, bk), bk)
        s = dot(k[at, :], qs, ((1,), (1,)))
        if masked:
            kp = j * bk + lax.broadcasted_iota(jnp.int32, (bk, 1), 0)
            ok = (kp <= pos2) & (kp < length[0])
            s = jnp.where(ok, s, LOWER)
        new = jnp.maximum(top, jnp.max(s, axis=0, keepdims=True) * scale2)
        p = jnp.exp2(s * scale2 - new)
        alpha = jnp.exp2(top - new)
        total = total * alpha + jnp.sum(p, axis=0, keepdims=True)
        acc = acc * alpha + dot(v[at, :], p.astype(BF), ((0,), (0,)))
        return new, total, acc
    state = (jnp.full((1, rows), LOWER, F32), jnp.zeros((1, rows), F32), jnp.zeros((LANES, rows), F32))
    full, end = bounds[0, i], bounds[1, i]
    state = lax.fori_loop(0, full, functools.partial(step, False), state)
    top, total, acc = lax.fori_loop(full, end, functools.partial(step, True), state)
    o = (acc / total).T
    first, second = o[:bq], pltpu.roll(o[bq:], HEAD_SIZE, 1)
    out[:, :LANES] = jnp.where(lane(first) < HEAD_SIZE, first, second).astype(BF)
    out[:, LANES:] = second[:, : OUT - LANES].astype(BF)
    lse[...] = (top + jnp.log2(total))[None]

def attend(q, k, v, qpos, bounds, length, bq, bk, scale2):
    groups, tokens, _ = q.shape
    n = tokens // bq
    out, lse = pl.pallas_call(
        functools.partial(attend_kernel, scale2, bq, bk),
        grid_spec=pltpu.PrefetchScalarGridSpec(
            num_scalar_prefetch=2, grid=(n,),
            in_specs=[
                pl.BlockSpec((groups, bq, LANES), lambda i, *_: (0, i, 0)),
                pl.BlockSpec(k.shape, lambda i, *_: (0, 0)),
                pl.BlockSpec(v.shape, lambda i, *_: (0, 0)),
                pl.BlockSpec((1, 1, bq), lambda i, *_: (i, 0, 0)),
            ],
            out_specs=[
                pl.BlockSpec((bq, OUT), lambda i, *_: (i, 0)),
                pl.BlockSpec((1, 1, groups * bq), lambda i, *_: (i, 0, 0)),
            ]),
        out_shape=[jax.ShapeDtypeStruct((tokens, OUT), BF), jax.ShapeDtypeStruct((n, 1, groups * bq), F32)],
        compiler_params=pltpu.CompilerParams(vmem_limit_bytes=VMEM_LIMIT),
        name="attend",
        cost_estimate=pl.CostEstimate(flops=0, bytes_accessed=45000000, transcendentals=0),
    )(bounds, length, q, k, v, qpos)
    return out, lse

def back_kernel(scale, scale2, bq, bk, bounds, length, q, k, v, qpos, o, do, lse, cosine, sine, dq, dk, dv):
    groups = q.shape[0]
    i = pl.program_id(0)
    @pl.when(i == 0)
    def _():
        dk[...] = jnp.zeros_like(dk)
        dv[...] = jnp.zeros_like(dv)
    qs = q[...].reshape(groups * bq, LANES)
    do0, do1 = do[:, :LANES].astype(F32), do[:, LANES : 2 * LANES].astype(F32)
    at = lane(do0)
    do1 = pltpu.roll(jnp.where(at >= HEAD_SIZE, do0, do1), LANES - HEAD_SIZE, 1)
    wide = jnp.concatenate([jnp.where(at < HEAD_SIZE, do0, 0.0), jnp.where(at < HEAD_SIZE, do1, 0.0)], axis=0)
    dos = wide.astype(BF)
    o0 = o[:, :LANES].astype(F32)
    o1 = jnp.concatenate([o[:, LANES:].astype(F32), jnp.zeros((bq, 2 * LANES - OUT), F32)], axis=1)
    o1 = pltpu.roll(jnp.where(at >= HEAD_SIZE, o0, o1), LANES - HEAD_SIZE, 1)
    delta = jnp.sum(wide * jnp.concatenate([o0, o1], axis=0), axis=1, keepdims=True).reshape(1, groups * bq)
    lse_row = lse[0]
    pos = qpos[0]
    pos2 = jnp.concatenate([pos] * groups, axis=1)
    def step(masked, j, acc):
        at = pl.ds(pl.multiple_of(j * bk, bk), bk)
        kb, vb = k[at, :], v[at, :]
        s = dot(kb, qs, ((1,), (1,)))
        p = jnp.exp2(s * scale2 - lse_row)
        if masked:
            kp = j * bk + lax.broadcasted_iota(jnp.int32, (bk, 1), 0)
            ok = (kp <= pos2) & (kp < length[0])
            p = jnp.where(ok, p, 0.0)
        dp = dot(vb, dos, ((1,), (1,)))
        ds = (p * (dp - delta)).astype(BF)
        dv[at, :] += dot(p.astype(BF), dos, ((1,), (0,)))
        dk[at, :] += dot(ds, qs, ((1,), (0,))) * scale
        return acc + dot(ds, kb, ((0,), (0,)))
    full, end = bounds[0, i], bounds[1, i]
    acc = jnp.zeros((groups * bq, LANES), F32)
    acc = lax.fori_loop(0, full, functools.partial(step, False), acc)
    acc = lax.fori_loop(full, end, functools.partial(step, True), acc) * scale
    for g in range(groups):
        dq[:, g * LANES:(g + 1) * LANES] = turn(acc[g * bq:(g + 1) * bq], cosine[...], -sine[...]).astype(BF)

def attend_back(q, k, v, qpos_row, o, do, lse, cosine, sine, bounds, length, bq, bk, scale, scale2):
    groups, tokens, _ = q.shape
    n = tokens // bq
    wide = pl.BlockSpec((bq, groups * LANES), lambda i, *_: (i, 0))
    narrow = pl.BlockSpec((bq, OUT), lambda i, *_: (i, 0))
    return pl.pallas_call(
        functools.partial(back_kernel, scale, scale2, bq, bk),
        grid_spec=pltpu.PrefetchScalarGridSpec(
            num_scalar_prefetch=2, grid=(n,),
            in_specs=[
                pl.BlockSpec((groups, bq, LANES), lambda i, *_: (0, i, 0)),
                pl.BlockSpec(k.shape, lambda i, *_: (0, 0)),
                pl.BlockSpec(v.shape, lambda i, *_: (0, 0)),
                pl.BlockSpec((1, 1, bq), lambda i, *_: (i, 0, 0)),
                narrow, wide,
                pl.BlockSpec((1, 1, groups * bq), lambda i, *_: (i, 0, 0)),
                pl.BlockSpec((bq, LANES), lambda i, *_: (i, 0)),
                pl.BlockSpec((bq, LANES), lambda i, *_: (i, 0)),
            ],
            out_specs=[wide, pl.BlockSpec(k.shape, lambda i, *_: (0, 0)), pl.BlockSpec(k.shape, lambda i, *_: (0, 0))]),
        out_shape=[jax.ShapeDtypeStruct((tokens, groups * LANES), BF), jax.ShapeDtypeStruct(k.shape, F32), jax.ShapeDtypeStruct(k.shape, F32)],
        compiler_params=pltpu.CompilerParams(vmem_limit_bytes=VMEM_LIMIT),
        name="attend_back",
        cost_estimate=pl.CostEstimate(flops=0, bytes_accessed=65000000, transcendentals=0),
    )(bounds, length, q, k, v, qpos_row, o, do, lse, cosine, sine)

def bounds_of(positions, length, bq, bk):
    p = positions.reshape(-1, bq)
    lo = jnp.minimum(jnp.min(p, axis=1) + 1, length) // bk
    hi = -(-jnp.minimum(jnp.max(p, axis=1) + 1, length) // bk)
    return jnp.stack([lo, hi]).astype(jnp.int32)


PLANE = ("x", "c", "y")

def together(*arrays):
    return lax.optimization_barrier(arrays)


def body(
    inputs,
    lengths,
    cotangent,
    attn_gain,
    w_query,
    key_projection,
    value_projection,
    w_out,
    mlp_gain,
    w_gate,
    w_up,
    w_down,
):
    sections = lax.axis_size("x") * lax.axis_size("c")
    planes = lax.axis_size("z")
    halves = lax.axis_size("y")
    extra = lax.axis_size("e")
    ranks = sections * halves
    layers = sections
    block = inputs.shape[1]
    width = inputs.shape[2]
    rows = w_query.shape[1]
    tokens = block * ranks
    all_tokens = tokens * extra
    head_group = QUERY_HEADS // KEY_VALUE_HEADS
    q_cols = head_group * HEAD_SIZE
    kv_cols = HEAD_SIZE
    ff_cols = FF // ranks
    scale = 1.0 / math.sqrt(HEAD_SIZE)
    scale2 = scale * math.log2(math.e)

    def by_rank(matrix):
        return matrix.reshape(rows, ranks, -1)

    attn_pack = jnp.concatenate(
        [
            by_rank(w_query[0]),
            by_rank(key_projection[0]),
            by_rank(value_projection[0]),
            by_rank(w_out[0].T),
            jnp.broadcast_to(jnp.stack([attn_gain[0], mlp_gain[0]], axis=1)[:, None, :], (rows, ranks, 2)),
            jnp.zeros((rows, ranks, PACK - GAIN_AT - 2), F32),
        ],
        axis=2,
    )
    mlp_pack = jnp.concatenate(
        [by_rank(w_gate[0]), by_rank(w_up[0]), by_rank(w_down[0].T)], axis=2
    )

    def by_layer(got):
        return got.reshape(layers, halves, rows, -1)

    def ready(pack):
        return jnp.swapaxes(pack.astype(BF), 0, 1)

    def whole(part):
        if extra > 1:
            part = lax.all_gather(part, "e", axis=1, tiled=False)
        return lax.all_gather(part.reshape(-1, part.shape[-1]), "z", axis=0, tiled=True)

    def reduce_rows(sums):
        mine = lax.psum_scatter(sums, "z", scatter_dimension=0, tiled=True)
        mine = mine.reshape(halves, extra, rows, -1)
        if extra > 1:
            return lax.psum_scatter(mine, "e", scatter_dimension=1, tiled=False)
        return mine[:, 0]

    cut = 3 * ff_cols * 7 // 12 // LANES * LANES
    mlp_blocks = ready(mlp_pack)
    (attn_got,) = exchange(4, ready(attn_pack))
    first_blocks, attn_got = together(mlp_blocks[..., :cut], attn_got)
    (first_got,) = exchange(5, first_blocks)
    second_blocks, first_got = together(mlp_blocks[..., cut:], first_got)
    second_got, hidden_state = exchange(6, second_blocks, inputs[0])
    attn_parts, first_parts, second_parts = by_layer(attn_got), by_layer(first_got), by_layer(second_got)

    token_x, token_c, token_y = token_place()
    rank = (token_x * 2 + token_c) * halves + token_y
    spot = lax.axis_index("e")
    length = lengths[lax.axis_index("z")]

    block_start = (jnp.arange(ranks) * extra + spot) * block
    positions = (block_start[:, None] + jnp.arange(block)[None, :]).reshape(tokens)
    exponents = 2.0 * jnp.arange(HEAD_SIZE // 2).astype(F32) / HEAD_SIZE
    angles = positions.astype(F32)[:, None] * (THETA ** (-exponents))[None, :]
    table = lambda values: jnp.pad(values, ((0, 0), (0, LANES // 2 - HALF)))
    cosine = jnp.concatenate([table(jnp.cos(angles))] * 2, axis=1)
    sine = jnp.concatenate([table(-jnp.sin(angles)), table(jnp.sin(angles))], axis=1)
    bq = math.gcd(tokens, 512)
    bk = math.gcd(all_tokens, 512)
    bounds = bounds_of(positions, length, bq, bk)
    length1 = length.reshape(1)
    query_rows = positions.astype(jnp.int32).reshape(-1, 1, bq)

    def all_keys(array):
        if extra == 1:
            return array
        stacked = lax.all_gather(array.reshape(ranks, block, -1), "e", axis=1, tiled=False)
        return stacked.reshape(all_tokens, -1)

    def own_keys(array):
        if extra == 1:
            return array
        stacked = array.astype(BF).reshape(ranks, extra, block, -1)
        return lax.psum_scatter(stacked, "e", scatter_dimension=1, tiled=False).reshape(tokens, -1).astype(F32)

    cosine3 = cosine.reshape(ranks, block, LANES)
    sine3 = sine.reshape(ranks, block, LANES)

    def flat(array):
        return array.reshape(tokens, array.shape[-1])

    saved = []
    attn_w, w_1 = whole(attn_parts[0]), whole(first_parts[0])
    hidden_state, attn_w, w_1, second_part = together(hidden_state, attn_w, w_1, second_parts[0])
    w_2 = whole(second_part)
    for layer in range(layers):
        a1, q, k, v, gain = attn_in(hidden_state, attn_w, cosine3, sine3)
        q, k, v = q.reshape(head_group, tokens, LANES), all_keys(flat(k)), all_keys(flat(v))
        o, log_total = attend(q, k, v, query_rows, bounds, length1, bq, bk, scale2)
        if layer + 1 < layers:
            o, attn_part, first_part = together(o, attn_parts[layer + 1], first_parts[layer + 1])
            next_attn, next_1 = whole(attn_part), whole(first_part)
        mid, a2, gu, hid, after_mlp, *moved = mlp(
            hidden_state, o.reshape(ranks, block, -1), gain, attn_w, w_1, w_2,
            cotangent[0] if layer + 1 == layers else None,
        )
        saved.append((hidden_state, a1, q, k, v, o, log_total, mid, a2, gu, hid, attn_w, w_1, w_2, gain))
        hidden_state = after_mlp
        if layer + 1 < layers:
            hidden_state, attn_w, w_1, second_part = together(hidden_state, next_attn, next_1, second_parts[layer + 1])
            w_2 = whole(second_part)
    output = hidden_state

    my_positions = (rank * extra + spot) * block + jnp.arange(block)
    (e,) = moved
    e = jnp.where((my_positions < length)[:, None], e, jnp.zeros_like(e))
    attn_grads = [None] * layers
    gu_grads = [None] * layers
    d_grads = [None] * layers
    for layer in reversed(range(layers)):
        (h, a1, q, k, v, o, log_total, mid, a2, gu, hid, attn_w, w_1, w_2, gain) = saved[layer]
        if layer > 0:
            dmid, gain2, dat, dob, gu_sums, d_sums, *moved = mlp_back(
                e, mid, gain, gu, hid, a2, w_1, w_2, attn_w, output if layer + 1 == layers else None
            )
            if moved:
                (output,) = moved
        else:
            dmid, gain2, dat, gu_sums, d_sums = mlp_back_alone(e, mid, gain, gu, hid, a2, w_1, w_2)
            dat, gu_sums, d_sums, attn_grads[1], d_grads[1] = together(
                dat, gu_sums, d_sums, attn_grads[1], d_grads[1]
            )
            dat, dob = dat_gather(dat, attn_w)
        if 0 < layer < layers - 1:
            dob, gu_sums, d_sums, attn_grads[layer + 1], d_grads[layer + 1] = together(
                dob, gu_sums, d_sums, attn_grads[layer + 1], d_grads[layer + 1]
            )
        gu_grads[layer] = reduce_rows(gu_sums)
        if layer == 0:
            d_grads[layer] = reduce_rows(d_sums)
        dq, dk, dv = attend_back(
            q, k, v, query_rows, o, flat(dob), log_total, cosine, sine, bounds, length1, bq, bk, scale, scale2
        )
        dk, dv = own_keys(dk), own_keys(dv)
        e, attn_sums = attn_back(
            h, dmid, gain, gain2, *(array.reshape(ranks, block, -1) for array in (dq, dk, dv)), cosine3, sine3,
            o.reshape(ranks, block, -1), a1, dat, attn_w,
        )
        if layer > 0:
            e, attn_sums, d_sums, gu_grads[layer] = together(e, attn_sums, d_sums, gu_grads[layer])
            d_grads[layer] = reduce_rows(d_sums)
        else:
            e, attn_sums, gu_grads[layer], d_grads[layer] = together(e, attn_sums, gu_grads[layer], d_grads[layer])
        attn_grads[layer] = reduce_rows(attn_sums)

    def by_place(grads):
        return jnp.stack(grads).reshape(ranks, rows, -1)

    mlp_blocks = by_place([jnp.concatenate(pair, axis=2) for pair in zip(gu_grads, d_grads)])
    mlp_home, input_grad = exchange(7, mlp_blocks, e, True)
    attn_blocks, mlp_home = together(by_place(attn_grads), mlp_home)
    (attn_home,) = exchange(10, attn_blocks)
    grad_gate, grad_up, grad_down = finish(mlp_home)
    attn_home = attn_home.astype(F32)
    gain_sums = jnp.sum(attn_home[:, :, GAIN_AT : GAIN_AT + 2], axis=0)

    def columns(start, count):
        return jnp.swapaxes(attn_home[:, :, start : start + count], 0, 1).reshape(rows, ranks * count)

    return (
        output[None],
        input_grad[None],
        gain_sums[:, 0][None],
        columns(0, q_cols)[None],
        columns(q_cols, kv_cols)[None],
        columns(q_cols + kv_cols, kv_cols)[None],
        columns(QKV, OUT).T[None],
        gain_sums[:, 1][None],
        grad_gate[None],
        grad_up[None],
        grad_down.T[None],
    )


def solution(mesh):
    section, seq = mesh.devices.shape
    halves = KEY_VALUE_HEADS // section
    extra = seq // (section * halves)
    fine = Mesh(
        mesh.devices.reshape(section // 2, 2, section, halves, extra), ("x", "c", "z", "y", "e")
    )
    sec, sq = ("x", "c"), ("z", "y", "e")
    rows3 = P(sec, sq, None)
    cols3 = P(sec, None, sq)
    in_specs = (rows3, P(), rows3, P(sec, sq), rows3, rows3, rows3, cols3, P(sec, sq), rows3, rows3, cols3)
    out_specs = (rows3, rows3, P(sec, sq), rows3, rows3, rows3, cols3, P(sec, sq), rows3, rows3, cols3)
    return jax.shard_map(body, mesh=fine, in_specs=in_specs, out_specs=out_specs, check_vma=False)
```

```python
import functools
import math

import jax
import jax.numpy as jnp
from jax import lax
from jax.experimental import pallas as pl
from jax.experimental.pallas import tpu as pltpu
from jax.sharding import Mesh
from jax.sharding import PartitionSpec as P

QUERY_HEADS = 16
KEY_VALUE_HEADS = 8
HEAD_SIZE = 96
FF = 4096

EPS = 1e-05
THETA = 100000.0
LOWER_LIMIT = -1e30

BF = jnp.bfloat16
F32 = jnp.float32

LANES = 128
HALF = HEAD_SIZE // 2
VMEM_LIMIT = 56 * 1024 * 1024


def dot(a, b, dims):
    return lax.dot_general(a, b, (dims, ((), ())), preferred_element_type=F32)


def dot_nn(a, b):
    return dot(a, b, ((1,), (0,)))


def dot_nt(a, b):
    return dot(a, b, ((1,), (1,)))


def dot_tn(a, b):
    return dot(a, b, ((0,), (0,)))


MESH = pl.DeviceIdType.MESH

OWN, X, Y, D = (0, 0), (1, 0), (0, 1), (1, 1)


def place():
    return lax.axis_index("x"), lax.axis_index("c"), lax.axis_index("y")


def xor(a, b):
    return a + b - 2 * a * b


def token_place():
    x, c, y = place()
    return xor(x, lax.rem(lax.axis_index("z"), 2)), c, y


def flip(index, by):
    return 1 - index if by else index


def rank_of(here, dx, dc, dy):
    x, c, y = here
    return (flip(x, dx) * 2 + flip(c, dc)) * 2 + flip(y, dy)


class Swap:
    def __init__(self, homeward, moving, moved, sem):
        x, c, _ = place()
        z = lax.axis_index("z")
        low = lax.rem(z, 2)
        out = {"x": xor(z // 2, c), "c": low, "z": x * 2 + c}
        back = {"x": z // 2, "c": low, "z": 2 * xor(x, low) + c}
        target, self.source = (back, out) if homeward else (out, back)
        self.away = (target["x"] != x) | (target["c"] != c) | (target["z"] != z)
        self.remote = pltpu.make_async_remote_copy(
            src_ref=moving,
            dst_ref=moved,
            send_sem=sem.at[0],
            recv_sem=sem.at[1],
            device_id=target,
            device_id_type=MESH,
        )
        self.local = pltpu.make_async_copy(moving, moved, sem.at[2])

    def greet(self, barrier):
        @pl.when(self.away)
        def _():
            pl.semaphore_signal(barrier, inc=1, device_id=self.source, device_id_type=MESH)

    def either(self, remote, local):
        pl.when(self.away)(remote)
        pl.when(jnp.logical_not(self.away))(local)

    def start(self):
        self.either(lambda: self.remote.start(), lambda: self.local.start())

    def met(self, barrier, count):
        self.either(lambda: pl.semaphore_wait(barrier, count + 1), lambda: pl.semaphore_wait(barrier, count))

    def wait(self):
        self.either(lambda: self.remote.wait(), lambda: self.local.wait())


def with_swap(kernel, inputs, outputs):
    def wrapped(*refs):
        last = inputs + 1 + outputs
        kernel(
            *refs[:inputs],
            *refs[inputs + 1 : last],
            *refs[last + 1 : -1],
            swap=(refs[inputs], refs[last], refs[-1]),
        )

    return wrapped


def greet(swap=None):
    x, c, y = place()
    barrier = pltpu.get_barrier_semaphore()
    for peer in ({"x": 1 - x}, {"c": 1 - c}, {"y": 1 - y}):
        pl.semaphore_signal(barrier, inc=1, device_id=peer, device_id_type=MESH)
    if swap is None:
        pl.semaphore_wait(barrier, 3)
    else:
        swap.greet(barrier)
        swap.met(barrier, 3)
        swap.start()


class Sender:
    def __init__(self, send_sem, recv_sem):
        x, c, y = place()
        self.peers = {"x": {"x": 1 - x}, "c": {"c": 1 - c}, "y": {"y": 1 - y}}
        self.send_sem, self.recv_sem = send_sem, recv_sem
        self.sent = []

    def copy(self, src, dst, index, to, number):
        return pltpu.make_async_remote_copy(
            src_ref=src,
            dst_ref=dst,
            send_sem=self.send_sem.at[number],
            recv_sem=self.recv_sem.at[index],
            device_id=self.peers[to],
            device_id_type=MESH,
        )

    def send(self, src, dst, index, to):
        started = self.copy(src, dst, index, to, len(self.sent))
        started.start()
        self.sent.append(started)

    def arrived(self, where, index):
        self.copy(where, where, index, "c", 0).wait_recv()

    def drain(self):
        for started in self.sent:
            started.wait_send()


def run_gather(here, full, sems, on_block, before_last=None):
    block = full.shape[1]
    piece = block // 4
    net = Sender(*sems)

    def index(role, chunk):
        return (role[0] * 4 + role[1] * 2 + role[2]) * 4 + chunk

    def slot(role, chunk, count=1):
        return full.at[rank_of(here, *role), pl.ds(chunk * piece, piece * count)]

    def send(role, chunk, to, as_role, count=1):
        where = slot(role, chunk, count)
        net.send(where, where, index(as_role, chunk), to)

    def arrived(role, chunk, count=1):
        net.arrived(slot(role, chunk, count), index(role, chunk))

    def whole(role):
        for chunk in range(4):
            arrived(role, chunk)

    def done(role):
        on_block(rank_of(here, *role))

    own, at_x, at_y, at_d, at_c = (0, 0, 0), (1, 0, 0), (0, 0, 1), (1, 0, 1), (0, 1, 0)
    xc, yc, dc = (1, 1, 0), (0, 1, 1), (1, 1, 1)
    for cx, cy in ((2, 0), (3, 1), (0, 2), (1, 3)):
        send(own, cx, "x", at_x)
        send(own, cy, "y", at_y)
    send(own, 0, "c", at_c, 4)

    def pass_on(cx, cy):
        arrived(at_x, cx)
        if cx >= 2:
            send(at_x, cx, "y", at_d)
        send(at_x, cx, "c", xc)
        arrived(at_y, cy)
        if cy < 2:
            send(at_y, cy, "x", at_d)
        send(at_y, cy, "c", yc)

    def pass_last(chunks):
        for chunk in chunks:
            arrived(at_d, chunk)
            send(at_d, chunk, "c", dc)

    done(own)
    pass_on(2, 0)
    arrived(at_c, 0, 4)
    done(at_c)
    pass_on(3, 1)
    pass_on(0, 2)
    pass_on(1, 3)
    done(at_x)
    done(at_y)
    pass_last((0, 2))
    whole(xc)
    done(xc)
    whole(yc)
    done(yc)
    if before_last is not None:
        before_last()
    pass_last((1, 3))
    done(at_d)
    whole(dc)
    done(dc)
    return net


class Scatter:
    order = (D, X, Y, OWN)

    def __init__(self, here, parts, total, bufs, sems, fill=None):
        self.here, self.parts, self.total, self.fill = here, parts, total, fill
        self.from_c, self.via_x, self.via_y, self.from_x, self.from_y = bufs
        half = parts.shape[1] // 2
        self.lower, self.upper = pl.ds(0, half), pl.ds(half, half)
        self.net = Sender(*sems)

    def rank(self, n, dc):
        return rank_of(self.here, self.order[n][0], dc, self.order[n][1])

    def make(self, r):
        if self.fill is not None:
            self.fill(r)

    def sibling(self, n):
        r = self.rank(n, 1)
        self.make(r)
        self.net.send(self.parts.at[r], self.from_c.at[n], n, "c")

    def add(self, n, where, more):
        r = self.rank(n, 0)
        self.parts[r, where] = (self.parts[r, where].astype(F32) + more.astype(F32)).astype(BF)

    def mine(self, n, where):
        return self.parts.at[self.rank(n, 0), where]

    def combine(self, n):
        self.make(self.rank(n, 0))
        self.net.arrived(self.from_c.at[n], n)
        if n < 3:
            self.add(n, pl.ds(0, self.parts.shape[1]), self.from_c[n])

    def to_diagonal(self):
        self.combine(0)
        self.net.send(self.mine(0, self.upper), self.via_x, 4, "x")
        self.net.send(self.mine(0, self.lower), self.via_y, 5, "y")

    def to_neighbours(self):
        self.combine(1)
        self.net.send(self.mine(1, self.upper), self.from_x.at[self.upper], 6, "x")
        self.combine(2)
        self.net.send(self.mine(2, self.lower), self.from_y.at[self.lower], 7, "y")

    def early(self):
        for n in (1, 2, 3):
            self.sibling(n)
        self.to_neighbours()

    def run(self, beside=None, early_done=False):
        net, total, lower, upper = self.net, self.total, self.lower, self.upper
        self.sibling(0)
        if early_done:
            self.to_diagonal()
        else:
            self.sibling(1)
            self.sibling(2)
            self.to_diagonal()
            self.to_neighbours()
            self.sibling(3)
        self.combine(3)
        total[...] = self.parts[self.rank(3, 0)].astype(F32) + self.from_c[3].astype(F32)
        if beside is not None:
            beside(0)
        net.arrived(self.via_y, 5)
        self.add(1, lower, self.via_y[...])
        net.send(self.mine(1, lower), self.from_x.at[lower], 8, "x")
        net.arrived(self.via_x, 4)
        self.add(2, upper, self.via_x[...])
        net.send(self.mine(2, upper), self.from_y.at[upper], 9, "y")
        if beside is not None:
            beside(1)
        net.arrived(self.from_x.at[upper], 6)
        net.arrived(self.from_y.at[lower], 7)
        total[upper] += self.from_x[upper].astype(F32)
        total[lower] += self.from_y[lower].astype(F32)
        net.arrived(self.from_x.at[lower], 8)
        net.arrived(self.from_y.at[upper], 9)
        total[lower] += self.from_x[lower].astype(F32)
        total[upper] += self.from_y[upper].astype(F32)
        return net


def gather_sems():
    return [pltpu.SemaphoreType.DMA((32,)), pltpu.SemaphoreType.DMA((32,))]


def scatter_scratch(block, width):
    half = block // 2
    return [
        pltpu.VMEM((4, block, width), BF),
        pltpu.VMEM((half, width), BF),
        pltpu.VMEM((half, width), BF),
        pltpu.VMEM((block, width), BF),
        pltpu.VMEM((block, width), BF),
        pltpu.SemaphoreType.DMA((10,)),
        pltpu.SemaphoreType.DMA((10,)),
    ]


class Loads:
    def __init__(self, sem):
        self.sem = sem
        self.count = 0

    def start(self, src, dst):
        copy = pltpu.make_async_copy(src, dst, self.sem.at[self.count])
        self.count += 1
        copy.start()
        return copy


def inverse_of(x):
    return lax.rsqrt(jnp.mean(x * x, axis=-1, keepdims=True) + EPS)


def lane(x):
    return lax.broadcasted_iota(jnp.int32, x.shape, 1)


def turn(head, cosine, sine):
    return head * cosine + pltpu.roll(head, LANES // 2, 1) * sine


def open_halves(head):
    return jnp.where(lane(head) < LANES // 2, head, pltpu.roll(head, LANES // 2 - HALF, 1))


def close_halves(head):
    low = lane(head) < LANES // 2
    return jnp.where(low, head, 0.0) + pltpu.roll(jnp.where(low, 0.0, head), LANES // 2 + HALF, 1)


def four_heads(a, b, c):
    at = lane(a)
    return (
        a,
        pltpu.roll(jnp.where(at >= 96, a, b), 32, 1),
        pltpu.roll(jnp.where(at >= 64, b, c), 64, 1),
        pltpu.roll(c, 96, 1),
    )


def three_lanes(heads):
    at = lane(heads[0])
    b, c, d = pltpu.roll(heads[1], 96, 1), pltpu.roll(heads[2], 64, 1), pltpu.roll(heads[3], 32, 1)
    return jnp.where(at < 96, heads[0], b), jnp.where(at < 64, b, c), jnp.where(at < 32, c, d)


def plane_call(kernel, name, number, out_shape, out_specs, in_specs, scratch, time_us, *operands, moving=None):
    if moving is not None:
        kernel = with_swap(kernel, len(in_specs), len(out_specs))
        out_shape = out_shape + [jax.ShapeDtypeStruct(moving.shape, moving.dtype)]
        in_specs, out_specs = in_specs + [ANYWHERE], out_specs + [ANYWHERE]
        scratch = scratch + [pltpu.SemaphoreType.DMA((3,))]
        operands = operands + (moving,)
    return pl.pallas_call(
        kernel,
        out_shape=out_shape,
        in_specs=in_specs,
        out_specs=out_specs,
        scratch_shapes=scratch,
        compiler_params=pltpu.CompilerParams(
            collective_id=number, has_side_effects=True, vmem_limit_bytes=VMEM_LIMIT
        ),
        cost_estimate=pl.CostEstimate(flops=0, bytes_accessed=time_us * 3000000, transcendentals=0),
        name=name,
    )(*operands)


ANYWHERE = pl.BlockSpec(memory_space=pl.ANY)
IN_VMEM = pl.BlockSpec(memory_space=pltpu.VMEM)
QKV = 4 * HEAD_SIZE
OUT = 2 * HEAD_SIZE
GAIN_AT = QKV + OUT
PACK = -(-(GAIN_AT + 2) // LANES) * LANES


def attn_in_kernel(h, w_hbm, cosine, sine, a1_out, q_out, k_out, v_out, gain_out, full, w, send, recv, local):
    here = token_place()
    loads = Loads(local)
    w_load = loads.start(w_hbm, w)
    x = h[...].astype(F32)
    n1 = x * inverse_of(x)
    w_load.wait()
    rows = w[:, PACK - LANES :].astype(F32).T
    gain_out[...] = rows[GAIN_AT - PACK + LANES : GAIN_AT - PACK + LANES + 2]
    full[rank_of(here, 0, 0, 0)] = (n1 * gain_out[0:1, :]).astype(BF)
    greet()
    saves = []

    def on_block(r):
        saves.append(loads.start(full.at[r], a1_out.at[r]))
        qkv = dot_nn(full[r], w[:, :QKV])
        heads = four_heads(*(qkv[:, n * LANES : (n + 1) * LANES] for n in range(3)))
        cos, sin = cosine[r], sine[r]
        for n in range(2):
            q_out[n, r] = turn(open_halves(heads[n]), cos, sin).astype(BF)
        k_out[r] = turn(open_halves(heads[2]), cos, sin).astype(BF)
        v_out[r] = jnp.where(lane(heads[3]) < HEAD_SIZE, heads[3], 0.0).astype(BF)

    net = run_gather(here, full, (send, recv), on_block)
    net.drain()
    for save in saves:
        save.wait()


def attn_in(h, w, cosine, sine):
    block, width = h.shape
    return plane_call(
        attn_in_kernel,
        "attn_in",
        0,
        [
            jax.ShapeDtypeStruct((8, block, width), BF),
            jax.ShapeDtypeStruct((2, 8, block, LANES), BF),
            jax.ShapeDtypeStruct((8, block, LANES), BF),
            jax.ShapeDtypeStruct((8, block, LANES), BF),
            jax.ShapeDtypeStruct((2, width), F32),
        ],
        [ANYWHERE, IN_VMEM, IN_VMEM, IN_VMEM, IN_VMEM],
        [IN_VMEM, ANYWHERE, IN_VMEM, IN_VMEM],
        [pltpu.VMEM((8, block, width), BF), pltpu.VMEM(w.shape, BF)]
        + gather_sems()
        + [pltpu.SemaphoreType.DMA((9,))],
        34,
        h, w, cosine, sine,
    )


def mlp_kernel(
    ff, homeward, h, o, gain, wa_hbm, w1_hbm, w2_hbm, mid_out, a2_out, gu_out, hid_out, next_out,
    full, parts, gu, hid, wa, wm, total,
    from_c, via_x, via_y, from_x, from_y, send1, recv1, send2, recv2,
    from_c3, via_x3, via_y3, from_x3, from_y3, send3, recv3, local, swap=None,
):
    here = token_place()
    swap = swap and Swap(homeward, *swap)
    loads = Loads(local)
    wa_load = loads.start(wa_hbm, wa)
    split = w1_hbm.shape[1]
    w1_load = loads.start(w1_hbm, wm.at[:, pl.ds(0, split)])
    w2_load = loads.start(w2_hbm, wm.at[:, pl.ds(split, 3 * ff - split)])
    greet(swap)
    wa_load.wait()

    def fill(r):
        parts[r] = dot_nt(o[r], wa[:, QKV:GAIN_AT]).astype(BF)

    bufs = (from_c, via_x, via_y, from_x, from_y)
    net1 = Scatter(here, parts, total, bufs, (send1, recv1), fill).run()
    mid = h[...].astype(F32) + total[...]
    mid_out[...] = mid
    full[rank_of(here, 0, 0, 0)] = (mid * inverse_of(mid) * gain[1:2, :]).astype(BF)
    net1.drain()
    saves = []

    def on_block(r):
        if not saves:
            w1_load.wait()
            w2_load.wait()
        saves.append(loads.start(full.at[r], a2_out.at[r]))
        a2 = full[r]
        g = dot_nn(a2, wm[:, :ff])
        u = dot_nn(a2, wm[:, ff : 2 * ff])
        gu[r, :, :ff] = g.astype(BF)
        gu[r, :, ff:] = u.astype(BF)
        low = (g * (1.0 / (1.0 + jnp.exp(-g))) * u).astype(BF)
        hid[r] = low
        saves.append(loads.start(gu.at[r], gu_out.at[r]))
        saves.append(loads.start(hid.at[r], hid_out.at[r]))
        parts[r] = dot_nt(low, wm[:, 2 * ff :]).astype(BF)

    bufs3 = (from_c3, via_x3, via_y3, from_x3, from_y3)
    scatter = Scatter(here, parts, total, bufs3, (send3, recv3))
    net2 = run_gather(here, full, (send2, recv2), on_block, scatter.early)
    net3 = scatter.run(early_done=True)
    next_out[...] = (mid_out[...] + total[...]).astype(BF)
    net2.drain()
    net3.drain()
    for save in saves:
        save.wait()
    if swap is not None:
        swap.wait()


def mlp(h, o, gain, wa, w1, w2, moving=None):
    block, width = h.shape
    ff = (w1.shape[1] + w2.shape[1]) // 3
    return plane_call(
        functools.partial(mlp_kernel, ff, False),
        "mlp",
        1 if moving is None else 8,
        [
            jax.ShapeDtypeStruct((block, width), F32),
            jax.ShapeDtypeStruct((8, block, width), BF),
            jax.ShapeDtypeStruct((8, block, 2 * ff), BF),
            jax.ShapeDtypeStruct((8, block, ff), BF),
            jax.ShapeDtypeStruct((block, width), BF),
        ],
        [IN_VMEM, ANYWHERE, ANYWHERE, ANYWHERE, IN_VMEM],
        [IN_VMEM, IN_VMEM, IN_VMEM, ANYWHERE, ANYWHERE, ANYWHERE],
        [
            pltpu.VMEM((8, block, width), BF),
            pltpu.VMEM((8, block, width), BF),
            pltpu.VMEM((8, block, 2 * ff), BF),
            pltpu.VMEM((8, block, ff), BF),
            pltpu.VMEM(wa.shape, BF),
            pltpu.VMEM((width, 3 * ff), BF),
            pltpu.VMEM((block, width), F32),
        ]
        + scatter_scratch(block, width)
        + gather_sems()
        + scatter_scratch(block, width)
        + [pltpu.SemaphoreType.DMA((27,))],
        96,
        h, o, gain, wa, w1, w2,
        moving=moving,
    )


def norm_back(upstream, normed, inverse, gain_row):
    scaled = upstream * gain_row
    return inverse * (scaled - normed * jnp.mean(scaled * normed, axis=-1, keepdims=True))


def flat_tn(a, cols, b):
    total = dot_tn(a[0, :, cols], b[0])
    for n in range(1, a.shape[0]):
        total = total + dot_tn(a[n, :, cols], b[n])
    return total


def mlp_back_kernel(
    ff, step, homeward, e, mid, gain, gu_hbm, hid_hbm, a2_hbm, w1_hbm, w2_hbm, wa_hbm, dmid_out, gain_out, dat_out, dob_out,
    first_sums, second_sums, full, full2, parts, a2, gu, hid, wm, wa, total, stage, send1, recv1,
    from_c, via_x, via_y, from_x, from_y, send2, recv2, send3, recv3, local, swap=None, alone=False,
):
    here = token_place()
    swap = swap and Swap(homeward, *swap)
    loads = Loads(local)
    split = w1_hbm.shape[1]
    w2_load = loads.start(w2_hbm, wm.at[:, pl.ds(split, 3 * ff - split)])
    gu_load = loads.start(gu_hbm, gu)
    w1_load = loads.start(w1_hbm, wm.at[:, pl.ds(0, split)])
    wa_load = None if alone else loads.start(wa_hbm, wa)
    a2_load = loads.start(a2_hbm, a2)
    hid_load = loads.start(hid_hbm, hid)
    own = rank_of(here, 0, 0, 0)
    full[own] = e[...]
    greet(swap)
    w2_load.wait()
    gu_load.wait()
    w1_load.wait()

    def on_block(r):
        dhid = dot_nn(full[r], wm[:, 2 * ff :])
        g = gu[r, :, :ff].astype(F32)
        u = gu[r, :, ff:].astype(F32)
        sig = 1.0 / (1.0 + jnp.exp(-g))
        du = dhid * g * sig
        dg = dhid * u * sig * (1.0 + g * (1.0 - sig))
        gu[r, :, :ff] = dg.astype(BF)
        gu[r, :, ff:] = du.astype(BF)
        parts[r] = dot_nt(gu[r], wm[:, : 2 * ff]).astype(BF)

    scatter = Scatter(here, parts, total, (from_c, via_x, via_y, from_x, from_y), (send2, recv2))
    net1 = run_gather(here, full, (send1, recv1), on_block, scatter.early)
    a2_load.wait()
    hid_load.wait()
    sums = []
    count = full.shape[2] // step
    middle = first_sums.shape[1]

    def beside(turn_number):
        half = (count + 1) // 2
        for number in range(turn_number * half, min((turn_number + 1) * half, count)):
            if number >= 2:
                for save in sums[number - 2]:
                    save.wait()
            at = slice(number * step, (number + 1) * step)
            held = stage.at[number % 2]
            held[:, : 2 * ff] = flat_tn(a2, at, gu).astype(BF)
            held[:, 2 * ff :] = flat_tn(full, at, hid).astype(BF)
            rows = pl.ds(number * step, step)
            sums.append(
                [
                    loads.start(held.at[:, pl.ds(0, middle)], first_sums.at[rows]),
                    loads.start(held.at[:, pl.ds(middle, 3 * ff - middle)], second_sums.at[rows]),
                ]
            )

    net2 = scatter.run(beside, True)
    da2 = total[...]
    m = mid[...]
    r2 = inverse_of(m)
    n2 = m * r2
    gain_out[...] = jnp.sum(da2 * n2, axis=0, keepdims=True)
    dmid = e[...].astype(F32) + norm_back(da2, n2, r2, gain[1:2, :])
    dmid_out[...] = dmid
    saves = [save for pair in sums[-2:] for save in pair]
    nets = [net1, net2]
    if alone:
        dat_out[...] = dmid.astype(BF)
    else:
        full2[own] = dmid.astype(BF)
        wa_load.wait()

        def on_second(r):
            saves.append(loads.start(full2.at[r], dat_out.at[r]))
            dob_out[r] = dot_nn(full2[r], wa[:, QKV:PACK]).astype(BF)

        nets.append(run_gather(here, full2, (send3, recv3), on_second))
    for net in nets:
        net.drain()
    for save in saves:
        save.wait()
    if swap is not None:
        swap.wait()


def dat_kernel(dat, wa_hbm, dat_out, dob_out, full, wa, send, recv, local):
    here = token_place()
    loads = Loads(local)
    wa_load = loads.start(wa_hbm, wa)
    full[rank_of(here, 0, 0, 0)] = dat[...]
    greet()
    wa_load.wait()
    saves = []

    def on_block(r):
        saves.append(loads.start(full.at[r], dat_out.at[r]))
        dob_out[r] = dot_nn(full[r], wa[:, QKV:PACK]).astype(BF)

    run_gather(here, full, (send, recv), on_block).drain()
    for save in saves:
        save.wait()


def dat_gather(dat, wa):
    block, width = dat.shape
    return plane_call(
        dat_kernel,
        "dat_gather",
        12,
        [jax.ShapeDtypeStruct((8, block, width), BF), jax.ShapeDtypeStruct((8, block, PACK - QKV), BF)],
        [ANYWHERE, IN_VMEM],
        [IN_VMEM, ANYWHERE],
        [pltpu.VMEM((8, block, width), BF), pltpu.VMEM(wa.shape, BF)] + gather_sems() + [pltpu.SemaphoreType.DMA((9,))],
        32,
        dat, wa,
    )


def mlp_back_alone_kernel(
    ff, step, homeward, e, mid, gain, gu_hbm, hid_hbm, a2_hbm, w1_hbm, w2_hbm, dmid_out, gain_out, dat_out,
    first_sums, second_sums, full, parts, a2, gu, hid, wm, total, stage, *rest
):
    mlp_back_kernel(
        ff, step, homeward, e, mid, gain, gu_hbm, hid_hbm, a2_hbm, w1_hbm, w2_hbm, None, dmid_out, gain_out,
        dat_out, None, first_sums, second_sums, full, None, parts, a2, gu, hid, wm, None, total, stage,
        *rest[:-1], None, None, rest[-1], alone=True,
    )


def mlp_back_alone(e, mid, gain, gu, hid, a2, w1, w2):
    block, width = e.shape
    ff = hid.shape[2]
    step = math.gcd(width, 256)
    return plane_call(
        functools.partial(mlp_back_alone_kernel, ff, step, True),
        "mlp_back_alone",
        11,
        [
            jax.ShapeDtypeStruct((block, width), F32),
            jax.ShapeDtypeStruct((1, width), F32),
            jax.ShapeDtypeStruct((block, width), BF),
            jax.ShapeDtypeStruct((width, 3 * ff // 2), BF),
            jax.ShapeDtypeStruct((width, 3 * ff // 2), BF),
        ],
        [IN_VMEM, IN_VMEM, IN_VMEM, ANYWHERE, ANYWHERE],
        [IN_VMEM, IN_VMEM, IN_VMEM] + [ANYWHERE] * 5,
        [
            pltpu.VMEM((8, block, width), BF),
            pltpu.VMEM((8, block, width), BF),
            pltpu.VMEM((8, block, width), BF),
            pltpu.VMEM((8, block, 2 * ff), BF),
            pltpu.VMEM((8, block, ff), BF),
            pltpu.VMEM((width, 3 * ff), BF),
            pltpu.VMEM((block, width), F32),
            pltpu.VMEM((2, step, 3 * ff), BF),
        ]
        + gather_sems()
        + scatter_scratch(block, width)
        + [pltpu.SemaphoreType.DMA((5 + 2 * (width // step),))],
        68,
        e, mid, gain, gu, hid, a2, w1, w2,
    )


def mlp_back(e, mid, gain, gu, hid, a2, w1, w2, wa, moving=None):
    block, width = e.shape
    ff = hid.shape[2]
    cols = PACK - QKV
    step = math.gcd(width, 256)
    return plane_call(
        functools.partial(mlp_back_kernel, ff, step, True),
        "mlp_back",
        2 if moving is None else 9,
        [
            jax.ShapeDtypeStruct((block, width), F32),
            jax.ShapeDtypeStruct((1, width), F32),
            jax.ShapeDtypeStruct((8, block, width), BF),
            jax.ShapeDtypeStruct((8, block, cols), BF),
            jax.ShapeDtypeStruct((width, 3 * ff // 2), BF),
            jax.ShapeDtypeStruct((width, 3 * ff // 2), BF),
        ],
        [IN_VMEM, IN_VMEM, ANYWHERE, IN_VMEM, ANYWHERE, ANYWHERE],
        [IN_VMEM, IN_VMEM, IN_VMEM] + [ANYWHERE] * 6,
        [
            pltpu.VMEM((8, block, width), BF),
            pltpu.VMEM((8, block, width), BF),
            pltpu.VMEM((8, block, width), BF),
            pltpu.VMEM((8, block, width), BF),
            pltpu.VMEM((8, block, 2 * ff), BF),
            pltpu.VMEM((8, block, ff), BF),
            pltpu.VMEM((width, 3 * ff), BF),
            pltpu.VMEM(wa.shape, BF),
            pltpu.VMEM((block, width), F32),
            pltpu.VMEM((2, step, 3 * ff), BF),
        ]
        + gather_sems()
        + scatter_scratch(block, width)
        + gather_sems()
        + [pltpu.SemaphoreType.DMA((14 + 2 * (width // step),))],
        100,
        e, mid, gain, gu, hid, a2, w1, w2, wa,
        moving=moving,
    )


def attn_back_kernel(
    step, h, dmid, gain, gain2_grad, dq, dk, dv, cosine, sine, o, a1_hbm, dat_hbm, w_hbm, e_out, sums,
    parts, a1, dat, w, dqkv, gain_rows, total, from_c, via_x, via_y, from_x, from_y, send, recv, local,
):
    here = token_place()
    loads = Loads(local)
    w_load = loads.start(w_hbm, w)
    a1_load = loads.start(a1_hbm, a1)
    dat_load = loads.start(dat_hbm, dat)
    greet()
    w_load.wait()

    def fill(r):
        heads = [dq[r, :, n * LANES : (n + 1) * LANES].astype(F32) for n in range(2)]
        heads.append(turn(dk[r], cosine[r], -sine[r]))
        lanes = three_lanes([close_halves(head) for head in heads] + [dv[r]])
        for n in range(3):
            dqkv[r, :, n * LANES : (n + 1) * LANES] = lanes[n].astype(BF)
        parts[r] = dot_nt(dqkv[r], w[:, :QKV]).astype(BF)

    count = a1.shape[2] // step

    def beside(turn_number):
        if turn_number == 0:
            a1_load.wait()
            dat_load.wait()
        half = (count + 1) // 2
        for number in range(turn_number * half, min((turn_number + 1) * half, count)):
            at = slice(number * step, (number + 1) * step)
            sums[at, :QKV] = flat_tn(a1, at, dqkv).astype(BF)
            sums[at, QKV:GAIN_AT] = flat_tn(dat, at, o).astype(BF)

    net = Scatter(here, parts, total, (from_c, via_x, via_y, from_x, from_y), (send, recv), fill).run(beside)
    da1 = total[...]
    x = h[...].astype(F32)
    r1 = inverse_of(x)
    n1 = x * r1
    e_out[...] = (dmid[...] + norm_back(da1, n1, r1, gain[0:1, :])).astype(BF)
    gain_rows[...] = jnp.zeros_like(gain_rows)
    first = GAIN_AT - PACK + LANES
    gain_rows[first : first + 1, :] = jnp.sum(da1 * n1, axis=0, keepdims=True)
    gain_rows[first + 1 : first + 2, :] = gain2_grad[...]
    columns = gain_rows[...].T
    last = sums[:, PACK - LANES :].astype(F32)
    sums[:, PACK - LANES :] = jnp.where(lane(last) < first, last, columns).astype(BF)
    net.drain()


def attn_back(h, dmid, gain, gain2_grad, dq, dk, dv, cosine, sine, o, a1, dat, w):
    block, width = h.shape
    step = math.gcd(width, 256)
    return plane_call(
        functools.partial(attn_back_kernel, step),
        "attn_back",
        3,
        [
            jax.ShapeDtypeStruct((block, width), BF),
            jax.ShapeDtypeStruct((width, PACK), BF),
        ],
        [IN_VMEM, IN_VMEM],
        [IN_VMEM] * 10 + [ANYWHERE] * 3,
        [
            pltpu.VMEM((8, block, width), BF),
            pltpu.VMEM((8, block, width), BF),
            pltpu.VMEM((8, block, width), BF),
            pltpu.VMEM(w.shape, BF),
            pltpu.VMEM((8, block, QKV), BF),
            pltpu.VMEM((LANES, width), F32),
            pltpu.VMEM((block, width), F32),
        ]
        + scatter_scratch(block, width)
        + [pltpu.SemaphoreType.DMA((3,))],
        36,
        h, dmid, gain, gain2_grad, dq, dk, dv, cosine, sine, o, a1, dat, w,
    )


def exchange_kernel(homeward, blocks, got, send_sem, recv_sem, local, swap=None):
    here = place()
    x, c, y = here
    swap = swap and Swap(homeward, *swap)
    masks = [(dx, dc, dy) for dx in range(2) for dc in range(2) for dy in range(2)][1:]
    peer = lambda mask: {"x": flip(x, mask[0]), "c": flip(c, mask[1]), "y": flip(y, mask[2])}
    own = rank_of(here, 0, 0, 0)
    mine = pltpu.make_async_copy(blocks.at[own], got.at[own], local)
    mine.start()
    barrier = pltpu.get_barrier_semaphore()
    for mask in masks:
        pl.semaphore_signal(barrier, inc=1, device_id=peer(mask), device_id_type=MESH)
    if swap is None:
        pl.semaphore_wait(barrier, 7)
    else:
        swap.greet(barrier)
        swap.met(barrier, 7)
        swap.start()

    def copy(n, src, dst):
        return pltpu.make_async_remote_copy(
            src_ref=src,
            dst_ref=dst,
            send_sem=send_sem.at[n],
            recv_sem=recv_sem.at[n],
            device_id=peer(masks[n]),
            device_id_type=MESH,
        )

    copies = [copy(n, blocks.at[rank_of(here, *mask)], got.at[own]) for n, mask in enumerate(masks)]
    for started in copies:
        started.start()
    mine.wait()
    for n, mask in enumerate(masks):
        where = got.at[rank_of(here, *mask)]
        copy(n, where, where).wait_recv()
    for started in copies:
        started.wait_send()
    if swap is not None:
        swap.wait()


def exchange(number, blocks, moving=None, homeward=False):
    return plane_call(
        functools.partial(exchange_kernel, homeward),
        "exchange",
        number,
        [jax.ShapeDtypeStruct(blocks.shape, BF)],
        [ANYWHERE],
        [ANYWHERE],
        [pltpu.SemaphoreType.DMA((7,)), pltpu.SemaphoreType.DMA((7,)), pltpu.SemaphoreType.DMA],
        blocks.size // 40000,
        blocks,
        moving=moving,
    )


def finish_kernel(ff, got, gate, up, down):
    gate[...] = got[0, :, :ff].astype(F32)
    up[...] = got[0, :, ff : 2 * ff].astype(F32)
    down[...] = got[0, :, 2 * ff :].astype(F32)


def finish(got):
    ranks, rows, cols = got.shape
    ff = cols // 3
    return pl.pallas_call(
        functools.partial(finish_kernel, ff),
        grid=(ranks,),
        out_shape=[jax.ShapeDtypeStruct((rows, ranks * ff), F32)] * 3,
        in_specs=[pl.BlockSpec((1, rows, cols), lambda i: (i, 0, 0))],
        out_specs=[pl.BlockSpec((rows, ff), lambda i: (0, i))] * 3,
        compiler_params=pltpu.CompilerParams(vmem_limit_bytes=VMEM_LIMIT),
        name="finish",
    )(got)


def finish_attn_kernel(got, query, key, value, out, gains):
    ranks = got.shape[0]

    def lanes(t, n):
        return got[t, :, n * LANES : (n + 1) * LANES].astype(F32)

    groups = [four_heads(*(lanes(t, n) for n in range(3))) for t in range(ranks)]

    def write(ref, heads):
        for n in range(0, len(heads), 4):
            for j, part in enumerate(three_lanes(heads[n : n + 4])):
                at = n * HEAD_SIZE + j * LANES
                ref[:, at : at + LANES] = part

    write(query, [head for group in groups for head in group[:2]])
    write(key, [group[2] for group in groups])
    write(value, [group[3] for group in groups])
    out_heads = []
    total = None
    for t in range(ranks):
        a, b = lanes(t, 3), lanes(t, 4)
        out_heads += [a, pltpu.roll(jnp.where(lane(a) >= HEAD_SIZE, a, b), LANES - HEAD_SIZE, 1)]
        total = b if total is None else total + b
    write(out, out_heads)
    first = GAIN_AT - PACK + LANES
    gains[...] = total.T[first : first + 2]


def finish_attn(got):
    ranks, rows, _ = got.shape
    wide, narrow = jax.ShapeDtypeStruct((rows, ranks * OUT), F32), jax.ShapeDtypeStruct((rows, ranks * HEAD_SIZE), F32)
    return pl.pallas_call(
        finish_attn_kernel,
        out_shape=[wide, narrow, narrow, wide, jax.ShapeDtypeStruct((2, rows), F32)],
        in_specs=[IN_VMEM],
        out_specs=[IN_VMEM] * 5,
        compiler_params=pltpu.CompilerParams(vmem_limit_bytes=VMEM_LIMIT),
        name="finish_attn",
    )(got)


LOWER=-1e30
def dot(a, b, dims):
    return lax.dot_general(a, b, (dims, ((), ())), preferred_element_type=F32)

def attend_kernel(scale2, bq, bk, bounds, length, q, k, v, qpos, out, lse):
    groups = q.shape[0]
    i = pl.program_id(0)
    rows = groups * bq
    qs = q[...].reshape(rows, LANES)
    pos = qpos[0]
    pos2 = jnp.concatenate([pos] * groups, axis=1)
    def step(masked, j, state):
        top, total, acc = state
        at = pl.ds(pl.multiple_of(j * bk, bk), bk)
        s = dot(k[at, :], qs, ((1,), (1,)))
        if masked:
            kp = j * bk + lax.broadcasted_iota(jnp.int32, (bk, 1), 0)
            ok = (kp <= pos2) & (kp < length[0])
            s = jnp.where(ok, s, LOWER)
        new = jnp.maximum(top, jnp.max(s, axis=0, keepdims=True) * scale2)
        p = jnp.exp2(s * scale2 - new)
        alpha = jnp.exp2(top - new)
        total = total * alpha + jnp.sum(p, axis=0, keepdims=True)
        acc = acc * alpha + dot(v[at, :], p.astype(BF), ((0,), (0,)))
        return new, total, acc
    state = (jnp.full((1, rows), LOWER, F32), jnp.zeros((1, rows), F32), jnp.zeros((LANES, rows), F32))
    full, end = bounds[0, i], bounds[1, i]
    state = lax.fori_loop(0, full, functools.partial(step, False), state)
    top, total, acc = lax.fori_loop(full, end, functools.partial(step, True), state)
    o = (acc / total).T
    first, second = o[:bq], pltpu.roll(o[bq:], HEAD_SIZE, 1)
    out[:, :LANES] = jnp.where(lane(first) < HEAD_SIZE, first, second).astype(BF)
    out[:, LANES:] = second[:, : OUT - LANES].astype(BF)
    lse[...] = (top + jnp.log2(total))[None]

def attend(q, k, v, qpos, bounds, length, bq, bk, scale2):
    groups, tokens, _ = q.shape
    n = tokens // bq
    out, lse = pl.pallas_call(
        functools.partial(attend_kernel, scale2, bq, bk),
        grid_spec=pltpu.PrefetchScalarGridSpec(
            num_scalar_prefetch=2, grid=(n,),
            in_specs=[
                pl.BlockSpec((groups, bq, LANES), lambda i, *_: (0, i, 0)),
                pl.BlockSpec(k.shape, lambda i, *_: (0, 0)),
                pl.BlockSpec(v.shape, lambda i, *_: (0, 0)),
                pl.BlockSpec((1, 1, bq), lambda i, *_: (i, 0, 0)),
            ],
            out_specs=[
                pl.BlockSpec((bq, OUT), lambda i, *_: (i, 0)),
                pl.BlockSpec((1, 1, groups * bq), lambda i, *_: (i, 0, 0)),
            ]),
        out_shape=[jax.ShapeDtypeStruct((tokens, OUT), BF), jax.ShapeDtypeStruct((n, 1, groups * bq), F32)],
        compiler_params=pltpu.CompilerParams(vmem_limit_bytes=VMEM_LIMIT),
        name="attend",
        cost_estimate=pl.CostEstimate(flops=0, bytes_accessed=45000000, transcendentals=0),
    )(bounds, length, q, k, v, qpos)
    return out, lse

def back_kernel(scale, scale2, bq, bk, bounds, length, q, k, v, qpos, o, do, lse, cosine, sine, dq, dk, dv):
    groups = q.shape[0]
    i = pl.program_id(0)
    @pl.when(i == 0)
    def _():
        dk[...] = jnp.zeros_like(dk)
        dv[...] = jnp.zeros_like(dv)
    qs = q[...].reshape(groups * bq, LANES)
    do0, do1 = do[:, :LANES].astype(F32), do[:, LANES : 2 * LANES].astype(F32)
    at = lane(do0)
    do1 = pltpu.roll(jnp.where(at >= HEAD_SIZE, do0, do1), LANES - HEAD_SIZE, 1)
    wide = jnp.concatenate([jnp.where(at < HEAD_SIZE, do0, 0.0), jnp.where(at < HEAD_SIZE, do1, 0.0)], axis=0)
    dos = wide.astype(BF)
    o0 = o[:, :LANES].astype(F32)
    o1 = jnp.concatenate([o[:, LANES:].astype(F32), jnp.zeros((bq, 2 * LANES - OUT), F32)], axis=1)
    o1 = pltpu.roll(jnp.where(at >= HEAD_SIZE, o0, o1), LANES - HEAD_SIZE, 1)
    delta = jnp.sum(wide * jnp.concatenate([o0, o1], axis=0), axis=1, keepdims=True).reshape(1, groups * bq)
    lse_row = lse[0]
    pos = qpos[0]
    pos2 = jnp.concatenate([pos] * groups, axis=1)
    def step(masked, j, acc):
        at = pl.ds(pl.multiple_of(j * bk, bk), bk)
        kb, vb = k[at, :], v[at, :]
        s = dot(kb, qs, ((1,), (1,)))
        p = jnp.exp2(s * scale2 - lse_row)
        if masked:
            kp = j * bk + lax.broadcasted_iota(jnp.int32, (bk, 1), 0)
            ok = (kp <= pos2) & (kp < length[0])
            p = jnp.where(ok, p, 0.0)
        dp = dot(vb, dos, ((1,), (1,)))
        ds = (p * (dp - delta)).astype(BF)
        dv[at, :] += dot(p.astype(BF), dos, ((1,), (0,)))
        dk[at, :] += dot(ds, qs, ((1,), (0,))) * scale
        return acc + dot(ds, kb, ((0,), (0,)))
    full, end = bounds[0, i], bounds[1, i]
    acc = jnp.zeros((groups * bq, LANES), F32)
    acc = lax.fori_loop(0, full, functools.partial(step, False), acc)
    acc = lax.fori_loop(full, end, functools.partial(step, True), acc) * scale
    for g in range(groups):
        dq[:, g * LANES:(g + 1) * LANES] = turn(acc[g * bq:(g + 1) * bq], cosine[...], -sine[...]).astype(BF)

def attend_back(q, k, v, qpos_row, o, do, lse, cosine, sine, bounds, length, bq, bk, scale, scale2):
    groups, tokens, _ = q.shape
    n = tokens // bq
    wide = pl.BlockSpec((bq, groups * LANES), lambda i, *_: (i, 0))
    narrow = pl.BlockSpec((bq, OUT), lambda i, *_: (i, 0))
    return pl.pallas_call(
        functools.partial(back_kernel, scale, scale2, bq, bk),
        grid_spec=pltpu.PrefetchScalarGridSpec(
            num_scalar_prefetch=2, grid=(n,),
            in_specs=[
                pl.BlockSpec((groups, bq, LANES), lambda i, *_: (0, i, 0)),
                pl.BlockSpec(k.shape, lambda i, *_: (0, 0)),
                pl.BlockSpec(v.shape, lambda i, *_: (0, 0)),
                pl.BlockSpec((1, 1, bq), lambda i, *_: (i, 0, 0)),
                narrow, wide,
                pl.BlockSpec((1, 1, groups * bq), lambda i, *_: (i, 0, 0)),
                pl.BlockSpec((bq, LANES), lambda i, *_: (i, 0)),
                pl.BlockSpec((bq, LANES), lambda i, *_: (i, 0)),
            ],
            out_specs=[wide, pl.BlockSpec(k.shape, lambda i, *_: (0, 0)), pl.BlockSpec(k.shape, lambda i, *_: (0, 0))]),
        out_shape=[jax.ShapeDtypeStruct((tokens, groups * LANES), BF), jax.ShapeDtypeStruct(k.shape, F32), jax.ShapeDtypeStruct(k.shape, F32)],
        compiler_params=pltpu.CompilerParams(vmem_limit_bytes=VMEM_LIMIT),
        name="attend_back",
        cost_estimate=pl.CostEstimate(flops=0, bytes_accessed=65000000, transcendentals=0),
    )(bounds, length, q, k, v, qpos_row, o, do, lse, cosine, sine)

def bounds_of(positions, length, bq, bk):
    p = positions.reshape(-1, bq)
    lo = jnp.minimum(jnp.min(p, axis=1) + 1, length) // bk
    hi = -(-jnp.minimum(jnp.max(p, axis=1) + 1, length) // bk)
    return jnp.stack([lo, hi]).astype(jnp.int32)


PLANE = ("x", "c", "y")

def together(*arrays):
    return lax.optimization_barrier(arrays)


def body(
    inputs,
    lengths,
    cotangent,
    attn_gain,
    w_query,
    key_projection,
    value_projection,
    w_out,
    mlp_gain,
    w_gate,
    w_up,
    w_down,
):
    sections = lax.axis_size("x") * lax.axis_size("c")
    planes = lax.axis_size("z")
    halves = lax.axis_size("y")
    extra = lax.axis_size("e")
    ranks = sections * halves
    layers = sections
    block = inputs.shape[1]
    width = inputs.shape[2]
    rows = w_query.shape[1]
    tokens = block * ranks
    all_tokens = tokens * extra
    head_group = QUERY_HEADS // KEY_VALUE_HEADS
    q_cols = head_group * HEAD_SIZE
    kv_cols = HEAD_SIZE
    ff_cols = FF // ranks
    scale = 1.0 / math.sqrt(HEAD_SIZE)
    scale2 = scale * math.log2(math.e)

    def by_rank(matrix):
        return matrix.reshape(rows, ranks, -1)

    attn_pack = jnp.concatenate(
        [
            by_rank(w_query[0]),
            by_rank(key_projection[0]),
            by_rank(value_projection[0]),
            by_rank(w_out[0].T),
            jnp.broadcast_to(jnp.stack([attn_gain[0], mlp_gain[0]], axis=1)[:, None, :], (rows, ranks, 2)),
            jnp.zeros((rows, ranks, PACK - GAIN_AT - 2), F32),
        ],
        axis=2,
    )
    mlp_pack = jnp.concatenate(
        [by_rank(w_gate[0]), by_rank(w_up[0]), by_rank(w_down[0].T)], axis=2
    )

    def by_layer(got):
        return got.reshape(layers, halves, rows, -1)

    def ready(pack):
        return jnp.swapaxes(pack.astype(BF), 0, 1)

    def whole(part):
        if extra > 1:
            part = lax.all_gather(part, "e", axis=1, tiled=False)
        return lax.all_gather(part.reshape(-1, part.shape[-1]), "z", axis=0, tiled=True)

    def reduce_rows(sums):
        mine = lax.psum_scatter(sums, "z", scatter_dimension=0, tiled=True)
        mine = mine.reshape(halves, extra, rows, -1)
        if extra > 1:
            return lax.psum_scatter(mine, "e", scatter_dimension=1, tiled=False)
        return mine[:, 0]

    cut = 3 * ff_cols // 2
    mlp_blocks = ready(mlp_pack)
    attn_got, hidden_state = exchange(4, ready(attn_pack), inputs[0])
    first_blocks, attn_got = together(mlp_blocks[..., :cut], attn_got)
    (first_got,) = exchange(5, first_blocks)
    second_blocks, first_got = together(mlp_blocks[..., cut:], first_got)
    (second_got,) = exchange(6, second_blocks)
    attn_parts, first_parts, second_parts = by_layer(attn_got), by_layer(first_got), by_layer(second_got)

    token_x, token_c, token_y = token_place()
    rank = (token_x * 2 + token_c) * halves + token_y
    spot = lax.axis_index("e")
    length = lengths[lax.axis_index("z")]

    block_start = (jnp.arange(ranks) * extra + spot) * block
    positions = (block_start[:, None] + jnp.arange(block)[None, :]).reshape(tokens)
    exponents = 2.0 * jnp.arange(HEAD_SIZE // 2).astype(F32) / HEAD_SIZE
    angles = positions.astype(F32)[:, None] * (THETA ** (-exponents))[None, :]
    table = lambda values: jnp.pad(values, ((0, 0), (0, LANES // 2 - HALF)))
    cosine = jnp.concatenate([table(jnp.cos(angles))] * 2, axis=1)
    sine = jnp.concatenate([table(-jnp.sin(angles)), table(jnp.sin(angles))], axis=1)
    bq = math.gcd(tokens, 512)
    bk = math.gcd(all_tokens, 512)
    bounds = bounds_of(positions, length, bq, bk)
    length1 = length.reshape(1)
    query_rows = positions.astype(jnp.int32).reshape(-1, 1, bq)

    def all_keys(array):
        if extra == 1:
            return array
        stacked = lax.all_gather(array.reshape(ranks, block, -1), "e", axis=1, tiled=False)
        return stacked.reshape(all_tokens, -1)

    def own_keys(array):
        if extra == 1:
            return array
        stacked = array.astype(BF).reshape(ranks, extra, block, -1)
        return lax.psum_scatter(stacked, "e", scatter_dimension=1, tiled=False).reshape(tokens, -1).astype(F32)

    cosine3 = cosine.reshape(ranks, block, LANES)
    sine3 = sine.reshape(ranks, block, LANES)

    def flat(array):
        return array.reshape(tokens, array.shape[-1])

    saved = []
    attn_w, w_1 = whole(attn_parts[0]), whole(first_parts[0])
    hidden_state, attn_w, w_1, second_part = together(hidden_state, attn_w, w_1, second_parts[0])
    w_2 = whole(second_part)
    for layer in range(layers):
        a1, q, k, v, gain = attn_in(hidden_state, attn_w, cosine3, sine3)
        q, k, v = q.reshape(head_group, tokens, LANES), all_keys(flat(k)), all_keys(flat(v))
        o, log_total = attend(q, k, v, query_rows, bounds, length1, bq, bk, scale2)
        if layer + 1 < layers:
            o, attn_part, first_part = together(o, attn_parts[layer + 1], first_parts[layer + 1])
            next_attn, next_1 = whole(attn_part), whole(first_part)
        mid, a2, gu, hid, after_mlp, *moved = mlp(
            hidden_state, o.reshape(ranks, block, -1), gain, attn_w, w_1, w_2,
            cotangent[0] if layer + 1 == layers else None,
        )
        saved.append((hidden_state, a1, q, k, v, o, log_total, mid, a2, gu, hid, attn_w, w_1, w_2, gain))
        hidden_state = after_mlp
        if layer + 1 < layers:
            hidden_state, attn_w, w_1, second_part = together(hidden_state, next_attn, next_1, second_parts[layer + 1])
            w_2 = whole(second_part)
    output = hidden_state

    my_positions = (rank * extra + spot) * block + jnp.arange(block)
    (e,) = moved
    e = jnp.where((my_positions < length)[:, None], e, jnp.zeros_like(e))
    attn_grads = [None] * layers
    first_grads = [None] * layers
    second_grads = [None] * layers
    for layer in reversed(range(layers)):
        (h, a1, q, k, v, o, log_total, mid, a2, gu, hid, attn_w, w_1, w_2, gain) = saved[layer]
        if layer > 0:
            dmid, gain2, dat, dob, first_sums, second_sums, *moved = mlp_back(
                e, mid, gain, gu, hid, a2, w_1, w_2, attn_w, output if layer + 1 == layers else None
            )
            if moved:
                (output,) = moved
        else:
            dmid, gain2, dat, first_sums, second_sums = mlp_back_alone(e, mid, gain, gu, hid, a2, w_1, w_2)
            dat, first_sums, second_sums, attn_grads[1], second_grads[1] = together(
                dat, first_sums, second_sums, attn_grads[1], second_grads[1]
            )
            dat, dob = dat_gather(dat, attn_w)
        if 0 < layer < layers - 1:
            dob, first_sums, second_sums, attn_grads[layer + 1], second_grads[layer + 1] = together(
                dob, first_sums, second_sums, attn_grads[layer + 1], second_grads[layer + 1]
            )
        first_grads[layer] = reduce_rows(first_sums)
        if layer == 0:
            second_grads[layer] = reduce_rows(second_sums)
        dq, dk, dv = attend_back(
            q, k, v, query_rows, o, flat(dob), log_total, cosine, sine, bounds, length1, bq, bk, scale, scale2
        )
        dk, dv = own_keys(dk), own_keys(dv)
        e, attn_sums = attn_back(
            h, dmid, gain, gain2, *(array.reshape(ranks, block, -1) for array in (dq, dk, dv)), cosine3, sine3,
            o.reshape(ranks, block, -1), a1, dat, attn_w,
        )
        if layer > 0:
            e, attn_sums, second_sums, first_grads[layer] = together(e, attn_sums, second_sums, first_grads[layer])
            second_grads[layer] = reduce_rows(second_sums)
        else:
            e, attn_sums, first_grads[layer], second_grads[layer] = together(e, attn_sums, first_grads[layer], second_grads[layer])
        attn_grads[layer] = reduce_rows(attn_sums)

    def by_place(grads):
        return jnp.stack(grads).reshape(ranks, rows, -1)

    mlp_blocks = by_place([jnp.concatenate(pair, axis=2) for pair in zip(first_grads, second_grads)])
    (mlp_home,) = exchange(7, mlp_blocks)
    attn_blocks, mlp_home = together(by_place(attn_grads), mlp_home)
    attn_home, input_grad = exchange(10, attn_blocks, e, True)
    grad_gate, grad_up, grad_down = finish(mlp_home)
    grad_query, grad_key, grad_value, grad_out, gain_sums = finish_attn(attn_home)
    return (
        output[None],
        input_grad[None],
        gain_sums[0:1],
        grad_query[None],
        grad_key[None],
        grad_value[None],
        grad_out.T[None],
        gain_sums[1:2],
        grad_gate[None],
        grad_up[None],
        grad_down.T[None],
    )


def solution(mesh):
    section, seq = mesh.devices.shape
    halves = KEY_VALUE_HEADS // section
    extra = seq // (section * halves)
    fine = Mesh(
        mesh.devices.reshape(section // 2, 2, section, halves, extra), ("x", "c", "z", "y", "e")
    )
    sec, sq = ("x", "c"), ("z", "y", "e")
    rows3 = P(sec, sq, None)
    cols3 = P(sec, None, sq)
    in_specs = (rows3, P(), rows3, P(sec, sq), rows3, rows3, rows3, cols3, P(sec, sq), rows3, rows3, cols3)
    out_specs = (rows3, rows3, P(sec, sq), rows3, rows3, rows3, cols3, P(sec, sq), rows3, rows3, cols3)
    return jax.shard_map(body, mesh=fine, in_specs=in_specs, out_specs=out_specs, check_vma=False)
```

```python
import functools
import math

import jax
import jax.numpy as jnp
from jax import lax
from jax.experimental import pallas as pl
from jax.experimental.pallas import tpu as pltpu
from jax.sharding import Mesh
from jax.sharding import PartitionSpec as P

QUERY_HEADS = 16
KEY_VALUE_HEADS = 8
HEAD_SIZE = 96
FF = 4096

EPS = 1e-05
THETA = 100000.0
LOWER_LIMIT = -1e30

BF = jnp.bfloat16
F32 = jnp.float32

LANES = 128
HALF = HEAD_SIZE // 2
VMEM_LIMIT = 56 * 1024 * 1024


def dot(a, b, dims):
    return lax.dot_general(a, b, (dims, ((), ())), preferred_element_type=F32)


def dot_nn(a, b):
    return dot(a, b, ((1,), (0,)))


def dot_nt(a, b):
    return dot(a, b, ((1,), (1,)))


def dot_tn(a, b):
    return dot(a, b, ((0,), (0,)))


MESH = pl.DeviceIdType.MESH

OWN, X, Y, D = (0, 0), (1, 0), (0, 1), (1, 1)


def place():
    return lax.axis_index("x"), lax.axis_index("c"), lax.axis_index("y")


def xor(a, b):
    return a + b - 2 * a * b


def token_place():
    x, c, y = place()
    z = lax.axis_index("z")
    return xor(x, xor(lax.rem(z, 2), z // 2)), c, y


def micro_of_plane():
    z = lax.axis_index("z")
    return lax.rem(z, 2) * 2 + z // 2


def flip(index, by):
    return 1 - index if by else index


def rank_of(here, dx, dc, dy):
    x, c, y = here
    return (flip(x, dx) * 2 + flip(c, dc)) * 2 + flip(y, dy)


class Swap:
    def __init__(self, homeward, moving, moved, sem):
        x, c, _ = place()
        z = lax.axis_index("z")
        low = lax.rem(z, 2)
        high = z // 2
        out = {"x": xor(high, xor(x, c)), "c": low, "z": c * 2 + x}
        back = {"x": low, "c": high, "z": 2 * xor(x, xor(low, high)) + c}
        target, self.source = (back, out) if homeward else (out, back)
        self.away = (target["x"] != x) | (target["c"] != c) | (target["z"] != z)
        self.remote = pltpu.make_async_remote_copy(
            src_ref=moving,
            dst_ref=moved,
            send_sem=sem.at[0],
            recv_sem=sem.at[1],
            device_id=target,
            device_id_type=MESH,
        )
        self.local = pltpu.make_async_copy(moving, moved, sem.at[2])

    def greet(self, barrier):
        @pl.when(self.away)
        def _():
            pl.semaphore_signal(barrier, inc=1, device_id=self.source, device_id_type=MESH)

    def either(self, remote, local):
        pl.when(self.away)(remote)
        pl.when(jnp.logical_not(self.away))(local)

    def start(self):
        self.either(lambda: self.remote.start(), lambda: self.local.start())

    def met(self, barrier, count):
        self.either(lambda: pl.semaphore_wait(barrier, count + 1), lambda: pl.semaphore_wait(barrier, count))

    def wait(self):
        self.either(lambda: self.remote.wait(), lambda: self.local.wait())


def with_swap(kernel, inputs, outputs):
    def wrapped(*refs):
        last = inputs + 1 + outputs
        kernel(
            *refs[:inputs],
            *refs[inputs + 1 : last],
            *refs[last + 1 : -1],
            swap=(refs[inputs], refs[last], refs[-1]),
        )

    return wrapped


def greet(swap=None):
    x, c, y = place()
    barrier = pltpu.get_barrier_semaphore()
    for peer in ({"x": 1 - x}, {"c": 1 - c}, {"y": 1 - y}):
        pl.semaphore_signal(barrier, inc=1, device_id=peer, device_id_type=MESH)
    if swap is None:
        pl.semaphore_wait(barrier, 3)
    else:
        swap.greet(barrier)
        swap.met(barrier, 3)
        swap.start()


class Sender:
    def __init__(self, send_sem, recv_sem):
        x, c, y = place()
        self.peers = {"x": {"x": 1 - x}, "c": {"c": 1 - c}, "y": {"y": 1 - y}}
        self.send_sem, self.recv_sem = send_sem, recv_sem
        self.sent = []

    def copy(self, src, dst, index, to, number):
        return pltpu.make_async_remote_copy(
            src_ref=src,
            dst_ref=dst,
            send_sem=self.send_sem.at[number],
            recv_sem=self.recv_sem.at[index],
            device_id=self.peers[to],
            device_id_type=MESH,
        )

    def send(self, src, dst, index, to):
        started = self.copy(src, dst, index, to, len(self.sent))
        started.start()
        self.sent.append(started)

    def arrived(self, where, index):
        self.copy(where, where, index, "c", 0).wait_recv()

    def drain(self):
        for started in self.sent:
            started.wait_send()


def run_gather(here, full, sems, on_block, before_last=None):
    block = full.shape[1]
    piece = block // 4
    net = Sender(*sems)

    def index(role, chunk):
        return (role[0] * 4 + role[1] * 2 + role[2]) * 4 + chunk

    def slot(role, chunk, count=1):
        return full.at[rank_of(here, *role), pl.ds(chunk * piece, piece * count)]

    def send(role, chunk, to, as_role, count=1):
        where = slot(role, chunk, count)
        net.send(where, where, index(as_role, chunk), to)

    def arrived(role, chunk, count=1):
        net.arrived(slot(role, chunk, count), index(role, chunk))

    def whole(role):
        for chunk in range(4):
            arrived(role, chunk)

    def done(role):
        on_block(rank_of(here, *role))

    own, at_x, at_y, at_d, at_c = (0, 0, 0), (1, 0, 0), (0, 0, 1), (1, 0, 1), (0, 1, 0)
    xc, yc, dc = (1, 1, 0), (0, 1, 1), (1, 1, 1)
    for cx, cy in ((2, 0), (3, 1), (0, 2), (1, 3)):
        send(own, cx, "x", at_x)
        send(own, cy, "y", at_y)
    send(own, 0, "c", at_c, 4)

    def pass_on(cx, cy):
        arrived(at_x, cx)
        if cx >= 2:
            send(at_x, cx, "y", at_d)
        send(at_x, cx, "c", xc)
        arrived(at_y, cy)
        if cy < 2:
            send(at_y, cy, "x", at_d)
        send(at_y, cy, "c", yc)

    def pass_last(chunks):
        for chunk in chunks:
            arrived(at_d, chunk)
            send(at_d, chunk, "c", dc)

    done(own)
    pass_on(2, 0)
    arrived(at_c, 0, 4)
    done(at_c)
    pass_on(3, 1)
    pass_on(0, 2)
    pass_on(1, 3)
    done(at_x)
    done(at_y)
    pass_last((0, 2))
    whole(xc)
    done(xc)
    whole(yc)
    done(yc)
    if before_last is not None:
        before_last()
    pass_last((1, 3))
    done(at_d)
    whole(dc)
    done(dc)
    return net


class Scatter:
    order = (D, X, Y, OWN)

    def __init__(self, here, parts, total, bufs, sems, fill=None):
        self.here, self.parts, self.total, self.fill = here, parts, total, fill
        self.from_c, self.via_x, self.via_y, self.from_x, self.from_y = bufs
        half = parts.shape[1] // 2
        self.lower, self.upper = pl.ds(0, half), pl.ds(half, half)
        self.net = Sender(*sems)

    def rank(self, n, dc):
        return rank_of(self.here, self.order[n][0], dc, self.order[n][1])

    def make(self, r):
        if self.fill is not None:
            self.fill(r)

    def sibling(self, n):
        r = self.rank(n, 1)
        self.make(r)
        self.net.send(self.parts.at[r], self.from_c.at[n], n, "c")

    def add(self, n, where, more):
        r = self.rank(n, 0)
        self.parts[r, where] = (self.parts[r, where].astype(F32) + more.astype(F32)).astype(BF)

    def mine(self, n, where):
        return self.parts.at[self.rank(n, 0), where]

    def combine(self, n):
        self.make(self.rank(n, 0))
        self.net.arrived(self.from_c.at[n], n)
        if n < 3:
            self.add(n, pl.ds(0, self.parts.shape[1]), self.from_c[n])

    def to_diagonal(self):
        self.combine(0)
        self.net.send(self.mine(0, self.upper), self.via_x, 4, "x")
        self.net.send(self.mine(0, self.lower), self.via_y, 5, "y")

    def to_neighbours(self):
        self.combine(1)
        self.net.send(self.mine(1, self.upper), self.from_x.at[self.upper], 6, "x")
        self.combine(2)
        self.net.send(self.mine(2, self.lower), self.from_y.at[self.lower], 7, "y")

    def early(self):
        for n in (1, 2, 3):
            self.sibling(n)
        self.to_neighbours()

    def run(self, beside=None, early_done=False):
        net, total, lower, upper = self.net, self.total, self.lower, self.upper
        self.sibling(0)
        if early_done:
            self.to_diagonal()
        else:
            self.sibling(1)
            self.sibling(2)
            self.to_diagonal()
            self.to_neighbours()
            self.sibling(3)
        self.combine(3)
        total[...] = self.parts[self.rank(3, 0)].astype(F32) + self.from_c[3].astype(F32)
        if beside is not None:
            beside(0)
        net.arrived(self.via_y, 5)
        self.add(1, lower, self.via_y[...])
        net.send(self.mine(1, lower), self.from_x.at[lower], 8, "x")
        net.arrived(self.via_x, 4)
        self.add(2, upper, self.via_x[...])
        net.send(self.mine(2, upper), self.from_y.at[upper], 9, "y")
        if beside is not None:
            beside(1)
        net.arrived(self.from_x.at[upper], 6)
        net.arrived(self.from_y.at[lower], 7)
        total[upper] += self.from_x[upper].astype(F32)
        total[lower] += self.from_y[lower].astype(F32)
        net.arrived(self.from_x.at[lower], 8)
        net.arrived(self.from_y.at[upper], 9)
        total[lower] += self.from_x[lower].astype(F32)
        total[upper] += self.from_y[upper].astype(F32)
        return net


def gather_sems():
    return [pltpu.SemaphoreType.DMA((32,)), pltpu.SemaphoreType.DMA((32,))]


def scatter_scratch(block, width):
    half = block // 2
    return [
        pltpu.VMEM((4, block, width), BF),
        pltpu.VMEM((half, width), BF),
        pltpu.VMEM((half, width), BF),
        pltpu.VMEM((block, width), BF),
        pltpu.VMEM((block, width), BF),
        pltpu.SemaphoreType.DMA((10,)),
        pltpu.SemaphoreType.DMA((10,)),
    ]


class Loads:
    def __init__(self, sem):
        self.sem = sem
        self.count = 0

    def start(self, src, dst):
        copy = pltpu.make_async_copy(src, dst, self.sem.at[self.count])
        self.count += 1
        copy.start()
        return copy


def inverse_of(x):
    return lax.rsqrt(jnp.mean(x * x, axis=-1, keepdims=True) + EPS)


def lane(x):
    return lax.broadcasted_iota(jnp.int32, x.shape, 1)


def turn(head, cosine, sine):
    return head * cosine + pltpu.roll(head, LANES // 2, 1) * sine


def open_halves(head):
    return jnp.where(lane(head) < LANES // 2, head, pltpu.roll(head, LANES // 2 - HALF, 1))


def close_halves(head):
    low = lane(head) < LANES // 2
    return jnp.where(low, head, 0.0) + pltpu.roll(jnp.where(low, 0.0, head), LANES // 2 + HALF, 1)


def four_heads(a, b, c):
    at = lane(a)
    return (
        a,
        pltpu.roll(jnp.where(at >= 96, a, b), 32, 1),
        pltpu.roll(jnp.where(at >= 64, b, c), 64, 1),
        pltpu.roll(c, 96, 1),
    )


def three_lanes(heads):
    at = lane(heads[0])
    b, c, d = pltpu.roll(heads[1], 96, 1), pltpu.roll(heads[2], 64, 1), pltpu.roll(heads[3], 32, 1)
    return jnp.where(at < 96, heads[0], b), jnp.where(at < 64, b, c), jnp.where(at < 32, c, d)


def plane_call(kernel, name, number, out_shape, out_specs, in_specs, scratch, time_us, *operands, moving=None):
    if moving is not None:
        kernel = with_swap(kernel, len(in_specs), len(out_specs))
        out_shape = out_shape + [jax.ShapeDtypeStruct(moving.shape, moving.dtype)]
        in_specs, out_specs = in_specs + [ANYWHERE], out_specs + [ANYWHERE]
        scratch = scratch + [pltpu.SemaphoreType.DMA((3,))]
        operands = operands + (moving,)
    return pl.pallas_call(
        kernel,
        out_shape=out_shape,
        in_specs=in_specs,
        out_specs=out_specs,
        scratch_shapes=scratch,
        compiler_params=pltpu.CompilerParams(
            collective_id=number, has_side_effects=True, vmem_limit_bytes=VMEM_LIMIT
        ),
        cost_estimate=pl.CostEstimate(flops=0, bytes_accessed=time_us * 3000000, transcendentals=0),
        name=name,
    )(*operands)


ANYWHERE = pl.BlockSpec(memory_space=pl.ANY)
IN_VMEM = pl.BlockSpec(memory_space=pltpu.VMEM)
QKV = 4 * HEAD_SIZE
OUT = 2 * HEAD_SIZE
GAIN_AT = QKV + OUT
PACK = -(-(GAIN_AT + 2) // LANES) * LANES


def attn_in_kernel(h, w_hbm, cosine, sine, a1_out, q_out, k_out, v_out, gain_out, full, w, send, recv, local):
    here = token_place()
    loads = Loads(local)
    w_load = loads.start(w_hbm, w)
    x = h[...].astype(F32)
    n1 = x * inverse_of(x)
    w_load.wait()
    rows = w[:, PACK - LANES :].astype(F32).T
    gain_out[...] = rows[GAIN_AT - PACK + LANES : GAIN_AT - PACK + LANES + 2]
    full[rank_of(here, 0, 0, 0)] = (n1 * gain_out[0:1, :]).astype(BF)
    greet()
    saves = []

    def on_block(r):
        saves.append(loads.start(full.at[r], a1_out.at[r]))
        qkv = dot_nn(full[r], w[:, :QKV])
        heads = four_heads(*(qkv[:, n * LANES : (n + 1) * LANES] for n in range(3)))
        cos, sin = cosine[r], sine[r]
        for n in range(2):
            q_out[n, r] = turn(open_halves(heads[n]), cos, sin).astype(BF)
        k_out[r] = turn(open_halves(heads[2]), cos, sin).astype(BF)
        v_out[r] = jnp.where(lane(heads[3]) < HEAD_SIZE, heads[3], 0.0).astype(BF)

    net = run_gather(here, full, (send, recv), on_block)
    net.drain()
    for save in saves:
        save.wait()


def attn_in(h, w, cosine, sine):
    block, width = h.shape
    return plane_call(
        attn_in_kernel,
        "attn_in",
        0,
        [
            jax.ShapeDtypeStruct((8, block, width), BF),
            jax.ShapeDtypeStruct((2, 8, block, LANES), BF),
            jax.ShapeDtypeStruct((8, block, LANES), BF),
            jax.ShapeDtypeStruct((8, block, LANES), BF),
            jax.ShapeDtypeStruct((2, width), F32),
        ],
        [ANYWHERE, IN_VMEM, IN_VMEM, IN_VMEM, IN_VMEM],
        [IN_VMEM, ANYWHERE, IN_VMEM, IN_VMEM],
        [pltpu.VMEM((8, block, width), BF), pltpu.VMEM(w.shape, BF)]
        + gather_sems()
        + [pltpu.SemaphoreType.DMA((9,))],
        34,
        h, w, cosine, sine,
    )


def mlp_kernel(
    ff, homeward, h, o, gain, wa_hbm, w1_hbm, w2_hbm, mid_out, a2_out, gu_out, hid_out, next_out,
    full, parts, gu, hid, wa, wm, total,
    from_c, via_x, via_y, from_x, from_y, send1, recv1, send2, recv2,
    from_c3, via_x3, via_y3, from_x3, from_y3, send3, recv3, local, swap=None,
):
    here = token_place()
    swap = swap and Swap(homeward, *swap)
    loads = Loads(local)
    wa_load = loads.start(wa_hbm, wa)
    split = w1_hbm.shape[1]
    w1_load = loads.start(w1_hbm, wm.at[:, pl.ds(0, split)])
    w2_load = loads.start(w2_hbm, wm.at[:, pl.ds(split, 3 * ff - split)])
    greet(swap)
    wa_load.wait()

    def fill(r):
        parts[r] = dot_nt(o[r], wa[:, QKV:GAIN_AT]).astype(BF)

    bufs = (from_c, via_x, via_y, from_x, from_y)
    net1 = Scatter(here, parts, total, bufs, (send1, recv1), fill).run()
    mid = h[...].astype(F32) + total[...]
    mid_out[...] = mid
    full[rank_of(here, 0, 0, 0)] = (mid * inverse_of(mid) * gain[1:2, :]).astype(BF)
    net1.drain()
    saves = []

    def on_block(r):
        if not saves:
            w1_load.wait()
            w2_load.wait()
        saves.append(loads.start(full.at[r], a2_out.at[r]))
        a2 = full[r]
        g = dot_nn(a2, wm[:, :ff])
        u = dot_nn(a2, wm[:, ff : 2 * ff])
        gu[r, :, :ff] = g.astype(BF)
        gu[r, :, ff:] = u.astype(BF)
        low = (g * (1.0 / (1.0 + jnp.exp(-g))) * u).astype(BF)
        hid[r] = low
        saves.append(loads.start(gu.at[r], gu_out.at[r]))
        saves.append(loads.start(hid.at[r], hid_out.at[r]))
        parts[r] = dot_nt(low, wm[:, 2 * ff :]).astype(BF)

    bufs3 = (from_c3, via_x3, via_y3, from_x3, from_y3)
    scatter = Scatter(here, parts, total, bufs3, (send3, recv3))
    net2 = run_gather(here, full, (send2, recv2), on_block, scatter.early)
    net3 = scatter.run(early_done=True)
    next_out[...] = (mid_out[...] + total[...]).astype(BF)
    net2.drain()
    net3.drain()
    for save in saves:
        save.wait()
    if swap is not None:
        swap.wait()


def mlp(h, o, gain, wa, w1, w2, moving=None):
    block, width = h.shape
    ff = (w1.shape[1] + w2.shape[1]) // 3
    return plane_call(
        functools.partial(mlp_kernel, ff, False),
        "mlp",
        1 if moving is None else 8,
        [
            jax.ShapeDtypeStruct((block, width), F32),
            jax.ShapeDtypeStruct((8, block, width), BF),
            jax.ShapeDtypeStruct((8, block, 2 * ff), BF),
            jax.ShapeDtypeStruct((8, block, ff), BF),
            jax.ShapeDtypeStruct((block, width), BF),
        ],
        [IN_VMEM, ANYWHERE, ANYWHERE, ANYWHERE, IN_VMEM],
        [IN_VMEM, IN_VMEM, IN_VMEM, ANYWHERE, ANYWHERE, ANYWHERE],
        [
            pltpu.VMEM((8, block, width), BF),
            pltpu.VMEM((8, block, width), BF),
            pltpu.VMEM((8, block, 2 * ff), BF),
            pltpu.VMEM((8, block, ff), BF),
            pltpu.VMEM(wa.shape, BF),
            pltpu.VMEM((width, 3 * ff), BF),
            pltpu.VMEM((block, width), F32),
        ]
        + scatter_scratch(block, width)
        + gather_sems()
        + scatter_scratch(block, width)
        + [pltpu.SemaphoreType.DMA((27,))],
        96,
        h, o, gain, wa, w1, w2,
        moving=moving,
    )


def norm_back(upstream, normed, inverse, gain_row):
    scaled = upstream * gain_row
    return inverse * (scaled - normed * jnp.mean(scaled * normed, axis=-1, keepdims=True))


def flat_tn(a, cols, b):
    total = dot_tn(a[0, :, cols], b[0])
    for n in range(1, a.shape[0]):
        total = total + dot_tn(a[n, :, cols], b[n])
    return total


def mlp_back_kernel(
    ff, step, homeward, e, mid, gain, gu_hbm, hid_hbm, a2_hbm, w1_hbm, w2_hbm, dmid_out, gain_out, dat_out, sums_out,
    full, parts, a2, gu, hid, wm, total, stage, send1, recv1,
    from_c, via_x, via_y, from_x, from_y, send2, recv2, local, swap=None,
):
    here = token_place()
    swap = swap and Swap(homeward, *swap)
    loads = Loads(local)
    split = w1_hbm.shape[1]
    w2_load = loads.start(w2_hbm, wm.at[:, pl.ds(split, 3 * ff - split)])
    gu_load = loads.start(gu_hbm, gu)
    w1_load = loads.start(w1_hbm, wm.at[:, pl.ds(0, split)])
    a2_load = loads.start(a2_hbm, a2)
    hid_load = loads.start(hid_hbm, hid)
    own = rank_of(here, 0, 0, 0)
    full[own] = e[...]
    greet(swap)
    w2_load.wait()
    gu_load.wait()
    w1_load.wait()

    def on_block(r):
        dhid = dot_nn(full[r], wm[:, 2 * ff :])
        g = gu[r, :, :ff].astype(F32)
        u = gu[r, :, ff:].astype(F32)
        sig = 1.0 / (1.0 + jnp.exp(-g))
        du = dhid * g * sig
        dg = dhid * u * sig * (1.0 + g * (1.0 - sig))
        gu[r, :, :ff] = dg.astype(BF)
        gu[r, :, ff:] = du.astype(BF)
        parts[r] = dot_nt(gu[r], wm[:, : 2 * ff]).astype(BF)

    scatter = Scatter(here, parts, total, (from_c, via_x, via_y, from_x, from_y), (send2, recv2))
    net1 = run_gather(here, full, (send1, recv1), on_block, scatter.early)
    a2_load.wait()
    hid_load.wait()
    sums = []
    count = full.shape[2] // step

    def beside(turn_number):
        half = (count + 1) // 2
        for number in range(turn_number * half, min((turn_number + 1) * half, count)):
            if number >= 2:
                sums[number - 2].wait()
            at = slice(number * step, (number + 1) * step)
            held = stage.at[number % 2]
            held[:, : 2 * ff] = flat_tn(a2, at, gu).astype(BF)
            held[:, 2 * ff :] = flat_tn(full, at, hid).astype(BF)
            sums.append(loads.start(held, sums_out.at[pl.ds(number * step, step)]))

    net2 = scatter.run(beside, True)
    da2 = total[...]
    m = mid[...]
    r2 = inverse_of(m)
    n2 = m * r2
    gain_out[...] = jnp.sum(da2 * n2, axis=0, keepdims=True)
    dmid = e[...].astype(F32) + norm_back(da2, n2, r2, gain[1:2, :])
    dmid_out[...] = dmid
    dat_out[...] = dmid.astype(BF)
    net1.drain()
    net2.drain()
    for save in sums[-2:]:
        save.wait()
    if swap is not None:
        swap.wait()


def dat_kernel(dat, wa_hbm, dat_out, dob_out, full, wa, send, recv, local):
    here = token_place()
    loads = Loads(local)
    wa_load = loads.start(wa_hbm, wa)
    full[rank_of(here, 0, 0, 0)] = dat[...]
    greet()
    wa_load.wait()
    saves = []

    def on_block(r):
        saves.append(loads.start(full.at[r], dat_out.at[r]))
        dob_out[r] = dot_nn(full[r], wa[:, QKV:PACK]).astype(BF)

    run_gather(here, full, (send, recv), on_block).drain()
    for save in saves:
        save.wait()


def dat_gather(dat, wa):
    block, width = dat.shape
    return plane_call(
        dat_kernel,
        "dat_gather",
        12,
        [jax.ShapeDtypeStruct((8, block, width), BF), jax.ShapeDtypeStruct((8, block, PACK - QKV), BF)],
        [ANYWHERE, IN_VMEM],
        [IN_VMEM, ANYWHERE],
        [pltpu.VMEM((8, block, width), BF), pltpu.VMEM(wa.shape, BF)] + gather_sems() + [pltpu.SemaphoreType.DMA((9,))],
        32,
        dat, wa,
    )


def mlp_back(e, mid, gain, gu, hid, a2, w1, w2, moving=None):
    block, width = e.shape
    ff = hid.shape[2]
    step = math.gcd(width, 256)
    return plane_call(
        functools.partial(mlp_back_kernel, ff, step, True),
        "mlp_back",
        2 if moving is None else 9,
        [
            jax.ShapeDtypeStruct((block, width), F32),
            jax.ShapeDtypeStruct((1, width), F32),
            jax.ShapeDtypeStruct((block, width), BF),
            jax.ShapeDtypeStruct((width, 3 * ff), BF),
        ],
        [IN_VMEM, IN_VMEM, IN_VMEM, ANYWHERE],
        [IN_VMEM, IN_VMEM, IN_VMEM] + [ANYWHERE] * 5,
        [
            pltpu.VMEM((8, block, width), BF),
            pltpu.VMEM((8, block, width), BF),
            pltpu.VMEM((8, block, width), BF),
            pltpu.VMEM((8, block, 2 * ff), BF),
            pltpu.VMEM((8, block, ff), BF),
            pltpu.VMEM((width, 3 * ff), BF),
            pltpu.VMEM((block, width), F32),
            pltpu.VMEM((2, step, 3 * ff), BF),
        ]
        + gather_sems()
        + scatter_scratch(block, width)
        + [pltpu.SemaphoreType.DMA((5 + width // step,))],
        68,
        e, mid, gain, gu, hid, a2, w1, w2,
        moving=moving,
    )


def attn_back_kernel(
    step, h, dmid, gain, gain2_grad, dq, dk, dv, cosine, sine, o, a1_hbm, dat_hbm, w_hbm, e_out, sums,
    parts, a1, dat, w, dqkv, gain_rows, total, from_c, via_x, via_y, from_x, from_y, send, recv, local,
):
    here = token_place()
    loads = Loads(local)
    w_load = loads.start(w_hbm, w)
    a1_load = loads.start(a1_hbm, a1)
    dat_load = loads.start(dat_hbm, dat)
    greet()
    w_load.wait()

    def fill(r):
        heads = [dq[r, :, n * LANES : (n + 1) * LANES].astype(F32) for n in range(2)]
        heads.append(turn(dk[r], cosine[r], -sine[r]))
        lanes = three_lanes([close_halves(head) for head in heads] + [dv[r]])
        for n in range(3):
            dqkv[r, :, n * LANES : (n + 1) * LANES] = lanes[n].astype(BF)
        parts[r] = dot_nt(dqkv[r], w[:, :QKV]).astype(BF)

    count = a1.shape[2] // step

    def beside(turn_number):
        if turn_number == 0:
            a1_load.wait()
            dat_load.wait()
        half = (count + 1) // 2
        for number in range(turn_number * half, min((turn_number + 1) * half, count)):
            at = slice(number * step, (number + 1) * step)
            sums[at, :QKV] = flat_tn(a1, at, dqkv).astype(BF)
            sums[at, QKV:GAIN_AT] = flat_tn(dat, at, o).astype(BF)

    net = Scatter(here, parts, total, (from_c, via_x, via_y, from_x, from_y), (send, recv), fill).run(beside)
    da1 = total[...]
    x = h[...].astype(F32)
    r1 = inverse_of(x)
    n1 = x * r1
    e_out[...] = (dmid[...] + norm_back(da1, n1, r1, gain[0:1, :])).astype(BF)
    gain_rows[...] = jnp.zeros_like(gain_rows)
    first = GAIN_AT - PACK + LANES
    gain_rows[first : first + 1, :] = jnp.sum(da1 * n1, axis=0, keepdims=True)
    gain_rows[first + 1 : first + 2, :] = gain2_grad[...]
    columns = gain_rows[...].T
    last = sums[:, PACK - LANES :].astype(F32)
    sums[:, PACK - LANES :] = jnp.where(lane(last) < first, last, columns).astype(BF)
    net.drain()


def attn_back(h, dmid, gain, gain2_grad, dq, dk, dv, cosine, sine, o, a1, dat, w):
    block, width = h.shape
    step = math.gcd(width, 256)
    return plane_call(
        functools.partial(attn_back_kernel, step),
        "attn_back",
        3,
        [
            jax.ShapeDtypeStruct((block, width), BF),
            jax.ShapeDtypeStruct((width, PACK), BF),
        ],
        [IN_VMEM, IN_VMEM],
        [IN_VMEM] * 10 + [ANYWHERE] * 3,
        [
            pltpu.VMEM((8, block, width), BF),
            pltpu.VMEM((8, block, width), BF),
            pltpu.VMEM((8, block, width), BF),
            pltpu.VMEM(w.shape, BF),
            pltpu.VMEM((8, block, QKV), BF),
            pltpu.VMEM((LANES, width), F32),
            pltpu.VMEM((block, width), F32),
        ]
        + scatter_scratch(block, width)
        + [pltpu.SemaphoreType.DMA((3,))],
        36,
        h, dmid, gain, gain2_grad, dq, dk, dv, cosine, sine, o, a1, dat, w,
    )


def exchange_kernel(homeward, blocks, got, send_sem, recv_sem, local, swap=None):
    here = place()
    x, c, y = here
    swap = swap and Swap(homeward, *swap)
    masks = [(dx, dc, dy) for dx in range(2) for dc in range(2) for dy in range(2)][1:]
    peer = lambda mask: {"x": flip(x, mask[0]), "c": flip(c, mask[1]), "y": flip(y, mask[2])}
    own = rank_of(here, 0, 0, 0)
    mine = pltpu.make_async_copy(blocks.at[own], got.at[own], local)
    mine.start()
    barrier = pltpu.get_barrier_semaphore()
    for mask in masks:
        pl.semaphore_signal(barrier, inc=1, device_id=peer(mask), device_id_type=MESH)
    if swap is None:
        pl.semaphore_wait(barrier, 7)
    else:
        swap.greet(barrier)
        swap.met(barrier, 7)
        swap.start()

    def copy(n, src, dst):
        return pltpu.make_async_remote_copy(
            src_ref=src,
            dst_ref=dst,
            send_sem=send_sem.at[n],
            recv_sem=recv_sem.at[n],
            device_id=peer(masks[n]),
            device_id_type=MESH,
        )

    copies = [copy(n, blocks.at[rank_of(here, *mask)], got.at[own]) for n, mask in enumerate(masks)]
    for started in copies:
        started.start()
    mine.wait()
    for n, mask in enumerate(masks):
        where = got.at[rank_of(here, *mask)]
        copy(n, where, where).wait_recv()
    for started in copies:
        started.wait_send()
    if swap is not None:
        swap.wait()


def exchange(number, blocks, moving=None, homeward=False):
    return plane_call(
        functools.partial(exchange_kernel, homeward),
        "exchange",
        number,
        [jax.ShapeDtypeStruct(blocks.shape, BF)],
        [ANYWHERE],
        [ANYWHERE],
        [pltpu.SemaphoreType.DMA((7,)), pltpu.SemaphoreType.DMA((7,)), pltpu.SemaphoreType.DMA],
        blocks.size // 40000,
        blocks,
        moving=moving,
    )


def finish_kernel(ff, got, gate, up, down):
    gate[...] = got[0, :, :ff].astype(F32)
    up[...] = got[0, :, ff : 2 * ff].astype(F32)
    down[...] = got[0, :, 2 * ff :].astype(F32)


def finish(got):
    ranks, rows, cols = got.shape
    ff = cols // 3
    return pl.pallas_call(
        functools.partial(finish_kernel, ff),
        grid=(ranks,),
        out_shape=[jax.ShapeDtypeStruct((rows, ranks * ff), F32)] * 3,
        in_specs=[pl.BlockSpec((1, rows, cols), lambda i: (i, 0, 0))],
        out_specs=[pl.BlockSpec((rows, ff), lambda i: (0, i))] * 3,
        compiler_params=pltpu.CompilerParams(vmem_limit_bytes=VMEM_LIMIT),
        name="finish",
    )(got)


def finish_attn_kernel(got, query, key, value, out, gains):
    ranks = got.shape[0]

    def lanes(t, n):
        return got[t, :, n * LANES : (n + 1) * LANES].astype(F32)

    groups = [four_heads(*(lanes(t, n) for n in range(3))) for t in range(ranks)]

    def write(ref, heads):
        for n in range(0, len(heads), 4):
            for j, part in enumerate(three_lanes(heads[n : n + 4])):
                at = n * HEAD_SIZE + j * LANES
                ref[:, at : at + LANES] = part

    write(query, [head for group in groups for head in group[:2]])
    write(key, [group[2] for group in groups])
    write(value, [group[3] for group in groups])
    out_heads = []
    total = None
    for t in range(ranks):
        a, b = lanes(t, 3), lanes(t, 4)
        out_heads += [a, pltpu.roll(jnp.where(lane(a) >= HEAD_SIZE, a, b), LANES - HEAD_SIZE, 1)]
        total = b if total is None else total + b
    write(out, out_heads)
    first = GAIN_AT - PACK + LANES
    gains[...] = total.T[first : first + 2]


def finish_attn(got):
    ranks, rows, _ = got.shape
    wide, narrow = jax.ShapeDtypeStruct((rows, ranks * OUT), F32), jax.ShapeDtypeStruct((rows, ranks * HEAD_SIZE), F32)
    return pl.pallas_call(
        finish_attn_kernel,
        out_shape=[wide, narrow, narrow, wide, jax.ShapeDtypeStruct((2, rows), F32)],
        in_specs=[IN_VMEM],
        out_specs=[IN_VMEM] * 5,
        compiler_params=pltpu.CompilerParams(vmem_limit_bytes=VMEM_LIMIT),
        name="finish_attn",
    )(got)


LOWER=-1e30
def dot(a, b, dims):
    return lax.dot_general(a, b, (dims, ((), ())), preferred_element_type=F32)

def attend_kernel(scale2, bq, bk, bounds, length, q, k, v, qpos, out, lse):
    groups = q.shape[0]
    i = pl.program_id(0)
    rows = groups * bq
    qs = q[...].reshape(rows, LANES)
    pos = qpos[0]
    pos2 = jnp.concatenate([pos] * groups, axis=1)
    def step(masked, j, state):
        top, total, acc = state
        at = pl.ds(pl.multiple_of(j * bk, bk), bk)
        s = dot(k[at, :], qs, ((1,), (1,)))
        if masked:
            kp = j * bk + lax.broadcasted_iota(jnp.int32, (bk, 1), 0)
            ok = (kp <= pos2) & (kp < length[0])
            s = jnp.where(ok, s, LOWER)
        new = jnp.maximum(top, jnp.max(s, axis=0, keepdims=True) * scale2)
        p = jnp.exp2(s * scale2 - new)
        alpha = jnp.exp2(top - new)
        total = total * alpha + jnp.sum(p, axis=0, keepdims=True)
        acc = acc * alpha + dot(v[at, :], p.astype(BF), ((0,), (0,)))
        return new, total, acc
    state = (jnp.full((1, rows), LOWER, F32), jnp.zeros((1, rows), F32), jnp.zeros((LANES, rows), F32))
    full, end = bounds[0, i], bounds[1, i]
    state = lax.fori_loop(0, full, functools.partial(step, False), state)
    top, total, acc = lax.fori_loop(full, end, functools.partial(step, True), state)
    o = (acc / total).T
    first, second = o[:bq], pltpu.roll(o[bq:], HEAD_SIZE, 1)
    out[:, :LANES] = jnp.where(lane(first) < HEAD_SIZE, first, second).astype(BF)
    out[:, LANES:] = second[:, : OUT - LANES].astype(BF)
    lse[...] = (top + jnp.log2(total))[None]

def attend(q, k, v, qpos, bounds, length, bq, bk, scale2):
    groups, tokens, _ = q.shape
    n = tokens // bq
    out, lse = pl.pallas_call(
        functools.partial(attend_kernel, scale2, bq, bk),
        grid_spec=pltpu.PrefetchScalarGridSpec(
            num_scalar_prefetch=2, grid=(n,),
            in_specs=[
                pl.BlockSpec((groups, bq, LANES), lambda i, *_: (0, i, 0)),
                pl.BlockSpec(k.shape, lambda i, *_: (0, 0)),
                pl.BlockSpec(v.shape, lambda i, *_: (0, 0)),
                pl.BlockSpec((1, 1, bq), lambda i, *_: (i, 0, 0)),
            ],
            out_specs=[
                pl.BlockSpec((bq, OUT), lambda i, *_: (i, 0)),
                pl.BlockSpec((1, 1, groups * bq), lambda i, *_: (i, 0, 0)),
            ]),
        out_shape=[jax.ShapeDtypeStruct((tokens, OUT), BF), jax.ShapeDtypeStruct((n, 1, groups * bq), F32)],
        compiler_params=pltpu.CompilerParams(vmem_limit_bytes=VMEM_LIMIT),
        name="attend",
        cost_estimate=pl.CostEstimate(flops=0, bytes_accessed=45000000, transcendentals=0),
    )(bounds, length, q, k, v, qpos)
    return out, lse

def back_kernel(scale, scale2, bq, bk, bounds, length, q, k, v, qpos, o, do, lse, cosine, sine, dq, dk, dv):
    groups = q.shape[0]
    i = pl.program_id(0)
    @pl.when(i == 0)
    def _():
        dk[...] = jnp.zeros_like(dk)
        dv[...] = jnp.zeros_like(dv)
    qs = q[...].reshape(groups * bq, LANES)
    do0, do1 = do[:, :LANES].astype(F32), do[:, LANES : 2 * LANES].astype(F32)
    at = lane(do0)
    do1 = pltpu.roll(jnp.where(at >= HEAD_SIZE, do0, do1), LANES - HEAD_SIZE, 1)
    wide = jnp.concatenate([jnp.where(at < HEAD_SIZE, do0, 0.0), jnp.where(at < HEAD_SIZE, do1, 0.0)], axis=0)
    dos = wide.astype(BF)
    o0 = o[:, :LANES].astype(F32)
    o1 = jnp.concatenate([o[:, LANES:].astype(F32), jnp.zeros((bq, 2 * LANES - OUT), F32)], axis=1)
    o1 = pltpu.roll(jnp.where(at >= HEAD_SIZE, o0, o1), LANES - HEAD_SIZE, 1)
    delta = jnp.sum(wide * jnp.concatenate([o0, o1], axis=0), axis=1, keepdims=True).reshape(1, groups * bq)
    lse_row = lse[0]
    pos = qpos[0]
    pos2 = jnp.concatenate([pos] * groups, axis=1)
    def step(masked, j, acc):
        at = pl.ds(pl.multiple_of(j * bk, bk), bk)
        kb, vb = k[at, :], v[at, :]
        s = dot(kb, qs, ((1,), (1,)))
        p = jnp.exp2(s * scale2 - lse_row)
        if masked:
            kp = j * bk + lax.broadcasted_iota(jnp.int32, (bk, 1), 0)
            ok = (kp <= pos2) & (kp < length[0])
            p = jnp.where(ok, p, 0.0)
        dp = dot(vb, dos, ((1,), (1,)))
        ds = (p * (dp - delta)).astype(BF)
        dv[at, :] += dot(p.astype(BF), dos, ((1,), (0,)))
        dk[at, :] += dot(ds, qs, ((1,), (0,))) * scale
        return acc + dot(ds, kb, ((0,), (0,)))
    full, end = bounds[0, i], bounds[1, i]
    acc = jnp.zeros((groups * bq, LANES), F32)
    acc = lax.fori_loop(0, full, functools.partial(step, False), acc)
    acc = lax.fori_loop(full, end, functools.partial(step, True), acc) * scale
    for g in range(groups):
        dq[:, g * LANES:(g + 1) * LANES] = turn(acc[g * bq:(g + 1) * bq], cosine[...], -sine[...]).astype(BF)

def attend_back(q, k, v, qpos_row, o, do, lse, cosine, sine, bounds, length, bq, bk, scale, scale2):
    groups, tokens, _ = q.shape
    n = tokens // bq
    wide = pl.BlockSpec((bq, groups * LANES), lambda i, *_: (i, 0))
    narrow = pl.BlockSpec((bq, OUT), lambda i, *_: (i, 0))
    return pl.pallas_call(
        functools.partial(back_kernel, scale, scale2, bq, bk),
        grid_spec=pltpu.PrefetchScalarGridSpec(
            num_scalar_prefetch=2, grid=(n,),
            in_specs=[
                pl.BlockSpec((groups, bq, LANES), lambda i, *_: (0, i, 0)),
                pl.BlockSpec(k.shape, lambda i, *_: (0, 0)),
                pl.BlockSpec(v.shape, lambda i, *_: (0, 0)),
                pl.BlockSpec((1, 1, bq), lambda i, *_: (i, 0, 0)),
                narrow, wide,
                pl.BlockSpec((1, 1, groups * bq), lambda i, *_: (i, 0, 0)),
                pl.BlockSpec((bq, LANES), lambda i, *_: (i, 0)),
                pl.BlockSpec((bq, LANES), lambda i, *_: (i, 0)),
            ],
            out_specs=[wide, pl.BlockSpec(k.shape, lambda i, *_: (0, 0)), pl.BlockSpec(k.shape, lambda i, *_: (0, 0))]),
        out_shape=[jax.ShapeDtypeStruct((tokens, groups * LANES), BF), jax.ShapeDtypeStruct(k.shape, F32), jax.ShapeDtypeStruct(k.shape, F32)],
        compiler_params=pltpu.CompilerParams(vmem_limit_bytes=VMEM_LIMIT),
        name="attend_back",
        cost_estimate=pl.CostEstimate(flops=0, bytes_accessed=65000000, transcendentals=0),
    )(bounds, length, q, k, v, qpos_row, o, do, lse, cosine, sine)

def bounds_of(positions, length, bq, bk):
    p = positions.reshape(-1, bq)
    lo = jnp.minimum(jnp.min(p, axis=1) + 1, length) // bk
    hi = -(-jnp.minimum(jnp.max(p, axis=1) + 1, length) // bk)
    return jnp.stack([lo, hi]).astype(jnp.int32)


PLANE = ("x", "c", "y")

def together(*arrays):
    return lax.optimization_barrier(arrays)


def body(
    inputs,
    lengths,
    cotangent,
    attn_gain,
    w_query,
    key_projection,
    value_projection,
    w_out,
    mlp_gain,
    w_gate,
    w_up,
    w_down,
):
    sections = lax.axis_size("x") * lax.axis_size("c")
    planes = lax.axis_size("z")
    halves = lax.axis_size("y")
    extra = lax.axis_size("e")
    ranks = sections * halves
    layers = sections
    block = inputs.shape[1]
    width = inputs.shape[2]
    rows = w_query.shape[1]
    tokens = block * ranks
    all_tokens = tokens * extra
    head_group = QUERY_HEADS // KEY_VALUE_HEADS
    q_cols = head_group * HEAD_SIZE
    kv_cols = HEAD_SIZE
    ff_cols = FF // ranks
    scale = 1.0 / math.sqrt(HEAD_SIZE)
    scale2 = scale * math.log2(math.e)

    def by_rank(matrix):
        return matrix.reshape(rows, ranks, -1)

    attn_pack = jnp.concatenate(
        [
            by_rank(w_query[0]),
            by_rank(key_projection[0]),
            by_rank(value_projection[0]),
            by_rank(w_out[0].T),
            jnp.broadcast_to(jnp.stack([attn_gain[0], mlp_gain[0]], axis=1)[:, None, :], (rows, ranks, 2)),
            jnp.zeros((rows, ranks, PACK - GAIN_AT - 2), F32),
        ],
        axis=2,
    )
    mlp_pack = jnp.concatenate(
        [by_rank(w_gate[0]), by_rank(w_up[0]), by_rank(w_down[0].T)], axis=2
    )

    def by_layer(got):
        return got.reshape(layers, halves, rows, -1)

    def ready(pack):
        return jnp.swapaxes(pack.astype(BF), 0, 1)

    def whole(part):
        if extra > 1:
            part = lax.all_gather(part, "e", axis=1, tiled=False)
        return lax.all_gather(part.reshape(-1, part.shape[-1]), "z", axis=0, tiled=True)

    def reduce_rows(sums):
        mine = lax.psum_scatter(sums, "z", scatter_dimension=0, tiled=True)
        mine = mine.reshape(halves, extra, rows, -1)
        if extra > 1:
            return lax.psum_scatter(mine, "e", scatter_dimension=1, tiled=False)
        return mine[:, 0]

    cut = 3 * ff_cols // 2
    mlp_blocks = ready(mlp_pack)
    attn_got, hidden_state = exchange(4, ready(attn_pack), inputs[0])
    first_blocks, attn_got = together(mlp_blocks[..., :cut], attn_got)
    (first_got,) = exchange(5, first_blocks)

    token_x, token_c, token_y = token_place()
    rank = (token_x * 2 + token_c) * halves + token_y
    spot = lax.axis_index("e")
    length = lengths[micro_of_plane()]

    block_start = (jnp.arange(ranks) * extra + spot) * block
    positions = (block_start[:, None] + jnp.arange(block)[None, :]).reshape(tokens)
    exponents = 2.0 * jnp.arange(HEAD_SIZE // 2).astype(F32) / HEAD_SIZE
    angles = positions.astype(F32)[:, None] * (THETA ** (-exponents))[None, :]
    table = lambda values: jnp.pad(values, ((0, 0), (0, LANES // 2 - HALF)))
    cosine = jnp.concatenate([table(jnp.cos(angles))] * 2, axis=1)
    sine = jnp.concatenate([table(-jnp.sin(angles)), table(jnp.sin(angles))], axis=1)
    bq = math.gcd(tokens, 512)
    bk = math.gcd(all_tokens, 512)
    bounds = bounds_of(positions, length, bq, bk)
    length1 = length.reshape(1)
    query_rows = positions.astype(jnp.int32).reshape(-1, 1, bq)

    def all_keys(array):
        if extra == 1:
            return array
        stacked = lax.all_gather(array.reshape(ranks, block, -1), "e", axis=1, tiled=False)
        return stacked.reshape(all_tokens, -1)

    def own_keys(array):
        if extra == 1:
            return array
        stacked = array.astype(BF).reshape(ranks, extra, block, -1)
        return lax.psum_scatter(stacked, "e", scatter_dimension=1, tiled=False).reshape(tokens, -1).astype(F32)

    cosine3 = cosine.reshape(ranks, block, LANES)
    sine3 = sine.reshape(ranks, block, LANES)

    second_blocks, first_got, cosine, sine, cosine3, sine3, bounds, query_rows = together(
        mlp_blocks[..., cut:], first_got, cosine, sine, cosine3, sine3, bounds, query_rows
    )
    (second_got,) = exchange(6, second_blocks)
    attn_parts, first_parts, second_parts = by_layer(attn_got), by_layer(first_got), by_layer(second_got)

    def flat(array):
        return array.reshape(tokens, array.shape[-1])

    saved = []
    attn_w, w_1 = whole(attn_parts[0]), whole(first_parts[0])
    hidden_state, attn_w, w_1, second_part = together(hidden_state, attn_w, w_1, second_parts[0])
    w_2 = whole(second_part)
    for layer in range(layers):
        a1, q, k, v, gain = attn_in(hidden_state, attn_w, cosine3, sine3)
        q, k, v = q.reshape(head_group, tokens, LANES), all_keys(flat(k)), all_keys(flat(v))
        o, log_total = attend(q, k, v, query_rows, bounds, length1, bq, bk, scale2)
        if layer + 1 < layers:
            o, attn_part, first_part = together(o, attn_parts[layer + 1], first_parts[layer + 1])
            next_attn, next_1 = whole(attn_part), whole(first_part)
        mid, a2, gu, hid, after_mlp, *moved = mlp(
            hidden_state, o.reshape(ranks, block, -1), gain, attn_w, w_1, w_2,
            cotangent[0] if layer + 1 == layers else None,
        )
        saved.append((hidden_state, a1, q, k, v, o, log_total, mid, a2, gu, hid, attn_w, w_1, w_2, gain))
        hidden_state = after_mlp
        if layer + 1 < layers:
            hidden_state, attn_w, w_1, second_part = together(hidden_state, next_attn, next_1, second_parts[layer + 1])
            w_2 = whole(second_part)
    output = hidden_state

    my_positions = (rank * extra + spot) * block + jnp.arange(block)
    (e,) = moved
    e = jnp.where((my_positions < length)[:, None], e, jnp.zeros_like(e))
    attn_grads = [None] * layers
    mlp_grads = [None] * layers
    for layer in reversed(range(layers)):
        (h, a1, q, k, v, o, log_total, mid, a2, gu, hid, attn_w, w_1, w_2, gain) = saved[layer]
        dmid, gain2, dat, mlp_sums, *moved = mlp_back(
            e, mid, gain, gu, hid, a2, w_1, w_2, output if layer + 1 == layers else None
        )
        if moved:
            (output,) = moved
        else:
            dat, mlp_sums, attn_grads[layer + 1] = together(dat, mlp_sums, attn_grads[layer + 1])
        mlp_grads[layer] = reduce_rows(mlp_sums)
        dat, dob = dat_gather(dat, attn_w)
        dq, dk, dv = attend_back(
            q, k, v, query_rows, o, flat(dob), log_total, cosine, sine, bounds, length1, bq, bk, scale, scale2
        )
        dk, dv = own_keys(dk), own_keys(dv)
        e, attn_sums = attn_back(
            h, dmid, gain, gain2, *(array.reshape(ranks, block, -1) for array in (dq, dk, dv)), cosine3, sine3,
            o.reshape(ranks, block, -1), a1, dat, attn_w,
        )
        e, attn_sums, mlp_grads[layer] = together(e, attn_sums, mlp_grads[layer])
        attn_grads[layer] = reduce_rows(attn_sums)

    def by_place(grads):
        return jnp.stack(grads).reshape(ranks, rows, -1)

    (mlp_home,) = exchange(7, by_place(mlp_grads))
    attn_blocks, mlp_home = together(by_place(attn_grads), mlp_home)
    attn_home, input_grad = exchange(10, attn_blocks, e, True)
    grad_gate, grad_up, grad_down = finish(mlp_home)
    grad_query, grad_key, grad_value, grad_out, gain_sums = finish_attn(attn_home)
    return (
        output[None],
        input_grad[None],
        gain_sums[0:1],
        grad_query[None],
        grad_key[None],
        grad_value[None],
        grad_out.T[None],
        gain_sums[1:2],
        grad_gate[None],
        grad_up[None],
        grad_down.T[None],
    )


def solution(mesh):
    section, seq = mesh.devices.shape
    halves = KEY_VALUE_HEADS // section
    extra = seq // (section * halves)
    fine = Mesh(
        mesh.devices.reshape(section // 2, 2, section, halves, extra), ("x", "c", "z", "y", "e")
    )
    sec, sq = ("x", "c"), ("z", "y", "e")
    rows3 = P(sec, sq, None)
    cols3 = P(sec, None, sq)
    in_specs = (rows3, P(), rows3, P(sec, sq), rows3, rows3, rows3, cols3, P(sec, sq), rows3, rows3, cols3)
    out_specs = (rows3, rows3, P(sec, sq), rows3, rows3, rows3, cols3, P(sec, sq), rows3, rows3, cols3)
    return jax.shard_map(body, mesh=fine, in_specs=in_specs, out_specs=out_specs, check_vma=False)
```

```python
import functools
import math

import jax
import jax.numpy as jnp
from jax import lax
from jax.experimental import pallas as pl
from jax.experimental.pallas import tpu as pltpu
from jax.sharding import Mesh
from jax.sharding import PartitionSpec as P

QUERY_HEADS = 16
KEY_VALUE_HEADS = 8
HEAD_SIZE = 96
FF = 4096

EPS = 1e-05
THETA = 100000.0
LOWER_LIMIT = -1e30

BF = jnp.bfloat16
F32 = jnp.float32

LANES = 128
HALF = HEAD_SIZE // 2
VMEM_LIMIT = 56 * 1024 * 1024


def dot(a, b, dims):
    return lax.dot_general(a, b, (dims, ((), ())), preferred_element_type=F32)


def dot_nn(a, b):
    return dot(a, b, ((1,), (0,)))


def dot_nt(a, b):
    return dot(a, b, ((1,), (1,)))


def dot_tn(a, b):
    return dot(a, b, ((0,), (0,)))


MESH = pl.DeviceIdType.MESH

OWN, X, Y, D = (0, 0), (1, 0), (0, 1), (1, 1)


def place():
    return lax.axis_index("x"), lax.axis_index("c"), lax.axis_index("y")


def xor(a, b):
    return a + b - 2 * a * b


def token_place():
    x, c, y = place()
    z = lax.axis_index("z")
    return xor(x, xor(lax.rem(z, 2), z // 2)), c, y


def micro_of_plane():
    z = lax.axis_index("z")
    return lax.rem(z, 2) * 2 + z // 2


def flip(index, by):
    return 1 - index if by else index


def rank_of(here, dx, dc, dy):
    x, c, y = here
    return (flip(x, dx) * 2 + flip(c, dc)) * 2 + flip(y, dy)


class Swap:
    def __init__(self, homeward, moving, moved, sem):
        x, c, _ = place()
        z = lax.axis_index("z")
        low = lax.rem(z, 2)
        high = z // 2
        out = {"x": xor(high, xor(x, c)), "c": low, "z": c * 2 + x}
        back = {"x": low, "c": high, "z": 2 * xor(x, xor(low, high)) + c}
        target, self.source = (back, out) if homeward else (out, back)
        self.away = (target["x"] != x) | (target["c"] != c) | (target["z"] != z)
        self.remote = pltpu.make_async_remote_copy(
            src_ref=moving,
            dst_ref=moved,
            send_sem=sem.at[0],
            recv_sem=sem.at[1],
            device_id=target,
            device_id_type=MESH,
        )
        self.local = pltpu.make_async_copy(moving, moved, sem.at[2])

    def greet(self, barrier):
        @pl.when(self.away)
        def _():
            pl.semaphore_signal(barrier, inc=1, device_id=self.source, device_id_type=MESH)

    def either(self, remote, local):
        pl.when(self.away)(remote)
        pl.when(jnp.logical_not(self.away))(local)

    def start(self):
        self.either(lambda: self.remote.start(), lambda: self.local.start())

    def met(self, barrier, count):
        self.either(lambda: pl.semaphore_wait(barrier, count + 1), lambda: pl.semaphore_wait(barrier, count))

    def wait(self):
        self.either(lambda: self.remote.wait(), lambda: self.local.wait())


def with_swap(kernel, inputs, outputs):
    def wrapped(*refs):
        last = inputs + 1 + outputs
        kernel(
            *refs[:inputs],
            *refs[inputs + 1 : last],
            *refs[last + 1 : -1],
            swap=(refs[inputs], refs[last], refs[-1]),
        )

    return wrapped


def greet(swap=None):
    x, c, y = place()
    barrier = pltpu.get_barrier_semaphore()
    for peer in ({"x": 1 - x}, {"c": 1 - c}, {"y": 1 - y}):
        pl.semaphore_signal(barrier, inc=1, device_id=peer, device_id_type=MESH)
    if swap is None:
        pl.semaphore_wait(barrier, 3)
    else:
        swap.greet(barrier)
        swap.met(barrier, 3)
        swap.start()


class Sender:
    def __init__(self, send_sem, recv_sem):
        x, c, y = place()
        self.peers = {"x": {"x": 1 - x}, "c": {"c": 1 - c}, "y": {"y": 1 - y}}
        self.send_sem, self.recv_sem = send_sem, recv_sem
        self.sent = []

    def copy(self, src, dst, index, to, number):
        return pltpu.make_async_remote_copy(
            src_ref=src,
            dst_ref=dst,
            send_sem=self.send_sem.at[number],
            recv_sem=self.recv_sem.at[index],
            device_id=self.peers[to],
            device_id_type=MESH,
        )

    def send(self, src, dst, index, to):
        started = self.copy(src, dst, index, to, len(self.sent))
        started.start()
        self.sent.append(started)

    def arrived(self, where, index):
        self.copy(where, where, index, "c", 0).wait_recv()

    def drain(self):
        for started in self.sent:
            started.wait_send()


class Gather:
    def __init__(self, here, full, sems):
        self.here, self.full = here, full
        self.piece = full.shape[1] // 4
        self.net = Sender(*sems)

    def index(self, role, chunk):
        return (role[0] * 4 + role[1] * 2 + role[2]) * 4 + chunk

    def slot(self, role, chunk):
        return self.full.at[rank_of(self.here, *role), pl.ds(chunk * self.piece, self.piece)]

    def send(self, role, chunk, to, as_role):
        where = self.slot(role, chunk)
        self.net.send(where, where, self.index(as_role, chunk), to)

    def arrived(self, role, chunk):
        self.net.arrived(self.slot(role, chunk), self.index(role, chunk))

    def own(self, cx, cy):
        self.send((0, 0, 0), cx, "x", (1, 0, 0))
        self.send((0, 0, 0), cy, "y", (0, 0, 1))

    def all_own(self):
        for cx, cy in ((2, 0), (3, 1), (0, 2), (1, 3)):
            self.own(cx, cy)
        return self

    def run(self, on_block, before_last=None):
        send, arrived = self.send, self.arrived
        at_x, at_y, at_d, at_c = (1, 0, 0), (0, 0, 1), (1, 0, 1), (0, 1, 0)
        xc, yc, dc = (1, 1, 0), (0, 1, 1), (1, 1, 1)

        def whole(role):
            for chunk in range(4):
                arrived(role, chunk)

        def done(role):
            on_block(rank_of(self.here, *role))

        def pass_on(cx, cy):
            arrived(at_x, cx)
            if cx >= 2:
                send(at_x, cx, "y", at_d)
            send(at_x, cx, "c", xc)
            arrived(at_y, cy)
            if cy < 2:
                send(at_y, cy, "x", at_d)
            send(at_y, cy, "c", yc)

        def pass_last(chunks):
            for chunk in chunks:
                arrived(at_d, chunk)
                send(at_d, chunk, "c", dc)

        for chunk in range(4):
            send((0, 0, 0), chunk, "c", at_c)
        done((0, 0, 0))
        pass_on(2, 0)
        whole(at_c)
        done(at_c)
        pass_on(3, 1)
        pass_on(0, 2)
        pass_on(1, 3)
        done(at_x)
        done(at_y)
        pass_last((0, 2))
        whole(xc)
        done(xc)
        whole(yc)
        done(yc)
        if before_last is not None:
            before_last()
        pass_last((1, 3))
        done(at_d)
        whole(dc)
        done(dc)
        return self.net


def run_gather(here, full, sems, on_block, before_last=None):
    return Gather(here, full, sems).all_own().run(on_block, before_last)


class Scatter:
    order = (D, X, Y, OWN)

    def __init__(self, here, parts, total, bufs, sems, fill=None):
        self.here, self.parts, self.total, self.fill = here, parts, total, fill
        self.from_c, self.via_x, self.via_y, self.from_x, self.from_y = bufs
        half = parts.shape[1] // 2
        self.piece = half // 2
        self.lower, self.upper = pl.ds(0, half), pl.ds(half, half)
        self.net = Sender(*sems)

    def rank(self, n, dc):
        return rank_of(self.here, self.order[n][0], dc, self.order[n][1])

    def make(self, r):
        if self.fill is not None:
            self.fill(r)

    def sibling(self, n):
        r = self.rank(n, 1)
        self.make(r)
        self.net.send(self.parts.at[r], self.from_c.at[n], n, "c")

    def add(self, n, where, more):
        r = self.rank(n, 0)
        self.parts[r, where] = (self.parts[r, where].astype(F32) + more.astype(F32)).astype(BF)

    def mine(self, n, where):
        return self.parts.at[self.rank(n, 0), where]

    def combine(self, n):
        self.make(self.rank(n, 0))
        self.net.arrived(self.from_c.at[n], n)
        if n < 3:
            self.add(n, pl.ds(0, self.parts.shape[1]), self.from_c[n])

    def rows(self, number):
        return pl.ds(number * self.piece, self.piece)

    def to_diagonal(self):
        self.combine(0)
        for n in range(2):
            self.net.send(self.mine(0, self.rows(n + 2)), self.via_x.at[self.rows(n)], 4 + n, "x")
            self.net.send(self.mine(0, self.rows(n)), self.via_y.at[self.rows(n)], 6 + n, "y")

    def to_x(self):
        self.combine(1)
        self.net.send(self.mine(1, self.upper), self.from_x.at[self.upper], 8, "x")

    def to_y(self):
        self.combine(2)
        self.net.send(self.mine(2, self.lower), self.from_y.at[self.lower], 9, "y")

    def early(self):
        for n in (1, 2, 3):
            self.sibling(n)
        self.to_x()
        self.to_y()

    def run(self, beside=None, early_done=False, on_rows=None):
        net, total, lower, upper = self.net, self.total, self.lower, self.upper
        self.sibling(0)
        self.to_diagonal()
        if not early_done:
            self.sibling(1)
            self.to_x()
            self.sibling(2)
            self.to_y()
            self.sibling(3)
        self.combine(3)
        total[...] = self.parts[self.rank(3, 0)].astype(F32) + self.from_c[3].astype(F32)
        if beside is not None:
            beside(0)
        for n in range(2):
            at, above = self.rows(n), self.rows(n + 2)
            net.arrived(self.via_y.at[at], 6 + n)
            self.add(1, at, self.via_y[at])
            net.send(self.mine(1, at), self.from_x.at[at], 10 + n, "x")
            net.arrived(self.via_x.at[at], 4 + n)
            self.add(2, above, self.via_x[at])
            net.send(self.mine(2, above), self.from_y.at[above], 12 + n, "y")
        if beside is not None:
            beside(1)
        net.arrived(self.from_x.at[upper], 8)
        net.arrived(self.from_y.at[lower], 9)
        total[upper] += self.from_x[upper].astype(F32)
        total[lower] += self.from_y[lower].astype(F32)
        for n in range(2):
            at, above = self.rows(n), self.rows(n + 2)
            net.arrived(self.from_x.at[at], 10 + n)
            net.arrived(self.from_y.at[above], 12 + n)
            total[at] += self.from_x[at].astype(F32)
            total[above] += self.from_y[above].astype(F32)
            if on_rows is not None:
                on_rows(n)
        return net


def gather_sems():
    return [pltpu.SemaphoreType.DMA((32,)), pltpu.SemaphoreType.DMA((32,))]


def scatter_scratch(block, width):
    half = block // 2
    return [
        pltpu.VMEM((4, block, width), BF),
        pltpu.VMEM((half, width), BF),
        pltpu.VMEM((half, width), BF),
        pltpu.VMEM((block, width), BF),
        pltpu.VMEM((block, width), BF),
        pltpu.SemaphoreType.DMA((14,)),
        pltpu.SemaphoreType.DMA((14,)),
    ]


class Loads:
    def __init__(self, sem):
        self.sem = sem
        self.count = 0

    def start(self, src, dst):
        copy = pltpu.make_async_copy(src, dst, self.sem.at[self.count])
        self.count += 1
        copy.start()
        return copy


def inverse_of(x):
    return lax.rsqrt(jnp.mean(x * x, axis=-1, keepdims=True) + EPS)


def lane(x):
    return lax.broadcasted_iota(jnp.int32, x.shape, 1)


def turn(head, cosine, sine):
    return head * cosine + pltpu.roll(head, LANES // 2, 1) * sine


def open_halves(head):
    return jnp.where(lane(head) < LANES // 2, head, pltpu.roll(head, LANES // 2 - HALF, 1))


def close_halves(head):
    low = lane(head) < LANES // 2
    return jnp.where(low, head, 0.0) + pltpu.roll(jnp.where(low, 0.0, head), LANES // 2 + HALF, 1)


def four_heads(a, b, c):
    at = lane(a)
    return (
        a,
        pltpu.roll(jnp.where(at >= 96, a, b), 32, 1),
        pltpu.roll(jnp.where(at >= 64, b, c), 64, 1),
        pltpu.roll(c, 96, 1),
    )


def three_lanes(heads):
    at = lane(heads[0])
    b, c, d = pltpu.roll(heads[1], 96, 1), pltpu.roll(heads[2], 64, 1), pltpu.roll(heads[3], 32, 1)
    return jnp.where(at < 96, heads[0], b), jnp.where(at < 64, b, c), jnp.where(at < 32, c, d)


def plane_call(kernel, name, number, out_shape, out_specs, in_specs, scratch, time_us, *operands, moving=None):
    if moving is not None:
        kernel = with_swap(kernel, len(in_specs), len(out_specs))
        out_shape = out_shape + [jax.ShapeDtypeStruct(moving.shape, moving.dtype)]
        in_specs, out_specs = in_specs + [ANYWHERE], out_specs + [ANYWHERE]
        scratch = scratch + [pltpu.SemaphoreType.DMA((3,))]
        operands = operands + (moving,)
    return pl.pallas_call(
        kernel,
        out_shape=out_shape,
        in_specs=in_specs,
        out_specs=out_specs,
        scratch_shapes=scratch,
        compiler_params=pltpu.CompilerParams(
            collective_id=number, has_side_effects=True, vmem_limit_bytes=VMEM_LIMIT
        ),
        cost_estimate=pl.CostEstimate(flops=0, bytes_accessed=time_us * 3000000, transcendentals=0),
        name=name,
    )(*operands)


ANYWHERE = pl.BlockSpec(memory_space=pl.ANY)
IN_VMEM = pl.BlockSpec(memory_space=pltpu.VMEM)
QKV = 4 * HEAD_SIZE
OUT = 2 * HEAD_SIZE
GAIN_AT = QKV + OUT
PACK = -(-(GAIN_AT + 2) // LANES) * LANES


def attn_in_kernel(h, w_hbm, cosine, sine, a1_out, q_out, k_out, v_out, gain_out, full, w, send, recv, local):
    here = token_place()
    loads = Loads(local)
    w_load = loads.start(w_hbm, w)
    x = h[...].astype(F32)
    n1 = x * inverse_of(x)
    w_load.wait()
    rows = w[:, PACK - LANES :].astype(F32).T
    gain_out[...] = rows[GAIN_AT - PACK + LANES : GAIN_AT - PACK + LANES + 2]
    full[rank_of(here, 0, 0, 0)] = (n1 * gain_out[0:1, :]).astype(BF)
    greet()
    saves = []

    def on_block(r):
        saves.append(loads.start(full.at[r], a1_out.at[r]))
        qkv = dot_nn(full[r], w[:, :QKV])
        heads = four_heads(*(qkv[:, n * LANES : (n + 1) * LANES] for n in range(3)))
        cos, sin = cosine[r], sine[r]
        for n in range(2):
            q_out[n, r] = turn(open_halves(heads[n]), cos, sin).astype(BF)
        k_out[r] = turn(open_halves(heads[2]), cos, sin).astype(BF)
        v_out[r] = jnp.where(lane(heads[3]) < HEAD_SIZE, heads[3], 0.0).astype(BF)

    net = run_gather(here, full, (send, recv), on_block)
    net.drain()
    for save in saves:
        save.wait()


def attn_in(h, w, cosine, sine):
    block, width = h.shape
    return plane_call(
        attn_in_kernel,
        "attn_in",
        0,
        [
            jax.ShapeDtypeStruct((8, block, width), BF),
            jax.ShapeDtypeStruct((2, 8, block, LANES), BF),
            jax.ShapeDtypeStruct((8, block, LANES), BF),
            jax.ShapeDtypeStruct((8, block, LANES), BF),
            jax.ShapeDtypeStruct((2, width), F32),
        ],
        [ANYWHERE, IN_VMEM, IN_VMEM, IN_VMEM, IN_VMEM],
        [IN_VMEM, ANYWHERE, IN_VMEM, IN_VMEM],
        [pltpu.VMEM((8, block, width), BF), pltpu.VMEM(w.shape, BF)]
        + gather_sems()
        + [pltpu.SemaphoreType.DMA((9,))],
        34,
        h, w, cosine, sine,
    )


def mlp_kernel(
    ff, homeward, h, o, gain, wa_hbm, w1_hbm, w2_hbm, mid_out, a2_out, gu_out, hid_out, next_out,
    full, parts, gu, hid, wa, wm, total,
    from_c, via_x, via_y, from_x, from_y, send1, recv1, send2, recv2,
    from_c3, via_x3, via_y3, from_x3, from_y3, send3, recv3, local, swap=None,
):
    here = token_place()
    swap = swap and Swap(homeward, *swap)
    loads = Loads(local)
    wa_load = loads.start(wa_hbm, wa)
    split = w1_hbm.shape[1]
    w1_load = loads.start(w1_hbm, wm.at[:, pl.ds(0, split)])
    w2_load = loads.start(w2_hbm, wm.at[:, pl.ds(split, 3 * ff - split)])
    greet(swap)
    wa_load.wait()

    def fill(r):
        parts[r] = dot_nt(o[r], wa[:, QKV:GAIN_AT]).astype(BF)

    bufs = (from_c, via_x, via_y, from_x, from_y)
    gather = Gather(here, full, (send2, recv2))
    own = rank_of(here, 0, 0, 0)

    def on_rows(n):
        for piece in (n + 2, n):
            rows = pl.ds(piece * gather.piece, gather.piece)
            mid = h[rows].astype(F32) + total[rows]
            mid_out[rows] = mid
            full[own, rows] = (mid * inverse_of(mid) * gain[1:2, :]).astype(BF)
        if n == 0:
            gather.own(2, 0)
        else:
            for pair in ((3, 1), (0, 2), (1, 3)):
                gather.own(*pair)

    net1 = Scatter(here, parts, total, bufs, (send1, recv1), fill).run(on_rows=on_rows)
    net1.drain()
    saves = []

    def on_block(r):
        if not saves:
            w1_load.wait()
            w2_load.wait()
        saves.append(loads.start(full.at[r], a2_out.at[r]))
        a2 = full[r]
        g = dot_nn(a2, wm[:, :ff])
        u = dot_nn(a2, wm[:, ff : 2 * ff])
        gu[r, :, :ff] = g.astype(BF)
        gu[r, :, ff:] = u.astype(BF)
        low = (g * (1.0 / (1.0 + jnp.exp(-g))) * u).astype(BF)
        hid[r] = low
        saves.append(loads.start(gu.at[r], gu_out.at[r]))
        saves.append(loads.start(hid.at[r], hid_out.at[r]))
        parts[r] = dot_nt(low, wm[:, 2 * ff :]).astype(BF)

    bufs3 = (from_c3, via_x3, via_y3, from_x3, from_y3)
    scatter = Scatter(here, parts, total, bufs3, (send3, recv3))
    net2 = gather.run(on_block, scatter.early)
    net3 = scatter.run(early_done=True)
    next_out[...] = (mid_out[...] + total[...]).astype(BF)
    net2.drain()
    net3.drain()
    for save in saves:
        save.wait()
    if swap is not None:
        swap.wait()


def mlp(h, o, gain, wa, w1, w2, moving=None):
    block, width = h.shape
    ff = (w1.shape[1] + w2.shape[1]) // 3
    return plane_call(
        functools.partial(mlp_kernel, ff, False),
        "mlp",
        1 if moving is None else 8,
        [
            jax.ShapeDtypeStruct((block, width), F32),
            jax.ShapeDtypeStruct((8, block, width), BF),
            jax.ShapeDtypeStruct((8, block, 2 * ff), BF),
            jax.ShapeDtypeStruct((8, block, ff), BF),
            jax.ShapeDtypeStruct((block, width), BF),
        ],
        [IN_VMEM, ANYWHERE, ANYWHERE, ANYWHERE, IN_VMEM],
        [IN_VMEM, IN_VMEM, IN_VMEM, ANYWHERE, ANYWHERE, ANYWHERE],
        [
            pltpu.VMEM((8, block, width), BF),
            pltpu.VMEM((8, block, width), BF),
            pltpu.VMEM((8, block, 2 * ff), BF),
            pltpu.VMEM((8, block, ff), BF),
            pltpu.VMEM(wa.shape, BF),
            pltpu.VMEM((width, 3 * ff), BF),
            pltpu.VMEM((block, width), F32),
        ]
        + scatter_scratch(block, width)
        + gather_sems()
        + scatter_scratch(block, width)
        + [pltpu.SemaphoreType.DMA((27,))],
        96,
        h, o, gain, wa, w1, w2,
        moving=moving,
    )


def norm_back(upstream, normed, inverse, gain_row):
    scaled = upstream * gain_row
    return inverse * (scaled - normed * jnp.mean(scaled * normed, axis=-1, keepdims=True))


def flat_tn(a, cols, b):
    total = dot_tn(a[0, :, cols], b[0])
    for n in range(1, a.shape[0]):
        total = total + dot_tn(a[n, :, cols], b[n])
    return total


def mlp_back_kernel(
    ff, step, homeward, e, mid, gain, gu_hbm, hid_hbm, a2_hbm, w1_hbm, w2_hbm, dmid_out, gain_out, dat_out, sums_out,
    full, parts, a2, gu, hid, wm, total, stage, send1, recv1,
    from_c, via_x, via_y, from_x, from_y, send2, recv2, local, swap=None,
):
    here = token_place()
    swap = swap and Swap(homeward, *swap)
    loads = Loads(local)
    split = w1_hbm.shape[1]
    w2_load = loads.start(w2_hbm, wm.at[:, pl.ds(split, 3 * ff - split)])
    gu_load = loads.start(gu_hbm, gu)
    w1_load = loads.start(w1_hbm, wm.at[:, pl.ds(0, split)])
    a2_load = loads.start(a2_hbm, a2)
    hid_load = loads.start(hid_hbm, hid)
    own = rank_of(here, 0, 0, 0)
    full[own] = e[...]
    greet(swap)
    w2_load.wait()
    gu_load.wait()
    w1_load.wait()

    def on_block(r):
        dhid = dot_nn(full[r], wm[:, 2 * ff :])
        g = gu[r, :, :ff].astype(F32)
        u = gu[r, :, ff:].astype(F32)
        sig = 1.0 / (1.0 + jnp.exp(-g))
        du = dhid * g * sig
        dg = dhid * u * sig * (1.0 + g * (1.0 - sig))
        gu[r, :, :ff] = dg.astype(BF)
        gu[r, :, ff:] = du.astype(BF)
        parts[r] = dot_nt(gu[r], wm[:, : 2 * ff]).astype(BF)

    scatter = Scatter(here, parts, total, (from_c, via_x, via_y, from_x, from_y), (send2, recv2))
    net1 = run_gather(here, full, (send1, recv1), on_block, scatter.early)
    a2_load.wait()
    hid_load.wait()
    sums = []
    count = full.shape[2] // step

    def beside(turn_number):
        half = (count + 1) // 2
        for number in range(turn_number * half, min((turn_number + 1) * half, count)):
            if number >= 2:
                sums[number - 2].wait()
            at = slice(number * step, (number + 1) * step)
            held = stage.at[number % 2]
            held[:, : 2 * ff] = flat_tn(a2, at, gu).astype(BF)
            held[:, 2 * ff :] = flat_tn(full, at, hid).astype(BF)
            sums.append(loads.start(held, sums_out.at[pl.ds(number * step, step)]))

    net2 = scatter.run(beside, True)
    da2 = total[...]
    m = mid[...]
    r2 = inverse_of(m)
    n2 = m * r2
    gain_out[...] = jnp.sum(da2 * n2, axis=0, keepdims=True)
    dmid = e[...].astype(F32) + norm_back(da2, n2, r2, gain[1:2, :])
    dmid_out[...] = dmid
    dat_out[...] = dmid.astype(BF)
    net1.drain()
    net2.drain()
    for save in sums[-2:]:
        save.wait()
    if swap is not None:
        swap.wait()


def dat_kernel(dat, wa_hbm, dat_out, dob_out, full, wa, send, recv, local):
    here = token_place()
    loads = Loads(local)
    wa_load = loads.start(wa_hbm, wa)
    full[rank_of(here, 0, 0, 0)] = dat[...]
    greet()
    wa_load.wait()
    saves = []

    def on_block(r):
        saves.append(loads.start(full.at[r], dat_out.at[r]))
        dob_out[r] = dot_nn(full[r], wa[:, QKV:PACK]).astype(BF)

    run_gather(here, full, (send, recv), on_block).drain()
    for save in saves:
        save.wait()


def dat_gather(dat, wa):
    block, width = dat.shape
    return plane_call(
        dat_kernel,
        "dat_gather",
        12,
        [jax.ShapeDtypeStruct((8, block, width), BF), jax.ShapeDtypeStruct((8, block, PACK - QKV), BF)],
        [ANYWHERE, IN_VMEM],
        [IN_VMEM, ANYWHERE],
        [pltpu.VMEM((8, block, width), BF), pltpu.VMEM(wa.shape, BF)] + gather_sems() + [pltpu.SemaphoreType.DMA((9,))],
        32,
        dat, wa,
    )


def mlp_back(e, mid, gain, gu, hid, a2, w1, w2, moving=None):
    block, width = e.shape
    ff = hid.shape[2]
    step = math.gcd(width, 256)
    return plane_call(
        functools.partial(mlp_back_kernel, ff, step, True),
        "mlp_back",
        2 if moving is None else 9,
        [
            jax.ShapeDtypeStruct((block, width), F32),
            jax.ShapeDtypeStruct((1, width), F32),
            jax.ShapeDtypeStruct((block, width), BF),
            jax.ShapeDtypeStruct((width, 3 * ff), BF),
        ],
        [IN_VMEM, IN_VMEM, IN_VMEM, ANYWHERE],
        [IN_VMEM, IN_VMEM, IN_VMEM] + [ANYWHERE] * 5,
        [
            pltpu.VMEM((8, block, width), BF),
            pltpu.VMEM((8, block, width), BF),
            pltpu.VMEM((8, block, width), BF),
            pltpu.VMEM((8, block, 2 * ff), BF),
            pltpu.VMEM((8, block, ff), BF),
            pltpu.VMEM((width, 3 * ff), BF),
            pltpu.VMEM((block, width), F32),
            pltpu.VMEM((2, step, 3 * ff), BF),
        ]
        + gather_sems()
        + scatter_scratch(block, width)
        + [pltpu.SemaphoreType.DMA((5 + width // step,))],
        68,
        e, mid, gain, gu, hid, a2, w1, w2,
        moving=moving,
    )


def attn_back_kernel(
    step, h, dmid, gain, gain2_grad, dq, dk, dv, cosine, sine, o, a1_hbm, dat_hbm, w_hbm, e_out, sums,
    parts, a1, dat, w, dqkv, gain_rows, total, from_c, via_x, via_y, from_x, from_y, send, recv, local,
):
    here = token_place()
    loads = Loads(local)
    w_load = loads.start(w_hbm, w)
    a1_load = loads.start(a1_hbm, a1)
    dat_load = loads.start(dat_hbm, dat)
    greet()
    w_load.wait()

    def fill(r):
        heads = [dq[r, :, n * LANES : (n + 1) * LANES].astype(F32) for n in range(2)]
        heads.append(turn(dk[r], cosine[r], -sine[r]))
        lanes = three_lanes([close_halves(head) for head in heads] + [dv[r]])
        for n in range(3):
            dqkv[r, :, n * LANES : (n + 1) * LANES] = lanes[n].astype(BF)
        parts[r] = dot_nt(dqkv[r], w[:, :QKV]).astype(BF)

    count = a1.shape[2] // step

    def beside(turn_number):
        if turn_number == 0:
            a1_load.wait()
            dat_load.wait()
        half = (count + 1) // 2
        for number in range(turn_number * half, min((turn_number + 1) * half, count)):
            at = slice(number * step, (number + 1) * step)
            sums[at, :QKV] = flat_tn(a1, at, dqkv).astype(BF)
            sums[at, QKV:GAIN_AT] = flat_tn(dat, at, o).astype(BF)

    net = Scatter(here, parts, total, (from_c, via_x, via_y, from_x, from_y), (send, recv), fill).run(beside)
    da1 = total[...]
    x = h[...].astype(F32)
    r1 = inverse_of(x)
    n1 = x * r1
    e_out[...] = (dmid[...] + norm_back(da1, n1, r1, gain[0:1, :])).astype(BF)
    gain_rows[...] = jnp.zeros_like(gain_rows)
    first = GAIN_AT - PACK + LANES
    gain_rows[first : first + 1, :] = jnp.sum(da1 * n1, axis=0, keepdims=True)
    gain_rows[first + 1 : first + 2, :] = gain2_grad[...]
    columns = gain_rows[...].T
    last = sums[:, PACK - LANES :].astype(F32)
    sums[:, PACK - LANES :] = jnp.where(lane(last) < first, last, columns).astype(BF)
    net.drain()


def attn_back(h, dmid, gain, gain2_grad, dq, dk, dv, cosine, sine, o, a1, dat, w):
    block, width = h.shape
    step = math.gcd(width, 256)
    return plane_call(
        functools.partial(attn_back_kernel, step),
        "attn_back",
        3,
        [
            jax.ShapeDtypeStruct((block, width), BF),
            jax.ShapeDtypeStruct((width, PACK), BF),
        ],
        [IN_VMEM, IN_VMEM],
        [IN_VMEM] * 10 + [ANYWHERE] * 3,
        [
            pltpu.VMEM((8, block, width), BF),
            pltpu.VMEM((8, block, width), BF),
            pltpu.VMEM((8, block, width), BF),
            pltpu.VMEM(w.shape, BF),
            pltpu.VMEM((8, block, QKV), BF),
            pltpu.VMEM((LANES, width), F32),
            pltpu.VMEM((block, width), F32),
        ]
        + scatter_scratch(block, width)
        + [pltpu.SemaphoreType.DMA((3,))],
        36,
        h, dmid, gain, gain2_grad, dq, dk, dv, cosine, sine, o, a1, dat, w,
    )


def exchange_kernel(homeward, blocks, got, send_sem, recv_sem, local, swap=None):
    here = place()
    x, c, y = here
    swap = swap and Swap(homeward, *swap)
    masks = [(dx, dc, dy) for dx in range(2) for dc in range(2) for dy in range(2)][1:]
    peer = lambda mask: {"x": flip(x, mask[0]), "c": flip(c, mask[1]), "y": flip(y, mask[2])}
    own = rank_of(here, 0, 0, 0)
    mine = pltpu.make_async_copy(blocks.at[own], got.at[own], local)
    mine.start()
    barrier = pltpu.get_barrier_semaphore()
    for mask in masks:
        pl.semaphore_signal(barrier, inc=1, device_id=peer(mask), device_id_type=MESH)
    if swap is None:
        pl.semaphore_wait(barrier, 7)
    else:
        swap.greet(barrier)
        swap.met(barrier, 7)
        swap.start()

    def copy(n, src, dst):
        return pltpu.make_async_remote_copy(
            src_ref=src,
            dst_ref=dst,
            send_sem=send_sem.at[n],
            recv_sem=recv_sem.at[n],
            device_id=peer(masks[n]),
            device_id_type=MESH,
        )

    copies = [copy(n, blocks.at[rank_of(here, *mask)], got.at[own]) for n, mask in enumerate(masks)]
    for started in copies:
        started.start()
    mine.wait()
    for n, mask in enumerate(masks):
        where = got.at[rank_of(here, *mask)]
        copy(n, where, where).wait_recv()
    for started in copies:
        started.wait_send()
    if swap is not None:
        swap.wait()


def exchange(number, blocks, moving=None, homeward=False):
    return plane_call(
        functools.partial(exchange_kernel, homeward),
        "exchange",
        number,
        [jax.ShapeDtypeStruct(blocks.shape, BF)],
        [ANYWHERE],
        [ANYWHERE],
        [pltpu.SemaphoreType.DMA((7,)), pltpu.SemaphoreType.DMA((7,)), pltpu.SemaphoreType.DMA],
        blocks.size // 40000,
        blocks,
        moving=moving,
    )


def finish_kernel(ff, got, gate, up, down):
    gate[...] = got[0, :, :ff].astype(F32)
    up[...] = got[0, :, ff : 2 * ff].astype(F32)
    down[...] = got[0, :, 2 * ff :].astype(F32)


def finish(got):
    ranks, rows, cols = got.shape
    ff = cols // 3
    return pl.pallas_call(
        functools.partial(finish_kernel, ff),
        grid=(ranks,),
        out_shape=[jax.ShapeDtypeStruct((rows, ranks * ff), F32)] * 3,
        in_specs=[pl.BlockSpec((1, rows, cols), lambda i: (i, 0, 0))],
        out_specs=[pl.BlockSpec((rows, ff), lambda i: (0, i))] * 3,
        compiler_params=pltpu.CompilerParams(vmem_limit_bytes=VMEM_LIMIT),
        name="finish",
    )(got)


def finish_attn_kernel(got, query, key, value, out, gains):
    ranks = got.shape[0]

    def lanes(t, n):
        return got[t, :, n * LANES : (n + 1) * LANES].astype(F32)

    groups = [four_heads(*(lanes(t, n) for n in range(3))) for t in range(ranks)]

    def write(ref, heads):
        for n in range(0, len(heads), 4):
            for j, part in enumerate(three_lanes(heads[n : n + 4])):
                at = n * HEAD_SIZE + j * LANES
                ref[:, at : at + LANES] = part

    write(query, [head for group in groups for head in group[:2]])
    write(key, [group[2] for group in groups])
    write(value, [group[3] for group in groups])
    out_heads = []
    total = None
    for t in range(ranks):
        a, b = lanes(t, 3), lanes(t, 4)
        out_heads += [a, pltpu.roll(jnp.where(lane(a) >= HEAD_SIZE, a, b), LANES - HEAD_SIZE, 1)]
        total = b if total is None else total + b
    write(out, out_heads)
    first = GAIN_AT - PACK + LANES
    gains[...] = total.T[first : first + 2]


def finish_attn(got):
    ranks, rows, _ = got.shape
    wide, narrow = jax.ShapeDtypeStruct((rows, ranks * OUT), F32), jax.ShapeDtypeStruct((rows, ranks * HEAD_SIZE), F32)
    return pl.pallas_call(
        finish_attn_kernel,
        out_shape=[wide, narrow, narrow, wide, jax.ShapeDtypeStruct((2, rows), F32)],
        in_specs=[IN_VMEM],
        out_specs=[IN_VMEM] * 5,
        compiler_params=pltpu.CompilerParams(vmem_limit_bytes=VMEM_LIMIT),
        name="finish_attn",
    )(got)


LOWER=-1e30
def dot(a, b, dims):
    return lax.dot_general(a, b, (dims, ((), ())), preferred_element_type=F32)

def attend_kernel(scale2, bq, bk, bounds, length, q, k, v, qpos, out, lse):
    groups = q.shape[0]
    i = pl.program_id(0)
    rows = groups * bq
    qs = q[...].reshape(rows, LANES)
    pos = qpos[0]
    pos2 = jnp.concatenate([pos] * groups, axis=1)
    def step(masked, j, state):
        top, total, acc = state
        at = pl.ds(pl.multiple_of(j * bk, bk), bk)
        s = dot(k[at, :], qs, ((1,), (1,)))
        if masked:
            kp = j * bk + lax.broadcasted_iota(jnp.int32, (bk, 1), 0)
            ok = (kp <= pos2) & (kp < length[0])
            s = jnp.where(ok, s, LOWER)
        new = jnp.maximum(top, jnp.max(s, axis=0, keepdims=True) * scale2)
        p = jnp.exp2(s * scale2 - new)
        alpha = jnp.exp2(top - new)
        total = total * alpha + jnp.sum(p, axis=0, keepdims=True)
        acc = acc * alpha + dot(v[at, :], p.astype(BF), ((0,), (0,)))
        return new, total, acc
    state = (jnp.full((1, rows), LOWER, F32), jnp.zeros((1, rows), F32), jnp.zeros((LANES, rows), F32))
    full, end = bounds[0, i], bounds[1, i]
    state = lax.fori_loop(0, full, functools.partial(step, False), state)
    top, total, acc = lax.fori_loop(full, end, functools.partial(step, True), state)
    o = (acc / total).T
    first, second = o[:bq], pltpu.roll(o[bq:], HEAD_SIZE, 1)
    out[:, :LANES] = jnp.where(lane(first) < HEAD_SIZE, first, second).astype(BF)
    out[:, LANES:] = second[:, : OUT - LANES].astype(BF)
    lse[...] = (top + jnp.log2(total))[None]

def attend(q, k, v, qpos, bounds, length, bq, bk, scale2):
    groups, tokens, _ = q.shape
    n = tokens // bq
    out, lse = pl.pallas_call(
        functools.partial(attend_kernel, scale2, bq, bk),
        grid_spec=pltpu.PrefetchScalarGridSpec(
            num_scalar_prefetch=2, grid=(n,),
            in_specs=[
                pl.BlockSpec((groups, bq, LANES), lambda i, *_: (0, i, 0)),
                pl.BlockSpec(k.shape, lambda i, *_: (0, 0)),
                pl.BlockSpec(v.shape, lambda i, *_: (0, 0)),
                pl.BlockSpec((1, 1, bq), lambda i, *_: (i, 0, 0)),
            ],
            out_specs=[
                pl.BlockSpec((bq, OUT), lambda i, *_: (i, 0)),
                pl.BlockSpec((1, 1, groups * bq), lambda i, *_: (i, 0, 0)),
            ]),
        out_shape=[jax.ShapeDtypeStruct((tokens, OUT), BF), jax.ShapeDtypeStruct((n, 1, groups * bq), F32)],
        compiler_params=pltpu.CompilerParams(vmem_limit_bytes=VMEM_LIMIT),
        name="attend",
        cost_estimate=pl.CostEstimate(flops=0, bytes_accessed=45000000, transcendentals=0),
    )(bounds, length, q, k, v, qpos)
    return out, lse

def back_kernel(scale, scale2, bq, bk, bounds, length, q, k, v, qpos, o, do, lse, cosine, sine, dq, dk, dv):
    groups = q.shape[0]
    i = pl.program_id(0)
    @pl.when(i == 0)
    def _():
        dk[...] = jnp.zeros_like(dk)
        dv[...] = jnp.zeros_like(dv)
    qs = q[...].reshape(groups * bq, LANES)
    do0, do1 = do[:, :LANES].astype(F32), do[:, LANES : 2 * LANES].astype(F32)
    at = lane(do0)
    do1 = pltpu.roll(jnp.where(at >= HEAD_SIZE, do0, do1), LANES - HEAD_SIZE, 1)
    wide = jnp.concatenate([jnp.where(at < HEAD_SIZE, do0, 0.0), jnp.where(at < HEAD_SIZE, do1, 0.0)], axis=0)
    dos = wide.astype(BF)
    o0 = o[:, :LANES].astype(F32)
    o1 = jnp.concatenate([o[:, LANES:].astype(F32), jnp.zeros((bq, 2 * LANES - OUT), F32)], axis=1)
    o1 = pltpu.roll(jnp.where(at >= HEAD_SIZE, o0, o1), LANES - HEAD_SIZE, 1)
    delta = jnp.sum(wide * jnp.concatenate([o0, o1], axis=0), axis=1, keepdims=True).reshape(1, groups * bq)
    lse_row = lse[0]
    pos = qpos[0]
    pos2 = jnp.concatenate([pos] * groups, axis=1)
    def step(masked, j, acc):
        at = pl.ds(pl.multiple_of(j * bk, bk), bk)
        kb, vb = k[at, :], v[at, :]
        s = dot(kb, qs, ((1,), (1,)))
        p = jnp.exp2(s * scale2 - lse_row)
        if masked:
            kp = j * bk + lax.broadcasted_iota(jnp.int32, (bk, 1), 0)
            ok = (kp <= pos2) & (kp < length[0])
            p = jnp.where(ok, p, 0.0)
        dp = dot(vb, dos, ((1,), (1,)))
        ds = (p * (dp - delta)).astype(BF)
        dv[at, :] += dot(p.astype(BF), dos, ((1,), (0,)))
        dk[at, :] += dot(ds, qs, ((1,), (0,))) * scale
        return acc + dot(ds, kb, ((0,), (0,)))
    full, end = bounds[0, i], bounds[1, i]
    acc = jnp.zeros((groups * bq, LANES), F32)
    acc = lax.fori_loop(0, full, functools.partial(step, False), acc)
    acc = lax.fori_loop(full, end, functools.partial(step, True), acc) * scale
    for g in range(groups):
        dq[:, g * LANES:(g + 1) * LANES] = turn(acc[g * bq:(g + 1) * bq], cosine[...], -sine[...]).astype(BF)

def attend_back(q, k, v, qpos_row, o, do, lse, cosine, sine, bounds, length, bq, bk, scale, scale2):
    groups, tokens, _ = q.shape
    n = tokens // bq
    wide = pl.BlockSpec((bq, groups * LANES), lambda i, *_: (i, 0))
    narrow = pl.BlockSpec((bq, OUT), lambda i, *_: (i, 0))
    return pl.pallas_call(
        functools.partial(back_kernel, scale, scale2, bq, bk),
        grid_spec=pltpu.PrefetchScalarGridSpec(
            num_scalar_prefetch=2, grid=(n,),
            in_specs=[
                pl.BlockSpec((groups, bq, LANES), lambda i, *_: (0, i, 0)),
                pl.BlockSpec(k.shape, lambda i, *_: (0, 0)),
                pl.BlockSpec(v.shape, lambda i, *_: (0, 0)),
                pl.BlockSpec((1, 1, bq), lambda i, *_: (i, 0, 0)),
                narrow, wide,
                pl.BlockSpec((1, 1, groups * bq), lambda i, *_: (i, 0, 0)),
                pl.BlockSpec((bq, LANES), lambda i, *_: (i, 0)),
                pl.BlockSpec((bq, LANES), lambda i, *_: (i, 0)),
            ],
            out_specs=[wide, pl.BlockSpec(k.shape, lambda i, *_: (0, 0)), pl.BlockSpec(k.shape, lambda i, *_: (0, 0))]),
        out_shape=[jax.ShapeDtypeStruct((tokens, groups * LANES), BF), jax.ShapeDtypeStruct(k.shape, F32), jax.ShapeDtypeStruct(k.shape, F32)],
        compiler_params=pltpu.CompilerParams(vmem_limit_bytes=VMEM_LIMIT),
        name="attend_back",
        cost_estimate=pl.CostEstimate(flops=0, bytes_accessed=65000000, transcendentals=0),
    )(bounds, length, q, k, v, qpos_row, o, do, lse, cosine, sine)

def bounds_of(positions, length, bq, bk):
    p = positions.reshape(-1, bq)
    lo = jnp.minimum(jnp.min(p, axis=1) + 1, length) // bk
    hi = -(-jnp.minimum(jnp.max(p, axis=1) + 1, length) // bk)
    return jnp.stack([lo, hi]).astype(jnp.int32)


PLANE = ("x", "c", "y")

def together(*arrays):
    return lax.optimization_barrier(arrays)


def body(
    inputs,
    lengths,
    cotangent,
    attn_gain,
    w_query,
    key_projection,
    value_projection,
    w_out,
    mlp_gain,
    w_gate,
    w_up,
    w_down,
):
    sections = lax.axis_size("x") * lax.axis_size("c")
    planes = lax.axis_size("z")
    halves = lax.axis_size("y")
    extra = lax.axis_size("e")
    ranks = sections * halves
    layers = sections
    block = inputs.shape[1]
    width = inputs.shape[2]
    rows = w_query.shape[1]
    tokens = block * ranks
    all_tokens = tokens * extra
    head_group = QUERY_HEADS // KEY_VALUE_HEADS
    q_cols = head_group * HEAD_SIZE
    kv_cols = HEAD_SIZE
    ff_cols = FF // ranks
    scale = 1.0 / math.sqrt(HEAD_SIZE)
    scale2 = scale * math.log2(math.e)

    def by_rank(matrix):
        return matrix.reshape(rows, ranks, -1)

    attn_pack = jnp.concatenate(
        [
            by_rank(w_query[0]),
            by_rank(key_projection[0]),
            by_rank(value_projection[0]),
            by_rank(w_out[0].T),
            jnp.broadcast_to(jnp.stack([attn_gain[0], mlp_gain[0]], axis=1)[:, None, :], (rows, ranks, 2)),
            jnp.zeros((rows, ranks, PACK - GAIN_AT - 2), F32),
        ],
        axis=2,
    )
    mlp_pack = jnp.concatenate(
        [by_rank(w_gate[0]), by_rank(w_up[0]), by_rank(w_down[0].T)], axis=2
    )

    def by_layer(got):
        return got.reshape(layers, halves, rows, -1)

    def ready(pack):
        return jnp.swapaxes(pack.astype(BF), 0, 1)

    def whole(part):
        if extra > 1:
            part = lax.all_gather(part, "e", axis=1, tiled=False)
        return lax.all_gather(part.reshape(-1, part.shape[-1]), "z", axis=0, tiled=True)

    def reduce_rows(sums):
        mine = lax.psum_scatter(sums, "z", scatter_dimension=0, tiled=True)
        mine = mine.reshape(halves, extra, rows, -1)
        if extra > 1:
            return lax.psum_scatter(mine, "e", scatter_dimension=1, tiled=False)
        return mine[:, 0]

    cut = 3 * ff_cols // 2
    mlp_blocks = ready(mlp_pack)
    attn_got, hidden_state = exchange(4, ready(attn_pack), inputs[0])
    first_blocks, attn_got = together(mlp_blocks[..., :cut], attn_got)
    (first_got,) = exchange(5, first_blocks)

    token_x, token_c, token_y = token_place()
    rank = (token_x * 2 + token_c) * halves + token_y
    spot = lax.axis_index("e")
    length = lengths[micro_of_plane()]

    block_start = (jnp.arange(ranks) * extra + spot) * block
    positions = (block_start[:, None] + jnp.arange(block)[None, :]).reshape(tokens)
    exponents = 2.0 * jnp.arange(HEAD_SIZE // 2).astype(F32) / HEAD_SIZE
    angles = positions.astype(F32)[:, None] * (THETA ** (-exponents))[None, :]
    table = lambda values: jnp.pad(values, ((0, 0), (0, LANES // 2 - HALF)))
    cosine = jnp.concatenate([table(jnp.cos(angles))] * 2, axis=1)
    sine = jnp.concatenate([table(-jnp.sin(angles)), table(jnp.sin(angles))], axis=1)
    bq = math.gcd(tokens, 512)
    bk = math.gcd(all_tokens, 512)
    bounds = bounds_of(positions, length, bq, bk)
    length1 = length.reshape(1)
    query_rows = positions.astype(jnp.int32).reshape(-1, 1, bq)

    def all_keys(array):
        if extra == 1:
            return array
        stacked = lax.all_gather(array.reshape(ranks, block, -1), "e", axis=1, tiled=False)
        return stacked.reshape(all_tokens, -1)

    def own_keys(array):
        if extra == 1:
            return array
        stacked = array.astype(BF).reshape(ranks, extra, block, -1)
        return lax.psum_scatter(stacked, "e", scatter_dimension=1, tiled=False).reshape(tokens, -1).astype(F32)

    cosine3 = cosine.reshape(ranks, block, LANES)
    sine3 = sine.reshape(ranks, block, LANES)

    second_blocks, first_got, cosine, sine, cosine3, sine3, bounds, query_rows = together(
        mlp_blocks[..., cut:], first_got, cosine, sine, cosine3, sine3, bounds, query_rows
    )
    (second_got,) = exchange(6, second_blocks)
    attn_parts, first_parts, second_parts = by_layer(attn_got), by_layer(first_got), by_layer(second_got)

    def flat(array):
        return array.reshape(tokens, array.shape[-1])

    saved = []
    attn_w, w_1 = whole(attn_parts[0]), whole(first_parts[0])
    hidden_state, attn_w, w_1, second_part = together(hidden_state, attn_w, w_1, second_parts[0])
    w_2 = whole(second_part)
    for layer in range(layers):
        a1, q, k, v, gain = attn_in(hidden_state, attn_w, cosine3, sine3)
        q, k, v = q.reshape(head_group, tokens, LANES), all_keys(flat(k)), all_keys(flat(v))
        o, log_total = attend(q, k, v, query_rows, bounds, length1, bq, bk, scale2)
        if layer + 1 < layers:
            o, attn_part, first_part = together(o, attn_parts[layer + 1], first_parts[layer + 1])
            next_attn, next_1 = whole(attn_part), whole(first_part)
        mid, a2, gu, hid, after_mlp, *moved = mlp(
            hidden_state, o.reshape(ranks, block, -1), gain, attn_w, w_1, w_2,
            cotangent[0] if layer + 1 == layers else None,
        )
        saved.append((hidden_state, a1, q, k, v, o, log_total, mid, a2, gu, hid, attn_w, w_1, w_2, gain))
        hidden_state = after_mlp
        if layer + 1 < layers:
            hidden_state, attn_w, w_1, second_part = together(hidden_state, next_attn, next_1, second_parts[layer + 1])
            w_2 = whole(second_part)
    output = hidden_state

    my_positions = (rank * extra + spot) * block + jnp.arange(block)
    (e,) = moved
    e = jnp.where((my_positions < length)[:, None], e, jnp.zeros_like(e))
    attn_grads = [None] * layers
    mlp_grads = [None] * layers
    for layer in reversed(range(layers)):
        (h, a1, q, k, v, o, log_total, mid, a2, gu, hid, attn_w, w_1, w_2, gain) = saved[layer]
        dmid, gain2, dat, mlp_sums, *moved = mlp_back(
            e, mid, gain, gu, hid, a2, w_1, w_2, output if layer + 1 == layers else None
        )
        if moved:
            (output,) = moved
        else:
            dat, mlp_sums, attn_grads[layer + 1] = together(dat, mlp_sums, attn_grads[layer + 1])
        mlp_grads[layer] = reduce_rows(mlp_sums)
        dat, dob = dat_gather(dat, attn_w)
        dq, dk, dv = attend_back(
            q, k, v, query_rows, o, flat(dob), log_total, cosine, sine, bounds, length1, bq, bk, scale, scale2
        )
        dk, dv = own_keys(dk), own_keys(dv)
        e, attn_sums = attn_back(
            h, dmid, gain, gain2, *(array.reshape(ranks, block, -1) for array in (dq, dk, dv)), cosine3, sine3,
            o.reshape(ranks, block, -1), a1, dat, attn_w,
        )
        e, attn_sums, mlp_grads[layer] = together(e, attn_sums, mlp_grads[layer])
        attn_grads[layer] = reduce_rows(attn_sums)

    def by_place(grads):
        return jnp.stack(grads).reshape(ranks, rows, -1)

    (mlp_home,) = exchange(7, by_place(mlp_grads))
    attn_blocks, mlp_home = together(by_place(attn_grads), mlp_home)
    attn_home, input_grad = exchange(10, attn_blocks, e, True)
    grad_gate, grad_up, grad_down = finish(mlp_home)
    grad_query, grad_key, grad_value, grad_out, gain_sums = finish_attn(attn_home)
    return (
        output[None],
        input_grad[None],
        gain_sums[0:1],
        grad_query[None],
        grad_key[None],
        grad_value[None],
        grad_out.T[None],
        gain_sums[1:2],
        grad_gate[None],
        grad_up[None],
        grad_down.T[None],
    )


def solution(mesh):
    section, seq = mesh.devices.shape
    halves = KEY_VALUE_HEADS // section
    extra = seq // (section * halves)
    fine = Mesh(
        mesh.devices.reshape(section // 2, 2, section, halves, extra), ("x", "c", "z", "y", "e")
    )
    sec, sq = ("x", "c"), ("z", "y", "e")
    rows3 = P(sec, sq, None)
    cols3 = P(sec, None, sq)
    in_specs = (rows3, P(), rows3, P(sec, sq), rows3, rows3, rows3, cols3, P(sec, sq), rows3, rows3, cols3)
    out_specs = (rows3, rows3, P(sec, sq), rows3, rows3, rows3, cols3, P(sec, sq), rows3, rows3, cols3)
    return jax.shard_map(body, mesh=fine, in_specs=in_specs, out_specs=out_specs, check_vma=False)
```

```python
import functools
import math

import jax
import jax.numpy as jnp
from jax import lax
from jax.experimental import pallas as pl
from jax.experimental.pallas import tpu as pltpu
from jax.sharding import Mesh
from jax.sharding import PartitionSpec as P

QUERY_HEADS = 16
KEY_VALUE_HEADS = 8
HEAD_SIZE = 96
FF = 4096

EPS = 1e-05
THETA = 100000.0
LOWER_LIMIT = -1e30

BF = jnp.bfloat16
F32 = jnp.float32

LANES = 128
HALF = HEAD_SIZE // 2
VMEM_LIMIT = 56 * 1024 * 1024


def dot(a, b, dims):
    return lax.dot_general(a, b, (dims, ((), ())), preferred_element_type=F32)


def dot_nn(a, b):
    return dot(a, b, ((1,), (0,)))


def dot_nt(a, b):
    return dot(a, b, ((1,), (1,)))


def dot_tn(a, b):
    return dot(a, b, ((0,), (0,)))


MESH = pl.DeviceIdType.MESH

OWN, X, Y, D = (0, 0), (1, 0), (0, 1), (1, 1)


def place():
    return lax.axis_index("x"), lax.axis_index("c"), lax.axis_index("y")


def xor(a, b):
    return a + b - 2 * a * b


def token_place():
    x, c, y = place()
    z = lax.axis_index("z")
    return xor(x, xor(lax.rem(z, 2), z // 2)), c, y


def micro_of_plane():
    z = lax.axis_index("z")
    return lax.rem(z, 2) * 2 + z // 2


def flip(index, by):
    return 1 - index if by else index


def rank_of(here, dx, dc, dy):
    x, c, y = here
    return (flip(x, dx) * 2 + flip(c, dc)) * 2 + flip(y, dy)


class Swap:
    def __init__(self, homeward, moving, moved, sem):
        x, c, _ = place()
        z = lax.axis_index("z")
        low = lax.rem(z, 2)
        high = z // 2
        out = {"x": xor(high, xor(x, c)), "c": low, "z": c * 2 + x}
        back = {"x": low, "c": high, "z": 2 * xor(x, xor(low, high)) + c}
        target, self.source = (back, out) if homeward else (out, back)
        self.away = (target["x"] != x) | (target["c"] != c) | (target["z"] != z)
        self.remote = pltpu.make_async_remote_copy(
            src_ref=moving,
            dst_ref=moved,
            send_sem=sem.at[0],
            recv_sem=sem.at[1],
            device_id=target,
            device_id_type=MESH,
        )
        self.local = pltpu.make_async_copy(moving, moved, sem.at[2])

    def greet(self, barrier):
        @pl.when(self.away)
        def _():
            pl.semaphore_signal(barrier, inc=1, device_id=self.source, device_id_type=MESH)

    def either(self, remote, local):
        pl.when(self.away)(remote)
        pl.when(jnp.logical_not(self.away))(local)

    def start(self):
        self.either(lambda: self.remote.start(), lambda: self.local.start())

    def met(self, barrier, count):
        self.either(lambda: pl.semaphore_wait(barrier, count + 1), lambda: pl.semaphore_wait(barrier, count))

    def wait(self):
        self.either(lambda: self.remote.wait(), lambda: self.local.wait())


def with_swap(kernel, inputs, outputs):
    def wrapped(*refs):
        last = inputs + 1 + outputs
        kernel(
            *refs[:inputs],
            *refs[inputs + 1 : last],
            *refs[last + 1 : -1],
            swap=(refs[inputs], refs[last], refs[-1]),
        )

    return wrapped


def greet(swap=None):
    x, c, y = place()
    barrier = pltpu.get_barrier_semaphore()
    for peer in ({"x": 1 - x}, {"c": 1 - c}, {"y": 1 - y}):
        pl.semaphore_signal(barrier, inc=1, device_id=peer, device_id_type=MESH)
    if swap is None:
        pl.semaphore_wait(barrier, 3)
    else:
        swap.greet(barrier)
        swap.met(barrier, 3)
        swap.start()


class Sender:
    def __init__(self, send_sem, recv_sem):
        x, c, y = place()
        self.peers = {"x": {"x": 1 - x}, "c": {"c": 1 - c}, "y": {"y": 1 - y}}
        self.send_sem, self.recv_sem = send_sem, recv_sem
        self.sent = []

    def copy(self, src, dst, index, to, number):
        return pltpu.make_async_remote_copy(
            src_ref=src,
            dst_ref=dst,
            send_sem=self.send_sem.at[number],
            recv_sem=self.recv_sem.at[index],
            device_id=self.peers[to],
            device_id_type=MESH,
        )

    def send(self, src, dst, index, to):
        started = self.copy(src, dst, index, to, len(self.sent))
        started.start()
        self.sent.append(started)

    def arrived(self, where, index):
        self.copy(where, where, index, "c", 0).wait_recv()

    def drain(self):
        for started in self.sent:
            started.wait_send()


class Gather:
    def __init__(self, here, full, sems):
        self.here, self.full = here, full
        self.piece = full.shape[1] // 4
        self.net = Sender(*sems)

    def index(self, role, chunk):
        return (role[0] * 4 + role[1] * 2 + role[2]) * 4 + chunk

    def slot(self, role, chunk):
        return self.full.at[rank_of(self.here, *role), pl.ds(chunk * self.piece, self.piece)]

    def send(self, role, chunk, to, as_role):
        where = self.slot(role, chunk)
        self.net.send(where, where, self.index(as_role, chunk), to)

    def arrived(self, role, chunk):
        self.net.arrived(self.slot(role, chunk), self.index(role, chunk))

    def own(self, cx, cy):
        self.send((0, 0, 0), cx, "x", (1, 0, 0))
        self.send((0, 0, 0), cy, "y", (0, 0, 1))

    def all_own(self):
        for cx, cy in ((2, 0), (3, 1), (0, 2), (1, 3)):
            self.own(cx, cy)
        return self

    def run(self, on_block, before_last=None):
        send, arrived = self.send, self.arrived
        at_x, at_y, at_d, at_c = (1, 0, 0), (0, 0, 1), (1, 0, 1), (0, 1, 0)
        xc, yc, dc = (1, 1, 0), (0, 1, 1), (1, 1, 1)

        def whole(role):
            for chunk in range(4):
                arrived(role, chunk)

        def done(role):
            on_block(rank_of(self.here, *role))

        def pass_on(cx, cy):
            arrived(at_x, cx)
            if cx >= 2:
                send(at_x, cx, "y", at_d)
            send(at_x, cx, "c", xc)
            arrived(at_y, cy)
            if cy < 2:
                send(at_y, cy, "x", at_d)
            send(at_y, cy, "c", yc)

        def pass_last(chunks):
            for chunk in chunks:
                arrived(at_d, chunk)
                send(at_d, chunk, "c", dc)

        for chunk in range(4):
            send((0, 0, 0), chunk, "c", at_c)
        done((0, 0, 0))
        pass_on(2, 0)
        whole(at_c)
        done(at_c)
        pass_on(3, 1)
        pass_on(0, 2)
        pass_on(1, 3)
        done(at_x)
        done(at_y)
        pass_last((0, 2))
        whole(xc)
        done(xc)
        whole(yc)
        done(yc)
        if before_last is not None:
            before_last()
        pass_last((1, 3))
        done(at_d)
        whole(dc)
        done(dc)
        return self.net


def run_gather(here, full, sems, on_block, before_last=None):
    return Gather(here, full, sems).all_own().run(on_block, before_last)


class Scatter:
    order = (D, X, Y, OWN)

    def __init__(self, here, parts, total, bufs, sems, fill=None):
        self.here, self.parts, self.total, self.fill = here, parts, total, fill
        self.from_c, self.via_x, self.via_y, self.from_x, self.from_y = bufs
        half = parts.shape[1] // 2
        self.piece = half // 2
        self.lower, self.upper = pl.ds(0, half), pl.ds(half, half)
        self.net = Sender(*sems)

    def rank(self, n, dc):
        return rank_of(self.here, self.order[n][0], dc, self.order[n][1])

    def make(self, r):
        if self.fill is not None:
            self.fill(r)

    def sibling(self, n):
        r = self.rank(n, 1)
        self.make(r)
        self.net.send(self.parts.at[r], self.from_c.at[n], n, "c")

    def add(self, n, where, more):
        r = self.rank(n, 0)
        self.parts[r, where] = (self.parts[r, where].astype(F32) + more.astype(F32)).astype(BF)

    def mine(self, n, where):
        return self.parts.at[self.rank(n, 0), where]

    def combine(self, n):
        self.make(self.rank(n, 0))
        self.net.arrived(self.from_c.at[n], n)
        if n < 3:
            self.add(n, pl.ds(0, self.parts.shape[1]), self.from_c[n])

    def rows(self, number):
        return pl.ds(number * self.piece, self.piece)

    def to_diagonal(self):
        self.combine(0)
        for n in range(2):
            self.net.send(self.mine(0, self.rows(n + 2)), self.via_x.at[self.rows(n)], 4 + n, "x")
            self.net.send(self.mine(0, self.rows(n)), self.via_y.at[self.rows(n)], 6 + n, "y")

    def to_x(self):
        self.combine(1)
        self.net.send(self.mine(1, self.upper), self.from_x.at[self.upper], 8, "x")

    def to_y(self):
        self.combine(2)
        self.net.send(self.mine(2, self.lower), self.from_y.at[self.lower], 9, "y")

    def early(self):
        for n in (1, 2, 3):
            self.sibling(n)
        self.to_x()
        self.to_y()

    def run(self, beside=None, early_done=False, on_rows=None):
        net, total, lower, upper = self.net, self.total, self.lower, self.upper
        self.sibling(0)
        self.to_diagonal()
        if not early_done:
            self.sibling(1)
            self.to_x()
            self.sibling(2)
            self.to_y()
            self.sibling(3)
        self.combine(3)
        total[...] = self.parts[self.rank(3, 0)].astype(F32) + self.from_c[3].astype(F32)
        if beside is not None:
            beside(0)
        for n in range(2):
            at, above = self.rows(n), self.rows(n + 2)
            net.arrived(self.via_y.at[at], 6 + n)
            self.add(1, at, self.via_y[at])
            net.send(self.mine(1, at), self.from_x.at[at], 10 + n, "x")
            net.arrived(self.via_x.at[at], 4 + n)
            self.add(2, above, self.via_x[at])
            net.send(self.mine(2, above), self.from_y.at[above], 12 + n, "y")
        if beside is not None:
            beside(1)
        net.arrived(self.from_x.at[upper], 8)
        net.arrived(self.from_y.at[lower], 9)
        total[upper] += self.from_x[upper].astype(F32)
        total[lower] += self.from_y[lower].astype(F32)
        for n in range(2):
            at, above = self.rows(n), self.rows(n + 2)
            net.arrived(self.from_x.at[at], 10 + n)
            net.arrived(self.from_y.at[above], 12 + n)
            total[at] += self.from_x[at].astype(F32)
            total[above] += self.from_y[above].astype(F32)
            if on_rows is not None:
                on_rows(n)
        return net


def gather_sems():
    return [pltpu.SemaphoreType.DMA((32,)), pltpu.SemaphoreType.DMA((32,))]


def scatter_scratch(block, width):
    half = block // 2
    return [
        pltpu.VMEM((4, block, width), BF),
        pltpu.VMEM((half, width), BF),
        pltpu.VMEM((half, width), BF),
        pltpu.VMEM((block, width), BF),
        pltpu.VMEM((block, width), BF),
        pltpu.SemaphoreType.DMA((14,)),
        pltpu.SemaphoreType.DMA((14,)),
    ]


class Loads:
    def __init__(self, sem):
        self.sem = sem
        self.count = 0

    def start(self, src, dst):
        copy = pltpu.make_async_copy(src, dst, self.sem.at[self.count])
        self.count += 1
        copy.start()
        return copy


def inverse_of(x):
    return lax.rsqrt(jnp.mean(x * x, axis=-1, keepdims=True) + EPS)


def lane(x):
    return lax.broadcasted_iota(jnp.int32, x.shape, 1)


def turn(head, cosine, sine):
    return head * cosine + pltpu.roll(head, LANES // 2, 1) * sine


def open_halves(head):
    return jnp.where(lane(head) < LANES // 2, head, pltpu.roll(head, LANES // 2 - HALF, 1))


def close_halves(head):
    low = lane(head) < LANES // 2
    return jnp.where(low, head, 0.0) + pltpu.roll(jnp.where(low, 0.0, head), LANES // 2 + HALF, 1)


def four_heads(a, b, c):
    at = lane(a)
    return (
        a,
        pltpu.roll(jnp.where(at >= 96, a, b), 32, 1),
        pltpu.roll(jnp.where(at >= 64, b, c), 64, 1),
        pltpu.roll(c, 96, 1),
    )


def three_lanes(heads):
    at = lane(heads[0])
    b, c, d = pltpu.roll(heads[1], 96, 1), pltpu.roll(heads[2], 64, 1), pltpu.roll(heads[3], 32, 1)
    return jnp.where(at < 96, heads[0], b), jnp.where(at < 64, b, c), jnp.where(at < 32, c, d)


def plane_call(kernel, name, number, out_shape, out_specs, in_specs, scratch, time_us, *operands, moving=None):
    if moving is not None:
        kernel = with_swap(kernel, len(in_specs), len(out_specs))
        out_shape = out_shape + [jax.ShapeDtypeStruct(moving.shape, moving.dtype)]
        in_specs, out_specs = in_specs + [ANYWHERE], out_specs + [ANYWHERE]
        scratch = scratch + [pltpu.SemaphoreType.DMA((3,))]
        operands = operands + (moving,)
    return pl.pallas_call(
        kernel,
        out_shape=out_shape,
        in_specs=in_specs,
        out_specs=out_specs,
        scratch_shapes=scratch,
        compiler_params=pltpu.CompilerParams(
            collective_id=number, has_side_effects=True, vmem_limit_bytes=VMEM_LIMIT
        ),
        cost_estimate=pl.CostEstimate(flops=0, bytes_accessed=time_us * 3000000, transcendentals=0),
        name=name,
    )(*operands)


ANYWHERE = pl.BlockSpec(memory_space=pl.ANY)
IN_VMEM = pl.BlockSpec(memory_space=pltpu.VMEM)
QKV = 4 * HEAD_SIZE
OUT = 2 * HEAD_SIZE
GAIN_AT = QKV + OUT
PACK = -(-(GAIN_AT + 2) // LANES) * LANES


def attn_in_kernel(h, w_hbm, cosine, sine, a1_out, q_out, k_out, v_out, gain_out, full, w, send, recv, local):
    here = token_place()
    loads = Loads(local)
    w_load = loads.start(w_hbm, w)
    x = h[...].astype(F32)
    n1 = x * inverse_of(x)
    w_load.wait()
    rows = w[:, PACK - LANES :].astype(F32).T
    gain_out[...] = rows[GAIN_AT - PACK + LANES : GAIN_AT - PACK + LANES + 2]
    full[rank_of(here, 0, 0, 0)] = (n1 * gain_out[0:1, :]).astype(BF)
    greet()
    saves = []

    def on_block(r):
        saves.append(loads.start(full.at[r], a1_out.at[r]))
        qkv = dot_nn(full[r], w[:, :QKV])
        heads = four_heads(*(qkv[:, n * LANES : (n + 1) * LANES] for n in range(3)))
        cos, sin = cosine[r], sine[r]
        for n in range(2):
            q_out[n, r] = turn(open_halves(heads[n]), cos, sin).astype(BF)
        k_out[r] = turn(open_halves(heads[2]), cos, sin).astype(BF)
        v_out[r] = jnp.where(lane(heads[3]) < HEAD_SIZE, heads[3], 0.0).astype(BF)

    net = run_gather(here, full, (send, recv), on_block)
    net.drain()
    for save in saves:
        save.wait()


def attn_in(h, w, cosine, sine):
    block, width = h.shape
    return plane_call(
        attn_in_kernel,
        "attn_in",
        0,
        [
            jax.ShapeDtypeStruct((8, block, width), BF),
            jax.ShapeDtypeStruct((2, 8, block, LANES), BF),
            jax.ShapeDtypeStruct((8, block, LANES), BF),
            jax.ShapeDtypeStruct((8, block, LANES), BF),
            jax.ShapeDtypeStruct((2, width), F32),
        ],
        [ANYWHERE, IN_VMEM, IN_VMEM, IN_VMEM, IN_VMEM],
        [IN_VMEM, ANYWHERE, IN_VMEM, IN_VMEM],
        [pltpu.VMEM((8, block, width), BF), pltpu.VMEM(w.shape, BF)]
        + gather_sems()
        + [pltpu.SemaphoreType.DMA((9,))],
        34,
        h, w, cosine, sine,
    )


def mlp_kernel(
    ff, homeward, h, o, gain, wa_hbm, w1_hbm, w2_hbm, mid_out, a2_out, gu_out, hid_out, next_out,
    full, parts, gu, hid, wa, wm, total,
    from_c, via_x, via_y, from_x, from_y, send1, recv1, send2, recv2,
    from_c3, via_x3, via_y3, from_x3, from_y3, send3, recv3, local, swap=None,
):
    here = token_place()
    swap = swap and Swap(homeward, *swap)
    loads = Loads(local)
    wa_load = loads.start(wa_hbm, wa)
    split = w1_hbm.shape[1]
    w1_load = loads.start(w1_hbm, wm.at[:, pl.ds(0, split)])
    w2_load = loads.start(w2_hbm, wm.at[:, pl.ds(split, 3 * ff - split)])
    greet(swap)
    wa_load.wait()

    def fill(r):
        parts[r] = dot_nt(o[r], wa[:, QKV:GAIN_AT]).astype(BF)

    bufs = (from_c, via_x, via_y, from_x, from_y)
    gather = Gather(here, full, (send2, recv2))
    own = rank_of(here, 0, 0, 0)

    def on_rows(n):
        for piece in (n + 2, n):
            rows = pl.ds(piece * gather.piece, gather.piece)
            mid = h[rows].astype(F32) + total[rows]
            mid_out[rows] = mid
            full[own, rows] = (mid * inverse_of(mid) * gain[1:2, :]).astype(BF)
        if n == 0:
            gather.own(2, 0)
        else:
            for pair in ((3, 1), (0, 2), (1, 3)):
                gather.own(*pair)

    net1 = Scatter(here, parts, total, bufs, (send1, recv1), fill).run(on_rows=on_rows)
    net1.drain()
    saves = []

    def on_block(r):
        if not saves:
            w1_load.wait()
            w2_load.wait()
        saves.append(loads.start(full.at[r], a2_out.at[r]))
        a2 = full[r]
        g = dot_nn(a2, wm[:, :ff])
        u = dot_nn(a2, wm[:, ff : 2 * ff])
        gu[r, :, :ff] = g.astype(BF)
        gu[r, :, ff:] = u.astype(BF)
        low = (g * (1.0 / (1.0 + jnp.exp(-g))) * u).astype(BF)
        hid[r] = low
        saves.append(loads.start(gu.at[r], gu_out.at[r]))
        saves.append(loads.start(hid.at[r], hid_out.at[r]))
        parts[r] = dot_nt(low, wm[:, 2 * ff :]).astype(BF)

    bufs3 = (from_c3, via_x3, via_y3, from_x3, from_y3)
    scatter = Scatter(here, parts, total, bufs3, (send3, recv3))
    net2 = gather.run(on_block, scatter.early)
    net3 = scatter.run(early_done=True)
    next_out[...] = (mid_out[...] + total[...]).astype(BF)
    net2.drain()
    net3.drain()
    for save in saves:
        save.wait()
    if swap is not None:
        swap.wait()


def mlp(h, o, gain, wa, w1, w2, moving=None):
    block, width = h.shape
    ff = (w1.shape[1] + w2.shape[1]) // 3
    return plane_call(
        functools.partial(mlp_kernel, ff, False),
        "mlp",
        1 if moving is None else 8,
        [
            jax.ShapeDtypeStruct((block, width), F32),
            jax.ShapeDtypeStruct((8, block, width), BF),
            jax.ShapeDtypeStruct((8, block, 2 * ff), BF),
            jax.ShapeDtypeStruct((8, block, ff), BF),
            jax.ShapeDtypeStruct((block, width), BF),
        ],
        [IN_VMEM, ANYWHERE, ANYWHERE, ANYWHERE, IN_VMEM],
        [IN_VMEM, IN_VMEM, IN_VMEM, ANYWHERE, ANYWHERE, ANYWHERE],
        [
            pltpu.VMEM((8, block, width), BF),
            pltpu.VMEM((8, block, width), BF),
            pltpu.VMEM((8, block, 2 * ff), BF),
            pltpu.VMEM((8, block, ff), BF),
            pltpu.VMEM(wa.shape, BF),
            pltpu.VMEM((width, 3 * ff), BF),
            pltpu.VMEM((block, width), F32),
        ]
        + scatter_scratch(block, width)
        + gather_sems()
        + scatter_scratch(block, width)
        + [pltpu.SemaphoreType.DMA((27,))],
        96,
        h, o, gain, wa, w1, w2,
        moving=moving,
    )


def norm_back(upstream, normed, inverse, gain_row):
    scaled = upstream * gain_row
    return inverse * (scaled - normed * jnp.mean(scaled * normed, axis=-1, keepdims=True))


def flat_tn(a, cols, b):
    total = dot_tn(a[0, :, cols], b[0])
    for n in range(1, a.shape[0]):
        total = total + dot_tn(a[n, :, cols], b[n])
    return total


def mlp_back_kernel(
    ff, step, homeward, e, mid, gain, gu_hbm, hid_hbm, a2_hbm, w1_hbm, w2_hbm, dmid_out, gain_out, dat_out, sums_out,
    full, parts, a2, gu, hid, wm, total, stage, send1, recv1,
    from_c, via_x, via_y, from_x, from_y, send2, recv2, local, swap=None,
):
    here = token_place()
    swap = swap and Swap(homeward, *swap)
    loads = Loads(local)
    split = w1_hbm.shape[1]
    w2_load = loads.start(w2_hbm, wm.at[:, pl.ds(split, 3 * ff - split)])
    gu_load = loads.start(gu_hbm, gu)
    w1_load = loads.start(w1_hbm, wm.at[:, pl.ds(0, split)])
    a2_load = loads.start(a2_hbm, a2)
    hid_load = loads.start(hid_hbm, hid)
    own = rank_of(here, 0, 0, 0)
    full[own] = e[...]
    greet(swap)
    w2_load.wait()
    gu_load.wait()
    w1_load.wait()

    def on_block(r):
        dhid = dot_nn(full[r], wm[:, 2 * ff :])
        g = gu[r, :, :ff].astype(F32)
        u = gu[r, :, ff:].astype(F32)
        sig = 1.0 / (1.0 + jnp.exp(-g))
        du = dhid * g * sig
        dg = dhid * u * sig * (1.0 + g * (1.0 - sig))
        gu[r, :, :ff] = dg.astype(BF)
        gu[r, :, ff:] = du.astype(BF)
        parts[r] = dot_nt(gu[r], wm[:, : 2 * ff]).astype(BF)

    scatter = Scatter(here, parts, total, (from_c, via_x, via_y, from_x, from_y), (send2, recv2))
    net1 = run_gather(here, full, (send1, recv1), on_block, scatter.early)
    a2_load.wait()
    hid_load.wait()
    sums = []
    count = full.shape[2] // step

    def beside(turn_number):
        half = (count + 1) // 2
        for number in range(turn_number * half, min((turn_number + 1) * half, count)):
            if number >= 2:
                sums[number - 2].wait()
            at = slice(number * step, (number + 1) * step)
            held = stage.at[number % 2]
            held[:, : 2 * ff] = flat_tn(a2, at, gu).astype(BF)
            held[:, 2 * ff :] = flat_tn(full, at, hid).astype(BF)
            sums.append(loads.start(held, sums_out.at[pl.ds(number * step, step)]))

    net2 = scatter.run(beside, True)
    da2 = total[...]
    m = mid[...]
    r2 = inverse_of(m)
    n2 = m * r2
    gain_out[...] = jnp.sum(da2 * n2, axis=0, keepdims=True)
    dmid = e[...].astype(F32) + norm_back(da2, n2, r2, gain[1:2, :])
    dmid_out[...] = dmid
    dat_out[...] = dmid.astype(BF)
    net1.drain()
    net2.drain()
    for save in sums[-2:]:
        save.wait()
    if swap is not None:
        swap.wait()


def dat_kernel(dat, wa_hbm, dat_out, dob_out, full, wa, send, recv, local):
    here = token_place()
    loads = Loads(local)
    wa_load = loads.start(wa_hbm, wa)
    full[rank_of(here, 0, 0, 0)] = dat[...]
    greet()
    wa_load.wait()
    saves = []

    def on_block(r):
        saves.append(loads.start(full.at[r], dat_out.at[r]))
        dob_out[r] = dot_nn(full[r], wa[:, QKV:PACK]).astype(BF)

    run_gather(here, full, (send, recv), on_block).drain()
    for save in saves:
        save.wait()


def dat_gather(dat, wa):
    block, width = dat.shape
    return plane_call(
        dat_kernel,
        "dat_gather",
        12,
        [jax.ShapeDtypeStruct((8, block, width), BF), jax.ShapeDtypeStruct((8, block, PACK - QKV), BF)],
        [ANYWHERE, IN_VMEM],
        [IN_VMEM, ANYWHERE],
        [pltpu.VMEM((8, block, width), BF), pltpu.VMEM(wa.shape, BF)] + gather_sems() + [pltpu.SemaphoreType.DMA((9,))],
        32,
        dat, wa,
    )


def mlp_back(e, mid, gain, gu, hid, a2, w1, w2, moving=None):
    block, width = e.shape
    ff = hid.shape[2]
    step = math.gcd(width, 256)
    return plane_call(
        functools.partial(mlp_back_kernel, ff, step, True),
        "mlp_back",
        2 if moving is None else 9,
        [
            jax.ShapeDtypeStruct((block, width), F32),
            jax.ShapeDtypeStruct((1, width), F32),
            jax.ShapeDtypeStruct((block, width), BF),
            jax.ShapeDtypeStruct((width, 3 * ff), BF),
        ],
        [IN_VMEM, IN_VMEM, IN_VMEM, ANYWHERE],
        [IN_VMEM, IN_VMEM, IN_VMEM] + [ANYWHERE] * 5,
        [
            pltpu.VMEM((8, block, width), BF),
            pltpu.VMEM((8, block, width), BF),
            pltpu.VMEM((8, block, width), BF),
            pltpu.VMEM((8, block, 2 * ff), BF),
            pltpu.VMEM((8, block, ff), BF),
            pltpu.VMEM((width, 3 * ff), BF),
            pltpu.VMEM((block, width), F32),
            pltpu.VMEM((2, step, 3 * ff), BF),
        ]
        + gather_sems()
        + scatter_scratch(block, width)
        + [pltpu.SemaphoreType.DMA((5 + width // step,))],
        68,
        e, mid, gain, gu, hid, a2, w1, w2,
        moving=moving,
    )


def attn_back_kernel(
    step, gain, gain2_grad, dq, dk, dv, cosine, sine, h_hbm, dmid_hbm, o_hbm, a1_hbm, dat_hbm, w_hbm, e_out, sums,
    parts, h, dmid, o, a1, dat, w, dqkv, gain_rows, total, from_c, via_x, via_y, from_x, from_y, send, recv, local,
):
    here = token_place()
    loads = Loads(local)
    w_load = loads.start(w_hbm, w)
    a1_load = loads.start(a1_hbm, a1)
    dat_load = loads.start(dat_hbm, dat)
    o_load = loads.start(o_hbm, o)
    h_load = loads.start(h_hbm, h)
    dmid_load = loads.start(dmid_hbm, dmid)
    greet()
    w_load.wait()

    def fill(r):
        heads = [dq[r, :, n * LANES : (n + 1) * LANES].astype(F32) for n in range(2)]
        heads.append(turn(dk[r], cosine[r], -sine[r]))
        lanes = three_lanes([close_halves(head) for head in heads] + [dv[r]])
        for n in range(3):
            dqkv[r, :, n * LANES : (n + 1) * LANES] = lanes[n].astype(BF)
        parts[r] = dot_nt(dqkv[r], w[:, :QKV]).astype(BF)

    count = a1.shape[2] // step

    def beside(turn_number):
        if turn_number == 0:
            a1_load.wait()
            dat_load.wait()
            o_load.wait()
        half = (count + 1) // 2
        for number in range(turn_number * half, min((turn_number + 1) * half, count)):
            at = slice(number * step, (number + 1) * step)
            sums[at, :QKV] = flat_tn(a1, at, dqkv).astype(BF)
            sums[at, QKV:GAIN_AT] = flat_tn(dat, at, o).astype(BF)

    net = Scatter(here, parts, total, (from_c, via_x, via_y, from_x, from_y), (send, recv), fill).run(beside)
    h_load.wait()
    dmid_load.wait()
    da1 = total[...]
    x = h[...].astype(F32)
    r1 = inverse_of(x)
    n1 = x * r1
    e_out[...] = (dmid[...] + norm_back(da1, n1, r1, gain[0:1, :])).astype(BF)
    gain_rows[...] = jnp.zeros_like(gain_rows)
    first = GAIN_AT - PACK + LANES
    gain_rows[first : first + 1, :] = jnp.sum(da1 * n1, axis=0, keepdims=True)
    gain_rows[first + 1 : first + 2, :] = gain2_grad[...]
    columns = gain_rows[...].T
    last = sums[:, PACK - LANES :].astype(F32)
    sums[:, PACK - LANES :] = jnp.where(lane(last) < first, last, columns).astype(BF)
    net.drain()


def attn_back(h, dmid, gain, gain2_grad, dq, dk, dv, cosine, sine, o, a1, dat, w):
    block, width = h.shape
    step = math.gcd(width, 256)
    return plane_call(
        functools.partial(attn_back_kernel, step),
        "attn_back",
        3,
        [
            jax.ShapeDtypeStruct((block, width), BF),
            jax.ShapeDtypeStruct((width, PACK), BF),
        ],
        [IN_VMEM, IN_VMEM],
        [IN_VMEM] * 7 + [ANYWHERE] * 6,
        [
            pltpu.VMEM((8, block, width), BF),
            pltpu.VMEM(h.shape, h.dtype),
            pltpu.VMEM(dmid.shape, dmid.dtype),
            pltpu.VMEM(o.shape, o.dtype),
            pltpu.VMEM((8, block, width), BF),
            pltpu.VMEM((8, block, width), BF),
            pltpu.VMEM(w.shape, BF),
            pltpu.VMEM((8, block, QKV), BF),
            pltpu.VMEM((LANES, width), F32),
            pltpu.VMEM((block, width), F32),
        ]
        + scatter_scratch(block, width)
        + [pltpu.SemaphoreType.DMA((6,))],
        36,
        gain, gain2_grad, dq, dk, dv, cosine, sine, h, dmid, o, a1, dat, w,
    )


def exchange_kernel(homeward, blocks, got, send_sem, recv_sem, local, swap=None):
    here = place()
    x, c, y = here
    swap = swap and Swap(homeward, *swap)
    masks = [(dx, dc, dy) for dx in range(2) for dc in range(2) for dy in range(2)][1:]
    peer = lambda mask: {"x": flip(x, mask[0]), "c": flip(c, mask[1]), "y": flip(y, mask[2])}
    own = rank_of(here, 0, 0, 0)
    mine = pltpu.make_async_copy(blocks.at[own], got.at[own], local)
    mine.start()
    barrier = pltpu.get_barrier_semaphore()
    for mask in masks:
        pl.semaphore_signal(barrier, inc=1, device_id=peer(mask), device_id_type=MESH)
    if swap is None:
        pl.semaphore_wait(barrier, 7)
    else:
        swap.greet(barrier)
        swap.met(barrier, 7)
        swap.start()

    def copy(n, src, dst):
        return pltpu.make_async_remote_copy(
            src_ref=src,
            dst_ref=dst,
            send_sem=send_sem.at[n],
            recv_sem=recv_sem.at[n],
            device_id=peer(masks[n]),
            device_id_type=MESH,
        )

    copies = [copy(n, blocks.at[rank_of(here, *mask)], got.at[own]) for n, mask in enumerate(masks)]
    for started in copies:
        started.start()
    mine.wait()
    for n, mask in enumerate(masks):
        where = got.at[rank_of(here, *mask)]
        copy(n, where, where).wait_recv()
    for started in copies:
        started.wait_send()
    if swap is not None:
        swap.wait()


def exchange(number, blocks, moving=None, homeward=False):
    return plane_call(
        functools.partial(exchange_kernel, homeward),
        "exchange",
        number,
        [jax.ShapeDtypeStruct(blocks.shape, BF)],
        [ANYWHERE],
        [ANYWHERE],
        [pltpu.SemaphoreType.DMA((7,)), pltpu.SemaphoreType.DMA((7,)), pltpu.SemaphoreType.DMA],
        blocks.size // 40000,
        blocks,
        moving=moving,
    )


def finish_kernel(ff, got, gate, up, down):
    gate[...] = got[0, :, :ff].astype(F32)
    up[...] = got[0, :, ff : 2 * ff].astype(F32)
    down[...] = got[0, :, 2 * ff :].astype(F32)


def finish(got):
    ranks, rows, cols = got.shape
    ff = cols // 3
    return pl.pallas_call(
        functools.partial(finish_kernel, ff),
        grid=(ranks,),
        out_shape=[jax.ShapeDtypeStruct((rows, ranks * ff), F32)] * 3,
        in_specs=[pl.BlockSpec((1, rows, cols), lambda i: (i, 0, 0))],
        out_specs=[pl.BlockSpec((rows, ff), lambda i: (0, i))] * 3,
        compiler_params=pltpu.CompilerParams(vmem_limit_bytes=VMEM_LIMIT),
        name="finish",
    )(got)


def finish_attn_kernel(got, query, key, value, out, gains):
    ranks = got.shape[0]

    def lanes(t, n):
        return got[t, :, n * LANES : (n + 1) * LANES].astype(F32)

    groups = [four_heads(*(lanes(t, n) for n in range(3))) for t in range(ranks)]

    def write(ref, heads):
        for n in range(0, len(heads), 4):
            for j, part in enumerate(three_lanes(heads[n : n + 4])):
                at = n * HEAD_SIZE + j * LANES
                ref[:, at : at + LANES] = part

    write(query, [head for group in groups for head in group[:2]])
    write(key, [group[2] for group in groups])
    write(value, [group[3] for group in groups])
    out_heads = []
    total = None
    for t in range(ranks):
        a, b = lanes(t, 3), lanes(t, 4)
        out_heads += [a, pltpu.roll(jnp.where(lane(a) >= HEAD_SIZE, a, b), LANES - HEAD_SIZE, 1)]
        total = b if total is None else total + b
    write(out, out_heads)
    first = GAIN_AT - PACK + LANES
    gains[...] = total.T[first : first + 2]


def finish_attn(got):
    ranks, rows, _ = got.shape
    wide, narrow = jax.ShapeDtypeStruct((rows, ranks * OUT), F32), jax.ShapeDtypeStruct((rows, ranks * HEAD_SIZE), F32)
    return pl.pallas_call(
        finish_attn_kernel,
        out_shape=[wide, narrow, narrow, wide, jax.ShapeDtypeStruct((2, rows), F32)],
        in_specs=[IN_VMEM],
        out_specs=[IN_VMEM] * 5,
        compiler_params=pltpu.CompilerParams(vmem_limit_bytes=VMEM_LIMIT),
        name="finish_attn",
    )(got)


LOWER=-1e30
def dot(a, b, dims):
    return lax.dot_general(a, b, (dims, ((), ())), preferred_element_type=F32)

def attend_kernel(scale2, bq, bk, bounds, length, q, k, v, qpos, out, lse):
    groups = q.shape[0]
    i = pl.program_id(0)
    rows = groups * bq
    qs = q[...].reshape(rows, LANES)
    pos = qpos[0]
    pos2 = jnp.concatenate([pos] * groups, axis=1)
    def step(masked, j, state):
        top, total, acc = state
        at = pl.ds(pl.multiple_of(j * bk, bk), bk)
        s = dot(k[at, :], qs, ((1,), (1,)))
        if masked:
            kp = j * bk + lax.broadcasted_iota(jnp.int32, (bk, 1), 0)
            ok = (kp <= pos2) & (kp < length[0])
            s = jnp.where(ok, s, LOWER)
        new = jnp.maximum(top, jnp.max(s, axis=0, keepdims=True) * scale2)
        p = jnp.exp2(s * scale2 - new)
        alpha = jnp.exp2(top - new)
        total = total * alpha + jnp.sum(p, axis=0, keepdims=True)
        acc = acc * alpha + dot(v[at, :], p.astype(BF), ((0,), (0,)))
        return new, total, acc
    state = (jnp.full((1, rows), LOWER, F32), jnp.zeros((1, rows), F32), jnp.zeros((LANES, rows), F32))
    full, end = bounds[0, i], bounds[1, i]
    state = lax.fori_loop(0, full, functools.partial(step, False), state)
    top, total, acc = lax.fori_loop(full, end, functools.partial(step, True), state)
    o = (acc / total).T
    first, second = o[:bq], pltpu.roll(o[bq:], HEAD_SIZE, 1)
    out[:, :LANES] = jnp.where(lane(first) < HEAD_SIZE, first, second).astype(BF)
    out[:, LANES:] = second[:, : OUT - LANES].astype(BF)
    lse[...] = (top + jnp.log2(total))[None]

def attend(q, k, v, qpos, bounds, length, bq, bk, scale2):
    groups, tokens, _ = q.shape
    n = tokens // bq
    out, lse = pl.pallas_call(
        functools.partial(attend_kernel, scale2, bq, bk),
        grid_spec=pltpu.PrefetchScalarGridSpec(
            num_scalar_prefetch=2, grid=(n,),
            in_specs=[
                pl.BlockSpec((groups, bq, LANES), lambda i, *_: (0, i, 0)),
                pl.BlockSpec(k.shape, lambda i, *_: (0, 0)),
                pl.BlockSpec(v.shape, lambda i, *_: (0, 0)),
                pl.BlockSpec((1, 1, bq), lambda i, *_: (i, 0, 0)),
            ],
            out_specs=[
                pl.BlockSpec((bq, OUT), lambda i, *_: (i, 0)),
                pl.BlockSpec((1, 1, groups * bq), lambda i, *_: (i, 0, 0)),
            ]),
        out_shape=[jax.ShapeDtypeStruct((tokens, OUT), BF), jax.ShapeDtypeStruct((n, 1, groups * bq), F32)],
        compiler_params=pltpu.CompilerParams(vmem_limit_bytes=VMEM_LIMIT),
        name="attend",
        cost_estimate=pl.CostEstimate(flops=0, bytes_accessed=45000000, transcendentals=0),
    )(bounds, length, q, k, v, qpos)
    return out, lse

def back_kernel(scale, scale2, bq, bk, bounds, length, q, k, v, qpos, o, do, lse, cosine, sine, dq, dk, dv):
    groups = q.shape[0]
    i = pl.program_id(0)
    @pl.when(i == 0)
    def _():
        dk[...] = jnp.zeros_like(dk)
        dv[...] = jnp.zeros_like(dv)
    qs = q[...].reshape(groups * bq, LANES)
    do0, do1 = do[:, :LANES].astype(F32), do[:, LANES : 2 * LANES].astype(F32)
    at = lane(do0)
    do1 = pltpu.roll(jnp.where(at >= HEAD_SIZE, do0, do1), LANES - HEAD_SIZE, 1)
    wide = jnp.concatenate([jnp.where(at < HEAD_SIZE, do0, 0.0), jnp.where(at < HEAD_SIZE, do1, 0.0)], axis=0)
    dos = wide.astype(BF)
    o0 = o[:, :LANES].astype(F32)
    o1 = jnp.concatenate([o[:, LANES:].astype(F32), jnp.zeros((bq, 2 * LANES - OUT), F32)], axis=1)
    o1 = pltpu.roll(jnp.where(at >= HEAD_SIZE, o0, o1), LANES - HEAD_SIZE, 1)
    delta = jnp.sum(wide * jnp.concatenate([o0, o1], axis=0), axis=1, keepdims=True).reshape(1, groups * bq)
    lse_row = lse[0]
    pos = qpos[0]
    pos2 = jnp.concatenate([pos] * groups, axis=1)
    def step(masked, j, acc):
        at = pl.ds(pl.multiple_of(j * bk, bk), bk)
        kb, vb = k[at, :], v[at, :]
        s = dot(kb, qs, ((1,), (1,)))
        p = jnp.exp2(s * scale2 - lse_row)
        if masked:
            kp = j * bk + lax.broadcasted_iota(jnp.int32, (bk, 1), 0)
            ok = (kp <= pos2) & (kp < length[0])
            p = jnp.where(ok, p, 0.0)
        dp = dot(vb, dos, ((1,), (1,)))
        ds = (p * (dp - delta)).astype(BF)
        dv[at, :] += dot(p.astype(BF), dos, ((1,), (0,)))
        dk[at, :] += dot(ds, qs, ((1,), (0,))) * scale
        return acc + dot(ds, kb, ((0,), (0,)))
    full, end = bounds[0, i], bounds[1, i]
    acc = jnp.zeros((groups * bq, LANES), F32)
    acc = lax.fori_loop(0, full, functools.partial(step, False), acc)
    acc = lax.fori_loop(full, end, functools.partial(step, True), acc) * scale
    for g in range(groups):
        dq[:, g * LANES:(g + 1) * LANES] = turn(acc[g * bq:(g + 1) * bq], cosine[...], -sine[...]).astype(BF)

def attend_back(q, k, v, qpos_row, o, do, lse, cosine, sine, bounds, length, bq, bk, scale, scale2):
    groups, tokens, _ = q.shape
    n = tokens // bq
    wide = pl.BlockSpec((bq, groups * LANES), lambda i, *_: (i, 0))
    narrow = pl.BlockSpec((bq, OUT), lambda i, *_: (i, 0))
    return pl.pallas_call(
        functools.partial(back_kernel, scale, scale2, bq, bk),
        grid_spec=pltpu.PrefetchScalarGridSpec(
            num_scalar_prefetch=2, grid=(n,),
            in_specs=[
                pl.BlockSpec((groups, bq, LANES), lambda i, *_: (0, i, 0)),
                pl.BlockSpec(k.shape, lambda i, *_: (0, 0)),
                pl.BlockSpec(v.shape, lambda i, *_: (0, 0)),
                pl.BlockSpec((1, 1, bq), lambda i, *_: (i, 0, 0)),
                narrow, wide,
                pl.BlockSpec((1, 1, groups * bq), lambda i, *_: (i, 0, 0)),
                pl.BlockSpec((bq, LANES), lambda i, *_: (i, 0)),
                pl.BlockSpec((bq, LANES), lambda i, *_: (i, 0)),
            ],
            out_specs=[wide, pl.BlockSpec(k.shape, lambda i, *_: (0, 0)), pl.BlockSpec(k.shape, lambda i, *_: (0, 0))]),
        out_shape=[jax.ShapeDtypeStruct((tokens, groups * LANES), BF), jax.ShapeDtypeStruct(k.shape, F32), jax.ShapeDtypeStruct(k.shape, F32)],
        compiler_params=pltpu.CompilerParams(vmem_limit_bytes=VMEM_LIMIT),
        name="attend_back",
        cost_estimate=pl.CostEstimate(flops=0, bytes_accessed=65000000, transcendentals=0),
    )(bounds, length, q, k, v, qpos_row, o, do, lse, cosine, sine)

def bounds_of(positions, length, bq, bk):
    p = positions.reshape(-1, bq)
    lo = jnp.minimum(jnp.min(p, axis=1) + 1, length) // bk
    hi = -(-jnp.minimum(jnp.max(p, axis=1) + 1, length) // bk)
    return jnp.stack([lo, hi]).astype(jnp.int32)


PLANE = ("x", "c", "y")

def together(*arrays):
    return lax.optimization_barrier(arrays)


def body(
    inputs,
    lengths,
    cotangent,
    attn_gain,
    w_query,
    key_projection,
    value_projection,
    w_out,
    mlp_gain,
    w_gate,
    w_up,
    w_down,
):
    sections = lax.axis_size("x") * lax.axis_size("c")
    planes = lax.axis_size("z")
    halves = lax.axis_size("y")
    extra = lax.axis_size("e")
    ranks = sections * halves
    layers = sections
    block = inputs.shape[1]
    width = inputs.shape[2]
    rows = w_query.shape[1]
    tokens = block * ranks
    all_tokens = tokens * extra
    head_group = QUERY_HEADS // KEY_VALUE_HEADS
    q_cols = head_group * HEAD_SIZE
    kv_cols = HEAD_SIZE
    ff_cols = FF // ranks
    scale = 1.0 / math.sqrt(HEAD_SIZE)
    scale2 = scale * math.log2(math.e)

    def by_rank(matrix):
        return matrix.reshape(rows, ranks, -1)

    attn_pack = jnp.concatenate(
        [
            by_rank(w_query[0]),
            by_rank(key_projection[0]),
            by_rank(value_projection[0]),
            by_rank(w_out[0].T),
            jnp.broadcast_to(jnp.stack([attn_gain[0], mlp_gain[0]], axis=1)[:, None, :], (rows, ranks, 2)),
            jnp.zeros((rows, ranks, PACK - GAIN_AT - 2), F32),
        ],
        axis=2,
    )
    def by_layer(got):
        return got.reshape(layers, halves, rows, -1)

    def ready(pack):
        return jnp.swapaxes(pack.astype(BF), 0, 1)

    def whole(part):
        if extra > 1:
            part = lax.all_gather(part, "e", axis=1, tiled=False)
        return lax.all_gather(part.reshape(-1, part.shape[-1]), "z", axis=0, tiled=True)

    def reduce_rows(sums):
        mine = lax.psum_scatter(sums, "z", scatter_dimension=0, tiled=True)
        mine = mine.reshape(halves, extra, rows, -1)
        if extra > 1:
            return lax.psum_scatter(mine, "e", scatter_dimension=1, tiled=False)
        return mine[:, 0]

    cut = 3 * ff_cols // 2
    attn_got, hidden_state = exchange(4, ready(attn_pack), inputs[0])
    gate, up, down, attn_got = together(w_gate[0], w_up[0], w_down[0].T, attn_got)
    mlp_blocks = ready(jnp.concatenate([by_rank(gate), by_rank(up), by_rank(down)], axis=2))
    (first_got,) = exchange(5, mlp_blocks[..., :cut])

    token_x, token_c, token_y = token_place()
    rank = (token_x * 2 + token_c) * halves + token_y
    spot = lax.axis_index("e")
    length = lengths[micro_of_plane()]

    block_start = (jnp.arange(ranks) * extra + spot) * block
    positions = (block_start[:, None] + jnp.arange(block)[None, :]).reshape(tokens)
    exponents = 2.0 * jnp.arange(HEAD_SIZE // 2).astype(F32) / HEAD_SIZE
    angles = positions.astype(F32)[:, None] * (THETA ** (-exponents))[None, :]
    table = lambda values: jnp.pad(values, ((0, 0), (0, LANES // 2 - HALF)))
    cosine = jnp.concatenate([table(jnp.cos(angles))] * 2, axis=1)
    sine = jnp.concatenate([table(-jnp.sin(angles)), table(jnp.sin(angles))], axis=1)
    bq = math.gcd(tokens, 512)
    bk = math.gcd(all_tokens, 512)
    bounds = bounds_of(positions, length, bq, bk)
    length1 = length.reshape(1)
    query_rows = positions.astype(jnp.int32).reshape(-1, 1, bq)

    def all_keys(array):
        if extra == 1:
            return array
        stacked = lax.all_gather(array.reshape(ranks, block, -1), "e", axis=1, tiled=False)
        return stacked.reshape(all_tokens, -1)

    def own_keys(array):
        if extra == 1:
            return array
        stacked = array.astype(BF).reshape(ranks, extra, block, -1)
        return lax.psum_scatter(stacked, "e", scatter_dimension=1, tiled=False).reshape(tokens, -1).astype(F32)

    cosine3 = cosine.reshape(ranks, block, LANES)
    sine3 = sine.reshape(ranks, block, LANES)

    second_blocks, first_got, cosine, sine, cosine3, sine3, bounds, query_rows = together(
        mlp_blocks[..., cut:], first_got, cosine, sine, cosine3, sine3, bounds, query_rows
    )
    (second_got,) = exchange(6, second_blocks)
    attn_parts, first_parts, second_parts = by_layer(attn_got), by_layer(first_got), by_layer(second_got)

    def flat(array):
        return array.reshape(tokens, array.shape[-1])

    saved = []
    attn_w, w_1 = whole(attn_parts[0]), whole(first_parts[0])
    hidden_state, attn_w, w_1, second_part = together(hidden_state, attn_w, w_1, second_parts[0])
    w_2 = whole(second_part)
    for layer in range(layers):
        a1, q, k, v, gain = attn_in(hidden_state, attn_w, cosine3, sine3)
        q, k, v = q.reshape(head_group, tokens, LANES), all_keys(flat(k)), all_keys(flat(v))
        o, log_total = attend(q, k, v, query_rows, bounds, length1, bq, bk, scale2)
        if layer + 1 < layers:
            o, attn_part, first_part = together(o, attn_parts[layer + 1], first_parts[layer + 1])
            next_attn, next_1 = whole(attn_part), whole(first_part)
        mid, a2, gu, hid, after_mlp, *moved = mlp(
            hidden_state, o.reshape(ranks, block, -1), gain, attn_w, w_1, w_2,
            cotangent[0] if layer + 1 == layers else None,
        )
        saved.append((hidden_state, a1, q, k, v, o, log_total, mid, a2, gu, hid, attn_w, w_1, w_2, gain))
        hidden_state = after_mlp
        if layer + 1 < layers:
            hidden_state, attn_w, w_1, second_part = together(hidden_state, next_attn, next_1, second_parts[layer + 1])
            w_2 = whole(second_part)
    output = hidden_state

    my_positions = (rank * extra + spot) * block + jnp.arange(block)
    (e,) = moved
    e = jnp.where((my_positions < length)[:, None], e, jnp.zeros_like(e))
    attn_grads = [None] * layers
    mlp_grads = [None] * layers
    for layer in reversed(range(layers)):
        (h, a1, q, k, v, o, log_total, mid, a2, gu, hid, attn_w, w_1, w_2, gain) = saved[layer]
        dmid, gain2, dat, mlp_sums, *moved = mlp_back(
            e, mid, gain, gu, hid, a2, w_1, w_2, output if layer + 1 == layers else None
        )
        if moved:
            (output,) = moved
        else:
            dat, mlp_sums, attn_grads[layer + 1] = together(dat, mlp_sums, attn_grads[layer + 1])
        mlp_grads[layer] = reduce_rows(mlp_sums)
        dat, dob = dat_gather(dat, attn_w)
        dq, dk, dv = attend_back(
            q, k, v, query_rows, o, flat(dob), log_total, cosine, sine, bounds, length1, bq, bk, scale, scale2
        )
        dk, dv = own_keys(dk), own_keys(dv)
        e, attn_sums = attn_back(
            h, dmid, gain, gain2, *(array.reshape(ranks, block, -1) for array in (dq, dk, dv)), cosine3, sine3,
            o.reshape(ranks, block, -1), a1, dat, attn_w,
        )
        e, attn_sums, mlp_grads[layer] = together(e, attn_sums, mlp_grads[layer])
        attn_grads[layer] = reduce_rows(attn_sums)

    def by_place(grads):
        return jnp.stack(grads).reshape(ranks, rows, -1)

    mlp_home, input_grad = exchange(7, by_place(mlp_grads), e, True)
    attn_blocks, mlp_home = together(by_place(attn_grads), mlp_home)
    (attn_home,) = exchange(10, attn_blocks)
    grad_gate, grad_up, grad_down = finish(mlp_home)
    grad_query, grad_key, grad_value, grad_out, gain_sums = finish_attn(attn_home)
    return (
        output[None],
        input_grad[None],
        gain_sums[0:1],
        grad_query[None],
        grad_key[None],
        grad_value[None],
        grad_out.T[None],
        gain_sums[1:2],
        grad_gate[None],
        grad_up[None],
        grad_down.T[None],
    )


def solution(mesh):
    section, seq = mesh.devices.shape
    halves = KEY_VALUE_HEADS // section
    extra = seq // (section * halves)
    fine = Mesh(
        mesh.devices.reshape(section // 2, 2, section, halves, extra), ("x", "c", "z", "y", "e")
    )
    sec, sq = ("x", "c"), ("z", "y", "e")
    rows3 = P(sec, sq, None)
    cols3 = P(sec, None, sq)
    in_specs = (rows3, P(), rows3, P(sec, sq), rows3, rows3, rows3, cols3, P(sec, sq), rows3, rows3, cols3)
    out_specs = (rows3, rows3, P(sec, sq), rows3, rows3, rows3, cols3, P(sec, sq), rows3, rows3, cols3)
    return jax.shard_map(body, mesh=fine, in_specs=in_specs, out_specs=out_specs, check_vma=False)
```

```python
import functools
import math

import jax
import jax.numpy as jnp
from jax import lax
from jax.experimental import pallas as pl
from jax.experimental.pallas import tpu as pltpu
from jax.sharding import Mesh
from jax.sharding import PartitionSpec as P

QUERY_HEADS = 16
KEY_VALUE_HEADS = 8
HEAD_SIZE = 96
FF = 4096

EPS = 1e-05
THETA = 100000.0
LOWER_LIMIT = -1e30

BF = jnp.bfloat16
F32 = jnp.float32

LANES = 128
HALF = HEAD_SIZE // 2
VMEM_LIMIT = 56 * 1024 * 1024


def dot(a, b, dims):
    return lax.dot_general(a, b, (dims, ((), ())), preferred_element_type=F32)


def dot_nn(a, b):
    return dot(a, b, ((1,), (0,)))


def dot_nt(a, b):
    return dot(a, b, ((1,), (1,)))


def dot_tn(a, b):
    return dot(a, b, ((0,), (0,)))


MESH = pl.DeviceIdType.MESH

OWN, X, Y, D = (0, 0), (1, 0), (0, 1), (1, 1)


def place():
    return lax.axis_index("x"), lax.axis_index("c"), lax.axis_index("y")


def xor(a, b):
    return a + b - 2 * a * b


def token_place():
    x, c, y = place()
    z = lax.axis_index("z")
    return xor(x, xor(lax.rem(z, 2), z // 2)), c, y


def micro_of_plane():
    z = lax.axis_index("z")
    return lax.rem(z, 2) * 2 + z // 2


def flip(index, by):
    return 1 - index if by else index


def rank_of(here, dx, dc, dy):
    x, c, y = here
    return (flip(x, dx) * 2 + flip(c, dc)) * 2 + flip(y, dy)


class Swap:
    def __init__(self, homeward, moving, moved, sem):
        x, c, _ = place()
        z = lax.axis_index("z")
        low = lax.rem(z, 2)
        high = z // 2
        out = {"x": xor(high, xor(x, c)), "c": low, "z": c * 2 + x}
        back = {"x": low, "c": high, "z": 2 * xor(x, xor(low, high)) + c}
        target, self.source = (back, out) if homeward else (out, back)
        self.away = (target["x"] != x) | (target["c"] != c) | (target["z"] != z)
        self.remote = pltpu.make_async_remote_copy(
            src_ref=moving,
            dst_ref=moved,
            send_sem=sem.at[0],
            recv_sem=sem.at[1],
            device_id=target,
            device_id_type=MESH,
        )
        self.local = pltpu.make_async_copy(moving, moved, sem.at[2])

    def greet(self, barrier):
        @pl.when(self.away)
        def _():
            pl.semaphore_signal(barrier, inc=1, device_id=self.source, device_id_type=MESH)

    def either(self, remote, local):
        pl.when(self.away)(remote)
        pl.when(jnp.logical_not(self.away))(local)

    def start(self):
        self.either(lambda: self.remote.start(), lambda: self.local.start())

    def met(self, barrier, count):
        self.either(lambda: pl.semaphore_wait(barrier, count + 1), lambda: pl.semaphore_wait(barrier, count))

    def wait(self):
        self.either(lambda: self.remote.wait(), lambda: self.local.wait())


def with_swap(kernel, inputs, outputs):
    def wrapped(*refs):
        last = inputs + 1 + outputs
        kernel(
            *refs[:inputs],
            *refs[inputs + 1 : last],
            *refs[last + 1 : -1],
            swap=(refs[inputs], refs[last], refs[-1]),
        )

    return wrapped


def greet(swap=None):
    x, c, y = place()
    barrier = pltpu.get_barrier_semaphore()
    for peer in ({"x": 1 - x}, {"c": 1 - c}, {"y": 1 - y}):
        pl.semaphore_signal(barrier, inc=1, device_id=peer, device_id_type=MESH)
    if swap is None:
        pl.semaphore_wait(barrier, 3)
    else:
        swap.greet(barrier)
        swap.met(barrier, 3)
        swap.start()


class Sender:
    def __init__(self, send_sem, recv_sem):
        x, c, y = place()
        self.peers = {"x": {"x": 1 - x}, "c": {"c": 1 - c}, "y": {"y": 1 - y}}
        self.send_sem, self.recv_sem = send_sem, recv_sem
        self.sent = []

    def copy(self, src, dst, index, to, number):
        return pltpu.make_async_remote_copy(
            src_ref=src,
            dst_ref=dst,
            send_sem=self.send_sem.at[number],
            recv_sem=self.recv_sem.at[index],
            device_id=self.peers[to],
            device_id_type=MESH,
        )

    def send(self, src, dst, index, to):
        started = self.copy(src, dst, index, to, len(self.sent))
        started.start()
        self.sent.append(started)

    def arrived(self, where, index):
        self.copy(where, where, index, "c", 0).wait_recv()

    def drain(self):
        for started in self.sent:
            started.wait_send()


class Gather:
    def __init__(self, here, full, sems):
        self.here, self.full = here, full
        self.piece = full.shape[1] // 4
        self.net = Sender(*sems)

    def index(self, role, chunk):
        return (role[0] * 4 + role[1] * 2 + role[2]) * 4 + chunk

    def slot(self, role, chunk):
        return self.full.at[rank_of(self.here, *role), pl.ds(chunk * self.piece, self.piece)]

    def send(self, role, chunk, to, as_role):
        where = self.slot(role, chunk)
        self.net.send(where, where, self.index(as_role, chunk), to)

    def arrived(self, role, chunk):
        self.net.arrived(self.slot(role, chunk), self.index(role, chunk))

    def own(self, cx, cy):
        self.send((0, 0, 0), cx, "x", (1, 0, 0))
        self.send((0, 0, 0), cy, "y", (0, 0, 1))

    def all_own(self):
        for cx, cy in ((2, 0), (3, 1), (0, 2), (1, 3)):
            self.own(cx, cy)
        return self

    def run(self, on_block, before_last=None):
        send, arrived = self.send, self.arrived
        at_x, at_y, at_d, at_c = (1, 0, 0), (0, 0, 1), (1, 0, 1), (0, 1, 0)
        xc, yc, dc = (1, 1, 0), (0, 1, 1), (1, 1, 1)

        def whole(role):
            for chunk in range(4):
                arrived(role, chunk)

        def done(role):
            on_block(rank_of(self.here, *role))

        def pass_on(cx, cy):
            arrived(at_x, cx)
            if cx >= 2:
                send(at_x, cx, "y", at_d)
            send(at_x, cx, "c", xc)
            arrived(at_y, cy)
            if cy < 2:
                send(at_y, cy, "x", at_d)
            send(at_y, cy, "c", yc)

        def pass_last(chunks):
            for chunk in chunks:
                arrived(at_d, chunk)
                send(at_d, chunk, "c", dc)

        for chunk in range(4):
            send((0, 0, 0), chunk, "c", at_c)
        done((0, 0, 0))
        pass_on(2, 0)
        whole(at_c)
        done(at_c)
        pass_on(3, 1)
        pass_on(0, 2)
        pass_on(1, 3)
        done(at_x)
        done(at_y)
        pass_last((0, 2))
        whole(xc)
        done(xc)
        whole(yc)
        done(yc)
        if before_last is not None:
            before_last()
        pass_last((1, 3))
        done(at_d)
        whole(dc)
        done(dc)
        return self.net


def run_gather(here, full, sems, on_block, before_last=None):
    return Gather(here, full, sems).all_own().run(on_block, before_last)


class Scatter:
    order = (D, X, Y, OWN)

    def __init__(self, here, parts, total, bufs, sems, fill=None):
        self.here, self.parts, self.total, self.fill = here, parts, total, fill
        self.from_c, self.via_x, self.via_y, self.from_x, self.from_y = bufs
        half = parts.shape[1] // 2
        self.piece = half // 2
        self.lower, self.upper = pl.ds(0, half), pl.ds(half, half)
        self.net = Sender(*sems)

    def rank(self, n, dc):
        return rank_of(self.here, self.order[n][0], dc, self.order[n][1])

    def make(self, r):
        if self.fill is not None:
            self.fill(r)

    def sibling(self, n):
        r = self.rank(n, 1)
        self.make(r)
        self.net.send(self.parts.at[r], self.from_c.at[n], n, "c")

    def add(self, n, where, more):
        r = self.rank(n, 0)
        self.parts[r, where] = (self.parts[r, where].astype(F32) + more.astype(F32)).astype(BF)

    def mine(self, n, where):
        return self.parts.at[self.rank(n, 0), where]

    def combine(self, n):
        self.make(self.rank(n, 0))
        self.net.arrived(self.from_c.at[n], n)
        if n < 3:
            self.add(n, pl.ds(0, self.parts.shape[1]), self.from_c[n])

    def rows(self, number):
        return pl.ds(number * self.piece, self.piece)

    def to_diagonal(self):
        self.combine(0)
        for n in range(2):
            self.net.send(self.mine(0, self.rows(n + 2)), self.via_x.at[self.rows(n)], 4 + n, "x")
            self.net.send(self.mine(0, self.rows(n)), self.via_y.at[self.rows(n)], 6 + n, "y")

    def to_x(self):
        self.combine(1)
        self.net.send(self.mine(1, self.upper), self.from_x.at[self.upper], 8, "x")

    def to_y(self):
        self.combine(2)
        self.net.send(self.mine(2, self.lower), self.from_y.at[self.lower], 9, "y")

    def early(self):
        for n in (1, 2, 3):
            self.sibling(n)
        self.to_x()
        self.to_y()

    def run(self, beside=None, early_done=False, on_rows=None):
        net, total, lower, upper = self.net, self.total, self.lower, self.upper
        self.sibling(0)
        self.to_diagonal()
        if not early_done:
            self.sibling(1)
            self.to_x()
            self.sibling(2)
            self.to_y()
            self.sibling(3)
        self.combine(3)
        total[...] = self.parts[self.rank(3, 0)].astype(F32) + self.from_c[3].astype(F32)
        if beside is not None:
            beside(0)
        for n in range(2):
            at, above = self.rows(n), self.rows(n + 2)
            net.arrived(self.via_y.at[at], 6 + n)
            self.add(1, at, self.via_y[at])
            net.send(self.mine(1, at), self.from_x.at[at], 10 + n, "x")
            net.arrived(self.via_x.at[at], 4 + n)
            self.add(2, above, self.via_x[at])
            net.send(self.mine(2, above), self.from_y.at[above], 12 + n, "y")
        if beside is not None:
            beside(1)
        net.arrived(self.from_x.at[upper], 8)
        net.arrived(self.from_y.at[lower], 9)
        total[upper] += self.from_x[upper].astype(F32)
        total[lower] += self.from_y[lower].astype(F32)
        for n in range(2):
            at, above = self.rows(n), self.rows(n + 2)
            net.arrived(self.from_x.at[at], 10 + n)
            net.arrived(self.from_y.at[above], 12 + n)
            total[at] += self.from_x[at].astype(F32)
            total[above] += self.from_y[above].astype(F32)
            if on_rows is not None:
                on_rows(n)
        return net


def gather_sems():
    return [pltpu.SemaphoreType.DMA((32,)), pltpu.SemaphoreType.DMA((32,))]


def scatter_scratch(block, width):
    half = block // 2
    return [
        pltpu.VMEM((4, block, width), BF),
        pltpu.VMEM((half, width), BF),
        pltpu.VMEM((half, width), BF),
        pltpu.VMEM((block, width), BF),
        pltpu.VMEM((block, width), BF),
        pltpu.SemaphoreType.DMA((14,)),
        pltpu.SemaphoreType.DMA((14,)),
    ]


class Loads:
    def __init__(self, sem):
        self.sem = sem
        self.count = 0

    def start(self, src, dst):
        copy = pltpu.make_async_copy(src, dst, self.sem.at[self.count])
        self.count += 1
        copy.start()
        return copy


def inverse_of(x):
    return lax.rsqrt(jnp.mean(x * x, axis=-1, keepdims=True) + EPS)


def lane(x):
    return lax.broadcasted_iota(jnp.int32, x.shape, 1)


def turn(head, cosine, sine):
    return head * cosine + pltpu.roll(head, LANES // 2, 1) * sine


def open_halves(head):
    return jnp.where(lane(head) < LANES // 2, head, pltpu.roll(head, LANES // 2 - HALF, 1))


def close_halves(head):
    low = lane(head) < LANES // 2
    return jnp.where(low, head, 0.0) + pltpu.roll(jnp.where(low, 0.0, head), LANES // 2 + HALF, 1)


def four_heads(a, b, c):
    at = lane(a)
    return (
        a,
        pltpu.roll(jnp.where(at >= 96, a, b), 32, 1),
        pltpu.roll(jnp.where(at >= 64, b, c), 64, 1),
        pltpu.roll(c, 96, 1),
    )


def three_lanes(heads):
    at = lane(heads[0])
    b, c, d = pltpu.roll(heads[1], 96, 1), pltpu.roll(heads[2], 64, 1), pltpu.roll(heads[3], 32, 1)
    return jnp.where(at < 96, heads[0], b), jnp.where(at < 64, b, c), jnp.where(at < 32, c, d)


def plane_call(kernel, name, number, out_shape, out_specs, in_specs, scratch, time_us, *operands, moving=None):
    if moving is not None:
        kernel = with_swap(kernel, len(in_specs), len(out_specs))
        out_shape = out_shape + [jax.ShapeDtypeStruct(moving.shape, moving.dtype)]
        in_specs, out_specs = in_specs + [ANYWHERE], out_specs + [ANYWHERE]
        scratch = scratch + [pltpu.SemaphoreType.DMA((3,))]
        operands = operands + (moving,)
    return pl.pallas_call(
        kernel,
        out_shape=out_shape,
        in_specs=in_specs,
        out_specs=out_specs,
        scratch_shapes=scratch,
        compiler_params=pltpu.CompilerParams(
            collective_id=number, has_side_effects=True, vmem_limit_bytes=VMEM_LIMIT
        ),
        cost_estimate=pl.CostEstimate(flops=0, bytes_accessed=time_us * 3000000, transcendentals=0),
        name=name,
    )(*operands)


ANYWHERE = pl.BlockSpec(memory_space=pl.ANY)
IN_VMEM = pl.BlockSpec(memory_space=pltpu.VMEM)
QKV = 4 * HEAD_SIZE
OUT = 2 * HEAD_SIZE
GAIN_AT = QKV + OUT
PACK = -(-(GAIN_AT + 2) // LANES) * LANES


def attn_in_kernel(h, w_hbm, cosine, sine, a1_out, q_out, k_out, v_out, gain_out, full, w, send, recv, local):
    here = token_place()
    loads = Loads(local)
    w_load = loads.start(w_hbm, w)
    x = h[...].astype(F32)
    n1 = x * inverse_of(x)
    w_load.wait()
    rows = w[:, PACK - LANES :].astype(F32).T
    gain_out[...] = rows[GAIN_AT - PACK + LANES : GAIN_AT - PACK + LANES + 2]
    full[rank_of(here, 0, 0, 0)] = (n1 * gain_out[0:1, :]).astype(BF)
    greet()
    saves = []

    def on_block(r):
        saves.append(loads.start(full.at[r], a1_out.at[r]))
        qkv = dot_nn(full[r], w[:, :QKV])
        heads = four_heads(*(qkv[:, n * LANES : (n + 1) * LANES] for n in range(3)))
        cos, sin = cosine[r], sine[r]
        for n in range(2):
            q_out[n, r] = turn(open_halves(heads[n]), cos, sin).astype(BF)
        k_out[r] = turn(open_halves(heads[2]), cos, sin).astype(BF)
        v_out[r] = jnp.where(lane(heads[3]) < HEAD_SIZE, heads[3], 0.0).astype(BF)

    net = run_gather(here, full, (send, recv), on_block)
    net.drain()
    for save in saves:
        save.wait()


def attn_in(h, w, cosine, sine):
    block, width = h.shape
    return plane_call(
        attn_in_kernel,
        "attn_in",
        0,
        [
            jax.ShapeDtypeStruct((8, block, width), BF),
            jax.ShapeDtypeStruct((2, 8, block, LANES), BF),
            jax.ShapeDtypeStruct((8, block, LANES), BF),
            jax.ShapeDtypeStruct((8, block, LANES), BF),
            jax.ShapeDtypeStruct((2, width), F32),
        ],
        [ANYWHERE, IN_VMEM, IN_VMEM, IN_VMEM, IN_VMEM],
        [IN_VMEM, ANYWHERE, IN_VMEM, IN_VMEM],
        [pltpu.VMEM((8, block, width), BF), pltpu.VMEM(w.shape, BF)]
        + gather_sems()
        + [pltpu.SemaphoreType.DMA((9,))],
        34,
        h, w, cosine, sine,
    )


def mlp_kernel(
    ff, homeward, h, o, gain, wa_hbm, w1_hbm, w2_hbm, mid_out, a2_out, gu_out, hid_out, next_out,
    full, parts, gu, hid, wa, wm, total,
    from_c, via_x, via_y, from_x, from_y, send1, recv1, send2, recv2,
    from_c3, via_x3, via_y3, from_x3, from_y3, send3, recv3, local, swap=None,
):
    here = token_place()
    swap = swap and Swap(homeward, *swap)
    loads = Loads(local)
    wa_load = loads.start(wa_hbm, wa)
    split = w1_hbm.shape[1]
    w1_load = loads.start(w1_hbm, wm.at[:, pl.ds(0, split)])
    w2_load = loads.start(w2_hbm, wm.at[:, pl.ds(split, 3 * ff - split)])
    greet(swap)
    wa_load.wait()

    def fill(r):
        parts[r] = dot_nt(o[r], wa[:, QKV:GAIN_AT]).astype(BF)

    bufs = (from_c, via_x, via_y, from_x, from_y)
    gather = Gather(here, full, (send2, recv2))
    own = rank_of(here, 0, 0, 0)

    def on_rows(n):
        for piece in (n + 2, n):
            rows = pl.ds(piece * gather.piece, gather.piece)
            mid = h[rows].astype(F32) + total[rows]
            mid_out[rows] = mid
            full[own, rows] = (mid * inverse_of(mid) * gain[1:2, :]).astype(BF)
        if n == 0:
            gather.own(2, 0)
        else:
            for pair in ((3, 1), (0, 2), (1, 3)):
                gather.own(*pair)

    net1 = Scatter(here, parts, total, bufs, (send1, recv1), fill).run(on_rows=on_rows)
    net1.drain()
    saves = []

    def on_block(r):
        if not saves:
            w1_load.wait()
            w2_load.wait()
        saves.append(loads.start(full.at[r], a2_out.at[r]))
        a2 = full[r]
        g = dot_nn(a2, wm[:, :ff])
        u = dot_nn(a2, wm[:, ff : 2 * ff])
        gu[r, :, :ff] = g.astype(BF)
        gu[r, :, ff:] = u.astype(BF)
        low = (g * (1.0 / (1.0 + jnp.exp(-g))) * u).astype(BF)
        hid[r] = low
        saves.append(loads.start(gu.at[r], gu_out.at[r]))
        saves.append(loads.start(hid.at[r], hid_out.at[r]))
        parts[r] = dot_nt(low, wm[:, 2 * ff :]).astype(BF)

    bufs3 = (from_c3, via_x3, via_y3, from_x3, from_y3)
    scatter = Scatter(here, parts, total, bufs3, (send3, recv3))
    net2 = gather.run(on_block, scatter.early)
    net3 = scatter.run(early_done=True)
    next_out[...] = (mid_out[...] + total[...]).astype(BF)
    net2.drain()
    net3.drain()
    for save in saves:
        save.wait()
    if swap is not None:
        swap.wait()


def mlp(h, o, gain, wa, w1, w2, moving=None):
    block, width = h.shape
    ff = (w1.shape[1] + w2.shape[1]) // 3
    return plane_call(
        functools.partial(mlp_kernel, ff, False),
        "mlp",
        1 if moving is None else 8,
        [
            jax.ShapeDtypeStruct((block, width), F32),
            jax.ShapeDtypeStruct((8, block, width), BF),
            jax.ShapeDtypeStruct((8, block, 2 * ff), BF),
            jax.ShapeDtypeStruct((8, block, ff), BF),
            jax.ShapeDtypeStruct((block, width), BF),
        ],
        [IN_VMEM, ANYWHERE, ANYWHERE, ANYWHERE, IN_VMEM],
        [IN_VMEM, IN_VMEM, IN_VMEM, ANYWHERE, ANYWHERE, ANYWHERE],
        [
            pltpu.VMEM((8, block, width), BF),
            pltpu.VMEM((8, block, width), BF),
            pltpu.VMEM((8, block, 2 * ff), BF),
            pltpu.VMEM((8, block, ff), BF),
            pltpu.VMEM(wa.shape, BF),
            pltpu.VMEM((width, 3 * ff), BF),
            pltpu.VMEM((block, width), F32),
        ]
        + scatter_scratch(block, width)
        + gather_sems()
        + scatter_scratch(block, width)
        + [pltpu.SemaphoreType.DMA((27,))],
        96,
        h, o, gain, wa, w1, w2,
        moving=moving,
    )


def norm_back(upstream, normed, inverse, gain_row):
    scaled = upstream * gain_row
    return inverse * (scaled - normed * jnp.mean(scaled * normed, axis=-1, keepdims=True))


def flat_tn(a, cols, b):
    total = dot_tn(a[0, :, cols], b[0])
    for n in range(1, a.shape[0]):
        total = total + dot_tn(a[n, :, cols], b[n])
    return total


def mlp_back_kernel(
    ff, step, homeward, e, mid, gain, gu_hbm, hid_hbm, a2_hbm, w1_hbm, w2_hbm, dmid_out, gain_out, dat_out, sums_out,
    full, parts, a2, gu, hid, wm, total, stage, send1, recv1,
    from_c, via_x, via_y, from_x, from_y, send2, recv2, local, swap=None,
):
    here = token_place()
    swap = swap and Swap(homeward, *swap)
    loads = Loads(local)
    split = w1_hbm.shape[1]
    w2_load = loads.start(w2_hbm, wm.at[:, pl.ds(split, 3 * ff - split)])
    gu_load = loads.start(gu_hbm, gu)
    w1_load = loads.start(w1_hbm, wm.at[:, pl.ds(0, split)])
    a2_load = loads.start(a2_hbm, a2)
    hid_load = loads.start(hid_hbm, hid)
    own = rank_of(here, 0, 0, 0)
    full[own] = e[...]
    greet(swap)
    w2_load.wait()
    gu_load.wait()
    w1_load.wait()

    def on_block(r):
        dhid = dot_nn(full[r], wm[:, 2 * ff :])
        g = gu[r, :, :ff].astype(F32)
        u = gu[r, :, ff:].astype(F32)
        sig = 1.0 / (1.0 + jnp.exp(-g))
        du = dhid * g * sig
        dg = dhid * u * sig * (1.0 + g * (1.0 - sig))
        gu[r, :, :ff] = dg.astype(BF)
        gu[r, :, ff:] = du.astype(BF)
        parts[r] = dot_nt(gu[r], wm[:, : 2 * ff]).astype(BF)

    scatter = Scatter(here, parts, total, (from_c, via_x, via_y, from_x, from_y), (send2, recv2))
    net1 = run_gather(here, full, (send1, recv1), on_block, scatter.early)
    a2_load.wait()
    hid_load.wait()
    sums = []
    count = full.shape[2] // step

    def beside(turn_number):
        half = (count + 1) // 2
        for number in range(turn_number * half, min((turn_number + 1) * half, count)):
            if number >= 2:
                sums[number - 2].wait()
            at = slice(number * step, (number + 1) * step)
            held = stage.at[number % 2]
            held[:, : 2 * ff] = flat_tn(a2, at, gu).astype(BF)
            held[:, 2 * ff :] = flat_tn(full, at, hid).astype(BF)
            sums.append(loads.start(held, sums_out.at[pl.ds(number * step, step)]))

    net2 = scatter.run(beside, True)
    da2 = total[...]
    m = mid[...]
    r2 = inverse_of(m)
    n2 = m * r2
    gain_out[...] = jnp.sum(da2 * n2, axis=0, keepdims=True)
    dmid = e[...].astype(F32) + norm_back(da2, n2, r2, gain[1:2, :])
    dmid_out[...] = dmid
    dat_out[...] = dmid.astype(BF)
    net1.drain()
    net2.drain()
    for save in sums[-2:]:
        save.wait()
    if swap is not None:
        swap.wait()


def dat_kernel(dat, wa_hbm, dat_out, dob_out, full, wa, send, recv, local):
    here = token_place()
    loads = Loads(local)
    wa_load = loads.start(wa_hbm, wa)
    full[rank_of(here, 0, 0, 0)] = dat[...]
    greet()
    wa_load.wait()
    saves = []

    def on_block(r):
        saves.append(loads.start(full.at[r], dat_out.at[r]))
        dob_out[r] = dot_nn(full[r], wa[:, QKV:PACK]).astype(BF)

    run_gather(here, full, (send, recv), on_block).drain()
    for save in saves:
        save.wait()


def dat_gather(dat, wa):
    block, width = dat.shape
    return plane_call(
        dat_kernel,
        "dat_gather",
        12,
        [jax.ShapeDtypeStruct((8, block, width), BF), jax.ShapeDtypeStruct((8, block, PACK - QKV), BF)],
        [ANYWHERE, IN_VMEM],
        [IN_VMEM, ANYWHERE],
        [pltpu.VMEM((8, block, width), BF), pltpu.VMEM(wa.shape, BF)] + gather_sems() + [pltpu.SemaphoreType.DMA((9,))],
        32,
        dat, wa,
    )


def mlp_back(e, mid, gain, gu, hid, a2, w1, w2, moving=None):
    block, width = e.shape
    ff = hid.shape[2]
    step = math.gcd(width, 256)
    return plane_call(
        functools.partial(mlp_back_kernel, ff, step, True),
        "mlp_back",
        2 if moving is None else 9,
        [
            jax.ShapeDtypeStruct((block, width), F32),
            jax.ShapeDtypeStruct((1, width), F32),
            jax.ShapeDtypeStruct((block, width), BF),
            jax.ShapeDtypeStruct((width, 3 * ff), BF),
        ],
        [IN_VMEM, IN_VMEM, IN_VMEM, ANYWHERE],
        [IN_VMEM, IN_VMEM, IN_VMEM] + [ANYWHERE] * 5,
        [
            pltpu.VMEM((8, block, width), BF),
            pltpu.VMEM((8, block, width), BF),
            pltpu.VMEM((8, block, width), BF),
            pltpu.VMEM((8, block, 2 * ff), BF),
            pltpu.VMEM((8, block, ff), BF),
            pltpu.VMEM((width, 3 * ff), BF),
            pltpu.VMEM((block, width), F32),
            pltpu.VMEM((2, step, 3 * ff), BF),
        ]
        + gather_sems()
        + scatter_scratch(block, width)
        + [pltpu.SemaphoreType.DMA((5 + width // step,))],
        68,
        e, mid, gain, gu, hid, a2, w1, w2,
        moving=moving,
    )


def attn_back_kernel(
    step, gain, gain2_grad, dq, dk, dv, cosine, sine, h_hbm, dmid_hbm, o_hbm, a1_hbm, dat_hbm, w_hbm, e_out, sums,
    parts, h, dmid, o, a1, dat, w, dqkv, gain_rows, total, from_c, via_x, via_y, from_x, from_y, send, recv, local,
):
    here = token_place()
    loads = Loads(local)
    w_load = loads.start(w_hbm, w)
    a1_load = loads.start(a1_hbm, a1)
    dat_load = loads.start(dat_hbm, dat)
    o_load = loads.start(o_hbm, o)
    h_load = loads.start(h_hbm, h)
    dmid_load = loads.start(dmid_hbm, dmid)
    greet()
    w_load.wait()

    def fill(r):
        heads = [dq[r, :, n * LANES : (n + 1) * LANES].astype(F32) for n in range(2)]
        heads.append(turn(dk[r], cosine[r], -sine[r]))
        lanes = three_lanes([close_halves(head) for head in heads] + [dv[r]])
        for n in range(3):
            dqkv[r, :, n * LANES : (n + 1) * LANES] = lanes[n].astype(BF)
        parts[r] = dot_nt(dqkv[r], w[:, :QKV]).astype(BF)

    count = a1.shape[2] // step

    def beside(turn_number):
        if turn_number == 0:
            a1_load.wait()
            dat_load.wait()
            o_load.wait()
        half = (count + 1) // 2
        for number in range(turn_number * half, min((turn_number + 1) * half, count)):
            at = slice(number * step, (number + 1) * step)
            sums[at, :QKV] = flat_tn(a1, at, dqkv).astype(BF)
            sums[at, QKV:GAIN_AT] = flat_tn(dat, at, o).astype(BF)

    net = Scatter(here, parts, total, (from_c, via_x, via_y, from_x, from_y), (send, recv), fill).run(beside)
    h_load.wait()
    dmid_load.wait()
    da1 = total[...]
    x = h[...].astype(F32)
    r1 = inverse_of(x)
    n1 = x * r1
    e_out[...] = (dmid[...] + norm_back(da1, n1, r1, gain[0:1, :])).astype(BF)
    gain_rows[...] = jnp.zeros_like(gain_rows)
    first = GAIN_AT - PACK + LANES
    gain_rows[first : first + 1, :] = jnp.sum(da1 * n1, axis=0, keepdims=True)
    gain_rows[first + 1 : first + 2, :] = gain2_grad[...]
    columns = gain_rows[...].T
    last = sums[:, PACK - LANES :].astype(F32)
    sums[:, PACK - LANES :] = jnp.where(lane(last) < first, last, columns).astype(BF)
    net.drain()


def attn_back(h, dmid, gain, gain2_grad, dq, dk, dv, cosine, sine, o, a1, dat, w):
    block, width = h.shape
    step = math.gcd(width, 256)
    return plane_call(
        functools.partial(attn_back_kernel, step),
        "attn_back",
        3,
        [
            jax.ShapeDtypeStruct((block, width), BF),
            jax.ShapeDtypeStruct((width, PACK), BF),
        ],
        [IN_VMEM, IN_VMEM],
        [IN_VMEM] * 7 + [ANYWHERE] * 6,
        [
            pltpu.VMEM((8, block, width), BF),
            pltpu.VMEM(h.shape, h.dtype),
            pltpu.VMEM(dmid.shape, dmid.dtype),
            pltpu.VMEM(o.shape, o.dtype),
            pltpu.VMEM((8, block, width), BF),
            pltpu.VMEM((8, block, width), BF),
            pltpu.VMEM(w.shape, BF),
            pltpu.VMEM((8, block, QKV), BF),
            pltpu.VMEM((LANES, width), F32),
            pltpu.VMEM((block, width), F32),
        ]
        + scatter_scratch(block, width)
        + [pltpu.SemaphoreType.DMA((6,))],
        36,
        gain, gain2_grad, dq, dk, dv, cosine, sine, h, dmid, o, a1, dat, w,
    )


def exchange_kernel(homeward, blocks, got, send_sem, recv_sem, local, swap=None):
    here = place()
    x, c, y = here
    swap = swap and Swap(homeward, *swap)
    masks = [(dx, dc, dy) for dx in range(2) for dc in range(2) for dy in range(2)][1:]
    peer = lambda mask: {"x": flip(x, mask[0]), "c": flip(c, mask[1]), "y": flip(y, mask[2])}
    own = rank_of(here, 0, 0, 0)
    mine = pltpu.make_async_copy(blocks.at[own], got.at[own], local)
    mine.start()
    barrier = pltpu.get_barrier_semaphore()
    for mask in masks:
        pl.semaphore_signal(barrier, inc=1, device_id=peer(mask), device_id_type=MESH)
    if swap is None:
        pl.semaphore_wait(barrier, 7)
    else:
        swap.greet(barrier)
        swap.met(barrier, 7)
        swap.start()

    def copy(n, src, dst):
        return pltpu.make_async_remote_copy(
            src_ref=src,
            dst_ref=dst,
            send_sem=send_sem.at[n],
            recv_sem=recv_sem.at[n],
            device_id=peer(masks[n]),
            device_id_type=MESH,
        )

    copies = [copy(n, blocks.at[rank_of(here, *mask)], got.at[own]) for n, mask in enumerate(masks)]
    for started in copies:
        started.start()
    mine.wait()
    for n, mask in enumerate(masks):
        where = got.at[rank_of(here, *mask)]
        copy(n, where, where).wait_recv()
    for started in copies:
        started.wait_send()
    if swap is not None:
        swap.wait()


def exchange(number, blocks, moving=None, homeward=False):
    return plane_call(
        functools.partial(exchange_kernel, homeward),
        "exchange",
        number,
        [jax.ShapeDtypeStruct(blocks.shape, BF)],
        [ANYWHERE],
        [ANYWHERE],
        [pltpu.SemaphoreType.DMA((7,)), pltpu.SemaphoreType.DMA((7,)), pltpu.SemaphoreType.DMA],
        blocks.size // 40000,
        blocks,
        moving=moving,
    )


def finish_kernel(ff, got, gate, up, down):
    gate[...] = got[0, :, :ff].astype(F32)
    up[...] = got[0, :, ff : 2 * ff].astype(F32)
    down[...] = got[0, :, 2 * ff :].astype(F32)


def finish(got):
    ranks, rows, cols = got.shape
    ff = cols // 3
    return pl.pallas_call(
        functools.partial(finish_kernel, ff),
        grid=(ranks,),
        out_shape=[jax.ShapeDtypeStruct((rows, ranks * ff), F32)] * 3,
        in_specs=[pl.BlockSpec((1, rows, cols), lambda i: (i, 0, 0))],
        out_specs=[pl.BlockSpec((rows, ff), lambda i: (0, i))] * 3,
        compiler_params=pltpu.CompilerParams(vmem_limit_bytes=VMEM_LIMIT),
        name="finish",
    )(got)


def finish_attn_kernel(got, query, key, value, out, gains):
    ranks = got.shape[0]

    def lanes(t, n):
        return got[t, :, n * LANES : (n + 1) * LANES].astype(F32)

    groups = [four_heads(*(lanes(t, n) for n in range(3))) for t in range(ranks)]

    def write(ref, heads):
        for n in range(0, len(heads), 4):
            for j, part in enumerate(three_lanes(heads[n : n + 4])):
                at = n * HEAD_SIZE + j * LANES
                ref[:, at : at + LANES] = part

    write(query, [head for group in groups for head in group[:2]])
    write(key, [group[2] for group in groups])
    write(value, [group[3] for group in groups])
    out_heads = []
    total = None
    for t in range(ranks):
        a, b = lanes(t, 3), lanes(t, 4)
        out_heads += [a, pltpu.roll(jnp.where(lane(a) >= HEAD_SIZE, a, b), LANES - HEAD_SIZE, 1)]
        total = b if total is None else total + b
    write(out, out_heads)
    first = GAIN_AT - PACK + LANES
    gains[...] = total.T[first : first + 2]


def finish_attn(got):
    ranks, rows, _ = got.shape
    wide, narrow = jax.ShapeDtypeStruct((rows, ranks * OUT), F32), jax.ShapeDtypeStruct((rows, ranks * HEAD_SIZE), F32)
    return pl.pallas_call(
        finish_attn_kernel,
        out_shape=[wide, narrow, narrow, wide, jax.ShapeDtypeStruct((2, rows), F32)],
        in_specs=[IN_VMEM],
        out_specs=[IN_VMEM] * 5,
        compiler_params=pltpu.CompilerParams(vmem_limit_bytes=VMEM_LIMIT),
        name="finish_attn",
    )(got)


LOWER=-1e30
def dot(a, b, dims):
    return lax.dot_general(a, b, (dims, ((), ())), preferred_element_type=F32)

def attend_kernel(scale2, bq, bk, bounds, length, q, k, v, qpos, out, lse):
    groups = q.shape[0]
    i = pl.program_id(0)
    rows = groups * bq
    qs = q[...].reshape(rows, LANES)
    pos = qpos[0]
    pos2 = jnp.concatenate([pos] * groups, axis=1)
    def step(masked, j, state):
        top, total, acc = state
        at = pl.ds(pl.multiple_of(j * bk, bk), bk)
        s = dot(k[at, :], qs, ((1,), (1,)))
        if masked:
            kp = j * bk + lax.broadcasted_iota(jnp.int32, (bk, 1), 0)
            ok = (kp <= pos2) & (kp < length[0])
            s = jnp.where(ok, s, LOWER)
        new = jnp.maximum(top, jnp.max(s, axis=0, keepdims=True) * scale2)
        p = jnp.exp2(s * scale2 - new)
        alpha = jnp.exp2(top - new)
        total = total * alpha + jnp.sum(p, axis=0, keepdims=True)
        acc = acc * alpha + dot(v[at, :], p.astype(BF), ((0,), (0,)))
        return new, total, acc
    state = (jnp.full((1, rows), LOWER, F32), jnp.zeros((1, rows), F32), jnp.zeros((LANES, rows), F32))
    full, end = bounds[0, i], bounds[1, i]
    state = lax.fori_loop(0, full, functools.partial(step, False), state)
    top, total, acc = lax.fori_loop(full, end, functools.partial(step, True), state)
    o = (acc / total).T
    first, second = o[:bq], pltpu.roll(o[bq:], HEAD_SIZE, 1)
    out[:, :LANES] = jnp.where(lane(first) < HEAD_SIZE, first, second).astype(BF)
    out[:, LANES:] = second[:, : OUT - LANES].astype(BF)
    lse[...] = (top + jnp.log2(total))[None]

def attend(q, k, v, qpos, bounds, length, bq, bk, scale2):
    groups, tokens, _ = q.shape
    n = tokens // bq
    out, lse = pl.pallas_call(
        functools.partial(attend_kernel, scale2, bq, bk),
        grid_spec=pltpu.PrefetchScalarGridSpec(
            num_scalar_prefetch=2, grid=(n,),
            in_specs=[
                pl.BlockSpec((groups, bq, LANES), lambda i, *_: (0, i, 0)),
                pl.BlockSpec(k.shape, lambda i, *_: (0, 0)),
                pl.BlockSpec(v.shape, lambda i, *_: (0, 0)),
                pl.BlockSpec((1, 1, bq), lambda i, *_: (i, 0, 0)),
            ],
            out_specs=[
                pl.BlockSpec((bq, OUT), lambda i, *_: (i, 0)),
                pl.BlockSpec((1, 1, groups * bq), lambda i, *_: (i, 0, 0)),
            ]),
        out_shape=[jax.ShapeDtypeStruct((tokens, OUT), BF), jax.ShapeDtypeStruct((n, 1, groups * bq), F32)],
        compiler_params=pltpu.CompilerParams(vmem_limit_bytes=VMEM_LIMIT),
        name="attend",
        cost_estimate=pl.CostEstimate(flops=0, bytes_accessed=45000000, transcendentals=0),
    )(bounds, length, q, k, v, qpos)
    return out, lse

def back_kernel(scale, scale2, bq, bk, bounds, length, q, k, v, qpos, o, do, lse, cosine, sine, dq, dk, dv):
    groups = q.shape[0]
    i = pl.program_id(0)
    @pl.when(i == 0)
    def _():
        dk[...] = jnp.zeros_like(dk)
        dv[...] = jnp.zeros_like(dv)
    qs = q[...].reshape(groups * bq, LANES)
    do0, do1 = do[:, :LANES].astype(F32), do[:, LANES : 2 * LANES].astype(F32)
    at = lane(do0)
    do1 = pltpu.roll(jnp.where(at >= HEAD_SIZE, do0, do1), LANES - HEAD_SIZE, 1)
    wide = jnp.concatenate([jnp.where(at < HEAD_SIZE, do0, 0.0), jnp.where(at < HEAD_SIZE, do1, 0.0)], axis=0)
    dos = wide.astype(BF)
    o0 = o[:, :LANES].astype(F32)
    o1 = jnp.concatenate([o[:, LANES:].astype(F32), jnp.zeros((bq, 2 * LANES - OUT), F32)], axis=1)
    o1 = pltpu.roll(jnp.where(at >= HEAD_SIZE, o0, o1), LANES - HEAD_SIZE, 1)
    delta = jnp.sum(wide * jnp.concatenate([o0, o1], axis=0), axis=1, keepdims=True).reshape(1, groups * bq)
    lse_row = lse[0]
    pos = qpos[0]
    pos2 = jnp.concatenate([pos] * groups, axis=1)
    def step(masked, j, acc):
        at = pl.ds(pl.multiple_of(j * bk, bk), bk)
        kb, vb = k[at, :], v[at, :]
        s = dot(kb, qs, ((1,), (1,)))
        p = jnp.exp2(s * scale2 - lse_row)
        if masked:
            kp = j * bk + lax.broadcasted_iota(jnp.int32, (bk, 1), 0)
            ok = (kp <= pos2) & (kp < length[0])
            p = jnp.where(ok, p, 0.0)
        dp = dot(vb, dos, ((1,), (1,)))
        ds = (p * (dp - delta)).astype(BF)
        dv[at, :] += dot(p.astype(BF), dos, ((1,), (0,)))
        dk[at, :] += dot(ds, qs, ((1,), (0,))) * scale
        return acc + dot(ds, kb, ((0,), (0,)))
    full, end = bounds[0, i], bounds[1, i]
    acc = jnp.zeros((groups * bq, LANES), F32)
    acc = lax.fori_loop(0, full, functools.partial(step, False), acc)
    acc = lax.fori_loop(full, end, functools.partial(step, True), acc) * scale
    for g in range(groups):
        dq[:, g * LANES:(g + 1) * LANES] = turn(acc[g * bq:(g + 1) * bq], cosine[...], -sine[...]).astype(BF)

def attend_back(q, k, v, qpos_row, o, do, lse, cosine, sine, bounds, length, bq, bk, scale, scale2):
    groups, tokens, _ = q.shape
    n = tokens // bq
    wide = pl.BlockSpec((bq, groups * LANES), lambda i, *_: (i, 0))
    narrow = pl.BlockSpec((bq, OUT), lambda i, *_: (i, 0))
    return pl.pallas_call(
        functools.partial(back_kernel, scale, scale2, bq, bk),
        grid_spec=pltpu.PrefetchScalarGridSpec(
            num_scalar_prefetch=2, grid=(n,),
            in_specs=[
                pl.BlockSpec((groups, bq, LANES), lambda i, *_: (0, i, 0)),
                pl.BlockSpec(k.shape, lambda i, *_: (0, 0)),
                pl.BlockSpec(v.shape, lambda i, *_: (0, 0)),
                pl.BlockSpec((1, 1, bq), lambda i, *_: (i, 0, 0)),
                narrow, wide,
                pl.BlockSpec((1, 1, groups * bq), lambda i, *_: (i, 0, 0)),
                pl.BlockSpec((bq, LANES), lambda i, *_: (i, 0)),
                pl.BlockSpec((bq, LANES), lambda i, *_: (i, 0)),
            ],
            out_specs=[wide, pl.BlockSpec(k.shape, lambda i, *_: (0, 0)), pl.BlockSpec(k.shape, lambda i, *_: (0, 0))]),
        out_shape=[jax.ShapeDtypeStruct((tokens, groups * LANES), BF), jax.ShapeDtypeStruct(k.shape, F32), jax.ShapeDtypeStruct(k.shape, F32)],
        compiler_params=pltpu.CompilerParams(vmem_limit_bytes=VMEM_LIMIT),
        name="attend_back",
        cost_estimate=pl.CostEstimate(flops=0, bytes_accessed=65000000, transcendentals=0),
    )(bounds, length, q, k, v, qpos_row, o, do, lse, cosine, sine)

def bounds_of(positions, length, bq, bk):
    p = positions.reshape(-1, bq)
    lo = jnp.minimum(jnp.min(p, axis=1) + 1, length) // bk
    hi = -(-jnp.minimum(jnp.max(p, axis=1) + 1, length) // bk)
    return jnp.stack([lo, hi]).astype(jnp.int32)


PLANE = ("x", "c", "y")

def together(*arrays):
    return lax.optimization_barrier(arrays)


def body(
    inputs,
    lengths,
    cotangent,
    attn_gain,
    w_query,
    key_projection,
    value_projection,
    w_out,
    mlp_gain,
    w_gate,
    w_up,
    w_down,
):
    sections = lax.axis_size("x") * lax.axis_size("c")
    planes = lax.axis_size("z")
    halves = lax.axis_size("y")
    extra = lax.axis_size("e")
    ranks = sections * halves
    layers = sections
    block = inputs.shape[1]
    width = inputs.shape[2]
    rows = w_query.shape[1]
    tokens = block * ranks
    all_tokens = tokens * extra
    head_group = QUERY_HEADS // KEY_VALUE_HEADS
    q_cols = head_group * HEAD_SIZE
    kv_cols = HEAD_SIZE
    ff_cols = FF // ranks
    scale = 1.0 / math.sqrt(HEAD_SIZE)
    scale2 = scale * math.log2(math.e)

    def by_rank(matrix):
        return matrix.reshape(rows, ranks, -1)

    attn_pack = jnp.concatenate(
        [
            by_rank(w_query[0]),
            by_rank(key_projection[0]),
            by_rank(value_projection[0]),
            by_rank(w_out[0].T),
            jnp.broadcast_to(jnp.stack([attn_gain[0], mlp_gain[0]], axis=1)[:, None, :], (rows, ranks, 2)),
            jnp.zeros((rows, ranks, PACK - GAIN_AT - 2), F32),
        ],
        axis=2,
    )
    def by_layer(got):
        return got.reshape(layers, halves, rows, -1)

    def ready(pack):
        return jnp.swapaxes(pack.astype(BF), 0, 1)

    def whole(part):
        if extra > 1:
            part = lax.all_gather(part, "e", axis=1, tiled=False)
        return lax.all_gather(part.reshape(-1, part.shape[-1]), "z", axis=0, tiled=True)

    def reduce_rows(sums):
        mine = lax.psum_scatter(sums, "z", scatter_dimension=0, tiled=True)
        mine = mine.reshape(halves, extra, rows, -1)
        if extra > 1:
            return lax.psum_scatter(mine, "e", scatter_dimension=1, tiled=False)
        return mine[:, 0]

    cut = 3 * ff_cols // 2
    (attn_got,) = exchange(4, ready(attn_pack))
    gate, up, down, attn_got = together(w_gate[0], w_up[0], w_down[0].T, attn_got)
    mlp_blocks = ready(jnp.concatenate([by_rank(gate), by_rank(up), by_rank(down)], axis=2))
    (first_got,) = exchange(5, mlp_blocks[..., :cut])

    token_x, token_c, token_y = token_place()
    rank = (token_x * 2 + token_c) * halves + token_y
    spot = lax.axis_index("e")
    length = lengths[micro_of_plane()]

    block_start = (jnp.arange(ranks) * extra + spot) * block
    positions = (block_start[:, None] + jnp.arange(block)[None, :]).reshape(tokens)
    exponents = 2.0 * jnp.arange(HEAD_SIZE // 2).astype(F32) / HEAD_SIZE
    angles = positions.astype(F32)[:, None] * (THETA ** (-exponents))[None, :]
    table = lambda values: jnp.pad(values, ((0, 0), (0, LANES // 2 - HALF)))
    cosine = jnp.concatenate([table(jnp.cos(angles))] * 2, axis=1)
    sine = jnp.concatenate([table(-jnp.sin(angles)), table(jnp.sin(angles))], axis=1)
    bq = math.gcd(tokens, 512)
    bk = math.gcd(all_tokens, 512)
    bounds = bounds_of(positions, length, bq, bk)
    length1 = length.reshape(1)
    query_rows = positions.astype(jnp.int32).reshape(-1, 1, bq)

    def all_keys(array):
        if extra == 1:
            return array
        stacked = lax.all_gather(array.reshape(ranks, block, -1), "e", axis=1, tiled=False)
        return stacked.reshape(all_tokens, -1)

    def own_keys(array):
        if extra == 1:
            return array
        stacked = array.astype(BF).reshape(ranks, extra, block, -1)
        return lax.psum_scatter(stacked, "e", scatter_dimension=1, tiled=False).reshape(tokens, -1).astype(F32)

    cosine3 = cosine.reshape(ranks, block, LANES)
    sine3 = sine.reshape(ranks, block, LANES)

    second_blocks, first_got, cosine, sine, cosine3, sine3, bounds, query_rows = together(
        mlp_blocks[..., cut:], first_got, cosine, sine, cosine3, sine3, bounds, query_rows
    )
    second_got, hidden_state = exchange(6, second_blocks, inputs[0])
    attn_parts, first_parts, second_parts = by_layer(attn_got), by_layer(first_got), by_layer(second_got)

    def flat(array):
        return array.reshape(tokens, array.shape[-1])

    saved = []
    attn_w, w_1 = whole(attn_parts[0]), whole(first_parts[0])
    hidden_state, attn_w, w_1, second_part = together(hidden_state, attn_w, w_1, second_parts[0])
    w_2 = whole(second_part)
    for layer in range(layers):
        a1, q, k, v, gain = attn_in(hidden_state, attn_w, cosine3, sine3)
        q, k, v = q.reshape(head_group, tokens, LANES), all_keys(flat(k)), all_keys(flat(v))
        o, log_total = attend(q, k, v, query_rows, bounds, length1, bq, bk, scale2)
        if layer + 1 < layers:
            o, attn_part, first_part = together(o, attn_parts[layer + 1], first_parts[layer + 1])
            next_attn, next_1 = whole(attn_part), whole(first_part)
        mid, a2, gu, hid, after_mlp, *moved = mlp(
            hidden_state, o.reshape(ranks, block, -1), gain, attn_w, w_1, w_2,
            cotangent[0] if layer + 1 == layers else None,
        )
        saved.append((hidden_state, a1, q, k, v, o, log_total, mid, a2, gu, hid, attn_w, w_1, w_2, gain))
        hidden_state = after_mlp
        if layer + 1 < layers:
            hidden_state, attn_w, w_1, second_part = together(hidden_state, next_attn, next_1, second_parts[layer + 1])
            w_2 = whole(second_part)
    output = hidden_state

    my_positions = (rank * extra + spot) * block + jnp.arange(block)
    (e,) = moved
    e = jnp.where((my_positions < length)[:, None], e, jnp.zeros_like(e))
    attn_grads = [None] * layers
    mlp_grads = [None] * layers
    for layer in reversed(range(layers)):
        (h, a1, q, k, v, o, log_total, mid, a2, gu, hid, attn_w, w_1, w_2, gain) = saved[layer]
        dmid, gain2, dat, mlp_sums, *moved = mlp_back(
            e, mid, gain, gu, hid, a2, w_1, w_2, output if layer + 1 == layers else None
        )
        if moved:
            (output,) = moved
        else:
            dat, mlp_sums, attn_grads[layer + 1] = together(dat, mlp_sums, attn_grads[layer + 1])
        mlp_grads[layer] = reduce_rows(mlp_sums)
        dat, dob = dat_gather(dat, attn_w)
        dq, dk, dv = attend_back(
            q, k, v, query_rows, o, flat(dob), log_total, cosine, sine, bounds, length1, bq, bk, scale, scale2
        )
        dk, dv = own_keys(dk), own_keys(dv)
        e, attn_sums = attn_back(
            h, dmid, gain, gain2, *(array.reshape(ranks, block, -1) for array in (dq, dk, dv)), cosine3, sine3,
            o.reshape(ranks, block, -1), a1, dat, attn_w,
        )
        e, attn_sums, mlp_grads[layer] = together(e, attn_sums, mlp_grads[layer])
        attn_grads[layer] = reduce_rows(attn_sums)

    def by_place(grads):
        return jnp.stack(grads).reshape(ranks, rows, -1)

    mlp_home, input_grad = exchange(7, by_place(mlp_grads), e, True)
    attn_blocks, mlp_home = together(by_place(attn_grads), mlp_home)
    (attn_home,) = exchange(10, attn_blocks)
    grad_gate, grad_up, grad_down = finish(mlp_home)
    grad_query, grad_key, grad_value, grad_out, gain_sums = finish_attn(attn_home)
    return (
        output[None],
        input_grad[None],
        gain_sums[0:1],
        grad_query[None],
        grad_key[None],
        grad_value[None],
        grad_out.T[None],
        gain_sums[1:2],
        grad_gate[None],
        grad_up[None],
        grad_down.T[None],
    )


def solution(mesh):
    section, seq = mesh.devices.shape
    halves = KEY_VALUE_HEADS // section
    extra = seq // (section * halves)
    fine = Mesh(
        mesh.devices.reshape(section // 2, 2, section, halves, extra), ("x", "c", "z", "y", "e")
    )
    sec, sq = ("x", "c"), ("z", "y", "e")
    rows3 = P(sec, sq, None)
    cols3 = P(sec, None, sq)
    in_specs = (rows3, P(), rows3, P(sec, sq), rows3, rows3, rows3, cols3, P(sec, sq), rows3, rows3, cols3)
    out_specs = (rows3, rows3, P(sec, sq), rows3, rows3, rows3, cols3, P(sec, sq), rows3, rows3, cols3)
    return jax.shard_map(body, mesh=fine, in_specs=in_specs, out_specs=out_specs, check_vma=False)
```
